32 devices in a mesh: wide: 16 (over z, y, core), narrow: 2 (over x).
Axes of the slice: x: 2, y: 2, z: 4, core: 2. Of those that a mesh axis runs over, the one named last changes fastest.
Arguments:
- tokens: bfloat16 [384, 128, 512], P(('wide', 'narrow')), may hold values from -6 to 6
- memory: bfloat16 [384, 256, 512], P(('wide', 'narrow')), may hold values from -6 to 6
- cotangent: bfloat16 [384, 128, 512], P(('wide', 'narrow')), may hold values from -6 to 6
- dec_segments: int32 [384, 128], P(('wide', 'narrow')), may hold values from 0 to 3, never falling along the last dimension, each value on 1 to 64 neighbouring positions
- mem_segments: int32 [384, 256], P(('wide', 'narrow')), may hold values from 0 to 3, never falling along the last dimension, each value on 1 to 128 neighbouring positions
- padding: int32 [384, 128], P(('wide', 'narrow')), may hold values 0 or 1
- buckets: int32 [128], replicated, may hold values from 0 to 31, as said below
- w_query: bfloat16 [512, 512], P(('wide', 'narrow')), may hold values from -0.03125 to 0.03125
- w_key: bfloat16 [512, 512], P(('wide', 'narrow')), may hold values from -0.25 to 0.25
- w_value: bfloat16 [512, 512], P(('wide', 'narrow')), may hold values from -0.25 to 0.25
- w_out: bfloat16 [512, 512], P(('wide', 'narrow')), may hold values from -1 to 1
- c_query: bfloat16 [512, 512], P(('wide', 'narrow')), may hold values from -0.03125 to 0.03125
- c_key: bfloat16 [512, 512], P(('wide', 'narrow')), may hold values from -0.25 to 0.25
- c_value: bfloat16 [512, 512], P(('wide', 'narrow')), may hold values from -0.25 to 0.25
- c_out: bfloat16 [512, 512], P(('wide', 'narrow')), may hold values from -1.5 to 1.5
- w_hidden: bfloat16 [512, 2048], P(('wide', 'narrow')), may hold values from -0.25 to 0.25
- w_back: bfloat16 [2048, 512], P(('wide', 'narrow')), may hold values from -0.1875 to 0.1875
- gain_self: bfloat16 [512], P(('wide', 'narrow')), may hold values from 0.2 to 4
- gain_cross: bfloat16 [512], P(('wide', 'narrow')), may hold values from 0.2 to 4
- gain_ff: bfloat16 [512], P(('wide', 'narrow')), may hold values from 0.2 to 4
- bias_table: bfloat16 [256], P(('wide', 'narrow')), may hold values from -4 to 4
Outputs:
- result: bfloat16 [384, 128, 512], P(('wide', 'narrow'))
- grad_tokens: bfloat16 [384, 128, 512], P(('wide', 'narrow'))
- grad_memory: bfloat16 [384, 256, 512], P(('wide', 'narrow'))
- grad_w_query: float32 [512, 512], P(('wide', 'narrow'))
- grad_w_key: float32 [512, 512], P(('wide', 'narrow'))
- grad_w_value: float32 [512, 512], P(('wide', 'narrow'))
- grad_w_out: float32 [512, 512], P(('wide', 'narrow'))
- grad_c_query: float32 [512, 512], P(('wide', 'narrow'))
- grad_c_key: float32 [512, 512], P(('wide', 'narrow'))
- grad_c_value: float32 [512, 512], P(('wide', 'narrow'))
- grad_c_out: float32 [512, 512], P(('wide', 'narrow'))
- grad_w_hidden: float32 [512, 2048], P(('wide', 'narrow'))
- grad_w_back: float32 [2048, 512], P(('wide', 'narrow'))
- grad_gain_self: float32 [512], P(('wide', 'narrow'))
- grad_gain_cross: float32 [512], P(('wide', 'narrow'))
- grad_gain_ff: float32 [512], P(('wide', 'narrow'))
- grad_bias_table: float32 [256], P(('wide', 'narrow'))
- example_norms: float32 [384, 4], P(('wide', 'narrow'))
- global_norm: float32 [], replicated
The draws below stay inside these ranges and needn't reach their ends.
Inputs may be any that keep to these rules, and one draw needn't show every extreme that they name: buckets never falls as the distance grows; buckets[0] = 0 and buckets[127] = 31. `dec_segments`: along a row the example numbers never fall; each of the 4 examples has 1 to 64 decoder tokens. `mem_segments`: along a row the example numbers never fall; each of the 4 examples has 1 to 128 memory tokens.
All inputs are finite; a program needn't handle non-finite values. No bound on the sum of `padding` on one device may be relied on, other than what follows from the above.
Results may differ from the reference program's by a relative error of at most 0.014.
Values may be sent and summed in bfloat16 or wider, within the bound.
No kernel may reach another device: no remote copies, remote signals or barrier semaphores. Data moves between devices by JAX's collectives and lax.ppermute only.
A program may use at most 192 MiB of HBM per device.

```python
import math
import jax
import jax.numpy as jnp
import numpy as np
from jax import lax

D = 512
FF = 2048
H = 8
DH = 64
NB = 32
LEN = 128
MEM = 256
NSEG = 4
SEQ_DEV = 12
ROWS = 384
COUNT = 4196096


def draw_buckets(key, part):
    key = jax.random.fold_in(key, 7)
    values = jnp.sort(jax.random.randint(key, (LEN,), 0, NB, dtype=jnp.int32))
    positions = jnp.arange(LEN, dtype=jnp.int32)
    values = jnp.where(positions == 0, 0, values)
    values = jnp.where(positions == LEN - 1, NB - 1, values)
    return values.astype(jnp.int32)


def rising_gain(key, start, finish, rough_lo, rough_hi):
    fraction = jnp.arange(D, dtype=jnp.float32) / (D - 1)
    trend = start * jnp.exp(fraction * jnp.log(finish / start))
    rough = jax.random.uniform(key, (D,), jnp.float32, rough_lo, rough_hi)
    return trend * rough


def draw_gain_self(key, part):
    key = jax.random.fold_in(key, 11)
    return rising_gain(key, 0.5, 2.0, 0.8, 1.25).astype(jnp.bfloat16)


def draw_gain_cross(key, part):
    key = jax.random.fold_in(key, 13)
    return rising_gain(key, 0.5, 2.0, 0.8, 1.25).astype(jnp.bfloat16)


def draw_gain_ff(key, part):
    key = jax.random.fold_in(key, 17)
    return rising_gain(key, 0.5, 2.0, 0.8, 1.25).astype(jnp.bfloat16)


def blend_rows(noise, common_key, scale_key, share, spread):
    count = noise.shape[0]
    width = noise.shape[2]
    common = jax.random.normal(common_key, (count, 1, width), jnp.float32)
    exponent = jax.random.uniform(scale_key, (count, 1, 1), jnp.float32, -1.0, 1.0)
    row_scale = jnp.exp(exponent * jnp.log(jnp.float32(spread)))
    mixed = jnp.sqrt(1.0 - share) * noise + jnp.sqrt(share) * common
    return jnp.clip(row_scale * mixed, -6.0, 6.0)


def draw_tokens(key, part):
    key = jax.random.fold_in(key, 19)
    noise_key, common_key, scale_key = jax.random.split(key, 3)
    noise = jax.random.normal(noise_key, (ROWS, LEN, D), jnp.float32)
    return blend_rows(noise, common_key, scale_key, 0.3, 1.0).astype(jnp.bfloat16)


def draw_memory(key, part):
    key = jax.random.fold_in(key, 23)
    noise_key, common_key, scale_key = jax.random.split(key, 3)
    noise = jax.random.normal(noise_key, (ROWS, MEM, D), jnp.float32)
    return blend_rows(noise, common_key, scale_key, 0.3, 1.0).astype(jnp.bfloat16)


def draw_cotangent(key, part):
    key = jax.random.fold_in(key, 29)
    noise_key, common_key, scale_key = jax.random.split(key, 3)
    noise = jax.random.normal(noise_key, (ROWS, LEN, D), jnp.float32)
    return blend_rows(noise, common_key, scale_key, 0.3, 1.0).astype(jnp.bfloat16)


def touch_ends(values, rng, smallest, top_value):
    longest = values.shape.index(max(values.shape))
    spots = []
    for shift in (0, 1):
        where = [jax.random.randint(jax.random.fold_in(rng, axis), (), 0, length) for axis, length in enumerate(values.shape)]
        where[longest] = (where[longest] + shift) % values.shape[longest]
        spots.append(tuple(where))
    return values.at[spots[0]].set(smallest).at[spots[1]].set(top_value)


def shard_levels(stream_key, extent, pieces, least, high):
    level, own = 1.0, jax.random.fold_in(stream_key, 6)
    for dim, parts in pieces:
        heights = jnp.exp(jax.random.uniform(jax.random.fold_in(own, dim), (parts,), jnp.float32, least / len(pieces), high / len(pieces)))
        level = level * jnp.repeat(heights, extent[dim] // parts).reshape([-1 if axis == dim else 1 for axis in range(len(extent))])
    return level


def split_up(number_of, total, reach, skew):
    weights = [(1 << 20) // math.isqrt(grade ** skew) + 1 for grade in range(2, number_of + 1)]
    surplus, given = total - reach - (number_of - 1), [1] * (number_of - 1)
    while surplus > 0:
        candidates = [i for i in range(number_of - 1) if given[i] < reach]
        pool, budget = sum([weights[i] for i in candidates]), surplus
        for i in candidates:
            extra = min(reach - given[i], max(1, budget * weights[i] // pool), surplus)
            given[i] = given[i] + extra
            surplus = surplus - extra
    return np.array([reach] + given)


def uneven(rng, amount, total, most, slope):
    if amount == 2:
        one = jax.random.randint(rng, (), max(1, total - most), min(most, total - 1) + 1)
        return jnp.stack([one, total - one])
    lengths = jnp.asarray(split_up(amount, total, most, slope), jnp.int32)
    twos = (amount - 1) // 2
    source_of, sink = lengths[1:1 + 2 * twos:2], lengths[2:2 + 2 * twos:2]
    slack = jnp.minimum(source_of - 1, most - sink)
    moved = jax.random.randint(jax.random.fold_in(rng, 1), (twos,), 0, 1 << 20) % (slack + 1)
    lengths = lengths.at[1:1 + 2 * twos:2].set(source_of - moved).at[2:2 + 2 * twos:2].set(sink + moved)
    return lengths[jax.random.permutation(jax.random.fold_in(rng, 2), amount)]


def bell_draw(own_key, dims, scale, bound, cuts=(), kind=jnp.bfloat16):
    level = shard_levels(own_key, dims, cuts, -0.22, 0.18) if cuts else 1.0
    entries = jax.random.normal(own_key, dims, jnp.float32) * scale * level
    return jnp.minimum(jnp.maximum(entries, -bound), bound).astype(kind)


def setup_inputs(seed: int = 0) -> dict:
    key_list = jax.random.split(jax.random.key(seed), 22)
    return {
        "tokens": draw_tokens(jax.random.fold_in(key_list[21], 71), 0),
        "memory": draw_memory(jax.random.fold_in(key_list[21], 71), 0),
        "cotangent": draw_cotangent(jax.random.fold_in(key_list[21], 71), 0),
        "dec_segments": jax.vmap(lambda own: jnp.searchsorted(jnp.cumsum(uneven(own, NSEG, LEN, LEN // 2, 1)), jnp.arange(LEN), side="right"))(jax.random.split(key_list[3], ROWS)).reshape((ROWS, LEN)).astype(jnp.int32),
        "mem_segments": jax.vmap(lambda own: jnp.searchsorted(jnp.cumsum(uneven(own, NSEG, MEM, MEM // 2, 1)), jnp.arange(MEM), side="right"))(jax.random.split(key_list[4], ROWS)).reshape((ROWS, MEM)).astype(jnp.int32),
        "padding": touch_ends((jax.random.randint(key_list[5], (ROWS, LEN), 0, 8) < 7).astype(jnp.int32), jax.random.fold_in(key_list[5], 1), 0, 1),
        "buckets": draw_buckets(jax.random.fold_in(key_list[21], 71), 0),
        "w_query": bell_draw(key_list[7], (D, H * DH), (D * DH) ** -0.5, 0.03125, ((0, 32),)),
        "w_key": bell_draw(key_list[8], (D, H * DH), D ** -0.5, 0.25, ((0, 32),)),
        "w_value": bell_draw(key_list[9], (D, H * DH), D ** -0.5, 0.25, ((0, 32),)),
        "w_out": bell_draw(key_list[10], (H * DH, D), (H * DH // 16) ** -0.5, 1.0, ((0, 32),)),
        "c_query": bell_draw(key_list[11], (D, H * DH), (D * DH) ** -0.5, 0.03125, ((0, 32),)),
        "c_key": bell_draw(key_list[12], (D, H * DH), D ** -0.5, 0.25, ((0, 32),)),
        "c_value": bell_draw(key_list[13], (D, H * DH), D ** -0.5, 0.25, ((0, 32),)),
        "c_out": bell_draw(key_list[14], (H * DH, D), (H * DH // 32) ** -0.5, 1.5, ((0, 32),)),
        "w_hidden": bell_draw(key_list[15], (D, FF), D ** -0.5, 0.25, ((0, 32),)),
        "w_back": bell_draw(key_list[16], (FF, D), (FF // 2) ** -0.5, 0.1875, ((0, 32),)),
        "gain_self": draw_gain_self(jax.random.fold_in(key_list[21], 71), 0),
        "gain_cross": draw_gain_cross(jax.random.fold_in(key_list[21], 71), 0),
        "gain_ff": draw_gain_ff(jax.random.fold_in(key_list[21], 71), 0),
        "bias_table": bell_draw(key_list[20], (NB * H,), 1.0, 4.0, ((0, 32),)),
    }


@jax.custom_vjp
def low(v):
    return lax.optimization_barrier(v.astype(jnp.bfloat16)).astype(jnp.float32)

@jax.custom_vjp
def low_back(v):
    return v

def low_keep(v):
    return (low(v), None)

def low_pass(kept, grad):
    return (grad,)

def back_keep(v):
    return (v, None)

def back_low(kept, grad):
    return (low(grad),)
low.defvjp(low_keep, low_pass)
low_back.defvjp(back_keep, back_low)
maximal_precision_mode = lax.Precision.HIGHEST
epsilon = 1e-06
floor_score = -1e+30

def matmul(left, right):
    return jnp.einsum('...i,io->...o', left, right, precision=maximal_precision_mode)

def rms_scale(values):
    return values * lax.rsqrt(lax.optimization_barrier(jnp.mean(values * values, axis=-1, keepdims=True)) + epsilon)

def split_heads(values):
    return values.reshape(values.shape[0], values.shape[1], H, DH)

def attend(queries, key_heads, values, biases, allowed):
    scores = low_back(jnp.einsum('gqhd,gkhd->ghqk', queries, key_heads, precision=maximal_precision_mode) + biases)
    scores = jnp.where(allowed[:, None], scores, floor_score)
    highest = lax.optimization_barrier(jnp.max(scores, axis=-1, keepdims=True))
    exponent = jnp.exp(scores - highest)
    weights = low(exponent / lax.optimization_barrier(jnp.sum(exponent, axis=-1, keepdims=True)))
    mixture = jnp.einsum('ghqk,gkhd->gqhd', weights, values, precision=maximal_precision_mode)
    return mixture.reshape(mixture.shape[0], mixture.shape[1], H * DH)

def layer(params, probes, inputs, memory_values, self_allowed, cross_allowed, indicator_matrix):
    w_query, w_key, w_value, w_out, c_query, c_key, c_value, c_out, w_hidden, w_back, gain_self, gain_cross, gain_ff, bias_table = params
    probe_na, probe_qa, probe_ka, probe_va, probe_scores, probe_oa, probe_nb, probe_qb, probe_kb, probe_vb, probe_ob, probe_nc, probe_hidden, probe_out = probes
    scaled_a = rms_scale(inputs)
    input_a = low(scaled_a * gain_self + probe_na)
    queries_a = split_heads(low(low_back(matmul(input_a, w_query) + probe_qa)))
    keys_a = split_heads(low(low_back(matmul(input_a, w_key) + probe_ka)))
    values_a = split_heads(low(low_back(matmul(input_a, w_value) + probe_va)))
    biases = jnp.einsum('qkn,nh->hqk', indicator_matrix, bias_table.reshape(NB, H), precision=maximal_precision_mode)[None] + probe_scores
    attended_a = low(low_back(attend(queries_a, keys_a, values_a, biases, self_allowed)))
    middle = inputs + low_back(matmul(attended_a, w_out) + probe_oa)
    scaled_b = rms_scale(middle)
    input_b = low(scaled_b * gain_cross + probe_nb)
    queries_b = split_heads(low(low_back(matmul(input_b, c_query) + probe_qb)))
    keys_b = split_heads(low(low_back(matmul(memory_values, c_key) + probe_kb)))
    values_b = split_heads(low(low_back(matmul(memory_values, c_value) + probe_vb)))
    attended_b = low(low_back(attend(queries_b, keys_b, values_b, 0.0, cross_allowed)))
    after_cross = middle + low_back(matmul(attended_b, c_out) + probe_ob)
    scaled_c = rms_scale(after_cross)
    input_c = low(scaled_c * gain_ff + probe_nc)
    hidden = low_back(matmul(input_c, w_hidden) + probe_hidden)
    activation = low(jax.nn.gelu(hidden, approximate=True))
    result = after_cross + low_back(matmul(activation, w_back) + probe_out)
    residual_values_kept = (input_a, attended_a, input_b, attended_b, input_c, activation, scaled_a, scaled_b, scaled_c)
    return (result, residual_values_kept)

def gram_rows(inputs, grads, same_seg, indicator_matrix):
    inner_dots = jnp.einsum('sid,sjd->sij', inputs, inputs, precision=maximal_precision_mode)
    outer_dots = sum((jnp.einsum('sio,sjo->sij', grad_piece, grad_piece, precision=maximal_precision_mode) for grad_piece in grads))
    per_token = lax.optimization_barrier(jnp.sum(jnp.where(same_seg, inner_dots * outer_dots, 0.0), axis=-1))
    return jnp.einsum('si,sie->se', per_token, indicator_matrix, precision=maximal_precision_mode)

def gain_rows(summand_pieces, indicator_matrix):
    example_wise_norms = jnp.einsum('aup,auv->avp', summand_pieces, indicator_matrix, precision=maximal_precision_mode)
    return lax.optimization_barrier(jnp.sum(example_wise_norms * example_wise_norms, axis=-1))

def table_rows(grad_scores, indicator_matrix, seg_onehot):
    per_bucket = jnp.einsum('ghqk,qkn->ghqn', grad_scores, indicator_matrix, precision=maximal_precision_mode)
    example_wise_norms = jnp.einsum('ghqn,gqe->gehn', per_bucket, seg_onehot, precision=maximal_precision_mode)
    return lax.optimization_barrier(jnp.sum(example_wise_norms * example_wise_norms, axis=(2, 3)))

def reference(tokens, memory, cotangent, dec_segments, mem_segments, padding, buckets, w_query, w_key, w_value, w_out, c_query, c_key, c_value, c_out, w_hidden, w_back, gain_self, gain_cross, gain_ff, bias_table):
    params = tuple((weight.astype(jnp.float32) for weight in (w_query, w_key, w_value, w_out, c_query, c_key, c_value, c_out, w_hidden, w_back, gain_self, gain_cross, gain_ff, bias_table)))
    positions = jnp.arange(LEN, dtype=jnp.int32)
    distance = jnp.clip(positions[:, None] - positions[None, :], 0, LEN - 1)
    indicator_matrix = (buckets[distance][..., None] == jnp.arange(NB, dtype=jnp.int32)).astype(jnp.float32)
    causal = positions[None, :] <= positions[:, None]
    diagonal = positions[None, :] == positions[:, None]
    groups = ROWS // SEQ_DEV

    def regroup(leaf_array):
        return leaf_array.reshape((groups, SEQ_DEV) + leaf_array.shape[1:])
    stacked = tuple((regroup(leaf_array) for leaf_array in (tokens, memory, cotangent, dec_segments, mem_segments, padding)))

    def group_step(totals, group):
        tokens_g, memory_g, cot_g, dec_g, mem_g, pad_g = group
        inputs = tokens_g.astype(jnp.float32)
        memory_values = memory_g.astype(jnp.float32)
        rows_here = inputs.shape[0]
        same_dec = dec_g[:, :, None] == dec_g[:, None, :]
        same_mem = mem_g[:, :, None] == mem_g[:, None, :]
        self_allowed = same_dec & causal[None] & ((pad_g[:, None, :] > 0) | diagonal[None])
        cross_allowed = dec_g[:, :, None] == mem_g[:, None, :]
        seg_onehot = (dec_g[..., None] == jnp.arange(NSEG, dtype=jnp.int32)).astype(jnp.float32)
        mem_onehot = (mem_g[..., None] == jnp.arange(NSEG, dtype=jnp.int32)).astype(jnp.float32)
        token_zero = jnp.zeros((rows_here, LEN, D), jnp.float32)
        head_zero = jnp.zeros((rows_here, LEN, H * DH), jnp.float32)
        mem_zero = jnp.zeros((rows_here, MEM, H * DH), jnp.float32)
        probes = (token_zero, head_zero, head_zero, head_zero, jnp.zeros((rows_here, H, LEN, LEN), jnp.float32), token_zero, token_zero, head_zero, mem_zero, mem_zero, token_zero, token_zero, jnp.zeros((rows_here, LEN, FF), jnp.float32), token_zero)
        result, pullback, residual_values_kept = jax.vjp(lambda weights, extras, values, mem_values: layer(weights, extras, values, mem_values, self_allowed, cross_allowed, indicator_matrix), params, probes, inputs, memory_values, has_aux=True)
        upstream = cot_g.astype(jnp.float32) * pad_g[..., None].astype(jnp.float32)
        grad_params, grad_probes, grad_inputs, grad_memory = pullback(upstream)
        input_a, attended_a, input_b, attended_b, input_c, activation, scaled_a, scaled_b, scaled_c = residual_values_kept
        grad_na, grad_qa, grad_ka, grad_va, grad_scores, grad_oa, grad_nb, grad_qb, grad_kb, grad_vb, grad_ob, grad_nc, grad_hidden, grad_out = grad_probes
        example_square = gram_rows(input_a, (grad_qa, grad_ka, grad_va), same_dec, seg_onehot)
        example_square = example_square + gram_rows(attended_a, (grad_oa,), same_dec, seg_onehot)
        example_square = example_square + gram_rows(input_b, (grad_qb,), same_dec, seg_onehot)
        example_square = example_square + gram_rows(memory_values, (grad_kb, grad_vb), same_mem, mem_onehot)
        example_square = example_square + gram_rows(attended_b, (grad_ob,), same_dec, seg_onehot)
        example_square = example_square + gram_rows(input_c, (grad_hidden,), same_dec, seg_onehot)
        example_square = example_square + gram_rows(activation, (grad_out,), same_dec, seg_onehot)
        example_square = example_square + gain_rows(grad_na * scaled_a, seg_onehot)
        example_square = example_square + gain_rows(grad_nb * scaled_b, seg_onehot)
        example_square = example_square + gain_rows(grad_nc * scaled_c, seg_onehot)
        example_square = example_square + table_rows(grad_scores, indicator_matrix, seg_onehot)
        example_square = example_square / COUNT
        new_totals = jax.tree.map(jnp.add, totals, grad_params)
        return (new_totals, (result.astype(jnp.bfloat16), grad_inputs.astype(jnp.bfloat16), grad_memory.astype(jnp.bfloat16), example_square))
    initial = tuple((jnp.zeros_like(weight) for weight in params))
    totals, outputs = lax.scan(group_step, initial, stacked)
    result, grad_tokens, grad_memory, example_norms = (leaf_array.reshape((ROWS,) + leaf_array.shape[2:]) for leaf_array in outputs)
    grad_w_query, grad_w_key, grad_w_value, grad_w_out, grad_c_query, grad_c_key, grad_c_value, grad_c_out, grad_w_hidden, grad_w_back, grad_gain_self, grad_gain_cross, grad_gain_ff, grad_bias_table = totals
    global_norm = sum((jnp.sum(weight * weight) for weight in totals)) / COUNT
    return (result, grad_tokens, grad_memory, grad_w_query, grad_w_key, grad_w_value, grad_w_out, grad_c_query, grad_c_key, grad_c_value, grad_c_out, grad_w_hidden, grad_w_back, grad_gain_self, grad_gain_cross, grad_gain_ff, grad_bias_table, example_norms, global_norm)
```

```python
from functools import partial

import jax
import jax.numpy as jnp
from jax import lax
from jax.sharding import PartitionSpec as P

H = 8
DH = 64
NB = 32
NSEG = 4
COUNT = 4196096


epsilon = 1e-06
floor_score = -1e30


def rms_scale(values):
    return values * lax.rsqrt(jnp.mean(values * values, axis=-1, keepdims=True) + epsilon)


def gelu_tanh(values):
    return jax.nn.gelu(values, approximate=True)


def product(left, right):
    return jnp.einsum("...i,io->...o", left, right, preferred_element_type=jnp.float32)


def back_product(grads, weight):
    return jnp.einsum("...o,io->...i", grads, weight, preferred_element_type=jnp.float32)


def weight_grad(inputs, grads):
    return jnp.einsum("sli,slo->io", inputs, grads, preferred_element_type=jnp.float32)


def by_blocks(function, arrays, row_block):
    shaped = jax.tree.map(
        lambda leaf_array: leaf_array.reshape(
            (leaf_array.shape[0] // row_block, row_block) + leaf_array.shape[1:]
        ),
        arrays,
    )
    results = lax.map(function, shaped)
    return jax.tree.map(
        lambda leaf_array: leaf_array.reshape(
            (leaf_array.shape[0] * leaf_array.shape[1],) + leaf_array.shape[2:]
        ),
        results,
    )


def attend_scores(queries, key_heads, allowed, biases):
    scores = (
        jnp.einsum("bqhd,bkhd->bhqk", queries, key_heads, preferred_element_type=jnp.float32)
        + biases
    )
    return jnp.where(allowed[:, None], scores, floor_score)


def attend_forward(biases, arrays):
    queries, key_heads, values, allowed = arrays
    scores = attend_scores(queries, key_heads, allowed, biases)
    highest = jnp.max(scores, axis=-1, keepdims=True)
    logarithm_partition_sum = highest + jnp.log(
        jnp.sum(jnp.exp(scores - highest), axis=-1, keepdims=True)
    )
    weights = jnp.exp(scores - logarithm_partition_sum).astype(jnp.bfloat16)
    mixture = jnp.einsum("bhqk,bkhd->bqhd", weights, values, preferred_element_type=jnp.float32)
    return (mixture.astype(jnp.bfloat16), logarithm_partition_sum[..., 0])


def attend_backward(biases, arrays):
    queries, key_heads, values, allowed, logarithm_partition_sum, grad_mixture = arrays
    scores = attend_scores(queries, key_heads, allowed, biases)
    soft_weights = jnp.exp(scores - logarithm_partition_sum[..., None])
    grad_weights = jnp.einsum(
        "bqhd,bkhd->bhqk", grad_mixture, values, preferred_element_type=jnp.float32
    )
    row_dots = jnp.sum(grad_weights * soft_weights, axis=-1, keepdims=True)
    grad_scores = (soft_weights * (grad_weights - row_dots)).astype(jnp.bfloat16)
    grad_queries = jnp.einsum(
        "bhqk,bkhd->bqhd", grad_scores, key_heads, preferred_element_type=jnp.float32
    ).astype(jnp.bfloat16)
    grad_keys = jnp.einsum(
        "bhqk,bqhd->bkhd", grad_scores, queries, preferred_element_type=jnp.float32
    ).astype(jnp.bfloat16)
    grad_values = jnp.einsum(
        "bhqk,bqhd->bkhd",
        soft_weights.astype(jnp.bfloat16),
        grad_mixture,
        preferred_element_type=jnp.float32,
    ).astype(jnp.bfloat16)
    return (grad_queries, grad_keys, grad_values, grad_scores)


def cross_backward(arrays):
    grad_queries, grad_keys, grad_values, grad_scores = attend_backward(0.0, arrays)
    return (grad_queries, grad_keys, grad_values)


def self_backward(biases, onehot_buckets, arrays):
    seg_onehot = arrays[6]
    grad_queries, grad_keys, grad_values, grad_scores = attend_backward(biases, arrays[:6])
    per_bucket = jnp.einsum(
        "bhqk,qkn->bhqn", grad_scores, onehot_buckets, preferred_element_type=jnp.float32
    )
    table_part = jnp.sum(per_bucket, axis=(0, 2))
    example_wise_norms = jnp.einsum(
        "bhqn,bqe->behn", per_bucket, seg_onehot, precision=lax.Precision.HIGHEST
    )
    table_square = jnp.sum(example_wise_norms * example_wise_norms, axis=(2, 3))
    return (grad_queries, grad_keys, grad_values, table_part[None], table_square)


def bucket_table(buckets, length):
    shape_three = (length, length, length)
    distance = lax.broadcasted_iota(jnp.int32, shape_three, 0) - lax.broadcasted_iota(
        jnp.int32, shape_three, 1
    )
    hits = (distance == lax.broadcasted_iota(jnp.int32, shape_three, 2)).astype(jnp.bfloat16)
    by_distance = (buckets[:, None] == lax.broadcasted_iota(jnp.int32, (length, NB), 1)).astype(
        jnp.bfloat16
    )
    return jnp.einsum("qkd,dn->qkn", hits, by_distance, preferred_element_type=jnp.float32).astype(
        jnp.bfloat16
    )


def norm_back(values, gain, grad_normed):
    scaled, pullback = jax.vjp(rms_scale, values)
    return (pullback(grad_normed * gain)[0], grad_normed * scaled)


def gram_rows(inputs, grads, same_seg, indicator_matrix):
    inner_dots = jnp.einsum("sid,sjd->sij", inputs, inputs, preferred_element_type=jnp.float32)
    outer_dots = sum(
        (
            jnp.einsum("sio,sjo->sij", grad_piece, grad_piece, preferred_element_type=jnp.float32)
            for grad_piece in grads
        )
    )
    per_token = jnp.sum(jnp.where(same_seg, inner_dots * outer_dots, 0.0), axis=-1)
    return jnp.einsum("si,sie->se", per_token, indicator_matrix, precision=lax.Precision.HIGHEST)


def gain_rows(summand_pieces, indicator_matrix):
    example_wise_norms = jnp.einsum(
        "aup,auv->avp", summand_pieces, indicator_matrix, precision=lax.Precision.HIGHEST
    )
    return jnp.sum(example_wise_norms * example_wise_norms, axis=-1)

AXES = ("wide", "narrow")


def shift(array, mask, count):
    return lax.ppermute(array, AXES, [(i, i ^ mask) for i in range(count)])


def gather_slots(shard, count):
    column = jnp.stack([shard] + [shift(shard, 8 * s, count) for s in (1, 2, 3)])
    plane = [column] + [shift(column, mask, count) for mask in (1, 4, 5)]
    other = [shift(piece, 2, count) for piece in plane]
    return jnp.concatenate(plane + other)


def scatter_slots(slots, count):
    mine, theirs = slots[:16], slots[16:]
    total = mine.astype(jnp.float32) + shift(theirs, 2, count).astype(jnp.float32)
    total = total.astype(slots.dtype)
    plane = total[:4].astype(jnp.float32)
    for t, mask in ((1, 1), (2, 4), (3, 5)):
        plane = plane + shift(total[4 * t : 4 * t + 4], mask, count).astype(jnp.float32)
    plane_low = plane.astype(slots.dtype)
    result = plane[0]
    for s in (1, 2, 3):
        result = result + shift(plane_low[s], 8 * s, count).astype(jnp.float32)
    return result


def slot_blocks():
    me = lax.axis_index(AXES)
    order = [
        2 * c + mask + 8 * s for c in (0, 1) for mask in (0, 1, 4, 5) for s in (0, 1, 2, 3)
    ]
    return me ^ jnp.array(order, jnp.int32)


def gather_rows(shard, count):
    if count != 32:
        return lax.all_gather(shard, AXES, axis=0, tiled=True)
    slots = gather_slots(shard, count)
    ordered = jnp.take(slots, jnp.argsort(slot_blocks()), axis=0)
    return ordered.reshape((count * shard.shape[0],) + shard.shape[1:])


def scatter_rows(partial_sums, count):
    if count != 32:
        return lax.psum_scatter(
            partial_sums.astype(jnp.float32), AXES, scatter_dimension=0, tiled=True
        )
    shape = (count, partial_sums.shape[0] // count) + partial_sums.shape[1:]
    return scatter_slots(jnp.take(partial_sums.reshape(shape), slot_blocks(), axis=0), count)


def sum_all(value, count):
    if count != 32:
        return lax.psum(value, AXES)
    total = value
    for masks in ((2,), (1, 4, 5), (8, 16, 24)):
        total = total + sum(shift(total, mask, count) for mask in masks)
    return total


def on_device(
    tokens,
    memory,
    cotangent,
    dec_segments,
    mem_segments,
    padding,
    buckets,
    w_query,
    w_key,
    w_value,
    w_out,
    c_query,
    c_key,
    c_value,
    c_out,
    w_hidden,
    w_back,
    gain_self,
    gain_cross,
    gain_ff,
    bias_table,
):
    seq_count, length = (tokens.shape[0], tokens.shape[1])
    mem_length = memory.shape[1]
    row_block = min(seq_count, max(1, 512 // length))
    rows_idx = lax.broadcasted_iota(jnp.int32, (length, length), 0)
    cols_idx = lax.broadcasted_iota(jnp.int32, (length, length), 1)
    same_dec = dec_segments[:, :, None] == dec_segments[:, None, :]
    same_mem = mem_segments[:, :, None] == mem_segments[:, None, :]
    self_allowed = (
        same_dec
        & (cols_idx <= rows_idx)[None]
        & ((padding[:, None, :] > 0) | (cols_idx == rows_idx)[None])
    )
    cross_allowed = dec_segments[:, :, None] == mem_segments[:, None, :]
    seg_onehot = (
        dec_segments[:, :, None] == lax.broadcasted_iota(jnp.int32, (1, 1, NSEG), 2)
    ).astype(jnp.float32)
    mem_onehot = (
        mem_segments[:, :, None] == lax.broadcasted_iota(jnp.int32, (1, 1, NSEG), 2)
    ).astype(jnp.float32)
    onehot_buckets = bucket_table(buckets, length)
    count = lax.axis_size(AXES)
    d = tokens.shape[2]
    small = jnp.concatenate([gain_self, gain_cross, gain_ff, bias_table])
    smalls = gather_rows(jnp.pad(small, (0, 128 - small.shape[0]))[None], count)
    self_full = gather_rows(jnp.concatenate([w_query, w_key, w_value, w_out], axis=1), count)
    cross_full = gather_rows(jnp.concatenate([c_query, c_key, c_value, c_out], axis=1), count)
    back_shape = w_back.shape
    feed_full = gather_rows(
        jnp.concatenate([w_hidden, w_back.reshape(w_hidden.shape)], axis=1), count
    )
    full_query, full_key, full_value, full_out = (self_full[:, k * d : k * d + d] for k in range(4))
    own_gain, own_table = gain_self.shape[0], bias_table.shape[0]
    full_gain_self, full_gain_cross, full_gain_ff = (
        smalls[:, k * own_gain : k * own_gain + own_gain].reshape(d) for k in range(3)
    )
    full_table = smalls[:, 3 * own_gain : 3 * own_gain + own_table].reshape(NB * H)
    full_c_query, full_c_key, full_c_value, full_c_out = (
        cross_full[:, k * d : k * d + d] for k in range(4)
    )
    ff = w_hidden.shape[1]
    full_hidden = feed_full[:, :ff]
    full_back = feed_full[:, ff:].reshape(ff, d)
    self_biases = jnp.einsum(
        "qkn,nh->hqk", onehot_buckets, full_table.reshape(NB, H), preferred_element_type=jnp.float32
    )
    inputs = tokens.astype(jnp.float32)
    input_a = (rms_scale(inputs) * full_gain_self.astype(jnp.float32)).astype(jnp.bfloat16)
    queries_a = product(input_a, full_query).astype(jnp.bfloat16).reshape(seq_count, length, H, DH)
    keys_a = product(input_a, full_key).astype(jnp.bfloat16).reshape(seq_count, length, H, DH)
    values_a = product(input_a, full_value).astype(jnp.bfloat16).reshape(seq_count, length, H, DH)
    attended_a, log_total_a = by_blocks(
        partial(attend_forward, self_biases), (queries_a, keys_a, values_a, self_allowed), row_block
    )
    attended_a = attended_a.reshape(seq_count, length, H * DH)
    middle = inputs + product(attended_a, full_out)
    input_b = (rms_scale(middle) * full_gain_cross.astype(jnp.float32)).astype(jnp.bfloat16)
    queries_b = (
        product(input_b, full_c_query).astype(jnp.bfloat16).reshape(seq_count, length, H, DH)
    )
    keys_b = product(memory, full_c_key).astype(jnp.bfloat16).reshape(seq_count, mem_length, H, DH)
    values_b = (
        product(memory, full_c_value).astype(jnp.bfloat16).reshape(seq_count, mem_length, H, DH)
    )
    attended_b, log_total_b = by_blocks(
        partial(attend_forward, 0.0), (queries_b, keys_b, values_b, cross_allowed), row_block
    )
    attended_b = attended_b.reshape(seq_count, length, H * DH)
    after_cross = middle + product(attended_b, full_c_out)
    input_c = (rms_scale(after_cross) * full_gain_ff.astype(jnp.float32)).astype(jnp.bfloat16)
    hidden = product(input_c, full_hidden)
    activation = gelu_tanh(hidden).astype(jnp.bfloat16)
    result = after_cross + product(activation, full_back)
    upstream = cotangent.astype(jnp.float32) * padding[..., None].astype(jnp.float32)
    grad_branch_c = upstream.astype(jnp.bfloat16)
    grad_w_back = weight_grad(activation, grad_branch_c)
    grad_activation = back_product(grad_branch_c, full_back)
    grad_hidden = jax.vjp(gelu_tanh, hidden)[1](grad_activation)[0].astype(jnp.bfloat16)
    grad_w_hidden = weight_grad(input_c, grad_hidden)
    grad_normed_c = back_product(grad_hidden, full_hidden)
    gradient_post_normalization, gain_terms_c = norm_back(
        after_cross, full_gain_ff.astype(jnp.float32), grad_normed_c
    )
    grad_gain_ff = jnp.sum(gain_terms_c, axis=(0, 1))
    grad_after = upstream + gradient_post_normalization
    feed = jnp.concatenate([grad_w_hidden, grad_w_back.reshape(d, ff)], axis=1)
    feed_shard = scatter_rows(feed.astype(jnp.bfloat16), count)
    shard_hidden = feed_shard[:, :ff]
    shard_back = feed_shard[:, ff:].reshape(back_shape)
    grad_branch_b = grad_after.astype(jnp.bfloat16)
    grad_c_out = weight_grad(attended_b, grad_branch_b)
    grad_attended_b = (
        back_product(grad_branch_b, full_c_out)
        .astype(jnp.bfloat16)
        .reshape(seq_count, length, H, DH)
    )
    grad_queries_b, grad_keys_b, grad_values_b = by_blocks(
        cross_backward,
        (queries_b, keys_b, values_b, cross_allowed, log_total_b, grad_attended_b),
        row_block,
    )
    grad_queries_b = grad_queries_b.reshape(seq_count, length, H * DH)
    grad_keys_b = grad_keys_b.reshape(seq_count, mem_length, H * DH)
    grad_values_b = grad_values_b.reshape(seq_count, mem_length, H * DH)
    grad_c_query = weight_grad(input_b, grad_queries_b)
    grad_c_key = weight_grad(memory, grad_keys_b)
    grad_c_value = weight_grad(memory, grad_values_b)
    grad_memory = (
        back_product(grad_keys_b, full_c_key) + back_product(grad_values_b, full_c_value)
    ).astype(jnp.bfloat16)
    grad_normed_b = back_product(grad_queries_b, full_c_query)
    grad_middle_norm, gain_terms_b = norm_back(
        middle, full_gain_cross.astype(jnp.float32), grad_normed_b
    )
    grad_gain_cross = jnp.sum(gain_terms_b, axis=(0, 1))
    grad_middle = grad_after + grad_middle_norm
    cross = jnp.concatenate([grad_c_query, grad_c_key, grad_c_value, grad_c_out], axis=1)
    cross_shard = scatter_rows(cross.astype(jnp.bfloat16), count)
    shard_c_query, shard_c_key, shard_c_value, shard_c_out = (
        cross_shard[:, k * d : k * d + d] for k in range(4)
    )
    grad_branch_a = grad_middle.astype(jnp.bfloat16)
    grad_w_out = weight_grad(attended_a, grad_branch_a)
    grad_attended_a = (
        back_product(grad_branch_a, full_out).astype(jnp.bfloat16).reshape(seq_count, length, H, DH)
    )
    grad_queries_a, grad_keys_a, grad_values_a, table_parts, table_square = by_blocks(
        partial(self_backward, self_biases, onehot_buckets),
        (queries_a, keys_a, values_a, self_allowed, log_total_a, grad_attended_a, seg_onehot),
        row_block,
    )
    grad_queries_a = grad_queries_a.reshape(seq_count, length, H * DH)
    grad_keys_a = grad_keys_a.reshape(seq_count, length, H * DH)
    grad_values_a = grad_values_a.reshape(seq_count, length, H * DH)
    grad_w_query = weight_grad(input_a, grad_queries_a)
    grad_w_key = weight_grad(input_a, grad_keys_a)
    grad_w_value = weight_grad(input_a, grad_values_a)
    grad_bias_table = jnp.sum(table_parts, axis=0).T.reshape(NB * H)
    grad_normed_a = (
        back_product(grad_queries_a, full_query)
        + back_product(grad_keys_a, full_key)
        + back_product(grad_values_a, full_value)
    )
    grad_tokens_norm, gain_terms_a = norm_back(
        inputs, full_gain_self.astype(jnp.float32), grad_normed_a
    )
    grad_gain_self = jnp.sum(gain_terms_a, axis=(0, 1))
    grad_tokens = (grad_middle + grad_tokens_norm).astype(jnp.bfloat16)
    own = jnp.concatenate([grad_w_query, grad_w_key, grad_w_value, grad_w_out], axis=1)
    own_shard = scatter_rows(own.astype(jnp.bfloat16), count)
    shard_query, shard_key, shard_value, shard_out = (
        own_shard[:, k * d : k * d + d] for k in range(4)
    )
    tiny = jnp.concatenate(
        [
            grad_gain_self.reshape(count, own_gain),
            grad_gain_cross.reshape(count, own_gain),
            grad_gain_ff.reshape(count, own_gain),
            grad_bias_table.reshape(count, own_table),
        ],
        axis=1,
    )
    tiny_shard = scatter_rows(jnp.pad(tiny, ((0, 0), (0, 128 - tiny.shape[1]))), count)[0]
    shard_gain_self, shard_gain_cross, shard_gain_ff = (
        tiny_shard[k * own_gain : k * own_gain + own_gain] for k in range(3)
    )
    partitioned_bias_table = tiny_shard[3 * own_gain : 3 * own_gain + own_table]
    example_square = gram_rows(
        input_a, (grad_queries_a, grad_keys_a, grad_values_a), same_dec, seg_onehot
    )
    example_square = example_square + gram_rows(attended_a, (grad_branch_a,), same_dec, seg_onehot)
    example_square = example_square + gram_rows(input_b, (grad_queries_b,), same_dec, seg_onehot)
    example_square = example_square + gram_rows(
        memory, (grad_keys_b, grad_values_b), same_mem, mem_onehot
    )
    example_square = example_square + gram_rows(attended_b, (grad_branch_b,), same_dec, seg_onehot)
    example_square = example_square + gram_rows(input_c, (grad_hidden,), same_dec, seg_onehot)
    example_square = example_square + gram_rows(activation, (grad_branch_c,), same_dec, seg_onehot)
    example_square = example_square + gain_rows(gain_terms_a, seg_onehot)
    example_square = example_square + gain_rows(gain_terms_b, seg_onehot)
    example_square = example_square + gain_rows(gain_terms_c, seg_onehot)
    example_norms = (example_square + table_square) / COUNT
    shard_list = (
        shard_query,
        shard_key,
        shard_value,
        shard_out,
        shard_c_query,
        shard_c_key,
        shard_c_value,
        shard_c_out,
        shard_hidden,
        shard_back,
        shard_gain_self,
        shard_gain_cross,
        shard_gain_ff,
        partitioned_bias_table,
    )
    local_square = sum((jnp.sum(shard_piece * shard_piece) for shard_piece in shard_list))
    global_norm = sum_all(local_square, count) / COUNT
    return (
        result.astype(jnp.bfloat16),
        grad_tokens,
        grad_memory,
        shard_query,
        shard_key,
        shard_value,
        shard_out,
        shard_c_query,
        shard_c_key,
        shard_c_value,
        shard_c_out,
        shard_hidden,
        shard_back,
        shard_gain_self,
        shard_gain_cross,
        shard_gain_ff,
        partitioned_bias_table,
        example_norms,
        global_norm,
    )


def solution(mesh):
    placed = (
        P(("wide", "narrow"), None, None),
        P(("wide", "narrow"), None, None),
        P(("wide", "narrow"), None, None),
        P(("wide", "narrow"), None),
        P(("wide", "narrow"), None),
        P(("wide", "narrow"), None),
        P(),
        P(("wide", "narrow"), None),
        P(("wide", "narrow"), None),
        P(("wide", "narrow"), None),
        P(("wide", "narrow"), None),
        P(("wide", "narrow"), None),
        P(("wide", "narrow"), None),
        P(("wide", "narrow"), None),
        P(("wide", "narrow"), None),
        P(("wide", "narrow"), None),
        P(("wide", "narrow"), None),
        P(("wide", "narrow")),
        P(("wide", "narrow")),
        P(("wide", "narrow")),
        P(("wide", "narrow")),
    )
    return jax.shard_map(
        on_device,
        mesh=mesh,
        in_specs=placed,
        out_specs=(
            P(("wide", "narrow"), None, None),
            P(("wide", "narrow"), None, None),
            P(("wide", "narrow"), None, None),
            P(("wide", "narrow"), None),
            P(("wide", "narrow"), None),
            P(("wide", "narrow"), None),
            P(("wide", "narrow"), None),
            P(("wide", "narrow"), None),
            P(("wide", "narrow"), None),
            P(("wide", "narrow"), None),
            P(("wide", "narrow"), None),
            P(("wide", "narrow"), None),
            P(("wide", "narrow"), None),
            P(("wide", "narrow")),
            P(("wide", "narrow")),
            P(("wide", "narrow")),
            P(("wide", "narrow")),
            P(("wide", "narrow"), None),
            P(),
        ),
        check_vma=False,
    )
```

```python
from functools import partial

import jax
import jax.numpy as jnp
from jax import lax
from jax.experimental import pallas as pl
from jax.experimental.pallas import tpu as pltpu
from jax.sharding import PartitionSpec as P

H = 8
DH = 64
NB = 32
NSEG = 4
COUNT = 4196096
AXES = ("wide", "narrow")
EPSILON = 1e-06
FLOOR = -1e30
F32 = jnp.float32
BF16 = jnp.bfloat16
PAIRS = H // 2
LANES = 128
STEP_ROWS = 4
VMEM_LIMIT = 50 * 2**20

COLUMN = (0, 8, 16, 24)
PLANE = (0, 1, 4, 5)
CODES = tuple(2 * c + mask + z for c in (0, 1) for mask in PLANE for z in COLUMN)


def nn(left, right):
    return lax.dot_general(left, right, (((1,), (0,)), ((), ())), preferred_element_type=F32)


def nt(left, right):
    return lax.dot_general(left, right, (((1,), (1,)), ((), ())), preferred_element_type=F32)


def tn(left, right):
    return lax.dot_general(left, right, (((0,), (0,)), ((), ())), preferred_element_type=F32)


def inverse_root(values):
    return lax.rsqrt(jnp.mean(values * values, axis=-1, keepdims=True) + EPSILON)


def head_pair(values):
    low = (lax.broadcasted_iota(jnp.int32, (1, LANES), 1) < DH).astype(BF16)
    return jnp.concatenate([values * low, values * (1 - low)], axis=0)


def fold_pair(both, queries):
    own = jnp.concatenate([both[:DH, :queries], both[DH:, queries:]], axis=0)
    return own.astype(BF16).T


def slot_copies(me_ref, pieces, sems, targets):
    copies = []
    for t, piece in enumerate(pieces):
        for s in range(len(COLUMN)):
            block = me_ref[0] ^ CODES[t * len(COLUMN) + s]
            for source, target in targets(piece, s, block):
                copies.append(pltpu.make_async_copy(source, target, sems.at[len(copies)]))
    return copies


def square_target(weight_ref):
    def targets(piece, s, block):
        rows = pl.ds(pl.multiple_of(block * 16, 16), 16)
        return [(piece.at[s], weight_ref.at[rows, :])]

    return targets


def store_slots(me_ref, low_ref, high_ref, read):
    for k, code in enumerate(CODES):
        target = low_ref if k < 16 else high_ref
        target[k % 16] = read(me_ref[0] ^ code)


def softmax_columns(scores):
    shifted = jnp.exp(scores - jnp.max(scores, axis=0, keepdims=True))
    return (shifted * (1.0 / jnp.sum(shifted, axis=0, keepdims=True))).astype(BF16)


def gram(left):
    return nt(left, left)


def self_forward_kernel(me_ref, tokens_ref, mask_ref, buckets_ref, *refs):
    pieces, refs = refs[:8], refs[8:]
    (input_ref, qkv_ref, prob_ref, attended_ref, middle_ref, weight_ref, gains_ref) = refs[:7]
    bias_ref, small_ref, sems = refs[7:]
    length = mask_ref.shape[1]
    width = tokens_ref.shape[1]

    @pl.when(pl.program_id(0) == 0)
    def _():
        def targets(piece, s, block):
            rows = pl.ds(pl.multiple_of(block * 16, 16), 16)
            cols = 4 * width
            return [
                (piece.at[s, :, :cols], weight_ref.at[rows, :]),
                (piece.at[s, :, cols:], small_ref.at[rows, :]),
            ]

        copies = slot_copies(me_ref, pieces, sems, targets)
        for copy in copies:
            copy.start()
        for copy in copies:
            copy.wait()
        small = small_ref[...].astype(F32).T
        gains_ref[...] = small[:8]
        place = lax.broadcasted_iota(jnp.int32, (H, width), 1) % 16
        head = lax.broadcasted_iota(jnp.int32, (H, width), 0)
        table = jnp.where(place == head, small[3:4], 0.0).astype(BF16)
        bucket = lax.broadcasted_iota(jnp.int32, (width, length), 0) // 16
        curves = nn(table, (bucket == buckets_ref[...]).astype(F32).astype(BF16))
        for h in range(H):
            curve = jnp.broadcast_to(curves[h : h + 1, :], (length, length))
            lanes = slice((h % 2) * length, (h % 2 + 1) * length)
            bias_ref[h // 2, :, lanes] = pltpu.roll(curve, 0, 1, stride=1, stride_axis=0)

    values = tokens_ref[...].astype(F32)
    normed = (values * inverse_root(values) * gains_ref[0:1, :]).astype(BF16)
    input_ref[...] = normed
    for k in range(3):
        cols = slice(k * width, (k + 1) * width)
        qkv_ref[:, cols] = nn(normed, weight_ref[:, cols]).astype(BF16)

    def row(r, carry):
        rows = pl.ds(pl.multiple_of(r * length, length), length)
        mask = mask_ref[r].astype(F32)
        mask = jnp.concatenate([mask, mask], axis=1)
        for p in range(PAIRS):
            query = qkv_ref[rows, p * LANES : (p + 1) * LANES]
            key = qkv_ref[rows, width + p * LANES : width + (p + 1) * LANES]
            value = qkv_ref[rows, 2 * width + p * LANES : 2 * width + (p + 1) * LANES]
            prob = softmax_columns(nt(key, head_pair(query)) + bias_ref[p] + mask)
            prob_ref[r, p] = prob
            attended_ref[rows, p * LANES : (p + 1) * LANES] = fold_pair(nn(value.T, prob), length)
        return carry

    lax.fori_loop(0, STEP_ROWS, row, 0)
    middle_ref[...] = values + nn(attended_ref[...], weight_ref[:, 3 * width :])


def cross_forward_kernel(me_ref, middle_ref, memory_ref, mask_ref, gains_ref, *refs):
    pieces, refs = refs[:8], refs[8:]
    input_ref, query_ref, kv_ref, prob_ref, attended_ref, after_ref, weight_ref, sems = refs
    mem_length, length = mask_ref.shape[1:]
    width = middle_ref.shape[1]

    @pl.when(pl.program_id(0) == 0)
    def _():
        copies = slot_copies(me_ref, pieces, sems, square_target(weight_ref))
        for copy in copies:
            copy.start()
        for copy in copies:
            copy.wait()

    values = middle_ref[...]
    normed = (values * inverse_root(values) * gains_ref[1:2, :]).astype(BF16)
    input_ref[...] = normed
    query_ref[...] = nn(normed, weight_ref[:, :width]).astype(BF16)
    for k in range(2):
        kv_ref[:, k * width : (k + 1) * width] = nn(
            memory_ref[...], weight_ref[:, (k + 1) * width : (k + 2) * width]
        ).astype(BF16)

    def row(r, carry):
        rows = pl.ds(pl.multiple_of(r * length, length), length)
        mem_rows = pl.ds(pl.multiple_of(r * mem_length, mem_length), mem_length)
        mask = mask_ref[r].astype(F32)
        mask = jnp.concatenate([mask, mask], axis=1)
        for p in range(PAIRS):
            query = query_ref[rows, p * LANES : (p + 1) * LANES]
            key = kv_ref[mem_rows, p * LANES : (p + 1) * LANES]
            value = kv_ref[mem_rows, width + p * LANES : width + (p + 1) * LANES]
            prob = softmax_columns(nt(key, head_pair(query)) + mask)
            prob_ref[r, p] = prob
            attended_ref[rows, p * LANES : (p + 1) * LANES] = fold_pair(nn(value.T, prob), length)
        return carry

    lax.fori_loop(0, STEP_ROWS, row, 0)
    after_ref[...] = values + nn(attended_ref[...], weight_ref[:, 3 * width :])


def norm_back(values, gain, grad_normed):
    inverse = inverse_root(values)
    scaled = values * inverse
    upper = grad_normed * gain
    grad = inverse * (upper - scaled * jnp.mean(upper * scaled, axis=-1, keepdims=True))
    return grad, grad_normed * scaled


def gain_sums(step, terms, members_ref, total_ref, square_ref):
    sums = nn(members_ref[0], terms.astype(BF16))
    total = jnp.sum(sums, axis=0, keepdims=True)
    total_ref[...] = jnp.where(step == 0, 0.0, total_ref[...]) + total
    square = jnp.sum(sums * sums, axis=1, keepdims=True)
    square_ref[0] = jnp.broadcast_to(square, square_ref.shape[1:])


def feed_kernel(me_ref, after_ref, upstream_ref, same_ref, members_ref, gains_ref, *refs):
    pieces, refs = refs[:8], refs[8:]
    (result_ref, grad_after_ref, low_ref, high_ref, total_ref, square_ref, token_ref) = refs[:7]
    hidden_w, back_w, grad_hidden_w, grad_back_w, flipped, gram_ref, sems = refs[7:]
    step = pl.program_id(0)
    length = same_ref.shape[1]
    width, ff = hidden_w.shape
    parts = ff // width

    @pl.when(step == 0)
    def _():
        def targets(piece, s, block):
            rows = pl.ds(pl.multiple_of(block * 16, 16), 16)
            pairs = [(piece.at[s, :, :ff], hidden_w.at[rows, :])]
            for j in range(parts):
                back = pl.ds(pl.multiple_of(block * 16 * parts + j * 16, 16), 16)
                source = piece.at[s, :, ff + j * width : ff + (j + 1) * width]
                pairs.append((source, back_w.at[back, :]))
            return pairs

        copies = slot_copies(me_ref, pieces, sems, targets)
        for copy in copies:
            copy.start()
        grad_hidden_w[...] = jnp.zeros_like(grad_hidden_w)
        grad_back_w[...] = jnp.zeros_like(grad_back_w)
        for copy in copies:
            copy.wait()

    values = after_ref[...]
    gain = gains_ref[2:3, :]
    normed = (values * inverse_root(values) * gain).astype(BF16)
    normed_flip = normed.T
    branch = upstream_ref[...]
    branch_flip = branch.T
    gram_ref[...] = jnp.zeros_like(gram_ref)
    root = 0.7978845608028654

    def chunk(c, carry):
        result, grad_normed = carry
        cols = pl.ds(pl.multiple_of(c * width, width), width)
        w_in = hidden_w[:, cols]
        w_out = back_w[cols, :]
        hidden = nn(normed, w_in)
        square = hidden * hidden
        bent = jnp.tanh(hidden * (root + (root * 0.044715) * square))
        half = 0.5 + 0.5 * bent
        active = (hidden * half).astype(BF16)
        slope = half + (0.5 * hidden) * (1.0 - bent * bent) * (
            root + (3.0 * root * 0.044715) * square
        )
        grad = (nt(branch, w_out) * slope).astype(BF16)
        result = result + nn(active, w_out)
        grad_normed = grad_normed + nt(grad, w_in)
        grad_hidden_w[:, cols] += nn(normed_flip, grad)
        grad_back_w[:, cols] += nn(branch_flip, active)
        for r in range(STEP_ROWS):
            rows = slice(r * length, (r + 1) * length)
            gram_ref[0, r] += gram(active[rows])
            gram_ref[1, r] += gram(grad[rows])
        return result, grad_normed

    zero = jnp.zeros_like(values)
    result, grad_normed = lax.fori_loop(0, parts, chunk, (zero, zero))
    result_ref[...] = (values + result).astype(BF16)
    grad, terms = norm_back(values, gain, grad_normed)
    grad_after_ref[...] = branch.astype(F32) + grad
    gain_sums(step, terms, members_ref, total_ref, square_ref)
    for r in range(STEP_ROWS):
        rows = slice(r * length, (r + 1) * length)
        products = gram_ref[0, r] * gram(branch[rows]) + gram_ref[1, r] * gram(normed[rows])
        token_ref[0, r : r + 1, :] = jnp.sum(products * same_ref[r], axis=0, keepdims=True)

    @pl.when(step == pl.num_programs(0) - 1)
    def _():
        for j in range(parts):
            flipped[j * width : (j + 1) * width, :] = (
                grad_back_w[:, j * width : (j + 1) * width].astype(BF16).T
            )

        def read(block):
            rows = pl.ds(pl.multiple_of(block * 16, 16), 16)
            own = [grad_hidden_w[rows, :].astype(BF16)]
            for j in range(parts):
                back = pl.ds(pl.multiple_of(block * 16 * parts + j * 16, 16), 16)
                own.append(flipped[back, :])
            return jnp.concatenate(own, axis=1)

        store_slots(me_ref, low_ref, high_ref, read)


def score_grads(prob, grad_prob):
    prob = prob.astype(F32)
    dots = jnp.sum(prob * grad_prob, axis=0, keepdims=True)
    return prob * (grad_prob - dots)


def cross_backward_kernel(me_ref, grad_after_ref, middle_ref, memory_ref, input_ref, query_ref,
                          kv_ref, prob_ref, attended_ref, members_ref, gains_ref, weight_ref,
                          grad_query_ref, grad_kv_ref, branch_ref, grad_middle_ref, low_ref,
                          high_ref, total_ref, square_ref, grad_w, grad_attended):
    step = pl.program_id(0)
    mem_length = prob_ref.shape[2]
    length = prob_ref.shape[3] // 2
    width = middle_ref.shape[1]
    grad_after = grad_after_ref[...]
    branch = grad_after.astype(BF16)
    branch_ref[...] = branch
    grad_attended[...] = nt(branch, weight_ref[:, 3 * width :]).astype(BF16)

    def row(r, carry):
        rows = pl.ds(pl.multiple_of(r * length, length), length)
        mem_rows = pl.ds(pl.multiple_of(r * mem_length, mem_length), mem_length)
        for p in range(PAIRS):
            lanes = slice(p * LANES, (p + 1) * LANES)
            upper = slice(width + p * LANES, width + (p + 1) * LANES)
            key = kv_ref[mem_rows, lanes]
            value = kv_ref[mem_rows, upper]
            query = head_pair(query_ref[rows, lanes])
            grad_out = head_pair(grad_attended[rows, lanes])
            prob = prob_ref[r, p]
            grad_score = score_grads(prob, nt(value, grad_out)).astype(BF16)
            grad_kv_ref[mem_rows, lanes] = nn(grad_score, query).astype(BF16)
            grad_kv_ref[mem_rows, upper] = nn(prob, grad_out).astype(BF16)
            grad_query_ref[rows, lanes] = fold_pair(nn(key.T, grad_score), length)
        return carry

    lax.fori_loop(0, STEP_ROWS, row, 0)
    grad_normed = nt(grad_query_ref[...], weight_ref[:, :width])
    grad, terms = norm_back(middle_ref[...], gains_ref[1:2, :], grad_normed)
    grad_middle_ref[...] = grad_after + grad
    gain_sums(step, terms, members_ref, total_ref, square_ref)

    @pl.when(step == 0)
    def _():
        grad_w[...] = jnp.zeros_like(grad_w)

    grad_w[:, :width] += tn(input_ref[...], grad_query_ref[...])
    grad_w[:, width : 3 * width] += tn(memory_ref[...], grad_kv_ref[...])
    grad_w[:, 3 * width :] += tn(attended_ref[...], branch)

    @pl.when(step == pl.num_programs(0) - 1)
    def _():
        store_slots(me_ref, low_ref, high_ref, partial(read_rows, grad_w))


def read_rows(grad_w, block):
    return grad_w[pl.ds(pl.multiple_of(block * 16, 16), 16), :].astype(BF16)


def self_backward_kernel(me_ref, grad_middle_ref, tokens_ref, input_ref, qkv_ref, prob_ref,
                         attended_ref, members_ref, keys_ref, turned_buckets_ref, gains_ref, weight_ref,
                         grad_qkv_ref, branch_ref, grad_tokens_ref, low_ref, high_ref, total_ref,
                         square_ref, table_ref, table_square_ref, grad_w, grad_attended, bands):
    step = pl.program_id(0)
    length = prob_ref.shape[2]
    width = tokens_ref.shape[1]
    grad_middle = grad_middle_ref[...]
    branch = grad_middle.astype(BF16)
    branch_ref[...] = branch
    grad_attended[...] = nt(branch, weight_ref[:, 3 * width :]).astype(BF16)

    @pl.when(step == 0)
    def _():
        grad_w[...] = jnp.zeros_like(grad_w)
        table_ref[...] = jnp.zeros_like(table_ref)

    row_i = lax.broadcasted_iota(jnp.int32, (2 * length, 2 * length), 0)
    col_i = lax.broadcasted_iota(jnp.int32, (2 * length, 2 * length), 1)
    turned = (row_i // length) * length + length - 1 - row_i % length
    flip = (turned == col_i).astype(F32).astype(BF16)

    def row(r, carry):
        rows = pl.ds(pl.multiple_of(r * length, length), length)
        keys = keys_ref[r]
        for p in range(PAIRS):
            lanes = slice(p * LANES, (p + 1) * LANES)
            middle = slice(width + p * LANES, width + (p + 1) * LANES)
            upper = slice(2 * width + p * LANES, 2 * width + (p + 1) * LANES)
            key = qkv_ref[rows, middle]
            value = qkv_ref[rows, upper]
            query = head_pair(qkv_ref[rows, lanes])
            grad_out = head_pair(grad_attended[rows, lanes])
            prob = prob_ref[r, p]
            grad_score = score_grads(prob, nt(value, grad_out)).astype(BF16)
            grad_qkv_ref[rows, middle] = nn(grad_score, query).astype(BF16)
            grad_qkv_ref[rows, upper] = nn(prob, grad_out).astype(BF16)
            grad_qkv_ref[rows, lanes] = fold_pair(nn(key.T, grad_score), length)
            mirrored = nn(grad_score, flip)
            for h in range(2):
                own = mirrored[:, h * length : (h + 1) * length]
                own = pltpu.roll(own, 0, 1, stride=1, stride_axis=0)
                bands[r, 2 * p + h] = nn(keys, own.astype(BF16))[:8]
        return carry

    lax.fori_loop(0, STEP_ROWS, row, 0)
    grad_qkv = grad_qkv_ref[...]
    grad_normed = nt(grad_qkv, weight_ref[:, : 3 * width])
    grad, terms = norm_back(tokens_ref[...].astype(F32), gains_ref[0:1, :], grad_normed)
    grad_tokens_ref[...] = (grad_middle + grad).astype(BF16)
    gain_sums(step, terms, members_ref, total_ref, square_ref)
    grad_w[:, : 3 * width] += tn(input_ref[...], grad_qkv)
    grad_w[:, 3 * width :] += tn(attended_ref[...], branch)

    bucket = lax.broadcasted_iota(jnp.int32, (LANES, length), 0)
    near = (bucket == turned_buckets_ref[...]).astype(F32)
    flat = bands[...].reshape(STEP_ROWS * H * 8, length)
    per_bucket = lax.dot_general(
        flat, near, (((1,), (1,)), ((), ())), preferred_element_type=F32,
        precision=lax.Precision.HIGHEST,
    ).reshape(STEP_ROWS, H, 8, LANES)
    table_ref[...] += jnp.sum(jnp.sum(per_bucket, axis=0), axis=1)
    squares = jnp.sum(jnp.sum(per_bucket * per_bucket, axis=1), axis=-1, keepdims=True)
    table_square_ref[0] = jnp.broadcast_to(squares, (STEP_ROWS, 8, LANES))

    @pl.when(step == pl.num_programs(0) - 1)
    def _():
        store_slots(me_ref, low_ref, high_ref, partial(read_rows, grad_w))


def memory_kernel(memory_ref, grad_kv_ref, same_ref, weight_ref, grad_memory_ref, token_ref):
    mem_length = same_ref.shape[1]
    width = memory_ref.shape[1]
    grad_kv = grad_kv_ref[...]
    grad_memory_ref[...] = nt(grad_kv, weight_ref[:, width : 3 * width]).astype(BF16)
    for r in range(STEP_ROWS):
        rows = slice(r * mem_length, (r + 1) * mem_length)
        products = gram(memory_ref[rows, :]) * gram(grad_kv_ref[rows, :])
        token_ref[0, r : r + 1, :] = jnp.sum(products * same_ref[r], axis=0, keepdims=True)


def gram_kernel(same_ref, *refs):
    pairs, token_ref = refs[:-1], refs[-1]
    length = same_ref.shape[1]
    for r in range(STEP_ROWS):
        rows = slice(r * length, (r + 1) * length)
        products = sum(
            gram(left[rows, :]) * gram(right[rows, :])
            for left, right in zip(pairs[::2], pairs[1::2])
        )
        token_ref[0, r : r + 1, :] = jnp.sum(products * same_ref[r], axis=0, keepdims=True)


def rows_spec(array, steps):
    shape = (array.shape[0] // steps,) + array.shape[1:]
    return pl.BlockSpec(shape, lambda i, *_: (i,) + (0,) * (len(shape) - 1))


def whole_spec(array):
    return pl.BlockSpec(array.shape, lambda i, *_: (0,) * len(array.shape))


def call(kernel, steps, me, blocked, whole, pieces, outs_blocked, outs_whole, scratch, flops,
         order):
    ins, in_specs = [], []
    blocked, whole = list(blocked), list(whole)
    for kind in order[0]:
        array = (blocked if kind == "i" else whole).pop(0)
        ins.append(array)
        in_specs.append(rows_spec(array, steps) if kind == "i" else whole_spec(array))
    ins += list(pieces)
    in_specs += [pl.BlockSpec(memory_space=pl.ANY)] * len(pieces)
    outs, out_specs = [], []
    outs_blocked, outs_whole = list(outs_blocked), list(outs_whole)
    for kind in order[1]:
        out = (outs_blocked if kind == "i" else outs_whole).pop(0)
        outs.append(out)
        out_specs.append(rows_spec(out, steps) if kind == "i" else whole_spec(out))
    moved = sum(a.size * a.dtype.itemsize for a in ins + outs)
    prefetch = 0 if me is None else 1
    return pl.pallas_call(
        kernel,
        out_shape=outs,
        grid_spec=pltpu.PrefetchScalarGridSpec(
            num_scalar_prefetch=prefetch,
            grid=(steps,),
            in_specs=in_specs,
            out_specs=out_specs,
            scratch_shapes=scratch,
        ),
        compiler_params=pltpu.CompilerParams(
            dimension_semantics=("arbitrary",), vmem_limit_bytes=VMEM_LIMIT
        ),
        cost_estimate=pl.CostEstimate(flops=flops, bytes_accessed=moved, transcendentals=0),
    )(*(() if me is None else (me,)), *ins)


def shape_of(shape, dtype):
    return jax.ShapeDtypeStruct(shape, dtype)


def shift(array, mask, count):
    return lax.ppermute(array, AXES, [(i, i ^ mask) for i in range(count)])


def gather_pieces(shard, count):
    column = jnp.stack([shard] + [shift(shard, code, count) for code in COLUMN[1:]])
    plane = [column] + [shift(column, mask, count) for mask in PLANE[1:]]
    return plane + [shift(piece, 2, count) for piece in plane]


def scatter_slots(low, high, count):
    total = (low.astype(F32) + shift(high, 2, count).astype(F32)).astype(low.dtype)
    plane = total[:4].astype(F32)
    for t, mask in enumerate(PLANE[1:], 1):
        plane = plane + shift(total[4 * t : 4 * t + 4], mask, count).astype(F32)
    sent = plane.astype(low.dtype)
    result = plane[0]
    for s, code in enumerate(COLUMN[1:], 1):
        result = result + shift(sent[s], code, count).astype(F32)
    return result


def sum_all(value, count):
    if count != 32:
        return lax.psum(value, AXES)
    for masks in ((2,), PLANE[1:], COLUMN[1:]):
        value = value + sum(shift(value, mask, count) for mask in masks)
    return value


def split_back(back):
    blocks = back.shape[0] // 64
    parts = back.reshape(blocks, 4, 16, back.shape[1]).transpose(0, 2, 1, 3)
    return parts.reshape(16 * blocks, 4 * back.shape[1])


def join_back(parts):
    blocks, width = parts.shape[0] // 16, parts.shape[1] // 4
    return parts.reshape(blocks, 16, 4, width).transpose(0, 2, 1, 3).reshape(64 * blocks, width)


def small_columns(gains, table):
    table = jnp.pad(table.reshape(-1, H), ((0, 0), (0, 16 - H))).reshape(-1)
    columns = jnp.stack(list(gains) + [table], axis=1)
    return jnp.pad(columns, ((0, 0), (0, LANES - columns.shape[1])))


def to_pieces(full):
    slots = full.reshape(32, 16, full.shape[1])[jnp.array(CODES)]
    return [slots[4 * t : 4 * t + 4] for t in range(8)]


def from_slots(low, high):
    slots = jnp.concatenate([low, high])
    places = [CODES.index(block) for block in range(32)]
    return slots[jnp.array(places)].reshape(-1, slots.shape[2])


def on_device(tokens, memory, cotangent, dec_segments, mem_segments, padding, buckets, w_query,
              w_key, w_value, w_out, c_query, c_key, c_value, c_out, w_hidden, w_back, gain_self,
              gain_cross, gain_ff, bias_table):
    count = lax.axis_size(AXES)
    fast = count == 32

    if fast:
        me = lax.axis_index(AXES)
        gathered = lambda shard: gather_pieces(shard, count)
    else:
        me = jnp.int32(0)
        full = lambda shard: lax.all_gather(shard, AXES, axis=0, tiled=True)
        w_query, w_key, w_value, w_out = map(full, (w_query, w_key, w_value, w_out))
        c_query, c_key, c_value, c_out = map(full, (c_query, c_key, c_value, c_out))
        w_hidden, w_back, bias_table = map(full, (w_hidden, w_back, bias_table))
        gain_self, gain_cross, gain_ff = map(full, (gain_self, gain_cross, gain_ff))
        gathered = to_pieces
    small = small_columns((gain_self, gain_cross, gain_ff), bias_table)
    self_pieces = gathered(jnp.concatenate([w_query, w_key, w_value, w_out, small], axis=1))
    cross_pieces = gathered(jnp.concatenate([c_query, c_key, c_value, c_out], axis=1))
    feed_pieces = gathered(jnp.concatenate([w_hidden, split_back(w_back)], axis=1))

    result, grad_tokens, grad_memory, slots, sums, examples = local_part(
        me[None].astype(jnp.int32), tokens, memory, cotangent, dec_segments, mem_segments,
        padding, buckets, self_pieces, cross_pieces, feed_pieces,
    )

    width = tokens.shape[2]
    if fast:
        feed, cross, own = (scatter_slots(low, high, count) for low, high in slots)
        back = join_back(feed[:, 4 * width :])
    else:
        scatter = lambda part: lax.psum_scatter(part, AXES, scatter_dimension=0, tiled=True)
        feed, cross, own = (from_slots(low, high).astype(F32) for low, high in slots)
        back = scatter(join_back(feed[:, 4 * width :]))
        feed, cross, own = scatter(feed[:, : 4 * width]), scatter(cross), scatter(own)
    tiny = jnp.concatenate([leaf.reshape(count, -1) for leaf in sums], axis=1)
    tiny = jnp.pad(tiny, ((0, 0), (0, LANES - tiny.shape[1])))
    if fast:
        order = me ^ jnp.array(CODES, jnp.int32)
        tiny = jnp.take(tiny, order, axis=0).reshape(2, 16, 1, LANES)
        tiny = scatter_slots(tiny[0], tiny[1], count)[0]
    else:
        tiny = lax.psum_scatter(tiny, AXES, scatter_dimension=0, tiled=True)[0]
    per = width // count
    shards = (
        [own[:, k * width : (k + 1) * width] for k in range(4)]
        + [cross[:, k * width : (k + 1) * width] for k in range(4)]
        + [feed[:, : 4 * width], back]
        + [tiny[k * per : (k + 1) * per] for k in range(3)]
        + [tiny[3 * per : 3 * per + NB * H // count]]
    )
    local_square = sum(jnp.sum(shard * shard) for shard in shards)
    global_norm = sum_all(local_square, count) / COUNT
    return (result, grad_tokens, grad_memory, *shards, examples, global_norm)


def local_part(me, tokens, memory, cotangent, dec_segments, mem_segments, padding, buckets,
               self_pieces, cross_pieces, feed_pieces):
    seqs, length, width = tokens.shape
    mem_length = memory.shape[1]
    steps = seqs // STEP_ROWS
    dec, mem = seqs * length, seqs * mem_length
    step_dec = STEP_ROWS * length
    ff = 4 * width

    same_dec = dec_segments[:, :, None] == dec_segments[:, None, :]
    same_mem = mem_segments[:, :, None] == mem_segments[:, None, :]
    keys_i = lax.broadcasted_iota(jnp.int32, (length, length), 0)
    queries_i = lax.broadcasted_iota(jnp.int32, (length, length), 1)
    allowed = same_dec & (keys_i <= queries_i) & ((padding[:, :, None] > 0) | (keys_i == queries_i))
    self_mask = jnp.where(allowed, 0.0, FLOOR).astype(BF16)
    cross_allowed = mem_segments[:, :, None] == dec_segments[:, None, :]
    cross_mask = jnp.where(cross_allowed, 0.0, FLOOR).astype(BF16)
    same_dec, same_mem = same_dec.astype(BF16), same_mem.astype(BF16)
    upstream = (cotangent * padding[..., None].astype(BF16)).reshape(dec, width)
    example = lax.broadcasted_iota(jnp.int32, (1, 16, 1), 1)
    keys = (dec_segments[:, None, :] == example).astype(BF16)
    member_row = lax.broadcasted_iota(jnp.int32, (1, 4 * STEP_ROWS, 1), 1)
    token_row = lax.broadcasted_iota(jnp.int32, (1, 1, step_dec), 2) // length
    members = (
        dec_segments.reshape(steps, 1, step_dec) + NSEG * token_row == member_row
    ).astype(BF16)
    buckets = buckets[None]
    tokens2, memory2 = tokens.reshape(dec, width), memory.reshape(mem, width)
    dma = pltpu.SemaphoreType.DMA

    input_a, qkv_a, prob_a, attended_a, middle, self_w, gains = call(
        self_forward_kernel, steps, me, (tokens2, self_mask), (buckets,), self_pieces,
        (
            shape_of((dec, width), BF16),
            shape_of((dec, 3 * width), BF16),
            shape_of((seqs, PAIRS, length, 2 * length), BF16),
            shape_of((dec, width), BF16),
            shape_of((dec, width), F32),
        ),
        (shape_of((width, ff), BF16), shape_of((8, width), F32)),
        [pltpu.VMEM((PAIRS, length, 2 * length), F32), pltpu.VMEM((width, LANES), BF16), dma((64,))],
        8 * dec * width * width, ("iiw", "iiiiiww"),
    )
    input_b, query_b, kv_b, prob_b, attended_b, after_cross, cross_w = call(
        cross_forward_kernel, steps, me, (middle, memory2, cross_mask), (gains,), cross_pieces,
        (
            shape_of((dec, width), BF16),
            shape_of((dec, width), BF16),
            shape_of((mem, 2 * width), BF16),
            shape_of((seqs, PAIRS, mem_length, 2 * length), BF16),
            shape_of((dec, width), BF16),
            shape_of((dec, width), F32),
        ),
        (shape_of((width, ff), BF16),),
        [dma((32,))],
        12 * dec * width * width, ("iiiw", "iiiiiiw"),
    )
    slot = shape_of((16, 16, ff), BF16)
    feed_slot = shape_of((16, 16, 2 * ff), BF16)
    total, square = shape_of((1, width), F32), shape_of((steps, 4 * STEP_ROWS, LANES), F32)
    token_shape = shape_of((steps, 8, length), F32)
    result, grad_after, feed_low, feed_high, gain_c, square_c, token_c = call(
        feed_kernel, steps, me, (after_cross, upstream, same_dec, members), (gains,), feed_pieces,
        (shape_of((dec, width), BF16), shape_of((dec, width), F32), square, token_shape),
        (feed_slot, feed_slot, total),
        [
            pltpu.VMEM((width, ff), BF16),
            pltpu.VMEM((ff, width), BF16),
            pltpu.VMEM((width, ff), F32),
            pltpu.VMEM((width, ff), F32),
            pltpu.VMEM((ff, width), BF16),
            pltpu.VMEM((2, STEP_ROWS, length, length), F32),
            dma((160,)),
        ],
        48 * dec * width * width, ("iiiiw", "iiwwwii"),
    )
    grad_query_b, grad_kv_b, branch_b, grad_middle, cross_low, cross_high, gain_b, square_b = call(
        cross_backward_kernel, steps, me,
        (grad_after, middle, memory2, input_b, query_b, kv_b, prob_b, attended_b, members),
        (gains, cross_w), (),
        (
            shape_of((dec, width), BF16),
            shape_of((mem, 2 * width), BF16),
            shape_of((dec, width), BF16),
            shape_of((dec, width), F32),
            square,
        ),
        (slot, slot, total),
        [pltpu.VMEM((width, ff), F32), pltpu.VMEM((step_dec, width), BF16)],
        32 * dec * width * width, ("iiiiiiiiiww", "iiiiwwwi"),
    )
    (grad_qkv_a, branch_a, grad_tokens, self_low, self_high, gain_a, square_a, table,
     table_square) = call(
        self_backward_kernel, steps, me,
        (grad_middle, tokens2, input_a, qkv_a, prob_a, attended_a, members, keys),
        (buckets[:, ::-1], gains, self_w), (),
        (
            shape_of((dec, 3 * width), BF16),
            shape_of((dec, width), BF16),
            shape_of((dec, width), BF16),
            square,
            shape_of((steps, STEP_ROWS, 8, LANES), F32),
        ),
        (slot, slot, total, shape_of((H, LANES), F32)),
        [
            pltpu.VMEM((width, ff), F32),
            pltpu.VMEM((step_dec, width), BF16),
            pltpu.VMEM((STEP_ROWS, H, 8, length), F32),
        ],
        32 * dec * width * width, ("iiiiiiiiwww", "iiiwwwiwi"),
    )
    grad_memory, token_m = call(
        memory_kernel, steps, None, (memory2, grad_kv_b, same_mem), (cross_w,), (),
        (shape_of((mem, width), BF16), shape_of((steps, 8, mem_length), F32)), (), [],
        12 * dec * width * width, ("iiiw", "ii"),
    )
    (token_d,) = call(
        gram_kernel, steps, None,
        (same_dec, input_a, grad_qkv_a, attended_a, branch_a, input_b, grad_query_b, attended_b,
         branch_b),
        (), (), (token_shape,), (), [], 20 * dec * width * length, ("iiiiiiiii", "i"),
    )

    def by_example(tokens_part, segments):
        part = tokens_part[:, :STEP_ROWS].reshape(segments.shape)
        hits = segments[:, None, :] == lax.broadcasted_iota(jnp.int32, (1, NSEG, 1), 1)
        return jnp.sum(jnp.where(hits, part[:, None, :], 0.0), axis=-1)

    examples = by_example(token_c + token_d, dec_segments) + by_example(token_m, mem_segments)
    squares = (square_a + square_b + square_c)[:, :, 0].reshape(seqs, NSEG)
    examples = examples + squares + table_square[..., :NSEG, 0].reshape(seqs, NSEG)
    sums = (gain_a[0], gain_b[0], gain_c[0], table[:, :NB].T.reshape(-1))
    slots = ((feed_low, feed_high), (cross_low, cross_high), (self_low, self_high))
    return (
        result.reshape(tokens.shape),
        grad_tokens.reshape(tokens.shape),
        grad_memory.reshape(memory.shape),
        slots,
        sums,
        examples / COUNT,
    )


def solution(mesh):
    rows = P(AXES)
    arrays, weights, vectors = (P(AXES, None, None),) * 3, (P(AXES, None),) * 10, (rows,) * 4
    placed = arrays + (P(AXES, None),) * 3 + (P(),) + weights + vectors
    return jax.shard_map(
        on_device,
        mesh=mesh,
        in_specs=placed,
        out_specs=arrays + weights + vectors + (P(AXES, None), P()),
        check_vma=False,
    )
```

```python
from functools import partial

import jax
import jax.numpy as jnp
from jax import lax
from jax.experimental import pallas as pl
from jax.experimental.pallas import tpu as pltpu
from jax.sharding import PartitionSpec as P

H = 8
DH = 64
NB = 32
NSEG = 4
COUNT = 4196096
EPSILON = 1e-06
FLOOR = -1e30
F32 = jnp.float32
BF16 = jnp.bfloat16
PAIRS = H // 2
LANES = 128
STEP_ROWS = 4
VMEM_LIMIT = 50 * 2**20

COLUMN = (0, 8, 16, 24)
PLANE = (0, 1, 4, 5)
CODES = tuple(2 * c + mask + z for c in (0, 1) for mask in PLANE for z in COLUMN)
CHIPS = tuple(z + mask for z in COLUMN for mask in PLANE)


def nn(left, right):
    return lax.dot_general(left, right, (((1,), (0,)), ((), ())), preferred_element_type=F32)


def nt(left, right):
    return lax.dot_general(left, right, (((1,), (1,)), ((), ())), preferred_element_type=F32)


def tn(left, right):
    return lax.dot_general(left, right, (((0,), (0,)), ((), ())), preferred_element_type=F32)


def inverse_root(values):
    return lax.rsqrt(jnp.mean(values * values, axis=-1, keepdims=True) + EPSILON)


def head_pair(values):
    low = (lax.broadcasted_iota(jnp.int32, (1, LANES), 1) < DH).astype(BF16)
    return jnp.concatenate([values * low, values * (1 - low)], axis=0)


def fold_pair(both, queries):
    own = jnp.concatenate([both[:DH, :queries], both[DH:, queries:]], axis=0)
    return own.astype(BF16).T


def block_rows(block):
    return pl.ds(pl.multiple_of(block * 16, 16), 16)


def start_copies(pairs, sems):
    copies = [pltpu.make_async_copy(*pair, sems.at[i]) for i, pair in enumerate(pairs)]
    for copy in copies:
        copy.start()
    return copies


def read_rows(grad_w, block):
    return grad_w[block_rows(block), :].astype(BF16)


def softmax_columns(scores):
    shifted = jnp.exp(scores - jnp.max(scores, axis=0, keepdims=True))
    return (shifted * (1.0 / jnp.sum(shifted, axis=0, keepdims=True))).astype(BF16)


def each_row(row):
    for r in range(STEP_ROWS):
        row(r, 0)


def gram(left):
    return nt(left, left)


def self_forward_kernel(me_ref, tokens_ref, mask_ref, buckets_ref, *refs):
    pieces, refs = refs[:8], refs[8:]
    input_ref, qkv_ref, prob_ref, attended_ref, weight_ref, gains_ref = refs[:6]
    bias_ref, small_ref, sems = refs[6:]
    length = mask_ref.shape[1]
    width = tokens_ref.shape[1]

    @pl.when(pl.program_id(0) == 0)
    def _():
        pairs = []
        for k, code in enumerate(CODES):
            rows = block_rows(me_ref[0] ^ code)
            source = pieces[k // 4].at[k % 4]
            pairs.append((source.at[:, : 3 * width], weight_ref.at[rows, :]))
            pairs.append((source.at[:, 3 * width :], small_ref.at[rows, :]))
        for copy in start_copies(pairs, sems):
            copy.wait()
        small = small_ref[...].astype(F32).T
        gains_ref[...] = small[:8]
        place = lax.broadcasted_iota(jnp.int32, (H, width), 1) % 16
        head = lax.broadcasted_iota(jnp.int32, (H, width), 0)
        table = jnp.where(place == head, small[3:4], 0.0).astype(BF16)
        bucket = lax.broadcasted_iota(jnp.int32, (width, length), 0) // 16
        curves = nn(table, (bucket == buckets_ref[...]).astype(F32).astype(BF16))
        for h in range(H):
            curve = jnp.broadcast_to(curves[h : h + 1, :], (length, length))
            lanes = slice((h % 2) * length, (h % 2 + 1) * length)
            bias_ref[h // 2, :, lanes] = pltpu.roll(curve, 0, 1, stride=1, stride_axis=0)

    values = tokens_ref[...].astype(F32)
    normed = (values * inverse_root(values) * gains_ref[0:1, :]).astype(BF16)
    input_ref[...] = normed
    for k in range(3):
        cols = slice(k * width, (k + 1) * width)
        qkv_ref[:, cols] = nn(normed, weight_ref[:, cols]).astype(BF16)

    def row(r, carry):
        rows = pl.ds(pl.multiple_of(r * length, length), length)
        mask = mask_ref[r].astype(F32)
        mask = jnp.concatenate([mask, mask], axis=1)
        for p in range(PAIRS):
            query = qkv_ref[rows, p * LANES : (p + 1) * LANES]
            key = qkv_ref[rows, width + p * LANES : width + (p + 1) * LANES]
            value = qkv_ref[rows, 2 * width + p * LANES : 2 * width + (p + 1) * LANES]
            prob = softmax_columns(nt(key, head_pair(query)) + bias_ref[p] + mask)
            prob_ref[r, p] = prob
            attended_ref[rows, p * LANES : (p + 1) * LANES] = fold_pair(nn(value.T, prob), length)
        return carry

    each_row(row)


def cross_forward_kernel(me_ref, tokens_ref, attended_a_ref, memory_ref, mask_ref, gains_ref,
                         own_ref, other_ref, middle_ref, input_ref, query_ref, kv_ref, prob_ref,
                         attended_ref, after_ref, weight_ref, sems):
    mem_length, length = mask_ref.shape[1:]
    width = tokens_ref.shape[1]

    @pl.when(pl.program_id(0) == 0)
    def _():
        core = me_ref[0] & 2
        pairs = []
        for k, code in enumerate(CHIPS):
            cols = slice(0, 5 * width)
            pairs.append((own_ref.at[k, :, cols], weight_ref.at[block_rows(code + core), :]))
            pairs.append((other_ref.at[k], weight_ref.at[block_rows(code + 2 - core), :]))
        for copy in start_copies(pairs, sems):
            copy.wait()

    values = tokens_ref[...].astype(F32) + nn(attended_a_ref[...], weight_ref[:, :width])
    middle_ref[...] = values
    normed = (values * inverse_root(values) * gains_ref[1:2, :]).astype(BF16)
    input_ref[...] = normed
    query_ref[...] = nn(normed, weight_ref[:, width : 2 * width]).astype(BF16)
    for k in range(2):
        kv_ref[:, k * width : (k + 1) * width] = nn(
            memory_ref[...], weight_ref[:, (k + 2) * width : (k + 3) * width]
        ).astype(BF16)

    def row(r, carry):
        rows = pl.ds(pl.multiple_of(r * length, length), length)
        mem_rows = pl.ds(pl.multiple_of(r * mem_length, mem_length), mem_length)
        mask = mask_ref[r].astype(F32)
        mask = jnp.concatenate([mask, mask], axis=1)
        for p in range(PAIRS):
            query = query_ref[rows, p * LANES : (p + 1) * LANES]
            key = kv_ref[mem_rows, p * LANES : (p + 1) * LANES]
            value = kv_ref[mem_rows, width + p * LANES : width + (p + 1) * LANES]
            prob = softmax_columns(nt(key, head_pair(query)) + mask)
            prob_ref[r, p] = prob
            attended_ref[rows, p * LANES : (p + 1) * LANES] = fold_pair(nn(value.T, prob), length)
        return carry

    each_row(row)
    after_ref[...] = middle_ref[...] + nn(attended_ref[...], weight_ref[:, 4 * width :])


def norm_back(values, gain, grad_normed):
    inverse = inverse_root(values)
    scaled = values * inverse
    upper = grad_normed * gain
    grad = inverse * (upper - scaled * jnp.mean(upper * scaled, axis=-1, keepdims=True))
    return grad, grad_normed * scaled


def gain_sums(step, terms, members_ref, total_ref, square_ref):
    sums = nn(members_ref[0], terms.astype(BF16))
    total = jnp.sum(sums, axis=0, keepdims=True)
    total_ref[...] = jnp.where(step == 0, 0.0, total_ref[...]) + total
    square = jnp.sum(sums * sums, axis=1, keepdims=True)
    square_ref[0] = jnp.broadcast_to(square, square_ref.shape[1:])


def feed_kernel(me_ref, after_ref, upstream_ref, same_ref, members_ref, gains_ref, own_ref,
                other_ref, result_ref, grad_after_ref, slots_ref, total_ref, square_ref, token_ref,
                hidden_w, back_w, grad_hidden_w, grad_back_w, flipped, gram_ref, sems):
    step = pl.program_id(0)
    length = same_ref.shape[1]
    width, ff = hidden_w.shape
    parts = ff // width

    @pl.when(step == 0)
    def _():
        core = me_ref[0] & 2
        pairs = []
        for k, code in enumerate(CHIPS):
            for piece, block in ((own_ref, code + core), (other_ref, code + 2 - core)):
                start = piece.shape[2] - 2 * ff
                source = piece.at[k, :, start : start + ff]
                pairs.append((source, hidden_w.at[block_rows(block), :]))
                for j in range(parts):
                    first = start + ff + j * width
                    source = piece.at[k, :, first : first + width]
                    pairs.append((source, back_w.at[block_rows(block * parts + j), :]))
        copies = start_copies(pairs, sems)
        grad_hidden_w[...] = jnp.zeros_like(grad_hidden_w)
        grad_back_w[...] = jnp.zeros_like(grad_back_w)
        for copy in copies:
            copy.wait()

    values = after_ref[...]
    gain = gains_ref[2:3, :]
    normed = (values * inverse_root(values) * gain).astype(BF16)
    normed_flip = normed.T
    branch = upstream_ref[...]
    branch_flip = branch.T
    gram_ref[...] = jnp.zeros_like(gram_ref)
    root = 0.7978845608028654

    def chunk(c, carry):
        result, grad_normed = carry
        cols = pl.ds(pl.multiple_of(c * width, width), width)
        w_in = hidden_w[:, cols]
        w_out = back_w[cols, :]
        hidden = nn(normed, w_in)
        square = hidden * hidden
        bent = jnp.tanh(hidden * (root + (root * 0.044715) * square))
        half = 0.5 + 0.5 * bent
        active = (hidden * half).astype(BF16)
        slope = half + (0.5 * hidden) * (1.0 - bent * bent) * (
            root + (3.0 * root * 0.044715) * square
        )
        grad = (nt(branch, w_out) * slope).astype(BF16)
        result = result + nn(active, w_out)
        grad_normed = grad_normed + nt(grad, w_in)
        grad_hidden_w[:, cols] += nn(normed_flip, grad)
        grad_back_w[:, cols] += nn(branch_flip, active)
        for r in range(STEP_ROWS):
            rows = slice(r * length, (r + 1) * length)
            gram_ref[0, r] += gram(active[rows])
            gram_ref[1, r] += gram(grad[rows])
        return result, grad_normed

    zero = jnp.zeros_like(values)
    result, grad_normed = lax.fori_loop(0, parts, chunk, (zero, zero))
    result_ref[...] = (values + result).astype(BF16)
    grad, terms = norm_back(values, gain, grad_normed)
    grad_after_ref[...] = branch.astype(F32) + grad
    gain_sums(step, terms, members_ref, total_ref, square_ref)
    for r in range(STEP_ROWS):
        rows = slice(r * length, (r + 1) * length)
        products = gram_ref[0, r] * gram(branch[rows]) + gram_ref[1, r] * gram(normed[rows])
        token_ref[0, r : r + 1, :] = jnp.sum(products * same_ref[r], axis=0, keepdims=True)

    @pl.when(step == pl.num_programs(0) - 1)
    def _():
        for j in range(parts):
            flipped[j * width : (j + 1) * width, :] = (
                grad_back_w[:, j * width : (j + 1) * width].astype(BF16).T
            )

        for k, block in enumerate(CODES):
            own = [read_rows(grad_hidden_w, block)]
            own += [flipped[block_rows(block * parts + j), :] for j in range(parts)]
            slots_ref[k] = jnp.concatenate(own, axis=1)


def score_grads(prob, grad_prob):
    prob = prob.astype(F32)
    dots = jnp.sum(prob * grad_prob, axis=0, keepdims=True)
    return prob * (grad_prob - dots)


def cross_scores_kernel(grad_after_ref, query_ref, kv_ref, prob_ref, weight_ref, grad_query_ref,
                        grad_kv_ref, branch_ref, grad_attended):
    mem_length = prob_ref.shape[2]
    length = prob_ref.shape[3] // 2
    width = grad_after_ref.shape[1]
    branch = grad_after_ref[...].astype(BF16)
    branch_ref[...] = branch
    grad_attended[...] = nt(branch, weight_ref[:, 4 * width :]).astype(BF16)

    def row(r, carry):
        rows = pl.ds(r * length, length)
        mem_rows = pl.ds(r * mem_length, mem_length)
        for p in range(PAIRS):
            lanes = slice(p * LANES, (p + 1) * LANES)
            upper = slice(width + p * LANES, width + (p + 1) * LANES)
            key = kv_ref[mem_rows, lanes]
            value = kv_ref[mem_rows, upper]
            query = head_pair(query_ref[rows, lanes])
            grad_out = head_pair(grad_attended[rows, lanes])
            prob = prob_ref[r, p]
            grad_score = score_grads(prob, nt(value, grad_out)).astype(BF16)
            grad_kv_ref[mem_rows, lanes] = nn(grad_score, query).astype(BF16)
            grad_kv_ref[mem_rows, upper] = nn(prob, grad_out).astype(BF16)
            grad_query_ref[rows, lanes] = fold_pair(nn(key.T, grad_score), length)

    each_row(row)


def cross_weights_kernel(grad_after_ref, middle_ref, memory_ref, attended_a_ref, input_ref,
                         grad_query_ref, grad_kv_ref, attended_ref, branch_ref, members_ref,
                         gains_ref, weight_ref, branch_a_ref, grad_middle_ref, slots_ref,
                         total_ref, square_ref, grad_w):
    step = pl.program_id(0)
    width = middle_ref.shape[1]
    grad_query = grad_query_ref[...]
    grad_normed = nt(grad_query, weight_ref[:, width : 2 * width])
    grad, terms = norm_back(middle_ref[...], gains_ref[1:2, :], grad_normed)
    grad_middle = grad_after_ref[...] + grad
    grad_middle_ref[...] = grad_middle
    branch_a = grad_middle.astype(BF16)
    branch_a_ref[...] = branch_a
    gain_sums(step, terms, members_ref, total_ref, square_ref)

    @pl.when(step == 0)
    def _():
        grad_w[...] = jnp.zeros_like(grad_w)

    grad_w[:, :width] += tn(attended_a_ref[...], branch_a)
    grad_w[:, width : 2 * width] += tn(input_ref[...], grad_query)
    grad_w[:, 2 * width : 4 * width] += tn(memory_ref[...], grad_kv_ref[...])
    grad_w[:, 4 * width :] += tn(attended_ref[...], branch_ref[...])

    @pl.when(step == pl.num_programs(0) - 1)
    def _():
        for k, block in enumerate(CODES):
            slots_ref[k] = read_rows(grad_w, block)


def self_scores_kernel(branch_ref, qkv_ref, prob_ref, keys_ref, turned_buckets_ref, weight_ref,
                       grad_qkv_ref, table_ref, table_square_ref, grad_attended, bands):
    step = pl.program_id(0)
    length = prob_ref.shape[2]
    width = branch_ref.shape[1]
    grad_attended[...] = nt(branch_ref[...], weight_ref[:, :width]).astype(BF16)

    @pl.when(step == 0)
    def _():
        table_ref[...] = jnp.zeros_like(table_ref)

    row_i = lax.broadcasted_iota(jnp.int32, (2 * length, 2 * length), 0)
    col_i = lax.broadcasted_iota(jnp.int32, (2 * length, 2 * length), 1)
    turned = (row_i // length) * length + length - 1 - row_i % length
    flip = (turned == col_i).astype(F32).astype(BF16)

    def row(r, carry):
        rows = pl.ds(r * length, length)
        keys = keys_ref[r]
        for p in range(PAIRS):
            lanes = slice(p * LANES, (p + 1) * LANES)
            middle = slice(width + p * LANES, width + (p + 1) * LANES)
            upper = slice(2 * width + p * LANES, 2 * width + (p + 1) * LANES)
            key = qkv_ref[rows, middle]
            value = qkv_ref[rows, upper]
            query = head_pair(qkv_ref[rows, lanes])
            grad_out = head_pair(grad_attended[rows, lanes])
            prob = prob_ref[r, p]
            grad_score = score_grads(prob, nt(value, grad_out)).astype(BF16)
            grad_qkv_ref[rows, middle] = nn(grad_score, query).astype(BF16)
            grad_qkv_ref[rows, upper] = nn(prob, grad_out).astype(BF16)
            grad_qkv_ref[rows, lanes] = fold_pair(nn(key.T, grad_score), length)
            mirrored = nn(grad_score, flip)
            for h in range(2):
                own = mirrored[:, h * length : (h + 1) * length]
                own = pltpu.roll(own, 0, 1, stride=1, stride_axis=0)
                bands[r, 2 * p + h] = nn(keys, own.astype(BF16))[:8]

    each_row(row)
    bucket = lax.broadcasted_iota(jnp.int32, (LANES, length), 0)
    near = (bucket == turned_buckets_ref[...]).astype(F32)
    flat = bands[...].reshape(STEP_ROWS * H * 8, length)
    per_bucket = lax.dot_general(
        flat, near, (((1,), (1,)), ((), ())), preferred_element_type=F32,
        precision=lax.Precision.HIGHEST,
    ).reshape(STEP_ROWS, H, 8, LANES)
    table_ref[...] += jnp.sum(jnp.sum(per_bucket, axis=0), axis=1)
    squares = jnp.sum(jnp.sum(per_bucket * per_bucket, axis=1), axis=-1, keepdims=True)
    table_square_ref[0] = jnp.broadcast_to(squares, (STEP_ROWS, 8, LANES))


def self_weights_kernel(me_ref, grad_middle_ref, tokens_ref, input_ref, grad_qkv_ref, members_ref,
                        gains_ref, weight_ref, table_ref, total_b_ref, total_c_ref,
                        grad_tokens_ref, low_ref, high_ref, square_ref, grad_w, total_ref,
                        small_ref):
    step = pl.program_id(0)
    width = tokens_ref.shape[1]
    grad_qkv = grad_qkv_ref[...]
    grad_normed = nt(grad_qkv, weight_ref[...])
    grad, terms = norm_back(tokens_ref[...].astype(F32), gains_ref[0:1, :], grad_normed)
    grad_tokens_ref[...] = (grad_middle_ref[...] + grad).astype(BF16)

    @pl.when(step == 0)
    def _():
        grad_w[...] = jnp.zeros_like(grad_w)
        total_ref[...] = jnp.zeros_like(total_ref)

    gain_sums(step, terms, members_ref, total_ref, square_ref)
    grad_w[...] += tn(input_ref[...], grad_qkv)

    @pl.when(step == pl.num_programs(0) - 1)
    def _():
        bucket = lax.broadcasted_iota(jnp.int32, (LANES, width), 0)
        place = lax.broadcasted_iota(jnp.int32, (LANES, width), 1)
        spread = nn(table_ref[...].astype(BF16), (place // 16 == bucket).astype(F32).astype(BF16))
        head = lax.broadcasted_iota(jnp.int32, (H, width), 0)
        lane = lax.broadcasted_iota(jnp.int32, (H, width), 1)
        table = jnp.sum(jnp.where(lane % 16 == head, spread, 0.0), axis=0, keepdims=True)
        small = jnp.zeros((LANES, width), F32)
        row_i = lax.broadcasted_iota(jnp.int32, (LANES, width), 0)
        for k, line in enumerate((total_ref[...], total_b_ref[...], total_c_ref[...], table)):
            small = jnp.where(row_i == k, line, small)
        small_ref[...] = small.T
        for k, code in enumerate(CODES):
            block = me_ref[0] ^ code
            target = low_ref if k < 16 else high_ref
            target[k % 16] = jnp.concatenate(
                [read_rows(grad_w, block), read_rows(small_ref, block)], axis=1
            )


def pair_sum_kernel(low_ref, sent_ref, *outs):
    for t, out in enumerate(outs):
        for s in range(4):
            k = 4 * t + s
            out[s] = (low_ref[k].astype(F32) + sent_ref[k].astype(F32)).astype(BF16)


def plane_sum_kernel(a_ref, b_ref, c_ref, d_ref, own_ref, *outs):
    for s in range(4):
        total = a_ref[s].astype(F32) + b_ref[s].astype(F32)
        total = total + c_ref[s].astype(F32) + d_ref[s].astype(F32)
        if s == 0:
            own_ref[...] = total
        else:
            outs[s - 1][...] = total.astype(BF16)


def column_sum_kernel(own_ref, b_ref, c_ref, d_ref, out_ref):
    total = own_ref[...] + b_ref[...].astype(F32)
    out_ref[...] = total + c_ref[...].astype(F32) + d_ref[...].astype(F32)


def small_call(kernel, ins, after, outs):
    return pl.pallas_call(
        ignoring(kernel, len(ins), len(after)),
        out_shape=outs,
        in_specs=[pl.BlockSpec(memory_space=pltpu.VMEM)] * len(ins)
        + [pl.BlockSpec(memory_space=pl.ANY)] * len(after),
        compiler_params=pltpu.CompilerParams(vmem_limit_bytes=20 * 2**20),
    )(*ins, *after)


def grad_memory_kernel(grad_kv_ref, weight_ref, grad_memory_ref):
    width = grad_memory_ref.shape[1]
    weight = weight_ref[:, 2 * width : 4 * width]
    grad_memory_ref[...] = nt(grad_kv_ref[...], weight).astype(BF16)


def memory_gram_kernel(memory_ref, grad_kv_ref, same_ref, token_ref):
    mem_length = same_ref.shape[1]
    for r in range(STEP_ROWS):
        rows = slice(r * mem_length, (r + 1) * mem_length)
        products = gram(memory_ref[rows, :]) * gram(grad_kv_ref[rows, :])
        token_ref[0, r : r + 1, :] = jnp.sum(products * same_ref[r], axis=0, keepdims=True)


def gram_kernel(same_ref, *refs):
    pairs, token_ref = refs[:-1], refs[-1]
    length = same_ref.shape[1]
    for r in range(STEP_ROWS):
        rows = slice(r * length, (r + 1) * length)
        products = sum(
            gram(left[rows, :]) * gram(right[rows, :])
            for left, right in zip(pairs[::2], pairs[1::2])
        )
        token_ref[0, r : r + 1, :] = jnp.sum(products * same_ref[r], axis=0, keepdims=True)


def rows_spec(array, steps):
    shape = (array.shape[0] // steps,) + array.shape[1:]
    return pl.BlockSpec(shape, lambda i, *_: (i,) + (0,) * (len(shape) - 1))


def whole_spec(array):
    return pl.BlockSpec(array.shape, lambda i, *_: (0,) * len(array.shape))


def ignoring(kernel, first, count):
    return lambda *refs: kernel(*refs[:first], *refs[first + count :])


def call(kernel, steps, me, blocked, whole, pieces, outs_blocked, outs_whole, scratch, flops,
         order, after=()):
    ins, in_specs = [], []
    blocked, whole = list(blocked), list(whole)
    for kind in order[0]:
        array = (blocked if kind == "i" else whole).pop(0)
        ins.append(array)
        in_specs.append(rows_spec(array, steps) if kind == "i" else whole_spec(array))
    kernel = ignoring(kernel, len(ins) + len(pieces) + (me is not None), len(after))
    ins += [*pieces, *after]
    in_specs += [pl.BlockSpec(memory_space=pl.ANY)] * (len(pieces) + len(after))
    outs, out_specs = [], []
    outs_blocked, outs_whole = list(outs_blocked), list(outs_whole)
    for kind in order[1]:
        out = (outs_blocked if kind == "i" else outs_whole).pop(0)
        outs.append(out)
        out_specs.append(rows_spec(out, steps) if kind == "i" else whole_spec(out))
    moved = sum(a.size * a.dtype.itemsize for a in ins + outs)
    prefetch = 0 if me is None else 1
    return pl.pallas_call(
        kernel,
        out_shape=outs,
        grid_spec=pltpu.PrefetchScalarGridSpec(
            num_scalar_prefetch=prefetch,
            grid=(steps,),
            in_specs=in_specs,
            out_specs=out_specs,
            scratch_shapes=scratch,
        ),
        compiler_params=pltpu.CompilerParams(
            dimension_semantics=("arbitrary",), vmem_limit_bytes=VMEM_LIMIT
        ),
        cost_estimate=pl.CostEstimate(flops=flops, bytes_accessed=moved, transcendentals=0),
    )(*(() if me is None else (me,)), *ins)


FINE = ("z", "y", "core", "x")


def shape_of(shape, dtype):
    return jax.ShapeDtypeStruct(shape, dtype)


def shift(array, mask):
    return lax.ppermute(array, FINE, [(i, i ^ mask) for i in range(32)])


def gather_pieces(shard):
    column = jnp.stack([shard] + [shift(shard, code) for code in COLUMN[1:]])
    plane = [column] + [shift(column, mask) for mask in PLANE[1:]]
    return plane + [shift(piece, 2) for piece in plane]


def gather_chips(shard):
    return lax.all_gather(shard, ("z", "y", "x"), axis=0)


def split_back(back):
    blocks = back.shape[0] // 64
    parts = back.reshape(blocks, 4, 16, back.shape[1]).transpose(0, 2, 1, 3)
    return parts.reshape(16 * blocks, 4 * back.shape[1])


def join_back(parts):
    blocks, width = parts.shape[0] // 16, parts.shape[1] // 4
    return parts.reshape(blocks, 16, 4, width).transpose(0, 2, 1, 3).reshape(64 * blocks, width)


def small_columns(gains, table):
    table = jnp.pad(table.reshape(-1, H), ((0, 0), (0, 16 - H))).reshape(-1)
    columns = jnp.stack(list(gains) + [table], axis=1)
    return jnp.pad(columns, ((0, 0), (0, LANES - columns.shape[1])))


def in_order(slots):
    return slots[jnp.array([CODES.index(block) for block in range(32)])].reshape(-1, slots.shape[2])


def hold(array, after):
    return lax.optimization_barrier((array, after))[0]


class Near:
    axes = FINE

    def __init__(self):
        self.me = lax.axis_index(FINE)

    def weights(self, own, cross, feed):
        self.own = gather_pieces(own)
        self.rest = gather_chips(jnp.concatenate([cross, feed], axis=1))
        self.split = cross.shape[1]

    def exchange_weights(self, after):
        rest = hold(self.rest, after)
        self.cross = (rest, shift(rest[:, :, : self.split], 2))
        self.feed = (rest, shift(rest[:, :, self.split :], 2))

    def scatter_core(self, slots):
        return lax.psum_scatter(slots.reshape((2, 4, 4) + slots.shape[1:]), "core")

    def scatter_plane(self, slots):
        return lax.psum_scatter(slots, ("y", "x"))

    def scatter_column(self, slots):
        return lax.psum_scatter(slots, "z")

    exchange = staticmethod(partial(shift, mask=2))

    def plane(self, pieces):
        return [shift(piece, mask) for piece, mask in zip(pieces, PLANE[1:])]

    def column(self, pieces):
        return [shift(piece, code) for piece, code in zip(pieces, COLUMN[1:])]

    def sum_all(self, value):
        sent = jnp.broadcast_to(value, (32, LANES))
        return jnp.sum(lax.all_to_all(sent, FINE, 0, 0, tiled=True)[:, 0])


class Far:
    axes = ("wide", "narrow")
    me = 0

    def scatter_core(self, slots):
        return slots

    scatter_plane = scatter_core

    def scatter_column(self, slots):
        return in_order(slots)

    def weights(self, own, cross, feed):
        blocks = own.reshape(32, 16, -1)[jnp.array(CODES)]
        self.own = [blocks[4 * t : 4 * t + 4] for t in range(8)]
        rest = jnp.concatenate([cross, feed], axis=1).reshape(32, 16, -1)
        mine, other = (rest[jnp.array(CHIPS) + core] for core in (0, 2))
        split = cross.shape[1]
        self.cross = (mine, other[:, :, :split])
        self.feed = (mine, other[:, :, split:])

    def exchange_weights(self, after):
        pass


def on_device(near, tokens, memory, cotangent, dec_segments, mem_segments, padding, buckets,
              w_query, w_key, w_value, w_out, c_query, c_key, c_value, c_out, w_hidden, w_back,
              gain_self, gain_cross, gain_ff, bias_table):
    weights = (w_query, w_key, w_value, w_out, c_query, c_key, c_value, c_out, w_hidden, w_back,
               gain_self, gain_cross, gain_ff, bias_table)
    way = Near() if near else Far()
    count = lax.axis_size(way.axes)
    if not near:
        weights = [lax.all_gather(w, way.axes, axis=0, tiled=True) for w in weights]
    small = small_columns(weights[10:13], weights[13])
    way.weights(
        jnp.concatenate([*weights[:3], small], axis=1),
        jnp.concatenate(weights[3:8], axis=1),
        jnp.concatenate([weights[8], split_back(weights[9])], axis=1),
    )
    result, grad_tokens, grad_memory, sums, examples = local_part(
        way, tokens, memory, cotangent, dec_segments, mem_segments, padding, buckets
    )
    feed, cross, own = sums
    width = tokens.shape[2]
    grads = [own[:, k * width : (k + 1) * width] for k in range(3)]
    grads += [cross[:, k * width : (k + 1) * width] for k in range(5)]
    grads += [feed[:, : 4 * width], join_back(feed[:, 4 * width :])]
    grads += [own[:, 3 * width + k] for k in range(3)]
    grads.append(own[:, 3 * width + 3].reshape(-1, 16)[:, :H].reshape(-1))
    if near:
        square = sum(jnp.sum(part * part) for part in sums)
        global_norm = way.sum_all(square)
    else:
        grads = [lax.psum_scatter(g, way.axes, scatter_dimension=0, tiled=True) for g in grads]
        global_norm = lax.psum(sum(jnp.sum(g * g) for g in grads), way.axes)
    return (result, grad_tokens, grad_memory, *grads, examples, global_norm / COUNT)


def local_part(way, tokens, memory, cotangent, dec_segments, mem_segments, padding, buckets):
    seqs, length, width = tokens.shape
    mem_length = memory.shape[1]
    steps = seqs // STEP_ROWS
    dec, mem = seqs * length, seqs * mem_length
    step_dec = STEP_ROWS * length
    ff = 4 * width

    same_dec = dec_segments[:, :, None] == dec_segments[:, None, :]
    same_mem = mem_segments[:, :, None] == mem_segments[:, None, :]
    keys_i = lax.broadcasted_iota(jnp.int32, (length, length), 0)
    queries_i = lax.broadcasted_iota(jnp.int32, (length, length), 1)
    allowed = same_dec & (keys_i <= queries_i) & ((padding[:, :, None] > 0) | (keys_i == queries_i))
    self_mask = jnp.where(allowed, 0.0, FLOOR).astype(BF16)
    cross_allowed = mem_segments[:, :, None] == dec_segments[:, None, :]
    cross_mask = jnp.where(cross_allowed, 0.0, FLOOR).astype(BF16)
    same_dec, same_mem = same_dec.astype(BF16), same_mem.astype(BF16)
    upstream = (cotangent * padding[..., None].astype(BF16)).reshape(dec, width)
    example = lax.broadcasted_iota(jnp.int32, (1, 16, 1), 1)
    keys = (dec_segments[:, None, :] == example).astype(BF16)
    member_row = lax.broadcasted_iota(jnp.int32, (1, 4 * STEP_ROWS, 1), 1)
    token_row = lax.broadcasted_iota(jnp.int32, (1, 1, step_dec), 2) // length
    members = (
        dec_segments.reshape(steps, 1, step_dec) + NSEG * token_row == member_row
    ).astype(BF16)
    buckets = buckets[None]
    tokens2, memory2 = tokens.reshape(dec, width), memory.reshape(mem, width)
    dma = pltpu.SemaphoreType.DMA

    me = jnp.full((1,), way.me, jnp.int32)
    flops = 2 * dec * width * width

    input_a, qkv_a, prob_a, attended_a, self_w, gains = call(
        self_forward_kernel, steps, me, (tokens2, self_mask), (buckets,), way.own,
        (
            shape_of((dec, width), BF16),
            shape_of((dec, 3 * width), BF16),
            shape_of((seqs, PAIRS, length, 2 * length), BF16),
            shape_of((dec, width), BF16),
        ),
        (shape_of((width, 3 * width), BF16), shape_of((8, width), F32)),
        [pltpu.VMEM((PAIRS, length, 2 * length), F32), pltpu.VMEM((width, LANES), BF16), dma((64,))],
        6 * flops, ("iiw", "iiiiww"),
    )
    way.exchange_weights(attended_a)
    middle, input_b, query_b, kv_b, prob_b, attended_b, after_cross, cross_w = call(
        cross_forward_kernel, steps, me, (tokens2, attended_a, memory2, cross_mask), (gains,),
        way.cross,
        (
            shape_of((dec, width), F32),
            shape_of((dec, width), BF16),
            shape_of((dec, width), BF16),
            shape_of((mem, 2 * width), BF16),
            shape_of((seqs, PAIRS, mem_length, 2 * length), BF16),
            shape_of((dec, width), BF16),
            shape_of((dec, width), F32),
        ),
        (shape_of((width, 5 * width), BF16),),
        [dma((32,))],
        10 * flops, ("iiiiw", "iiiiiiiw"),
    )
    total, square = shape_of((1, width), F32), shape_of((steps, 4 * STEP_ROWS, LANES), F32)
    token_shape = shape_of((steps, 8, length), F32)
    result, grad_after, feed_slots, gain_c, square_c, token_c = call(
        feed_kernel, steps, me, (after_cross, upstream, same_dec, members), (gains,), way.feed,
        (shape_of((dec, width), BF16), shape_of((dec, width), F32), square, token_shape),
        (shape_of((32, 16, 2 * ff), BF16), total),
        [
            pltpu.VMEM((width, ff), BF16),
            pltpu.VMEM((ff, width), BF16),
            pltpu.VMEM((width, ff), F32),
            pltpu.VMEM((width, ff), F32),
            pltpu.VMEM((ff, width), BF16),
            pltpu.VMEM((2, STEP_ROWS, length, length), F32),
            dma((160,)),
        ],
        26 * flops, ("iiiiw", "iiwwii"),
    )
    feed_sum = way.scatter_core(feed_slots)
    grad_query_b, grad_kv_b, branch_b = call(
        cross_scores_kernel, steps, None, (grad_after, query_b, kv_b, prob_b), (cross_w,), (),
        (
            shape_of((dec, width), BF16),
            shape_of((mem, 2 * width), BF16),
            shape_of((dec, width), BF16),
        ),
        (),
        [pltpu.VMEM((step_dec, width), BF16)],
        12 * flops, ("iiiiw", "iii"),
    )
    feed_sum = hold(feed_sum, grad_query_b)
    branch_a, grad_middle, cross_slots, gain_b, square_b = call(
        cross_weights_kernel, steps, None,
        (grad_after, middle, memory2, attended_a, input_b, grad_query_b, grad_kv_b, attended_b,
         branch_b, members),
        (gains, cross_w), (),
        (shape_of((dec, width), BF16), shape_of((dec, width), F32), square),
        (shape_of((32, 16, 5 * width), BF16), total),
        [pltpu.VMEM((width, 5 * width), F32)],
        9 * flops, ("iiiiiiiiiiww", "iiwwi"), (feed_sum,),
    )
    feed_sum = way.scatter_plane(feed_sum)
    cross_sum = way.scatter_core(cross_slots)
    grad_qkv_a, table, table_square = call(
        self_scores_kernel, steps, None, (branch_a, qkv_a, prob_a, keys),
        (buckets[:, ::-1], cross_w), (),
        (shape_of((dec, 3 * width), BF16), shape_of((steps, STEP_ROWS, 8, LANES), F32)),
        (shape_of((H, LANES), F32),),
        [pltpu.VMEM((step_dec, width), BF16), pltpu.VMEM((STEP_ROWS, H, 8, length), F32)],
        10 * flops, ("iiiiww", "iwi"),
    )
    feed_sum, cross_sum = hold(feed_sum, grad_qkv_a), hold(cross_sum, grad_qkv_a)
    slot = shape_of((16, 16, 3 * width + LANES), BF16)
    grad_tokens, self_low, self_high, square_a = call(
        self_weights_kernel, steps, me, (grad_middle, tokens2, input_a, grad_qkv_a, members),
        (gains, self_w, table, gain_b, gain_c), (),
        (shape_of((dec, width), BF16), square),
        (slot, slot),
        [
            pltpu.VMEM((width, 3 * width), F32),
            pltpu.VMEM((1, width), F32),
            pltpu.VMEM((width, LANES), F32),
        ],
        7 * flops, ("iiiiiwwwww", "iwwi"), (feed_sum, cross_sum),
    )
    feed_sum, cross_sum = way.scatter_column(feed_sum), way.scatter_plane(cross_sum)

    def fill(*after):
        (grad_memory,) = call(
            grad_memory_kernel, steps, None, (grad_kv_b,), (cross_w,), (),
            (shape_of((mem, width), BF16),), (), [], 6 * flops, ("iw", "i"), after,
        )
        return grad_memory

    def fill_grams(*after):
        (token_m,) = call(
            memory_gram_kernel, steps, None, (memory2, grad_kv_b, same_mem), (), (),
            (shape_of((steps, 8, mem_length), F32),), (), [], 4 * flops, ("iii", "i"), after,
        )
        return token_m

    def fill_tokens(*after):
        (token_d,) = call(
            gram_kernel, steps, None,
            (same_dec, input_a, grad_qkv_a, attended_a, branch_a, input_b, grad_query_b,
             attended_b, branch_b),
            (), (), (token_shape,), (), [], 4 * flops, ("iiiiiiiii", "i"), after,
        )
        return token_d

    grad_memory = fill(self_low)
    if isinstance(way, Near):
        sent = way.exchange(self_high)
        piece = shape_of((4,) + slot.shape[1:], BF16)
        parts = small_call(pair_sum_kernel, (self_low, sent), (grad_memory,), (piece,) * 4)
        crossed = way.plane(parts[1:])
        cross_sum = hold(cross_sum, grad_memory)
        token_m = fill_grams(parts[0], cross_sum)
        cross_sum = way.scatter_column(cross_sum)
        line = slot.shape[1:]
        own, *rest = small_call(
            plane_sum_kernel, (parts[0], *crossed), (token_m,),
            (shape_of(line, F32),) + (shape_of(line, BF16),) * 3,
        )
        crossed = way.column(rest)
        token_d = fill_tokens(own)
        self_sum = small_call(column_sum_kernel, (own, *crossed), (token_d,), shape_of(line, F32))
    else:
        token_m, token_d = fill_grams(grad_memory), fill_tokens(grad_memory)
        cross_sum = way.scatter_column(cross_sum)
        self_sum = in_order(jnp.concatenate([self_low, self_high])).astype(F32)

    def by_example(tokens_part, segments):
        part = tokens_part[:, :STEP_ROWS].reshape(segments.shape)
        hits = segments[:, None, :] == lax.broadcasted_iota(jnp.int32, (1, NSEG, 1), 1)
        return jnp.sum(jnp.where(hits, part[:, None, :], 0.0), axis=-1)

    examples = by_example(token_c + token_d, dec_segments) + by_example(token_m, mem_segments)
    squares = (square_a + square_b + square_c)[:, :, 0].reshape(seqs, NSEG)
    examples = examples + squares + table_square[..., :NSEG, 0].reshape(seqs, NSEG)
    return (
        result.reshape(tokens.shape),
        grad_tokens.reshape(tokens.shape),
        grad_memory.reshape(memory.shape),
        (feed_sum.astype(F32), cross_sum.astype(F32), self_sum),
        examples / COUNT,
    )


def solution(mesh):
    near = tuple(mesh.shape.values()) == (16, 2)
    if near:
        mesh = jax.sharding.Mesh(mesh.devices.reshape(4, 2, 2, 2), FINE)
    axes = tuple(mesh.axis_names)
    rows = P(axes)
    arrays, weights, vectors = (P(axes, None, None),) * 3, (P(axes, None),) * 10, (rows,) * 4
    placed = arrays + (P(axes, None),) * 3 + (P(),) + weights + vectors
    return jax.shard_map(
        partial(on_device, near),
        mesh=mesh,
        in_specs=placed,
        out_specs=arrays + weights + vectors + (P(axes, None), P()),
        check_vma=False,
    )
```

```python
import math
from functools import partial

import jax
import jax.numpy as jnp
from jax import lax
from jax.experimental import pallas as pl
from jax.experimental.pallas import tpu as pltpu
from jax.sharding import PartitionSpec as P

H = 8
DH = 64
NB = 32
NSEG = 4
COUNT = 4196096
EPSILON = 1e-06
FLOOR = -1e30
F32 = jnp.float32
BF16 = jnp.bfloat16
PAIRS = H // 2
LANES = 128
STEP_ROWS = 4
VMEM_LIMIT = 60 * 2**20
GATHERED_LIMIT = 36 * 2**20

COLUMN = (0, 8, 16, 24)
PLANE = (0, 1, 4, 5)
CODES = tuple(2 * c + mask + z for c in (0, 1) for mask in PLANE for z in COLUMN)
CHIPS = tuple(z + mask for z in COLUMN for mask in PLANE)


def nn(left, right):
    return lax.dot_general(left, right, (((1,), (0,)), ((), ())), preferred_element_type=F32)


def nt(left, right):
    return lax.dot_general(left, right, (((1,), (1,)), ((), ())), preferred_element_type=F32)


def tn(left, right):
    return lax.dot_general(left, right, (((0,), (0,)), ((), ())), preferred_element_type=F32)


def inverse_root(values):
    return lax.rsqrt(jnp.mean(values * values, axis=-1, keepdims=True) + EPSILON)


def head_pair(values):
    low = (lax.broadcasted_iota(jnp.int32, (1, LANES), 1) < DH).astype(BF16)
    return jnp.concatenate([values * low, values * (1 - low)], axis=0)


def fold_pair(both, queries):
    own = jnp.concatenate([both[:DH, :queries], both[DH:, queries:]], axis=0)
    return own.astype(BF16).T


def block_rows(block):
    return pl.ds(pl.multiple_of(block * 16, 16), 16)


def start_copies(pairs, sems):
    copies = [pltpu.make_async_copy(*pair, sems.at[i]) for i, pair in enumerate(pairs)]
    for copy in copies:
        copy.start()
    return copies


def read_rows(grad_w, block):
    return grad_w[block_rows(block), :].astype(BF16)


def store_slots(me_ref, low_ref, high_ref, read):
    for k, code in enumerate(CODES):
        target = low_ref if k < 16 else high_ref
        target[k % 16] = read(me_ref[0] ^ code)


def softmax_columns(scores):
    shifted = jnp.exp(scores - jnp.max(scores, axis=0, keepdims=True))
    return (shifted * (1.0 / jnp.sum(shifted, axis=0, keepdims=True))).astype(BF16)


def each_row(row):
    for r in range(STEP_ROWS):
        row(r, 0)


def gram(left):
    return nt(left, left)


def self_forward_kernel(me_ref, tokens_ref, mask_ref, buckets_ref, *refs):
    pieces, refs = refs[:8], refs[8:]
    input_ref, qkv_ref, prob_ref, attended_ref, weight_ref, gains_ref = refs[:6]
    bias_ref, small_ref, sems = refs[6:]
    length = mask_ref.shape[1]
    width = tokens_ref.shape[1]

    @pl.when(pl.program_id(0) == 0)
    def _():
        pairs = []
        for k, code in enumerate(CODES):
            rows = block_rows(me_ref[0] ^ code)
            source = pieces[k // 4].at[k % 4]
            pairs.append((source.at[:, : 3 * width], weight_ref.at[rows, :]))
            pairs.append((source.at[:, 3 * width :], small_ref.at[rows, :]))
        for copy in start_copies(pairs, sems):
            copy.wait()
        first = lax.broadcasted_iota(jnp.int32, (32, width), 1)
        pick = first == 16 * lax.broadcasted_iota(jnp.int32, (32, width), 0)
        small = nn(pick.astype(F32).astype(BF16), small_ref[...]).astype(BF16)
        lane = lax.broadcasted_iota(jnp.int32, (LANES, width), 0)
        feature = lax.broadcasted_iota(jnp.int32, (LANES, width), 1)
        block = lax.broadcasted_iota(jnp.int32, (32, width), 0)
        lines = []
        for k in range(4):
            spread = nn(small, (lane == 16 * k + feature % 16).astype(F32).astype(BF16))
            lines.append(
                jnp.sum(jnp.where(block == first // 16, spread, 0.0), axis=0, keepdims=True)
            )
        gains_ref[...] = jnp.concatenate(lines + lines, axis=0)
        place = lax.broadcasted_iota(jnp.int32, (H, width), 1) % 16
        head = lax.broadcasted_iota(jnp.int32, (H, width), 0)
        table = jnp.where(place == head, lines[3], 0.0).astype(BF16)
        bucket = lax.broadcasted_iota(jnp.int32, (width, length), 0) // 16
        curves = nn(table, (bucket == buckets_ref[...]).astype(F32).astype(BF16))
        for h in range(H):
            curve = jnp.broadcast_to(curves[h : h + 1, :], (length, length))
            lanes = slice((h % 2) * length, (h % 2 + 1) * length)
            bias_ref[h // 2, :, lanes] = pltpu.roll(curve, 0, 1, stride=1, stride_axis=0)

    values = tokens_ref[...].astype(F32)
    normed = (values * inverse_root(values) * gains_ref[0:1, :]).astype(BF16)
    input_ref[...] = normed
    for k in range(3):
        cols = slice(k * width, (k + 1) * width)
        qkv_ref[:, cols] = nn(normed, weight_ref[:, cols]).astype(BF16)

    def row(r, carry):
        rows = pl.ds(pl.multiple_of(r * length, length), length)
        mask = mask_ref[r].astype(F32)
        mask = jnp.concatenate([mask, mask], axis=1)
        for p in range(PAIRS):
            query = qkv_ref[rows, p * LANES : (p + 1) * LANES]
            key = qkv_ref[rows, width + p * LANES : width + (p + 1) * LANES]
            value = qkv_ref[rows, 2 * width + p * LANES : 2 * width + (p + 1) * LANES]
            prob = softmax_columns(nt(key, head_pair(query)) + bias_ref[p] + mask)
            prob_ref[r, p] = prob
            attended_ref[rows, p * LANES : (p + 1) * LANES] = fold_pair(nn(value.T, prob), length)
        return carry

    each_row(row)


def memory_forward_kernel(me_ref, memory_ref, *refs):
    pieces, (kv_ref, weight_ref, sems) = refs[:-3], refs[-3:]
    width = memory_ref.shape[1]

    @pl.when(pl.program_id(0) == 0)
    def _():
        pairs = []
        for k, code in enumerate(CODES):
            source = pieces[k // 4].at[k % 4]
            pairs.append((source, weight_ref.at[block_rows(me_ref[0] ^ code), :]))
        for copy in start_copies(pairs, sems):
            copy.wait()

    for k in range(2):
        kv_ref[:, k * width : (k + 1) * width] = nn(
            memory_ref[...], weight_ref[:, (k + 2) * width : (k + 3) * width]
        ).astype(BF16)


def cross_forward_kernel(tokens_ref, attended_a_ref, kv_ref, mask_ref, gains_ref, weight_ref,
                         middle_ref, input_ref, query_ref, prob_ref, attended_ref, after_ref):
    mem_length, length = mask_ref.shape[1:]
    width = tokens_ref.shape[1]
    values = tokens_ref[...].astype(F32) + nn(attended_a_ref[...], weight_ref[:, :width])
    middle_ref[...] = values.astype(BF16)
    normed = (values * inverse_root(values) * gains_ref[1:2, :]).astype(BF16)
    input_ref[...] = normed
    query_ref[...] = nn(normed, weight_ref[:, width : 2 * width]).astype(BF16)

    def row(r, carry):
        rows = pl.ds(pl.multiple_of(r * length, length), length)
        mem_rows = pl.ds(pl.multiple_of(r * mem_length, mem_length), mem_length)
        mask = mask_ref[r].astype(F32)
        mask = jnp.concatenate([mask, mask], axis=1)
        for p in range(PAIRS):
            query = query_ref[rows, p * LANES : (p + 1) * LANES]
            key = kv_ref[mem_rows, p * LANES : (p + 1) * LANES]
            value = kv_ref[mem_rows, width + p * LANES : width + (p + 1) * LANES]
            prob = softmax_columns(nt(key, head_pair(query)) + mask)
            prob_ref[r, p] = prob
            attended_ref[rows, p * LANES : (p + 1) * LANES] = fold_pair(nn(value.T, prob), length)
        return carry

    each_row(row)
    after = values + nn(attended_ref[...], weight_ref[:, 4 * width :])
    after_ref[...] = after.astype(BF16)


def norm_back(values, gain, grad_normed):
    inverse = inverse_root(values)
    scaled = values * inverse
    upper = grad_normed * gain
    grad = inverse * (upper - scaled * jnp.mean(upper * scaled, axis=-1, keepdims=True))
    return grad, grad_normed * scaled


def gain_sums(step, terms, members_ref, total_ref, square_ref):
    sums = nn(members_ref[0], terms.astype(BF16))
    total = jnp.sum(sums, axis=0, keepdims=True)
    total_ref[...] = jnp.where(step == 0, 0.0, total_ref[...]) + total
    square = jnp.sum(sums * sums, axis=1, keepdims=True)
    square_ref[0] = jnp.broadcast_to(square, square_ref.shape[1:])


def feed_kernel(me_ref, after_ref, upstream_ref, same_ref, members_ref, gains_ref, own_ref,
                other_ref, result_ref, branch_b_ref, slots_ref, total_ref, square_ref, token_ref,
                hidden_w, back_w, grad_hidden_w, grad_back_w, flipped, gram_ref, sems):
    step = pl.program_id(0)
    length = same_ref.shape[1]
    width, ff = hidden_w.shape
    parts = ff // width

    @pl.when(step == 0)
    def _():
        core = me_ref[0] & 2
        pairs = []
        for k, code in enumerate(CHIPS):
            for piece, block in ((own_ref, code + core), (other_ref, code + 2 - core)):
                source = piece.at[k, :, :ff]
                pairs.append((source, hidden_w.at[block_rows(block), :]))
                for j in range(parts):
                    first = ff + j * width
                    source = piece.at[k, :, first : first + width]
                    pairs.append((source, back_w.at[block_rows(block * parts + j), :]))
        copies = start_copies(pairs, sems)
        grad_hidden_w[...] = jnp.zeros_like(grad_hidden_w)
        grad_back_w[...] = jnp.zeros_like(grad_back_w)
        for copy in copies:
            copy.wait()

    values = after_ref[...].astype(F32)
    gain = gains_ref[2:3, :]
    normed = (values * inverse_root(values) * gain).astype(BF16)
    normed_flip = normed.T
    branch = upstream_ref[...]
    branch_flip = branch.T
    gram_ref[...] = jnp.zeros_like(gram_ref)
    root = 0.7978845608028654

    def chunk(c, carry):
        result, grad_normed = carry
        cols = slice(c * width, (c + 1) * width)
        w_in = hidden_w[:, cols]
        w_out = back_w[cols, :]
        hidden = nn(normed, w_in)
        square = hidden * hidden
        bent = jnp.tanh(hidden * (root + (root * 0.044715) * square))
        half = 0.5 + 0.5 * bent
        active = (hidden * half).astype(BF16)
        slope = half + (0.5 * hidden) * (1.0 - bent * bent) * (
            root + (3.0 * root * 0.044715) * square
        )
        grad = (nt(branch, w_out) * slope).astype(BF16)
        result = result + nn(active, w_out)
        grad_normed = grad_normed + nt(grad, w_in)
        grad_hidden_w[:, cols] += nn(normed_flip, grad)
        grad_back_w[:, cols] += nn(branch_flip, active)
        for r in range(STEP_ROWS):
            rows = slice(r * length, (r + 1) * length)
            gram_ref[0, r] += gram(active[rows])
            gram_ref[1, r] += gram(grad[rows])
        return result, grad_normed

    result = grad_normed = jnp.zeros_like(values)
    for c in range(parts):
        result, grad_normed = chunk(c, (result, grad_normed))
    result_ref[...] = (values + result).astype(BF16)
    grad, terms = norm_back(values, gain, grad_normed)
    branch_b_ref[...] = (branch.astype(F32) + grad).astype(BF16)
    gain_sums(step, terms, members_ref, total_ref, square_ref)
    for r in range(STEP_ROWS):
        rows = slice(r * length, (r + 1) * length)
        products = gram_ref[0, r] * gram(branch[rows]) + gram_ref[1, r] * gram(normed[rows])
        token_ref[0, r : r + 1, :] = jnp.sum(products * same_ref[r], axis=0, keepdims=True)

    @pl.when(step == pl.num_programs(0) - 1)
    def _():
        for j in range(parts):
            flipped[j * width : (j + 1) * width, :] = (
                grad_back_w[:, j * width : (j + 1) * width].astype(BF16).T
            )

        for k, block in enumerate(CODES):
            own = [read_rows(grad_hidden_w, block)]
            own += [flipped[block_rows(block * parts + j), :] for j in range(parts)]
            slots_ref[k] = jnp.concatenate(own, axis=1)


def score_grads(prob, grad_prob):
    prob = prob.astype(F32)
    dots = jnp.sum(prob * grad_prob, axis=0, keepdims=True)
    return prob * (grad_prob - dots)


def cross_scores_kernel(branch_ref, query_ref, kv_ref, prob_ref, weight_ref, grad_query_ref,
                        grad_kv_ref, grad_attended):
    mem_length = prob_ref.shape[2]
    length = prob_ref.shape[3] // 2
    width = branch_ref.shape[1]
    grad_attended[...] = nt(branch_ref[...], weight_ref[:, 4 * width :]).astype(BF16)

    def row(r, carry):
        rows = pl.ds(r * length, length)
        mem_rows = pl.ds(r * mem_length, mem_length)
        for p in range(PAIRS):
            lanes = slice(p * LANES, (p + 1) * LANES)
            upper = slice(width + p * LANES, width + (p + 1) * LANES)
            key = kv_ref[mem_rows, lanes]
            value = kv_ref[mem_rows, upper]
            query = head_pair(query_ref[rows, lanes])
            grad_out = head_pair(grad_attended[rows, lanes])
            prob = prob_ref[r, p]
            grad_score = score_grads(prob, nt(value, grad_out)).astype(BF16)
            grad_kv_ref[mem_rows, lanes] = nn(grad_score, query).astype(BF16)
            grad_kv_ref[mem_rows, upper] = nn(prob, grad_out).astype(BF16)
            grad_query_ref[rows, lanes] = fold_pair(nn(key.T, grad_score), length)

    each_row(row)


def cross_weights_kernel(me_ref, branch_ref, middle_ref, memory_ref, attended_a_ref, input_ref,
                         grad_query_ref, grad_kv_ref, attended_ref, members_ref, gains_ref,
                         weight_ref, branch_a_ref, low_ref, high_ref, total_ref, square_ref,
                         grad_w):
    step = pl.program_id(0)
    width = middle_ref.shape[1]
    grad_query = grad_query_ref[...]
    grad_normed = nt(grad_query, weight_ref[:, width : 2 * width])
    grad, terms = norm_back(middle_ref[...].astype(F32), gains_ref[1:2, :], grad_normed)
    branch_a = (branch_ref[...].astype(F32) + grad).astype(BF16)
    branch_a_ref[...] = branch_a
    gain_sums(step, terms, members_ref, total_ref, square_ref)

    @pl.when(step == 0)
    def _():
        grad_w[...] = jnp.zeros_like(grad_w)

    grad_w[:, :width] += tn(attended_a_ref[...], branch_a)
    grad_w[:, width : 2 * width] += tn(input_ref[...], grad_query)
    grad_w[:, 2 * width : 4 * width] += tn(memory_ref[...], grad_kv_ref[...])
    grad_w[:, 4 * width :] += tn(attended_ref[...], branch_ref[...])

    @pl.when(step == pl.num_programs(0) - 1)
    def _():
        store_slots(me_ref, low_ref, high_ref, partial(read_rows, grad_w))


def self_scores_kernel(branch_ref, qkv_ref, prob_ref, keys_ref, turned_buckets_ref, weight_ref,
                       grad_qkv_ref, table_ref, table_square_ref, grad_attended, bands):
    step = pl.program_id(0)
    length = prob_ref.shape[2]
    width = branch_ref.shape[1]
    grad_attended[...] = nt(branch_ref[...], weight_ref[:, :width]).astype(BF16)

    @pl.when(step == 0)
    def _():
        table_ref[...] = jnp.zeros_like(table_ref)

    row_i = lax.broadcasted_iota(jnp.int32, (2 * length, 2 * length), 0)
    col_i = lax.broadcasted_iota(jnp.int32, (2 * length, 2 * length), 1)
    turned = (row_i // length) * length + length - 1 - row_i % length
    flip = (turned == col_i).astype(F32).astype(BF16)

    def row(r, carry):
        rows = pl.ds(r * length, length)
        keys = keys_ref[r]
        for p in range(PAIRS):
            lanes = slice(p * LANES, (p + 1) * LANES)
            middle = slice(width + p * LANES, width + (p + 1) * LANES)
            upper = slice(2 * width + p * LANES, 2 * width + (p + 1) * LANES)
            key = qkv_ref[rows, middle]
            value = qkv_ref[rows, upper]
            query = head_pair(qkv_ref[rows, lanes])
            grad_out = head_pair(grad_attended[rows, lanes])
            prob = prob_ref[r, p]
            grad_score = score_grads(prob, nt(value, grad_out)).astype(BF16)
            grad_qkv_ref[rows, middle] = nn(grad_score, query).astype(BF16)
            grad_qkv_ref[rows, upper] = nn(prob, grad_out).astype(BF16)
            grad_qkv_ref[rows, lanes] = fold_pair(nn(key.T, grad_score), length)
            mirrored = nn(grad_score, flip)
            for h in range(2):
                own = mirrored[:, h * length : (h + 1) * length]
                own = pltpu.roll(own, 0, 1, stride=1, stride_axis=0)
                bands[r, 2 * p + h] = nn(keys, own.astype(BF16))[:8]

    each_row(row)
    bucket = lax.broadcasted_iota(jnp.int32, (LANES, length), 0)
    near = (bucket == turned_buckets_ref[...]).astype(F32)
    flat = bands[...].reshape(STEP_ROWS * H * 8, length)
    per_bucket = lax.dot_general(
        flat, near, (((1,), (1,)), ((), ())), preferred_element_type=F32,
        precision=lax.Precision.HIGHEST,
    ).reshape(STEP_ROWS, H, 8, LANES)
    table_ref[...] += jnp.sum(jnp.sum(per_bucket, axis=0), axis=1)
    squares = jnp.sum(jnp.sum(per_bucket * per_bucket, axis=1), axis=-1, keepdims=True)
    table_square_ref[0] = jnp.broadcast_to(squares, (STEP_ROWS, 8, LANES))


def self_weights_kernel(me_ref, branch_ref, tokens_ref, input_ref, grad_qkv_ref, members_ref,
                        gains_ref, weight_ref, table_ref, total_b_ref, total_c_ref,
                        grad_tokens_ref, low_ref, high_ref, square_ref, grad_w, total_ref,
                        small_ref):
    step = pl.program_id(0)
    width = tokens_ref.shape[1]
    grad_qkv = grad_qkv_ref[...]
    grad_normed = nt(grad_qkv, weight_ref[...])
    grad, terms = norm_back(tokens_ref[...].astype(F32), gains_ref[0:1, :], grad_normed)
    grad_tokens_ref[...] = (branch_ref[...].astype(F32) + grad).astype(BF16)

    @pl.when(step == 0)
    def _():
        grad_w[...] = jnp.zeros_like(grad_w)
        total_ref[...] = jnp.zeros_like(total_ref)

    gain_sums(step, terms, members_ref, total_ref, square_ref)
    grad_w[...] += tn(input_ref[...], grad_qkv)

    @pl.when(step == pl.num_programs(0) - 1)
    def _():
        bucket = lax.broadcasted_iota(jnp.int32, (LANES, width), 0)
        place = lax.broadcasted_iota(jnp.int32, (LANES, width), 1)
        spread = nn(table_ref[...].astype(BF16), (place // 16 == bucket).astype(F32).astype(BF16))
        head = lax.broadcasted_iota(jnp.int32, (H, width), 0)
        lane = lax.broadcasted_iota(jnp.int32, (H, width), 1)
        table = jnp.sum(jnp.where(lane % 16 == head, spread, 0.0), axis=0, keepdims=True)
        small = jnp.zeros((LANES, width), F32)
        row_i = lax.broadcasted_iota(jnp.int32, (LANES, width), 0)
        for k, line in enumerate((total_ref[...], total_b_ref[...], total_c_ref[...], table)):
            small = jnp.where(row_i == k, line, small)
        small_ref[...] = small.T

        def read(block):
            return jnp.concatenate(
                [read_rows(grad_w, block), read_rows(small_ref, block)], axis=1
            )

        store_slots(me_ref, low_ref, high_ref, read)


def pair_sum_kernel(low_ref, sent_ref, *refs):
    outs, (low, sent, total, load_sems, store_sems) = refs[:4], refs[4:]
    places = [pl.ds(4 * t, 4) for t in range(4)]
    lows = start_copies([(low_ref.at[p], low.at[p]) for p in places], load_sems.at[0])
    sents = start_copies([(sent_ref.at[p], sent.at[p]) for p in places], load_sems.at[1])
    stores = []
    for t, p in enumerate(places):
        lows[t].wait()
        sents[t].wait()
        total[p] = (low[p].astype(F32) + sent[p].astype(F32)).astype(BF16)
        stores.append(pltpu.make_async_copy(total.at[p], outs[t], store_sems.at[t]))
        stores[t].start()
    for store in stores:
        store.wait()


def pair_sum(low, sent, after):
    piece = shape_of((4,) + low.shape[1:], BF16)
    return pl.pallas_call(
        ignoring(pair_sum_kernel, 2, len(after)),
        out_shape=(piece,) * 4,
        in_specs=[pl.BlockSpec(memory_space=pl.ANY)] * (2 + len(after)),
        out_specs=[pl.BlockSpec(memory_space=pl.ANY)] * 4,
        scratch_shapes=[pltpu.VMEM(low.shape, BF16)] * 3
        + [pltpu.SemaphoreType.DMA((2, 4)), pltpu.SemaphoreType.DMA((4,))],
        compiler_params=pltpu.CompilerParams(vmem_limit_bytes=VMEM_LIMIT),
    )(low, sent, *after)


def plane_sum_kernel(a_ref, b_ref, c_ref, d_ref, own_ref, *outs):
    for s in range(4):
        total = a_ref[s].astype(F32) + b_ref[s].astype(F32)
        total = total + c_ref[s].astype(F32) + d_ref[s].astype(F32)
        if s == 0:
            own_ref[...] = total
        else:
            outs[s - 1][...] = total.astype(BF16)


def plane_sum(pieces, after):
    line = pieces[0].shape[1:]
    return small_call(
        plane_sum_kernel, pieces, after, (shape_of(line, F32),) + (shape_of(line, BF16),) * 3
    )


def square_sum(values):
    return jnp.sum(jnp.sum(values * values, axis=0, keepdims=True), axis=1, keepdims=True)


def feed_end_kernel(sum_ref, hidden_ref, back_ref, square_ref):
    total = sum_ref[...].astype(F32)
    ff = hidden_ref.shape[1]
    width = back_ref.shape[1]
    hidden_ref[...] = total[:, :ff]
    for j in range(ff // width):
        back_ref[16 * j : 16 * (j + 1), :] = total[:, ff + j * width : ff + (j + 1) * width]
    square_ref[...] = jnp.broadcast_to(square_sum(total), square_ref.shape)


def column_end_kernel(own_ref, b_ref, c_ref, d_ref, *refs):
    squares, outs, square_ref = refs[:2], refs[2:-1], refs[-1]
    total = own_ref[...] + b_ref[...].astype(F32)
    total = total + c_ref[...].astype(F32) + d_ref[...].astype(F32)
    start = 0
    for out in outs:
        out[...] = total[:, start : start + out.shape[1]]
        start += out.shape[1]
    square = square_sum(total)
    for given in squares:
        square = square + given[0:1, 0:1]
    square_ref[...] = jnp.broadcast_to(square, square_ref.shape)


def staged(kernel, ins, outs):
    def run(*refs):
        count = ins + outs
        given, inner, sems = refs[:count], refs[count : 2 * count], refs[2 * count]
        for copy in start_copies(list(zip(given[:ins], inner[:ins])), sems):
            copy.wait()
        kernel(*inner)
        for copy in start_copies(list(zip(inner[ins:], given[ins:])), sems):
            copy.wait()

    return run


def small_call(kernel, ins, after, outs):
    arrays = [*ins, *outs]
    return pl.pallas_call(
        ignoring(staged(kernel, len(ins), len(outs)), len(ins), len(after)),
        out_shape=outs,
        in_specs=[pl.BlockSpec(memory_space=pl.ANY)] * (len(ins) + len(after)),
        out_specs=[pl.BlockSpec(memory_space=pl.ANY)] * len(outs),
        scratch_shapes=[pltpu.VMEM(array.shape, array.dtype) for array in arrays]
        + [pltpu.SemaphoreType.DMA((len(arrays),))],
        compiler_params=pltpu.CompilerParams(vmem_limit_bytes=VMEM_LIMIT),
    )(*ins, *after)


def pack_kernel(*refs):
    ins, outs, sems = refs[:11], refs[11:14], refs[14]
    self_ref, cross_ref, feed_ref = outs
    width = ins[0].shape[1]
    pairs = []
    for k in range(3):
        pairs.append((ins[k], self_ref.at[:, k * width : (k + 1) * width]))
    pairs.append((ins[10], self_ref.at[:, 3 * width :]))
    for k in range(5):
        pairs.append((ins[3 + k], cross_ref.at[:, k * width : (k + 1) * width]))
    ff = ins[8].shape[1]
    pairs.append((ins[8], feed_ref.at[:, :ff]))
    for j in range(ff // width):
        cols = slice(ff + j * width, ff + (j + 1) * width)
        pairs.append((ins[9].at[16 * j : 16 * (j + 1), :], feed_ref.at[:, cols]))
    for copy in start_copies(pairs, sems):
        copy.wait()


def pack(weights, small):
    width, ff = weights[0].shape[1], weights[8].shape[1]
    return pl.pallas_call(
        pack_kernel,
        out_shape=[
            shape_of((16, cols), BF16) for cols in (3 * width + LANES, 5 * width, 2 * ff)
        ],
        in_specs=[pl.BlockSpec(memory_space=pl.ANY)] * 11,
        out_specs=[pl.BlockSpec(memory_space=pl.ANY)] * 3,
        scratch_shapes=[pltpu.SemaphoreType.DMA((16,))],
        compiler_params=pltpu.CompilerParams(vmem_limit_bytes=VMEM_LIMIT),
    )(*weights, small)


def memory_backward_kernel(memory_ref, grad_kv_ref, same_ref, weight_ref, grad_memory_ref,
                           token_ref):
    mem_length = same_ref.shape[1]
    width = memory_ref.shape[1]
    weight = weight_ref[:, 2 * width : 4 * width]
    grad_memory_ref[...] = nt(grad_kv_ref[...], weight).astype(BF16)
    for r in range(STEP_ROWS):
        rows = slice(r * mem_length, (r + 1) * mem_length)
        products = gram(memory_ref[rows, :]) * gram(grad_kv_ref[rows, :])
        token_ref[0, r : r + 1, :] = jnp.sum(products * same_ref[r], axis=0, keepdims=True)


def gram_kernel(same_ref, *refs):
    pairs, token_ref = refs[:-1], refs[-1]
    length = same_ref.shape[1]
    for r in range(STEP_ROWS):
        rows = slice(r * length, (r + 1) * length)
        products = sum(
            gram(left[rows, :]) * gram(right[rows, :])
            for left, right in zip(pairs[::2], pairs[1::2])
        )
        token_ref[0, r : r + 1, :] = jnp.sum(products * same_ref[r], axis=0, keepdims=True)


def rows_spec(array, steps):
    shape = (array.shape[0] // steps,) + array.shape[1:]
    return pl.BlockSpec(shape, lambda i, *_: (i,) + (0,) * (len(shape) - 1))


def whole_spec(array):
    return pl.BlockSpec(array.shape, lambda i, *_: (0,) * len(array.shape))


def ignoring(kernel, first, count):
    return lambda *refs: kernel(*refs[:first], *refs[first + count :])


def call(kernel, steps, me, blocked, whole, pieces, outs_blocked, outs_whole, scratch, flops,
         order, after=(), limit=VMEM_LIMIT):
    ins, in_specs = [], []
    blocked, whole = list(blocked), list(whole)
    for kind in order[0]:
        array = (blocked if kind == "i" else whole).pop(0)
        ins.append(array)
        in_specs.append(rows_spec(array, steps) if kind == "i" else whole_spec(array))
    kernel = ignoring(kernel, len(ins) + len(pieces) + (me is not None), len(after))
    ins += [*pieces, *after]
    in_specs += [pl.BlockSpec(memory_space=pl.ANY)] * (len(pieces) + len(after))
    outs, out_specs = [], []
    outs_blocked, outs_whole = list(outs_blocked), list(outs_whole)
    for kind in order[1]:
        out = (outs_blocked if kind == "i" else outs_whole).pop(0)
        outs.append(out)
        out_specs.append(rows_spec(out, steps) if kind == "i" else whole_spec(out))
    moved = sum(math.prod(a.shape) * a.dtype.itemsize for a in ins + outs)
    prefetch = 0 if me is None else 1
    return pl.pallas_call(
        kernel,
        out_shape=outs,
        grid_spec=pltpu.PrefetchScalarGridSpec(
            num_scalar_prefetch=prefetch,
            grid=(steps,),
            in_specs=in_specs,
            out_specs=out_specs,
            scratch_shapes=scratch,
        ),
        compiler_params=pltpu.CompilerParams(
            dimension_semantics=("arbitrary",), vmem_limit_bytes=limit
        ),
        cost_estimate=pl.CostEstimate(flops=flops, bytes_accessed=moved, transcendentals=0),
    )(*(() if me is None else (me,)), *ins)


FINE = ("z", "y", "core", "x")


def shape_of(shape, dtype):
    return jax.ShapeDtypeStruct(shape, dtype)


def kept(shape, dtype):
    return pltpu.HBM(shape, dtype)


def shift(array, mask):
    return lax.ppermute(array, FINE, [(i, i ^ mask) for i in range(32)])


def hold(array, after):
    return lax.optimization_barrier((array, after))[0]


def split_back(back):
    blocks = back.shape[0] // 64
    parts = back.reshape(blocks, 4, 16, back.shape[1]).transpose(0, 2, 1, 3)
    return parts.reshape(16 * blocks, 4 * back.shape[1])


def join_back(parts):
    blocks, width = parts.shape[0] // 16, parts.shape[1] // 4
    return parts.reshape(blocks, 16, 4, width).transpose(0, 2, 1, 3).reshape(64 * blocks, width)


def small_row(gains, table):
    table = jnp.pad(table.reshape(-1, H), ((0, 0), (0, 16 - H)))
    row = jnp.concatenate([gain.reshape(-1, 16) for gain in gains] + [table], axis=1)
    row = jnp.pad(row, ((0, 0), (0, LANES - row.shape[1])))
    return jnp.pad(row[:, None], ((0, 0), (0, 15), (0, 0))).reshape(-1, LANES)


def in_order(slots):
    return slots[jnp.array([CODES.index(block) for block in range(32)])].reshape(-1, slots.shape[2])


def shift_plane(pieces):
    return [shift(piece, mask) for piece, mask in zip(pieces, PLANE[1:])]


def shift_column(pieces):
    return [shift(piece, code) for piece, code in zip(pieces, COLUMN[1:])]


class Near:
    axes = FINE

    def __init__(self, weights):
        self.me = lax.axis_index(FINE)
        own, self.cross_shard, feed = pack(weights[:10], small_row(weights[10:13], weights[13]))
        self.chips = lax.all_gather(feed, ("z", "y", "x"), axis=0)
        column = jnp.stack([own, *shift_column([own] * 3)])
        line = hold(self.cross_shard, column)
        line = jnp.stack([line, *shift_column([line] * 3)])
        plane = [column, *shift_plane([column] * 3)]
        line = hold(line, plane[3])
        self.plane = [line, *shift_plane([line] * 3)]
        self.own = plane + [shift(piece, 2) for piece in plane]

    def cross(self, after):
        plane = [hold(piece, after) for piece in self.plane]
        return plane + [shift(piece, 2) for piece in plane]

    def feed(self, after):
        chips = hold(self.chips, after)
        return chips, shift(chips, 2)

    def feed_core(self, slots):
        return lax.psum_scatter(slots.reshape((2, 4, 4) + slots.shape[1:]), "core")

    def feed_plane(self, slots):
        return lax.psum_scatter(slots, ("y", "x"))

    def feed_column(self, slots):
        return lax.psum_scatter(slots, "z")


class Far:
    axes = ("wide", "narrow")
    me = 0

    def __init__(self, weights):
        weights = [lax.all_gather(w, self.axes, axis=0, tiled=True) for w in weights]
        self.take(weights)

    def take(self, weights):
        self.own = self.pieces(*weights[:3], small_row(weights[10:13], weights[13]))
        self.rest = self.pieces(*weights[3:8])
        feed = jnp.concatenate([weights[8], split_back(weights[9])], axis=1).reshape(32, 16, -1)
        self.chips = tuple(feed[jnp.array(CHIPS) + core] for core in (0, 2))

    def pieces(self, *parts):
        blocks = jnp.concatenate(parts, axis=1).reshape(32, 16, -1)[jnp.array(CODES)]
        return [blocks[4 * t : 4 * t + 4] for t in range(8)]

    def cross(self, after):
        return self.rest

    def feed(self, after):
        return self.chips

    def feed_core(self, slots):
        return slots

    feed_plane = feed_column = feed_core


def on_device(near, tokens, memory, cotangent, dec_segments, mem_segments, padding, buckets,
              *weights):
    way = (Near if near else Far)(weights)
    result, grad_tokens, grad_memory, grads, examples, square = local_part(
        way, tokens, memory, cotangent, dec_segments, mem_segments, padding, buckets
    )
    if near:
        sent = lax.all_to_all(square, FINE, 0, 0, tiled=True)
        global_norm = jnp.sum(sent[:, 0])
    else:
        grads = [lax.psum_scatter(g, way.axes, scatter_dimension=0, tiled=True) for g in grads]
        global_norm = lax.psum(sum(jnp.sum(g * g) for g in grads), way.axes)
    return (result, grad_tokens, grad_memory, *grads, examples, global_norm / COUNT)


def local_part(way, tokens, memory, cotangent, dec_segments, mem_segments, padding, buckets):
    seqs, length, width = tokens.shape
    mem_length = memory.shape[1]
    steps = seqs // STEP_ROWS
    dec, mem = seqs * length, seqs * mem_length
    step_dec = STEP_ROWS * length
    ff = 4 * width

    same_dec = dec_segments[:, :, None] == dec_segments[:, None, :]
    same_mem = mem_segments[:, :, None] == mem_segments[:, None, :]
    keys_i = lax.broadcasted_iota(jnp.int32, (length, length), 0)
    queries_i = lax.broadcasted_iota(jnp.int32, (length, length), 1)
    allowed = same_dec & (keys_i <= queries_i) & ((padding[:, :, None] > 0) | (keys_i == queries_i))
    self_mask = jnp.where(allowed, 0.0, FLOOR).astype(BF16)
    cross_allowed = mem_segments[:, :, None] == dec_segments[:, None, :]
    cross_mask = jnp.where(cross_allowed, 0.0, FLOOR).astype(BF16)
    same_dec, same_mem = same_dec.astype(BF16), same_mem.astype(BF16)
    upstream = (cotangent * padding[..., None].astype(BF16)).reshape(dec, width)
    example = lax.broadcasted_iota(jnp.int32, (1, 16, 1), 1)
    keys = (dec_segments[:, None, :] == example).astype(BF16)
    member_row = lax.broadcasted_iota(jnp.int32, (1, 4 * STEP_ROWS, 1), 1)
    token_row = lax.broadcasted_iota(jnp.int32, (1, 1, step_dec), 2) // length
    members = (
        dec_segments.reshape(steps, 1, step_dec) + NSEG * token_row == member_row
    ).astype(BF16)
    buckets = buckets[None]
    turned_buckets = buckets[:, ::-1]
    prepared = (cross_mask, same_dec, same_mem, upstream, keys, members, turned_buckets)
    tokens2, memory2 = tokens.reshape(dec, width), memory.reshape(mem, width)
    dma = pltpu.SemaphoreType.DMA

    me = jnp.full((1,), way.me, jnp.int32)
    flops = 2 * dec * width * width

    input_a, qkv_a, prob_a, attended_a, self_w, gains = call(
        self_forward_kernel, steps, me, (tokens2, self_mask), (buckets,), way.own,
        (
            kept((dec, width), BF16),
            kept((dec, 3 * width), BF16),
            kept((seqs, PAIRS, length, 2 * length), BF16),
            kept((dec, width), BF16),
        ),
        (kept((width, 3 * width), BF16), kept((8, width), F32)),
        [pltpu.VMEM((PAIRS, length, 2 * length), F32), pltpu.VMEM((width, LANES), BF16), dma((64,))],
        6 * flops, ("iiw", "iiiiww"), prepared, GATHERED_LIMIT,
    )
    kv_b, cross_w = call(
        memory_forward_kernel, steps, me, (memory2,), (), way.cross(attended_a),
        (kept((mem, 2 * width), BF16),), (kept((width, 5 * width), BF16),), [dma((32,))],
        4 * flops, ("i", "iw"), (), GATHERED_LIMIT,
    )
    feed_pieces = way.feed(kv_b)
    middle, input_b, query_b, prob_b, attended_b, after_cross = call(
        cross_forward_kernel, steps, None, (tokens2, attended_a, kv_b, cross_mask),
        (gains, cross_w), (),
        (
            kept((dec, width), BF16),
            kept((dec, width), BF16),
            kept((dec, width), BF16),
            kept((seqs, PAIRS, mem_length, 2 * length), BF16),
            kept((dec, width), BF16),
            kept((dec, width), BF16),
        ),
        (), [], 6 * flops, ("iiiiww", "iiiiii"),
    )
    total, square = kept((1, width), F32), shape_of((steps, 4 * STEP_ROWS, LANES), F32)
    token_shape = shape_of((steps, 8, length), F32)
    result, branch_b, feed_slots, gain_c, square_c, token_c = call(
        feed_kernel, steps, me, (after_cross, upstream, same_dec, members), (gains,), feed_pieces,
        (shape_of((dec, width), BF16), kept((dec, width), BF16), square, token_shape),
        (shape_of((32, 16, 2 * ff), BF16), total),
        [
            pltpu.VMEM((width, ff), BF16),
            pltpu.VMEM((ff, width), BF16),
            pltpu.VMEM((width, ff), F32),
            pltpu.VMEM((width, ff), F32),
            pltpu.VMEM((ff, width), BF16),
            pltpu.VMEM((2, STEP_ROWS, length, length), F32),
            dma((160,)),
        ],
        26 * flops, ("iiiiw", "iiwwii"),
    )
    feed_sum = way.feed_core(feed_slots)
    grad_query_b, grad_kv_b = call(
        cross_scores_kernel, steps, None, (branch_b, query_b, kv_b, prob_b), (cross_w,), (),
        (kept((dec, width), BF16), kept((mem, 2 * width), BF16)), (),
        [pltpu.VMEM((step_dec, width), BF16)],
        12 * flops, ("iiiiw", "ii"),
    )
    feed_sum = hold(feed_sum, grad_query_b)
    slot = shape_of((16, 16, 5 * width), BF16)
    branch_a, cross_low, cross_high, gain_b, square_b = call(
        cross_weights_kernel, steps, me,
        (branch_b, middle, memory2, attended_a, input_b, grad_query_b, grad_kv_b, attended_b,
         members),
        (gains, cross_w), (),
        (kept((dec, width), BF16), square), (slot, slot, total),
        [pltpu.VMEM((width, 5 * width), F32)],
        9 * flops, ("iiiiiiiiiww", "iwwwi"), (feed_sum,),
    )
    feed_sum = way.feed_plane(feed_sum)
    near = isinstance(way, Near)
    if near:
        sent = shift(cross_high, 2)
    grad_qkv_a, table, table_square = call(
        self_scores_kernel, steps, None, (branch_a, qkv_a, prob_a, keys),
        (turned_buckets, cross_w), (),
        (kept((dec, 3 * width), BF16), shape_of((steps, STEP_ROWS, 8, LANES), F32)),
        (kept((H, LANES), F32),),
        [pltpu.VMEM((step_dec, width), BF16), pltpu.VMEM((STEP_ROWS, H, 8, length), F32)],
        10 * flops, ("iiiiww", "iwi"),
    )
    feed_sum = hold(feed_sum, grad_qkv_a)
    waits = (feed_sum,)
    if near:
        cross_parts = pair_sum(cross_low, sent, (grad_qkv_a,))
        crossed = shift_plane(cross_parts[1:])
        waits += (cross_parts[0],)
    slot = shape_of((16, 16, 3 * width + LANES), BF16)
    grad_tokens, self_low, self_high, square_a = call(
        self_weights_kernel, steps, me, (branch_a, tokens2, input_a, grad_qkv_a, members),
        (gains, self_w, table, gain_b, gain_c), (),
        (shape_of((dec, width), BF16), square),
        (slot, slot),
        [
            pltpu.VMEM((width, 3 * width), F32),
            pltpu.VMEM((1, width), F32),
            pltpu.VMEM((width, LANES), F32),
        ],
        7 * flops, ("iiiiiwwwww", "iwwi"), waits,
    )
    feed_sum = way.feed_column(feed_sum)

    def grams(pairs, *after):
        (tokens_part,) = call(
            gram_kernel, steps, None, (same_dec, *pairs), (), (), (token_shape,), (), [],
            2 * flops, ("i" * (len(pairs) + 1), "i"), after,
        )
        return tokens_part

    def fill_cross(*after):
        return grams((input_b, grad_query_b, attended_b, branch_b), *after)

    def fill_self(*after):
        return grams((input_a, grad_qkv_a, attended_a, branch_a), *after)

    def fill_memory(*after):
        return call(
            memory_backward_kernel, steps, None, (memory2, grad_kv_b, same_mem), (cross_w,), (),
            (shape_of((mem, width), BF16), shape_of((steps, 8, mem_length), F32)), (), [],
            10 * flops, ("iiiw", "ii"), after,
        )

    if near:
        no_square = jnp.zeros((8, LANES), F32)
        sent = shift(hold(self_high, crossed), 2)
        cross_own, *rest = plane_sum([cross_parts[0], *crossed], (self_low,))
        crossed = shift_column(rest)
        token_b = fill_cross(cross_own)
        self_parts = pair_sum(self_low, sent, (token_b,))
        self_sent = shift_plane(self_parts[1:])
        line = (slot.shape[1], width)
        *cross_grads, square = small_call(
            column_end_kernel, (cross_own, *crossed, no_square, no_square),
            (self_parts[0],), [shape_of(line, F32)] * 5 + [shape_of((8, LANES), F32)],
        )
        grad_memory, token_m = fill_memory(self_parts[0], square)
        feed_sum = hold(feed_sum, token_m).reshape(slot.shape[1], 2 * ff)
        self_own, *rest = plane_sum([self_parts[0], *self_sent], (token_m,))
        self_sent = shift_column(rest)
        grad_hidden, grad_back, feed_square = small_call(
            feed_end_kernel, (feed_sum,), (self_own,),
            [shape_of((16, ff), F32), shape_of((64, width), F32), shape_of((8, LANES), F32)],
        )
        token_a = fill_self(self_own, feed_square)
        *self_grads, small, square = small_call(
            column_end_kernel, (self_own, *self_sent, square, feed_square), (token_a,),
            [shape_of(line, F32)] * 3 + [shape_of((16, LANES), F32), shape_of((32, LANES), F32)],
        )
        token_a = hold(token_a, square)
    else:
        token_b, token_a = fill_cross(), fill_self()
        grad_memory, token_m = fill_memory()
        cross_sum = in_order(jnp.concatenate([cross_low, cross_high])).astype(F32)
        self_sum = in_order(jnp.concatenate([self_low, self_high])).astype(F32)
        feed_sum = in_order(feed_sum).astype(F32)
        cross_grads = [cross_sum[:, k * width : (k + 1) * width] for k in range(5)]
        self_grads = [self_sum[:, k * width : (k + 1) * width] for k in range(3)]
        small = self_sum[:, 3 * width :]
        grad_hidden, grad_back = feed_sum[:, :ff], join_back(feed_sum[:, ff:])
        square = None
    grads = self_grads + cross_grads + [grad_hidden, grad_back]
    grads += [small[:, k] for k in range(3)]
    grads.append(small[:, 3].reshape(-1, 16)[:, :H].reshape(-1))

    def by_example(tokens_part, segments):
        part = tokens_part[:, :STEP_ROWS].reshape(segments.shape)
        hits = segments[:, None, :] == lax.broadcasted_iota(jnp.int32, (1, NSEG, 1), 1)
        return jnp.sum(jnp.where(hits, part[:, None, :], 0.0), axis=-1)

    examples = by_example(token_a + token_b + token_c, dec_segments) + by_example(token_m, mem_segments)
    squares = (square_a + square_b + square_c)[:, :, 0].reshape(seqs, NSEG)
    examples = examples + squares + table_square[..., :NSEG, 0].reshape(seqs, NSEG)
    return (
        result.reshape(tokens.shape),
        grad_tokens.reshape(tokens.shape),
        grad_memory.reshape(memory.shape),
        grads,
        examples / COUNT,
        square,
    )


def solution(mesh):
    near = tuple(mesh.shape.values()) == (16, 2)
    if near:
        mesh = jax.sharding.Mesh(mesh.devices.reshape(4, 2, 2, 2), FINE)
    axes = tuple(mesh.axis_names)
    rows = P(axes)
    arrays, weights, vectors = (P(axes, None, None),) * 3, (P(axes, None),) * 10, (rows,) * 4
    placed = arrays + (P(axes, None),) * 3 + (P(),) + weights + vectors
    return jax.shard_map(
        partial(on_device, near),
        mesh=mesh,
        in_specs=placed,
        out_specs=arrays + weights + vectors + (P(axes, None), P()),
        check_vma=False,
    )
```

```python
import math
from functools import partial

import jax
import jax.numpy as jnp
from jax import lax
from jax.experimental import pallas as pl
from jax.experimental.pallas import tpu as pltpu
from jax.sharding import PartitionSpec as P

H = 8
DH = 64
NB = 32
NSEG = 4
COUNT = 4196096
EPSILON = 1e-06
FLOOR = -1e30
F32 = jnp.float32
BF16 = jnp.bfloat16
PAIRS = H // 2
LANES = 128
STEP_ROWS = 4
VMEM_LIMIT = 60 * 2**20
GATHERED_LIMIT = 36 * 2**20

COLUMN = (0, 8, 16, 24)
PLANE = (0, 1, 4, 5)
CODES = tuple(2 * c + mask + z for c in (0, 1) for mask in PLANE for z in COLUMN)
CHIPS = tuple(z + mask for z in COLUMN for mask in PLANE)


def nn(left, right):
    return lax.dot_general(left, right, (((1,), (0,)), ((), ())), preferred_element_type=F32)


def nt(left, right):
    return lax.dot_general(left, right, (((1,), (1,)), ((), ())), preferred_element_type=F32)


def tn(left, right):
    return lax.dot_general(left, right, (((0,), (0,)), ((), ())), preferred_element_type=F32)


def inverse_root(values):
    return lax.rsqrt(jnp.mean(values * values, axis=-1, keepdims=True) + EPSILON)


def head_masks(values):
    low = (lax.broadcasted_iota(jnp.int32, (1, LANES), 1) < DH).astype(BF16)
    return values * low, values * (1 - low)


def head_pair(values):
    return jnp.concatenate(head_masks(values), axis=0)


def fold_pair(both, queries):
    own = jnp.concatenate([both[:DH, :queries], both[DH:, queries:]], axis=0)
    return own.astype(BF16).T


def block_rows(block):
    return pl.ds(pl.multiple_of(block * 16, 16), 16)


def start_copies(pairs, sems):
    copies = [pltpu.make_async_copy(*pair, sems.at[i]) for i, pair in enumerate(pairs)]
    for copy in copies:
        copy.start()
    return copies


def read_rows(grad_w, block):
    return grad_w[block_rows(block), :].astype(BF16)


def store_slots(me_ref, low_ref, high_ref, read):
    for k, code in enumerate(CODES):
        target = low_ref if k < 16 else high_ref
        target[k % 16] = read(me_ref[0] ^ code)


def softmax_columns(scores):
    shifted = jnp.exp(scores - jnp.max(scores, axis=0, keepdims=True))
    return (shifted * (1.0 / jnp.sum(shifted, axis=0, keepdims=True))).astype(BF16)


def step_rows(ref, step):
    whole = ref[...].astype(F32)
    rows = whole[:STEP_ROWS]
    for s in range(1, whole.shape[0] // STEP_ROWS):
        rows = jnp.where(step == s, whole[s * STEP_ROWS : (s + 1) * STEP_ROWS], rows)
    return rows


def token_columns(lines):
    pad = 8 - lines.shape[0] % 8
    return jnp.concatenate([lines] + [lines[:1]] * (pad % 8), axis=0).T


def member_lines(lines):
    count, length = lines.shape
    codes = jnp.concatenate([lines[r : r + 1] + float(NSEG * r) for r in range(count)], axis=1)
    places = lax.broadcasted_iota(jnp.int32, (NSEG * count, count * length), 0).astype(F32)
    return (codes == places).astype(F32).astype(BF16)


def same_sum(products, lines, columns, r):
    same = columns[:, r : r + 1] == lines[r : r + 1]
    return jnp.sum(jnp.where(same, products, 0.0), axis=0, keepdims=True)


def each_row(row):
    for r in range(STEP_ROWS):
        row(r, 0)


def gram(left):
    return nt(left, left)


def self_forward_kernel(me_ref, tokens_ref, dec_ref, padding_ref, buckets_ref, *refs):
    pieces, refs = refs[:8], refs[8:]
    input_ref, qkv_ref, prob_ref, attended_ref, weight_ref, gains_ref = refs[:6]
    bias_ref, small_ref, sems = refs[6:]
    length = dec_ref.shape[1]
    width = tokens_ref.shape[1]

    @pl.when(pl.program_id(0) == 0)
    def _():
        pairs = []
        for k, code in enumerate(CODES):
            rows = block_rows(me_ref[0] ^ code)
            source = pieces[k // 4].at[k % 4]
            pairs.append((source.at[:, : 3 * width], weight_ref.at[rows, :]))
            pairs.append((source.at[:, 3 * width :], small_ref.at[rows, :]))
        for copy in start_copies(pairs, sems):
            copy.wait()
        first = lax.broadcasted_iota(jnp.int32, (32, width), 1)
        pick = first == 16 * lax.broadcasted_iota(jnp.int32, (32, width), 0)
        small = nn(pick.astype(F32).astype(BF16), small_ref[...]).astype(BF16)
        lane = lax.broadcasted_iota(jnp.int32, (LANES, width), 0)
        feature = lax.broadcasted_iota(jnp.int32, (LANES, width), 1)
        block = lax.broadcasted_iota(jnp.int32, (32, width), 0)
        lines = []
        for k in range(4):
            spread = nn(small, (lane == 16 * k + feature % 16).astype(F32).astype(BF16))
            lines.append(
                jnp.sum(jnp.where(block == first // 16, spread, 0.0), axis=0, keepdims=True)
            )
        gains_ref[...] = jnp.concatenate(lines + lines, axis=0)
        place = lax.broadcasted_iota(jnp.int32, (H, width), 1) % 16
        head = lax.broadcasted_iota(jnp.int32, (H, width), 0)
        table = jnp.where(place == head, lines[3], 0.0).astype(BF16)
        bucket = lax.broadcasted_iota(jnp.int32, (width, length), 0) // 16
        curves = nn(table, (bucket == buckets_ref[...]).astype(F32).astype(BF16))
        for h in range(H):
            curve = jnp.broadcast_to(curves[h : h + 1, :], (length, length))
            lanes = slice((h % 2) * length, (h % 2 + 1) * length)
            bias_ref[h // 2, :, lanes] = pltpu.roll(curve, 0, 1, stride=1, stride_axis=0)

    values = tokens_ref[...].astype(F32)
    normed = (values * inverse_root(values) * gains_ref[0:1, :]).astype(BF16)
    input_ref[...] = normed
    for k in range(3):
        cols = slice(k * width, (k + 1) * width)
        qkv_ref[:, cols] = nn(normed, weight_ref[:, cols]).astype(BF16)

    step = pl.program_id(0)
    segments, real = step_rows(dec_ref, step), step_rows(padding_ref, step)
    segment_columns, real_columns = token_columns(segments), token_columns(real)
    key_i = lax.broadcasted_iota(jnp.int32, (length, length), 0)
    query_i = lax.broadcasted_iota(jnp.int32, (length, length), 1)

    def row(r, carry):
        rows = slice(r * length, (r + 1) * length)
        allowed = (segment_columns[:, r : r + 1] == segments[r : r + 1]) & (key_i <= query_i)
        allowed = allowed & ((real_columns[:, r : r + 1] > 0.0) | (key_i == query_i))
        mask = jnp.where(allowed, 0.0, FLOOR)
        mask = jnp.concatenate([mask, mask], axis=1)
        for p in range(PAIRS):
            query = qkv_ref[rows, p * LANES : (p + 1) * LANES]
            key = qkv_ref[rows, width + p * LANES : width + (p + 1) * LANES]
            value = qkv_ref[rows, 2 * width + p * LANES : 2 * width + (p + 1) * LANES]
            prob = softmax_columns(nt(key, head_pair(query)) + bias_ref[p] + mask)
            prob_ref[r, p] = prob
            attended_ref[rows, p * LANES : (p + 1) * LANES] = fold_pair(nn(value.T, prob), length)
        return carry

    each_row(row)


def memory_forward_kernel(me_ref, memory_ref, *refs):
    pieces, (kv_ref, weight_ref, sems) = refs[:-3], refs[-3:]
    width = memory_ref.shape[1]

    @pl.when(pl.program_id(0) == 0)
    def _():
        pairs = []
        for k, code in enumerate(CODES):
            source = pieces[k // 4].at[k % 4]
            pairs.append((source, weight_ref.at[block_rows(me_ref[0] ^ code), :]))
        for copy in start_copies(pairs, sems):
            copy.wait()

    for k in range(2):
        kv_ref[:, k * width : (k + 1) * width] = nn(
            memory_ref[...], weight_ref[:, (k + 2) * width : (k + 3) * width]
        ).astype(BF16)


def cross_forward_kernel(tokens_ref, attended_a_ref, kv_ref, dec_ref, mem_ref, gains_ref,
                         weight_ref, middle_ref, input_ref, query_ref, prob_ref, attended_ref, after_ref):
    mem_length, length = mem_ref.shape[1], dec_ref.shape[1]
    width = tokens_ref.shape[1]
    values = tokens_ref[...].astype(F32) + nn(attended_a_ref[...], weight_ref[:, :width])
    middle_ref[...] = values.astype(BF16)
    normed = (values * inverse_root(values) * gains_ref[1:2, :]).astype(BF16)
    input_ref[...] = normed
    query_ref[...] = nn(normed, weight_ref[:, width : 2 * width]).astype(BF16)

    step = pl.program_id(0)
    segments, mem_columns = step_rows(dec_ref, step), token_columns(step_rows(mem_ref, step))

    def row(r, carry):
        rows = slice(r * length, (r + 1) * length)
        mem_rows = slice(r * mem_length, (r + 1) * mem_length)
        mask = jnp.where(mem_columns[:, r : r + 1] == segments[r : r + 1], 0.0, FLOOR)
        for p in range(PAIRS):
            lanes = slice(p * LANES, (p + 1) * LANES)
            key = kv_ref[mem_rows, lanes]
            value = kv_ref[mem_rows, width + p * LANES : width + (p + 1) * LANES].T
            both = []
            for h, query in enumerate(head_masks(query_ref[rows, lanes])):
                prob = softmax_columns(nt(key, query) + mask)
                prob_ref[r, p, :, h * length : (h + 1) * length] = prob
                both.append(nn(value[h * DH : (h + 1) * DH], prob))
            attended_ref[rows, lanes] = jnp.concatenate(both, axis=0).astype(BF16).T

    each_row(row)
    after = values + nn(attended_ref[...], weight_ref[:, 4 * width :])
    after_ref[...] = after.astype(BF16)


def norm_back(values, gain, grad_normed):
    inverse = inverse_root(values)
    scaled = values * inverse
    upper = grad_normed * gain
    grad = inverse * (upper - scaled * jnp.mean(upper * scaled, axis=-1, keepdims=True))
    return grad, grad_normed * scaled


def gain_sums(terms, segments, total_ref, square_ref):
    sums = nn(member_lines(segments), terms.astype(BF16))
    total_ref[...] += jnp.sum(sums, axis=0, keepdims=True)
    square = jnp.sum(sums * sums, axis=1, keepdims=True)
    square_ref[...] = jnp.broadcast_to(square, square_ref.shape)


def feed_kernel(me_ref, after_ref, cotangent_ref, dec_ref, padding_ref, gains_ref, own_ref,
                other_ref, result_ref, branch_b_ref, slots_ref, total_ref, square_ref, token_ref,
                weight, normed_ref, branch_ref, active_ref, grad_ref, sum_ref, back_ref, gram_ref,
                sems):
    part = pl.program_id(0)
    count, length = dec_ref.shape
    dec, width = after_ref.shape
    ff = weight.shape[1] // 2
    tile = STEP_ROWS * length
    tiles = [slice(t * tile, (t + 1) * tile) for t in range(dec // tile)]

    @pl.when(part == 0)
    def _():
        core = me_ref[0] & 2
        pairs = []
        for k, code in enumerate(CHIPS):
            pairs.append((own_ref.at[k], weight.at[block_rows(code + core), :]))
            pairs.append((other_ref.at[k], weight.at[block_rows(code + 2 - core), :]))
        copies = start_copies(pairs, sems)
        real = token_columns(padding_ref[...].astype(F32))
        for r in range(count):
            rows = slice(r * length, (r + 1) * length)
            branch_ref[rows, :] = (
                cotangent_ref[rows, :].astype(F32) * real[:, r : r + 1]
            ).astype(BF16)
        for rows in tiles:
            values = after_ref[rows, :].astype(F32)
            normed_ref[rows, :] = (values * inverse_root(values) * gains_ref[2:3, :]).astype(BF16)
        sum_ref[...] = jnp.zeros_like(sum_ref)
        back_ref[...] = jnp.zeros_like(back_ref)
        gram_ref[...] = jnp.zeros_like(gram_ref)
        for copy in copies:
            copy.wait()

    w_in = weight[:, pl.ds(pl.multiple_of(part * width, width), width)]
    w_out = weight[:, pl.ds(pl.multiple_of(ff + part * width, width), width)]
    root = 0.7978845608028654
    for t, rows in enumerate(tiles):
        hidden = nn(normed_ref[rows, :], w_in)
        square = hidden * hidden
        bent = jnp.tanh(hidden * (root + (root * 0.044715) * square))
        half = 0.5 + 0.5 * bent
        slope = hidden * (2.0 * root + (6.0 * root * 0.044715) * square)
        slope = half + half * (slope * (1.0 - half))
        active_ref[rows, :] = (hidden * half).astype(BF16)
        grad_ref[rows, :] = (nt(branch_ref[rows, :], w_out) * slope).astype(BF16)
        sum_ref[rows, :] += nn(active_ref[rows, :], w_out)
        back_ref[rows, :] += nt(grad_ref[rows, :], w_in)
        for r in range(t * STEP_ROWS, (t + 1) * STEP_ROWS):
            own = slice(r * length, (r + 1) * length)
            gram_ref[0, r] += gram(active_ref[own, :])
            gram_ref[1, r] += gram(grad_ref[own, :])
    grad_in = tn(normed_ref[...], grad_ref[...]).astype(BF16)
    grad_out = tn(branch_ref[...], active_ref[...]).astype(BF16).T
    in_cols = pl.ds(pl.multiple_of(part * width, width), width)
    out_cols = pl.ds(pl.multiple_of(ff + part * width, width), width)
    for k, block in enumerate(CODES):
        rows = slice(16 * block, 16 * block + 16)
        slots_ref[k, :, in_cols] = grad_in[rows]
        slots_ref[k, :, out_cols] = grad_out[rows]

    @pl.when(part == pl.num_programs(0) - 1)
    def _():
        segments = dec_ref[...].astype(F32)
        columns = token_columns(segments)
        total_ref[...] = jnp.zeros_like(total_ref)
        for t, rows in enumerate(tiles):
            values = after_ref[rows, :].astype(F32)
            result_ref[rows, :] = (values + sum_ref[rows, :]).astype(BF16)
            grad, terms = norm_back(values, gains_ref[2:3, :], back_ref[rows, :])
            branch_b_ref[rows, :] = (branch_ref[rows, :].astype(F32) + grad).astype(BF16)
            own = segments[t * STEP_ROWS : (t + 1) * STEP_ROWS]
            gain_sums(terms, own, total_ref, square_ref.at[t])
        for r in range(count):
            own = slice(r * length, (r + 1) * length)
            products = gram_ref[0, r] * gram(branch_ref[own, :])
            products = products + gram_ref[1, r] * gram(normed_ref[own, :])
            token_ref[r // STEP_ROWS, r % STEP_ROWS : r % STEP_ROWS + 1, :] = same_sum(
                products, segments, columns, r
            )


def score_grads(prob, grad_prob):
    prob = prob.astype(F32)
    dots = jnp.sum(prob * grad_prob, axis=0, keepdims=True)
    return prob * (grad_prob - dots)


def cross_backward_kernel(me_ref, branch_ref, middle_ref, memory_ref, attended_a_ref, input_ref,
                          query_ref, kv_ref, prob_ref, attended_ref, dec_ref, gains_ref,
                          weight_ref, grad_query_ref, grad_kv_ref, branch_a_ref, low_ref, high_ref,
                          total_ref, square_ref, grad_w, grad_attended):
    step = pl.program_id(0)
    mem_length = prob_ref.shape[2]
    length = prob_ref.shape[3] // 2
    width = branch_ref.shape[1]

    @pl.when(step == 0)
    def _():
        grad_w[...] = jnp.zeros_like(grad_w)
        total_ref[...] = jnp.zeros_like(total_ref)

    branch = branch_ref[...]
    grad_attended[...] = nt(branch, weight_ref[:, 4 * width :]).astype(BF16)

    def row(r, carry):
        rows = slice(r * length, (r + 1) * length)
        mem_rows = slice(r * mem_length, (r + 1) * mem_length)
        for p in range(PAIRS):
            lanes = slice(p * LANES, (p + 1) * LANES)
            upper = slice(width + p * LANES, width + (p + 1) * LANES)
            value = kv_ref[mem_rows, upper]
            grad_outs = head_masks(grad_attended[rows, lanes])
            grad_scores = []
            for h, grad_out in enumerate(grad_outs):
                prob = prob_ref[r, p, :, h * length : (h + 1) * length]
                grad_scores.append(score_grads(prob, nt(value, grad_out)).astype(BF16))
            grad_score = jnp.concatenate(grad_scores, axis=1)
            query = head_pair(query_ref[rows, lanes])
            grad_kv_ref[mem_rows, lanes] = nn(grad_score, query).astype(BF16)
            grad_kv_ref[mem_rows, upper] = nn(
                prob_ref[r, p], jnp.concatenate(grad_outs, axis=0)
            ).astype(BF16)
            key = kv_ref[mem_rows, lanes].T
            grad_query_ref[rows, lanes] = fold_pair(nn(key, grad_score), length)

    each_row(row)
    grad_query = grad_query_ref[...]
    grad_normed = nt(grad_query, weight_ref[:, width : 2 * width])
    grad, terms = norm_back(middle_ref[...].astype(F32), gains_ref[1:2, :], grad_normed)
    branch_a = (branch.astype(F32) + grad).astype(BF16)
    branch_a_ref[...] = branch_a
    gain_sums(terms, step_rows(dec_ref, step), total_ref, square_ref.at[0])
    grad_w[:, :width] += tn(attended_a_ref[...], branch_a)
    grad_w[:, width : 2 * width] += tn(input_ref[...], grad_query)
    grad_w[:, 2 * width : 4 * width] += tn(memory_ref[...], grad_kv_ref[...])
    grad_w[:, 4 * width :] += tn(attended_ref[...], branch)

    @pl.when(step == pl.num_programs(0) - 1)
    def _():
        store_slots(me_ref, low_ref, high_ref, partial(read_rows, grad_w))


def self_scores_kernel(branch_ref, qkv_ref, prob_ref, dec_ref, buckets_ref, weight_ref,
                       grad_qkv_ref, table_ref, table_square_ref, grad_attended, bands):
    step = pl.program_id(0)
    length = prob_ref.shape[2]
    width = branch_ref.shape[1]
    grad_attended[...] = nt(branch_ref[...], weight_ref[:, :width]).astype(BF16)

    @pl.when(step == 0)
    def _():
        table_ref[...] = jnp.zeros_like(table_ref)
        bands[...] = jnp.zeros_like(bands)

    row_i = lax.broadcasted_iota(jnp.int32, (length, length), 0)
    col_i = lax.broadcasted_iota(jnp.int32, (length, length), 1)
    flip = (row_i + col_i == length - 1).astype(F32).astype(BF16)
    columns = token_columns(step_rows(dec_ref, step)).astype(BF16)
    turned = nn(flip, columns)

    def row(r, carry):
        rows = slice(r * length, (r + 1) * length)
        member = [
            jnp.broadcast_to((turned[:, r : r + 1] == float(e)).astype(F32), (length, length))
            for e in range(NSEG)
        ]
        for p in range(PAIRS):
            lanes = slice(p * LANES, (p + 1) * LANES)
            middle = slice(width + p * LANES, width + (p + 1) * LANES)
            upper = slice(2 * width + p * LANES, 2 * width + (p + 1) * LANES)
            value = qkv_ref[rows, upper]
            query = head_pair(qkv_ref[rows, lanes])
            grad_out = head_pair(grad_attended[rows, lanes])
            prob = prob_ref[r, p]
            grad_score = score_grads(prob, nt(value, grad_out)).astype(BF16)
            grad_qkv_ref[rows, middle] = nn(grad_score, query).astype(BF16)
            grad_qkv_ref[rows, upper] = nn(prob, grad_out).astype(BF16)
            key = jnp.concatenate([qkv_ref[rows, middle].T, flip], axis=0)
            both = nn(key, grad_score)
            grad_qkv_ref[rows, lanes] = fold_pair(both[:length], length)
            for h in range(2):
                own = both[length:, h * length : (h + 1) * length]
                own = pltpu.roll(own, 1, 1, stride=1, stride_axis=0)
                for e in range(NSEG):
                    bands[r, 2 * p + h, e : e + 1, :] = jnp.sum(
                        own * member[e], axis=0, keepdims=True
                    )

    each_row(row)
    bucket = lax.broadcasted_iota(jnp.int32, (LANES, length), 0)
    near = (bucket == buckets_ref[...]).astype(F32)
    flat = bands[...].reshape(STEP_ROWS * H * 8, length)
    per_bucket = lax.dot_general(
        flat, near, (((1,), (1,)), ((), ())), preferred_element_type=F32,
        precision=lax.Precision.HIGHEST,
    ).reshape(STEP_ROWS, H, 8, LANES)
    table_ref[...] += jnp.sum(jnp.sum(per_bucket, axis=0), axis=1)
    squares = jnp.sum(jnp.sum(per_bucket * per_bucket, axis=1), axis=-1, keepdims=True)
    table_square_ref[0] = jnp.broadcast_to(squares, (STEP_ROWS, 8, LANES))


def self_weights_kernel(me_ref, branch_ref, tokens_ref, input_ref, grad_qkv_ref, dec_ref,
                        gains_ref, weight_ref, table_ref, total_b_ref, total_c_ref,
                        grad_tokens_ref, low_ref, high_ref, square_ref, grad_w, total_ref,
                        small_ref):
    step = pl.program_id(0)
    width = tokens_ref.shape[1]
    grad_qkv = grad_qkv_ref[...]
    grad_normed = nt(grad_qkv, weight_ref[...])
    grad, terms = norm_back(tokens_ref[...].astype(F32), gains_ref[0:1, :], grad_normed)
    grad_tokens_ref[...] = (branch_ref[...].astype(F32) + grad).astype(BF16)

    @pl.when(step == 0)
    def _():
        grad_w[...] = jnp.zeros_like(grad_w)
        total_ref[...] = jnp.zeros_like(total_ref)

    gain_sums(terms, step_rows(dec_ref, step), total_ref, square_ref.at[0])
    grad_w[...] += tn(input_ref[...], grad_qkv)

    @pl.when(step == pl.num_programs(0) - 1)
    def _():
        bucket = lax.broadcasted_iota(jnp.int32, (LANES, width), 0)
        place = lax.broadcasted_iota(jnp.int32, (LANES, width), 1)
        spread = nn(table_ref[...].astype(BF16), (place // 16 == bucket).astype(F32).astype(BF16))
        head = lax.broadcasted_iota(jnp.int32, (H, width), 0)
        lane = lax.broadcasted_iota(jnp.int32, (H, width), 1)
        table = jnp.sum(jnp.where(lane % 16 == head, spread, 0.0), axis=0, keepdims=True)
        small = jnp.zeros((LANES, width), F32)
        row_i = lax.broadcasted_iota(jnp.int32, (LANES, width), 0)
        for k, line in enumerate((total_ref[...], total_b_ref[...], total_c_ref[...], table)):
            small = jnp.where(row_i == k, line, small)
        small_ref[...] = small.T

        def read(block):
            return jnp.concatenate(
                [read_rows(grad_w, block), read_rows(small_ref, block)], axis=1
            )

        store_slots(me_ref, low_ref, high_ref, read)


def pair_sum_kernel(low_ref, sent_ref, *refs):
    outs, (low, sent, total, load_sems, store_sems) = refs[:4], refs[4:]
    places = [pl.ds(4 * t, 4) for t in range(4)]
    lows = start_copies([(low_ref.at[p], low.at[p]) for p in places], load_sems.at[0])
    sents = start_copies([(sent_ref.at[p], sent.at[p]) for p in places], load_sems.at[1])
    stores = []
    for t, p in enumerate(places):
        lows[t].wait()
        sents[t].wait()
        total[p] = (low[p].astype(F32) + sent[p].astype(F32)).astype(BF16)
        stores.append(pltpu.make_async_copy(total.at[p], outs[t], store_sems.at[t]))
        stores[t].start()
    for store in stores:
        store.wait()


def pair_sum(low, sent, after):
    piece = shape_of((4,) + low.shape[1:], BF16)
    return pl.pallas_call(
        ignoring(pair_sum_kernel, 2, len(after)),
        out_shape=(piece,) * 4,
        in_specs=[pl.BlockSpec(memory_space=pl.ANY)] * (2 + len(after)),
        out_specs=[pl.BlockSpec(memory_space=pl.ANY)] * 4,
        scratch_shapes=[pltpu.VMEM(low.shape, BF16)] * 3
        + [pltpu.SemaphoreType.DMA((2, 4)), pltpu.SemaphoreType.DMA((4,))],
        compiler_params=pltpu.CompilerParams(vmem_limit_bytes=VMEM_LIMIT),
    )(low, sent, *after)


def plane_sum_kernel(a_ref, b_ref, c_ref, d_ref, own_ref, *outs):
    for s in range(4):
        total = a_ref[s].astype(F32) + b_ref[s].astype(F32)
        total = total + c_ref[s].astype(F32) + d_ref[s].astype(F32)
        if s == 0:
            own_ref[...] = total
        else:
            outs[s - 1][...] = total.astype(BF16)


def plane_sum(pieces, after):
    line = pieces[0].shape[1:]
    return small_call(
        plane_sum_kernel, pieces, after, (shape_of(line, F32),) + (shape_of(line, BF16),) * 3
    )


def square_sum(values):
    return jnp.sum(jnp.sum(values * values, axis=0, keepdims=True), axis=1, keepdims=True)


def feed_end_kernel(sum_ref, hidden_ref, back_ref, square_ref):
    total = sum_ref[...].astype(F32)
    ff = hidden_ref.shape[1]
    width = back_ref.shape[1]
    hidden_ref[...] = total[:, :ff]
    for j in range(ff // width):
        back_ref[16 * j : 16 * (j + 1), :] = total[:, ff + j * width : ff + (j + 1) * width]
    square_ref[...] = jnp.broadcast_to(square_sum(total), square_ref.shape)


def column_end_kernel(own_ref, b_ref, c_ref, d_ref, *refs):
    squares, outs, square_ref = refs[:2], refs[2:-1], refs[-1]
    total = own_ref[...] + b_ref[...].astype(F32)
    total = total + c_ref[...].astype(F32) + d_ref[...].astype(F32)
    start = 0
    for out in outs:
        out[...] = total[:, start : start + out.shape[1]]
        start += out.shape[1]
    square = square_sum(total)
    for given in squares:
        square = square + given[0:1, 0:1]
    square_ref[...] = jnp.broadcast_to(square, square_ref.shape)


def staged(kernel, ins, outs):
    def run(*refs):
        count = ins + outs
        given, inner, sems = refs[:count], refs[count : 2 * count], refs[2 * count]
        for copy in start_copies(list(zip(given[:ins], inner[:ins])), sems):
            copy.wait()
        kernel(*inner)
        for copy in start_copies(list(zip(inner[ins:], given[ins:])), sems):
            copy.wait()

    return run


def small_call(kernel, ins, after, outs):
    arrays = [*ins, *outs]
    return pl.pallas_call(
        ignoring(staged(kernel, len(ins), len(outs)), len(ins), len(after)),
        out_shape=outs,
        in_specs=[pl.BlockSpec(memory_space=pl.ANY)] * (len(ins) + len(after)),
        out_specs=[pl.BlockSpec(memory_space=pl.ANY)] * len(outs),
        scratch_shapes=[pltpu.VMEM(array.shape, array.dtype) for array in arrays]
        + [pltpu.SemaphoreType.DMA((len(arrays),))],
        compiler_params=pltpu.CompilerParams(vmem_limit_bytes=VMEM_LIMIT),
    )(*ins, *after)


def pack_kernel(*refs):
    ins, (self_ref, cross_ref, feed_ref) = refs[:11], refs[11:]
    width = ins[0].shape[1]
    for k in range(3):
        self_ref[:, k * width : (k + 1) * width] = ins[k][...]
    self_ref[:, 3 * width :] = ins[10][...]
    for k in range(5):
        cross_ref[:, k * width : (k + 1) * width] = ins[3 + k][...]
    ff = ins[8].shape[1]
    feed_ref[:, :ff] = ins[8][...]
    for j in range(ff // width):
        feed_ref[:, ff + j * width : ff + (j + 1) * width] = ins[9][16 * j : 16 * (j + 1), :]


def pack(weights, small):
    width, ff = weights[0].shape[1], weights[8].shape[1]
    outs = [shape_of((16, cols), BF16) for cols in (3 * width + LANES, 5 * width, 2 * ff)]
    return small_call(pack_kernel, (*weights, small), (), outs)


def memory_backward_kernel(memory_ref, grad_kv_ref, mem_ref, weight_ref, grad_memory_ref,
                           token_ref):
    mem_length = mem_ref.shape[1]
    width = memory_ref.shape[1]
    weight = weight_ref[:, 2 * width : 4 * width]
    grad_memory_ref[...] = nt(grad_kv_ref[...], weight).astype(BF16)
    segments = step_rows(mem_ref, pl.program_id(0))
    columns = token_columns(segments)
    for r in range(STEP_ROWS):
        rows = slice(r * mem_length, (r + 1) * mem_length)
        products = gram(memory_ref[rows, :]) * gram(grad_kv_ref[rows, :])
        token_ref[0, r : r + 1, :] = same_sum(products, segments, columns, r)


def gram_kernel(*refs):
    pairs, dec_ref, token_ref = refs[:-2], refs[-2], refs[-1]
    length = dec_ref.shape[1]
    segments = step_rows(dec_ref, pl.program_id(0))
    columns = token_columns(segments)
    for r in range(STEP_ROWS):
        rows = slice(r * length, (r + 1) * length)
        products = sum(
            gram(left[rows, :]) * gram(right[rows, :])
            for left, right in zip(pairs[::2], pairs[1::2])
        )
        token_ref[0, r : r + 1, :] = same_sum(products, segments, columns, r)


def rows_spec(array, steps):
    shape = (array.shape[0] // steps,) + array.shape[1:]
    return pl.BlockSpec(shape, lambda i, *_: (i,) + (0,) * (len(shape) - 1))


def whole_spec(array):
    return pl.BlockSpec(array.shape, lambda i, *_: (0,) * len(array.shape))


def ignoring(kernel, first, count):
    return lambda *refs: kernel(*refs[:first], *refs[first + count :])


def call(kernel, steps, me, blocked, whole, pieces, outs_blocked, outs_whole, scratch, flops,
         order, after=(), limit=VMEM_LIMIT):
    ins, in_specs = [], []
    blocked, whole = list(blocked), list(whole)
    for kind in order[0]:
        array = (blocked if kind == "i" else whole).pop(0)
        ins.append(array)
        in_specs.append(rows_spec(array, steps) if kind == "i" else whole_spec(array))
    kernel = ignoring(kernel, len(ins) + len(pieces) + (me is not None), len(after))
    ins += [*pieces, *after]
    in_specs += [pl.BlockSpec(memory_space=pl.ANY)] * (len(pieces) + len(after))
    outs, out_specs = [], []
    outs_blocked, outs_whole = list(outs_blocked), list(outs_whole)
    for kind in order[1]:
        out = (outs_blocked if kind == "i" else outs_whole).pop(0)
        outs.append(out)
        out_specs.append(rows_spec(out, steps) if kind == "i" else whole_spec(out))
    moved = sum(math.prod(a.shape) * a.dtype.itemsize for a in ins + outs)
    prefetch = 0 if me is None else 1
    return pl.pallas_call(
        kernel,
        out_shape=outs,
        grid_spec=pltpu.PrefetchScalarGridSpec(
            num_scalar_prefetch=prefetch,
            grid=(steps,),
            in_specs=in_specs,
            out_specs=out_specs,
            scratch_shapes=scratch,
        ),
        compiler_params=pltpu.CompilerParams(
            dimension_semantics=("arbitrary",), vmem_limit_bytes=limit
        ),
        cost_estimate=pl.CostEstimate(flops=flops, bytes_accessed=moved, transcendentals=0),
    )(*(() if me is None else (me,)), *ins)


FINE = ("z", "y", "core", "x")


def shape_of(shape, dtype):
    return jax.ShapeDtypeStruct(shape, dtype)


def kept(shape, dtype):
    return pltpu.HBM(shape, dtype)


def shift(array, mask):
    return lax.ppermute(array, FINE, [(i, i ^ mask) for i in range(32)])


def hold(array, after):
    return lax.optimization_barrier((array, after))[0]


def split_back(back):
    blocks = back.shape[0] // 64
    parts = back.reshape(blocks, 4, 16, back.shape[1]).transpose(0, 2, 1, 3)
    return parts.reshape(16 * blocks, 4 * back.shape[1])


def fold_columns(weight):
    parts = weight.reshape(weight.shape[0], -1, 4, 16).transpose(0, 2, 1, 3)
    return parts.reshape(weight.shape)


def unfold_columns(weight):
    parts = weight.reshape(weight.shape[0], 4, -1, 16).transpose(0, 2, 1, 3)
    return parts.reshape(weight.shape)


def join_back(parts):
    blocks, width = parts.shape[0] // 16, parts.shape[1] // 4
    return parts.reshape(blocks, 16, 4, width).transpose(0, 2, 1, 3).reshape(64 * blocks, width)


def small_row(gains, table):
    table = jnp.pad(table.reshape(-1, H), ((0, 0), (0, 16 - H)))
    row = jnp.concatenate([gain.reshape(-1, 16) for gain in gains] + [table], axis=1)
    row = jnp.pad(row, ((0, 0), (0, LANES - row.shape[1])))
    return jnp.pad(row[:, None], ((0, 0), (0, 15), (0, 0))).reshape(-1, LANES)


def in_order(slots):
    return slots[jnp.array([CODES.index(block) for block in range(32)])].reshape(-1, slots.shape[2])


def shift_plane(pieces):
    return [shift(piece, mask) for piece, mask in zip(pieces, PLANE[1:])]


def shift_column(pieces):
    return [shift(piece, code) for piece, code in zip(pieces, COLUMN[1:])]


class Near:
    axes = FINE

    def __init__(self, weights):
        self.me = lax.axis_index(FINE)
        shards = [*weights[:8], fold_columns(weights[8]), weights[9]]
        own, self.cross_shard, feed = pack(shards, small_row(weights[10:13], weights[13]))
        self.chips = lax.all_gather(feed, ("z", "y", "x"), axis=0)
        column = jnp.stack([own, *shift_column([own] * 3)])
        line = hold(self.cross_shard, column)
        line = jnp.stack([line, *shift_column([line] * 3)])
        plane = [column, *shift_plane([column] * 3)]
        line = hold(line, plane[3])
        self.plane = [line, *shift_plane([line] * 3)]
        self.own = plane + [shift(piece, 2) for piece in plane]

    def cross(self, after):
        plane = [hold(piece, after) for piece in self.plane]
        return plane + [shift(piece, 2) for piece in plane]

    def feed(self, after):
        chips = hold(self.chips, after)
        return chips, shift(chips, 2)

    def feed_core(self, slots):
        return lax.psum_scatter(slots.reshape((2, 4, 4) + slots.shape[1:]), "core")

    def feed_plane(self, slots):
        return lax.psum_scatter(slots, ("y", "x"))

    def feed_column(self, slots):
        return lax.psum_scatter(slots, "z")


class Far:
    axes = ("wide", "narrow")
    me = 0

    def __init__(self, weights):
        weights = [lax.all_gather(w, self.axes, axis=0, tiled=True) for w in weights]
        self.take(weights)

    def take(self, weights):
        self.own = self.pieces(*weights[:3], small_row(weights[10:13], weights[13]))
        self.rest = self.pieces(*weights[3:8])
        feed = [fold_columns(weights[8]), split_back(weights[9])]
        feed = jnp.concatenate(feed, axis=1).reshape(32, 16, -1)
        self.chips = tuple(feed[jnp.array(CHIPS) + core] for core in (0, 2))

    def pieces(self, *parts):
        blocks = jnp.concatenate(parts, axis=1).reshape(32, 16, -1)[jnp.array(CODES)]
        return [blocks[4 * t : 4 * t + 4] for t in range(8)]

    def cross(self, after):
        return self.rest

    def feed(self, after):
        return self.chips

    def feed_core(self, slots):
        return slots

    feed_plane = feed_column = feed_core


def on_device(near, tokens, memory, cotangent, dec_segments, mem_segments, padding, buckets,
              *weights):
    way = (Near if near else Far)(weights)
    result, grad_tokens, grad_memory, grads, examples, square = local_part(
        way, tokens, memory, cotangent, dec_segments, mem_segments, padding, buckets
    )
    if near:
        sent = lax.all_to_all(square, FINE, 0, 0, tiled=True)
        global_norm = jnp.sum(sent[:, 0])
    else:
        grads = [lax.psum_scatter(g, way.axes, scatter_dimension=0, tiled=True) for g in grads]
        global_norm = lax.psum(sum(jnp.sum(g * g) for g in grads), way.axes)
    return (result, grad_tokens, grad_memory, *grads, examples, global_norm / COUNT)


def local_part(way, tokens, memory, cotangent, dec_segments, mem_segments, padding, buckets):
    seqs, length, width = tokens.shape
    mem_length = memory.shape[1]
    steps = seqs // STEP_ROWS
    dec, mem = seqs * length, seqs * mem_length
    step_dec = STEP_ROWS * length
    ff = 4 * width

    buckets = buckets[None]
    tokens2, memory2 = tokens.reshape(dec, width), memory.reshape(mem, width)
    dma = pltpu.SemaphoreType.DMA

    me = jnp.full((1,), way.me, jnp.int32)
    flops = 2 * dec * width * width

    input_a, qkv_a, prob_a, attended_a, self_w, gains = call(
        self_forward_kernel, steps, me, (tokens2,), (dec_segments, padding, buckets), way.own,
        (
            kept((dec, width), BF16),
            kept((dec, 3 * width), BF16),
            kept((seqs, PAIRS, length, 2 * length), BF16),
            kept((dec, width), BF16),
        ),
        (kept((width, 3 * width), BF16), kept((8, width), F32)),
        [pltpu.VMEM((PAIRS, length, 2 * length), F32), pltpu.VMEM((width, LANES), BF16), dma((64,))],
        6 * flops, ("iwww", "iiiiww"), (), GATHERED_LIMIT,
    )
    kv_b, cross_w = call(
        memory_forward_kernel, steps, me, (memory2,), (), way.cross(attended_a),
        (kept((mem, 2 * width), BF16),), (kept((width, 5 * width), BF16),), [dma((32,))],
        4 * flops, ("i", "iw"), (), GATHERED_LIMIT,
    )
    feed_pieces = way.feed(kv_b)
    middle, input_b, query_b, prob_b, attended_b, after_cross = call(
        cross_forward_kernel, steps, None, (tokens2, attended_a, kv_b),
        (dec_segments, mem_segments, gains, cross_w), (),
        (
            kept((dec, width), BF16),
            kept((dec, width), BF16),
            kept((dec, width), BF16),
            kept((seqs, PAIRS, mem_length, 2 * length), BF16),
            kept((dec, width), BF16),
            kept((dec, width), BF16),
        ),
        (), [], 6 * flops, ("iiiwwww", "iiiiii"),
    )
    total, square = kept((1, width), F32), shape_of((steps, 4 * STEP_ROWS, LANES), F32)
    token_shape = shape_of((steps, 8, length), F32)
    result, branch_b, feed_slots, gain_c, square_c, token_c = call(
        feed_kernel, ff // width, me, (),
        (after_cross, cotangent.reshape(dec, width), dec_segments, padding, gains), feed_pieces,
        (),
        (
            shape_of((dec, width), BF16),
            kept((dec, width), BF16),
            shape_of((32, 16, 2 * ff), BF16),
            total,
            square,
            token_shape,
        ),
        [
            pltpu.VMEM((width, 2 * ff), BF16),
            *[pltpu.VMEM((dec, width), BF16)] * 4,
            *[pltpu.VMEM((dec, width), F32)] * 2,
            pltpu.VMEM((2, seqs, length, length), F32),
            dma((32,)),
        ],
        26 * flops, ("wwwww", "wwwwww"),
    )
    feed_sum = way.feed_core(feed_slots)
    slot = shape_of((16, 16, 5 * width), BF16)
    grad_query_b, grad_kv_b, branch_a, cross_low, cross_high, gain_b, square_b = call(
        cross_backward_kernel, steps, me,
        (branch_b, middle, memory2, attended_a, input_b, query_b, kv_b, prob_b, attended_b),
        (dec_segments, gains, cross_w), (),
        (
            kept((dec, width), BF16),
            kept((mem, 2 * width), BF16),
            kept((dec, width), BF16),
            square,
        ),
        (slot, slot, total),
        [pltpu.VMEM((width, 5 * width), F32), pltpu.VMEM((step_dec, width), BF16)],
        20 * flops, ("iiiiiiiiiwww", "iiiwwwi"),
    )
    feed_sum = way.feed_plane(hold(feed_sum, grad_query_b))
    near = isinstance(way, Near)
    if near:
        sent = shift(cross_high, 2)
    grad_qkv_a, table, table_square = call(
        self_scores_kernel, steps, None, (branch_a, qkv_a, prob_a),
        (dec_segments, buckets, cross_w), (),
        (kept((dec, 3 * width), BF16), shape_of((steps, STEP_ROWS, 8, LANES), F32)),
        (kept((H, LANES), F32),),
        [pltpu.VMEM((step_dec, width), BF16), pltpu.VMEM((STEP_ROWS, H, 8, length), F32)],
        10 * flops, ("iiiwww", "iwi"),
    )
    waits = ()
    if near:
        cross_parts = pair_sum(cross_low, sent, (grad_qkv_a,))
        crossed = shift_plane(cross_parts[1:])
        waits = (cross_parts[0],)
    slot = shape_of((16, 16, 3 * width + LANES), BF16)
    grad_tokens, self_low, self_high, square_a = call(
        self_weights_kernel, steps, me, (branch_a, tokens2, input_a, grad_qkv_a),
        (dec_segments, gains, self_w, table, gain_b, gain_c), (),
        (shape_of((dec, width), BF16), square),
        (slot, slot),
        [
            pltpu.VMEM((width, 3 * width), F32),
            pltpu.VMEM((1, width), F32),
            pltpu.VMEM((width, LANES), F32),
        ],
        7 * flops, ("iiiiwwwwww", "iwwi"), waits,
    )
    feed_sum = way.feed_column(hold(feed_sum, self_low))

    def grams(pairs, *after):
        (tokens_part,) = call(
            gram_kernel, steps, None, pairs, (dec_segments,), (), (token_shape,), (), [],
            2 * flops, ("i" * len(pairs) + "w", "i"), after,
        )
        return tokens_part

    def fill_cross(*after):
        return grams((input_b, grad_query_b, attended_b, branch_b), *after)

    def fill_self(*after):
        return grams((input_a, grad_qkv_a, attended_a, branch_a), *after)

    def fill_memory(*after):
        return call(
            memory_backward_kernel, steps, None, (memory2, grad_kv_b), (mem_segments, cross_w), (),
            (shape_of((mem, width), BF16), shape_of((steps, 8, mem_length), F32)), (), [],
            10 * flops, ("iiww", "ii"), after,
        )

    if near:
        no_square = jnp.zeros((8, LANES), F32)
        sent = shift(hold(self_high, crossed), 2)
        cross_own, *rest = plane_sum([cross_parts[0], *crossed], (self_low,))
        crossed = shift_column(rest)
        token_b = fill_cross(cross_own)
        self_parts = pair_sum(self_low, sent, (token_b,))
        self_sent = shift_plane(self_parts[1:])
        line = (slot.shape[1], width)
        *cross_grads, square = small_call(
            column_end_kernel, (cross_own, *crossed, no_square, no_square),
            (self_parts[0],), [shape_of(line, F32)] * 5 + [shape_of((8, LANES), F32)],
        )
        grad_memory, token_m = fill_memory(self_parts[0], square)
        feed_sum = hold(feed_sum, token_m).reshape(slot.shape[1], 2 * ff)
        self_own, *rest = plane_sum([self_parts[0], *self_sent], (token_m,))
        self_sent = shift_column(rest)
        grad_hidden, grad_back, feed_square = small_call(
            feed_end_kernel, (feed_sum,), (self_own,),
            [shape_of((16, ff), F32), shape_of((64, width), F32), shape_of((8, LANES), F32)],
        )
        token_a = fill_self(self_own, feed_square)
        *self_grads, small, square = small_call(
            column_end_kernel, (self_own, *self_sent, square, feed_square), (token_a,),
            [shape_of(line, F32)] * 3 + [shape_of((16, LANES), F32), shape_of((32, LANES), F32)],
        )
        token_a = hold(token_a, square)
    else:
        token_b, token_a = fill_cross(), fill_self()
        grad_memory, token_m = fill_memory()
        cross_sum = in_order(jnp.concatenate([cross_low, cross_high])).astype(F32)
        self_sum = in_order(jnp.concatenate([self_low, self_high])).astype(F32)
        feed_sum = in_order(feed_sum).astype(F32)
        cross_grads = [cross_sum[:, k * width : (k + 1) * width] for k in range(5)]
        self_grads = [self_sum[:, k * width : (k + 1) * width] for k in range(3)]
        small = self_sum[:, 3 * width :]
        grad_hidden, grad_back = feed_sum[:, :ff], join_back(feed_sum[:, ff:])
        square = None
    grads = self_grads + cross_grads + [unfold_columns(grad_hidden), grad_back]
    grads += [small[:, k] for k in range(3)]
    grads.append(small[:, 3].reshape(-1, 16)[:, :H].reshape(-1))

    def by_example(tokens_part, segments):
        part = tokens_part[:, :STEP_ROWS].reshape(segments.shape)
        hits = segments[:, None, :] == lax.broadcasted_iota(jnp.int32, (1, NSEG, 1), 1)
        return jnp.sum(jnp.where(hits, part[:, None, :], 0.0), axis=-1)

    examples = by_example(token_a + token_b + token_c, dec_segments) + by_example(token_m, mem_segments)
    squares = (square_a + square_b + square_c)[:, :, 0].reshape(seqs, NSEG)
    examples = examples + squares + table_square[..., :NSEG, 0].reshape(seqs, NSEG)
    return (
        result.reshape(tokens.shape),
        grad_tokens.reshape(tokens.shape),
        grad_memory.reshape(memory.shape),
        grads,
        examples / COUNT,
        square,
    )


def solution(mesh):
    near = tuple(mesh.shape.values()) == (16, 2)
    if near:
        mesh = jax.sharding.Mesh(mesh.devices.reshape(4, 2, 2, 2), FINE)
    axes = tuple(mesh.axis_names)
    rows = P(axes)
    arrays, weights, vectors = (P(axes, None, None),) * 3, (P(axes, None),) * 10, (rows,) * 4
    placed = arrays + (P(axes, None),) * 3 + (P(),) + weights + vectors
    return jax.shard_map(
        partial(on_device, near),
        mesh=mesh,
        in_specs=placed,
        out_specs=arrays + weights + vectors + (P(axes, None), P()),
        check_vma=False,
    )
```

```python
import math
from functools import partial

import jax
import jax.numpy as jnp
from jax import lax
from jax.experimental import pallas as pl
from jax.experimental.pallas import tpu as pltpu
from jax.sharding import PartitionSpec as P

H = 8
DH = 64
NB = 32
NSEG = 4
COUNT = 4196096
EPSILON = 1e-06
FLOOR = -1e30
F32 = jnp.float32
BF16 = jnp.bfloat16
PAIRS = H // 2
LANES = 128
STEP_ROWS = 4
SMALL_ROWS = 2
VMEM_LIMIT = 60 * 2**20
SHARED_LIMIT = 48 * 2**20

COLUMN = (0, 8, 16, 24)
PLANE = (0, 1, 4, 5)
CODES = tuple(2 * c + mask + z for c in (0, 1) for mask in PLANE for z in COLUMN)


def nn(left, right):
    return lax.dot_general(left, right, (((1,), (0,)), ((), ())), preferred_element_type=F32)


def nt(left, right):
    return lax.dot_general(left, right, (((1,), (1,)), ((), ())), preferred_element_type=F32)


def tn(left, right):
    return lax.dot_general(left, right, (((0,), (0,)), ((), ())), preferred_element_type=F32)


def inverse_root(values):
    return lax.rsqrt(jnp.mean(values * values, axis=-1, keepdims=True) + EPSILON)


def head_masks(values):
    low = (lax.broadcasted_iota(jnp.int32, (1, LANES), 1) < DH).astype(BF16)
    return values * low, values * (1 - low)


def head_pair(values):
    return jnp.concatenate(head_masks(values), axis=0)


def fold_pair(both, queries):
    own = jnp.concatenate([both[:DH, :queries], both[DH:, queries:]], axis=0)
    return own.astype(BF16).T


def block_rows(block):
    return pl.ds(pl.multiple_of(block * 16, 16), 16)


def start_copies(pairs, sems):
    copies = [pltpu.make_async_copy(*pair, sems.at[i]) for i, pair in enumerate(pairs)]
    for copy in copies:
        copy.start()
    return copies


def read_rows(grad_w, block):
    return grad_w[block_rows(block), :].astype(BF16)


def store_slots(me_ref, low_ref, high_ref, read):
    for k, code in enumerate(CODES):
        target = low_ref if k < 16 else high_ref
        target[k % 16] = read(me_ref[0] ^ code)


def softmax_columns(scores):
    shifted = jnp.exp(scores - jnp.max(scores, axis=0, keepdims=True))
    return (shifted * (1.0 / jnp.sum(shifted, axis=0, keepdims=True))).astype(BF16)


def step_rows(ref, step, count):
    whole = ref[...].astype(F32)
    rows = whole[:count]
    for s in range(1, whole.shape[0] // count):
        rows = jnp.where(step == s, whole[s * count : (s + 1) * count], rows)
    return rows


def token_columns(lines):
    pad = 8 - lines.shape[0] % 8
    return jnp.concatenate([lines] + [lines[:1]] * (pad % 8), axis=0).T


def member_lines(lines):
    count, length = lines.shape
    codes = jnp.concatenate([lines[r : r + 1] + float(NSEG * r) for r in range(count)], axis=1)
    places = lax.broadcasted_iota(jnp.int32, (NSEG * count, count * length), 0).astype(F32)
    return (codes == places).astype(F32).astype(BF16)


def same_sum(products, lines, columns, r):
    same = columns[:, r : r + 1] == lines[r : r + 1]
    return jnp.sum(jnp.where(same, products, 0.0), axis=0, keepdims=True)


def each_row(row, count):
    for r in range(count):
        row(r, 0)


def gram(left):
    return nt(left, left)


def self_forward_kernel(me_ref, tokens_ref, dec_ref, padding_ref, buckets_ref, *refs):
    pieces, refs = refs[:8], refs[8:]
    input_ref, qkv_ref, prob_ref, attended_ref, weight_ref, gains_ref = refs[:6]
    bias_ref, small_ref, sems = refs[6:]
    length = dec_ref.shape[1]
    width = tokens_ref.shape[1]

    @pl.when(pl.program_id(0) == 0)
    def _():
        pairs = []
        for k, code in enumerate(CODES):
            rows = block_rows(me_ref[0] ^ code)
            source = pieces[k // 4].at[k % 4]
            pairs.append((source.at[:, : 3 * width], weight_ref.at[rows, :]))
            pairs.append((source.at[:, 3 * width :], small_ref.at[rows, :]))
        for copy in start_copies(pairs, sems):
            copy.wait()
        first = lax.broadcasted_iota(jnp.int32, (32, width), 1)
        pick = first == 16 * lax.broadcasted_iota(jnp.int32, (32, width), 0)
        small = nn(pick.astype(F32).astype(BF16), small_ref[...]).astype(BF16)
        lane = lax.broadcasted_iota(jnp.int32, (LANES, width), 0)
        feature = lax.broadcasted_iota(jnp.int32, (LANES, width), 1)
        block = lax.broadcasted_iota(jnp.int32, (32, width), 0)
        lines = []
        for k in range(4):
            spread = nn(small, (lane == 16 * k + feature % 16).astype(F32).astype(BF16))
            lines.append(
                jnp.sum(jnp.where(block == first // 16, spread, 0.0), axis=0, keepdims=True)
            )
        gains_ref[...] = jnp.concatenate(lines + lines, axis=0)
        place = lax.broadcasted_iota(jnp.int32, (H, width), 1) % 16
        head = lax.broadcasted_iota(jnp.int32, (H, width), 0)
        table = jnp.where(place == head, lines[3], 0.0).astype(BF16)
        bucket = lax.broadcasted_iota(jnp.int32, (width, length), 0) // 16
        curves = nn(table, (bucket == buckets_ref[...]).astype(F32).astype(BF16))
        for h in range(H):
            curve = jnp.broadcast_to(curves[h : h + 1, :], (length, length))
            lanes = slice((h % 2) * length, (h % 2 + 1) * length)
            bias_ref[h // 2, :, lanes] = pltpu.roll(curve, 0, 1, stride=1, stride_axis=0)

    values = tokens_ref[...].astype(F32)
    normed = (values * inverse_root(values) * gains_ref[0:1, :]).astype(BF16)
    input_ref[...] = normed
    for k in range(3):
        cols = slice(k * width, (k + 1) * width)
        qkv_ref[:, cols] = nn(normed, weight_ref[:, cols]).astype(BF16)

    step = pl.program_id(0)
    count = tokens_ref.shape[0] // length
    segments, real = step_rows(dec_ref, step, count), step_rows(padding_ref, step, count)
    segment_columns, real_columns = token_columns(segments), token_columns(real)
    key_i = lax.broadcasted_iota(jnp.int32, (length, length), 0)
    query_i = lax.broadcasted_iota(jnp.int32, (length, length), 1)

    def row(r, carry):
        rows = slice(r * length, (r + 1) * length)
        allowed = (segment_columns[:, r : r + 1] == segments[r : r + 1]) & (key_i <= query_i)
        allowed = allowed & ((real_columns[:, r : r + 1] > 0.0) | (key_i == query_i))
        mask = jnp.where(allowed, 0.0, FLOOR)
        mask = jnp.concatenate([mask, mask], axis=1)
        for p in range(PAIRS):
            query = qkv_ref[rows, p * LANES : (p + 1) * LANES]
            key = qkv_ref[rows, width + p * LANES : width + (p + 1) * LANES]
            value = qkv_ref[rows, 2 * width + p * LANES : 2 * width + (p + 1) * LANES]
            prob = softmax_columns(nt(key, head_pair(query)) + bias_ref[p] + mask)
            prob_ref[r, p] = prob
            attended_ref[rows, p * LANES : (p + 1) * LANES] = fold_pair(nn(value.T, prob), length)
        return carry

    each_row(row, count)


def memory_forward_kernel(me_ref, memory_ref, *refs):
    pieces, (kv_ref, weight_ref, sems) = refs[:-3], refs[-3:]
    width = memory_ref.shape[1]

    @pl.when(pl.program_id(0) == 0)
    def _():
        pairs = []
        for k, code in enumerate(CODES):
            source = pieces[k // 4].at[k % 4]
            pairs.append((source, weight_ref.at[block_rows(me_ref[0] ^ code), :]))
        for copy in start_copies(pairs, sems):
            copy.wait()

    for k in range(2):
        kv_ref[:, k * width : (k + 1) * width] = nn(
            memory_ref[...], weight_ref[:, (k + 2) * width : (k + 3) * width]
        ).astype(BF16)


def cross_forward_kernel(tokens_ref, attended_a_ref, kv_ref, dec_ref, mem_ref, gains_ref,
                         weight_ref, middle_ref, input_ref, query_ref, prob_ref, attended_ref, after_ref):
    mem_length, length = mem_ref.shape[1], dec_ref.shape[1]
    width = tokens_ref.shape[1]
    values = tokens_ref[...].astype(F32) + nn(attended_a_ref[...], weight_ref[:, :width])
    middle_ref[...] = values.astype(BF16)
    normed = (values * inverse_root(values) * gains_ref[1:2, :]).astype(BF16)
    input_ref[...] = normed
    query_ref[...] = nn(normed, weight_ref[:, width : 2 * width]).astype(BF16)

    step = pl.program_id(0)
    count = tokens_ref.shape[0] // length
    segments = step_rows(dec_ref, step, count)
    mem_columns = token_columns(step_rows(mem_ref, step, count))

    def row(r, carry):
        rows = slice(r * length, (r + 1) * length)
        mem_rows = slice(r * mem_length, (r + 1) * mem_length)
        mask = jnp.where(mem_columns[:, r : r + 1] == segments[r : r + 1], 0.0, FLOOR)
        for p in range(PAIRS):
            lanes = slice(p * LANES, (p + 1) * LANES)
            key = kv_ref[mem_rows, lanes]
            value = kv_ref[mem_rows, width + p * LANES : width + (p + 1) * LANES].T
            both = []
            for h, query in enumerate(head_masks(query_ref[rows, lanes])):
                prob = softmax_columns(nt(key, query) + mask)
                prob_ref[r, p, :, h * length : (h + 1) * length] = prob
                both.append(nn(value[h * DH : (h + 1) * DH], prob))
            attended_ref[rows, lanes] = jnp.concatenate(both, axis=0).astype(BF16).T

    each_row(row, count)
    after = values + nn(attended_ref[...], weight_ref[:, 4 * width :])
    after_ref[...] = after.astype(BF16)


def norm_back(values, gain, grad_normed):
    inverse = inverse_root(values)
    scaled = values * inverse
    upper = grad_normed * gain
    grad = inverse * (upper - scaled * jnp.mean(upper * scaled, axis=-1, keepdims=True))
    return grad, grad_normed * scaled


def gain_sums(terms, segments, total_ref, square_ref):
    sums = nn(member_lines(segments), terms.astype(BF16))
    total_ref[...] += jnp.sum(sums, axis=0, keepdims=True)
    square = jnp.sum(sums * sums, axis=1, keepdims=True)
    square_ref[...] = jnp.broadcast_to(square, square_ref.shape)


def feed_kernel(after_ref, cotangent_ref, dec_ref, padding_ref, gains_ref, in_ref, out_ref,
                result_ref, branch_b_ref, slots_ref, total_ref, square_ref, token_ref, normed_ref,
                branch_ref, active_ref, grad_ref, sum_ref, back_ref, gram_ref, in_slots,
                out_slots, sems):
    part = pl.program_id(0)
    count, length = dec_ref.shape
    dec, width = after_ref.shape
    tile = STEP_ROWS * length
    tiles = [slice(t * tile, (t + 1) * tile) for t in range(dec // tile)]

    @pl.when(part == 0)
    def _():
        real = token_columns(padding_ref[...].astype(F32))
        for r in range(count):
            rows = slice(r * length, (r + 1) * length)
            branch_ref[rows, :] = (
                cotangent_ref[rows, :].astype(F32) * real[:, r : r + 1]
            ).astype(BF16)
        for rows in tiles:
            values = after_ref[rows, :].astype(F32)
            normed_ref[rows, :] = (values * inverse_root(values) * gains_ref[2:3, :]).astype(BF16)
        sum_ref[...] = jnp.zeros_like(sum_ref)
        back_ref[...] = jnp.zeros_like(back_ref)
        gram_ref[...] = jnp.zeros_like(gram_ref)

    w_in = in_ref[...].reshape(width, width)
    w_out = out_ref[...].reshape(width, width)
    root = 0.7978845608028654
    for t, rows in enumerate(tiles):
        hidden = nn(normed_ref[rows, :], w_in)
        square = hidden * hidden
        bent = jnp.tanh(hidden * (root + (root * 0.044715) * square))
        half = 0.5 + 0.5 * bent
        slope = hidden * (2.0 * root + (6.0 * root * 0.044715) * square)
        slope = half + half * (slope * (1.0 - half))
        active_ref[rows, :] = (hidden * half).astype(BF16)
        grad_ref[rows, :] = (nt(branch_ref[rows, :], w_out) * slope).astype(BF16)
        sum_ref[rows, :] += nn(active_ref[rows, :], w_out)
        back_ref[rows, :] += nt(grad_ref[rows, :], w_in)
        for r in range(t * STEP_ROWS, (t + 1) * STEP_ROWS):
            own = slice(r * length, (r + 1) * length)
            gram_ref[0, r] += gram(active_ref[own, :])
            gram_ref[1, r] += gram(grad_ref[own, :])
    grad_in = tn(normed_ref[...], grad_ref[...]).astype(BF16)
    grad_out = tn(branch_ref[...], active_ref[...]).astype(BF16).T

    def sends(which):
        pairs = [(in_slots, slots_ref.at[:, pl.ds(pl.multiple_of(which * 16, 16), 16), :])]
        for i, k in enumerate(range(0, 32, 4)):
            pairs.append((out_slots.at[i], slots_ref.at[k + which, 64:, :]))
        return [pltpu.make_async_copy(*pair, sems.at[i]) for i, pair in enumerate(pairs)]

    @pl.when(part > 0)
    def _():
        for copy in sends(part - 1):
            copy.wait()

    for k, block in enumerate(CODES):
        in_slots[k] = grad_in[16 * block : 16 * block + 16]
    for i, k in enumerate(range(0, 32, 4)):
        block = CODES[k]
        out_slots[i] = grad_out[64 * block : 64 * block + 64]
    for copy in sends(part):
        copy.start()

    @pl.when(part == pl.num_programs(0) - 1)
    def _():
        segments = dec_ref[...].astype(F32)
        columns = token_columns(segments)
        total_ref[...] = jnp.zeros_like(total_ref)
        for t, rows in enumerate(tiles):
            values = after_ref[rows, :].astype(F32)
            result_ref[rows, :] = (values + sum_ref[rows, :]).astype(BF16)
            grad, terms = norm_back(values, gains_ref[2:3, :], back_ref[rows, :])
            branch_b_ref[rows, :] = (branch_ref[rows, :].astype(F32) + grad).astype(BF16)
            own = segments[t * STEP_ROWS : (t + 1) * STEP_ROWS]
            gain_sums(terms, own, total_ref, square_ref.at[t])
        for r in range(count):
            own = slice(r * length, (r + 1) * length)
            products = gram_ref[0, r] * gram(branch_ref[own, :])
            products = products + gram_ref[1, r] * gram(normed_ref[own, :])
            token_ref[r // STEP_ROWS, r % STEP_ROWS : r % STEP_ROWS + 1, :] = same_sum(
                products, segments, columns, r
            )
        for copy in sends(part):
            copy.wait()


def score_grads(prob, grad_prob):
    prob = prob.astype(F32)
    dots = jnp.sum(prob * grad_prob, axis=0, keepdims=True)
    return prob * (grad_prob - dots)


def cross_backward_kernel(me_ref, branch_ref, middle_ref, memory_ref, attended_a_ref, input_ref,
                          query_ref, kv_ref, prob_ref, attended_ref, dec_ref, gains_ref,
                          weight_ref, grad_query_ref, grad_kv_ref, branch_a_ref, low_ref, high_ref,
                          total_ref, square_ref, grad_w, grad_attended):
    step = pl.program_id(0)
    mem_length = prob_ref.shape[2]
    length = prob_ref.shape[3] // 2
    width = branch_ref.shape[1]

    @pl.when(step == 0)
    def _():
        grad_w[...] = jnp.zeros_like(grad_w)
        total_ref[...] = jnp.zeros_like(total_ref)

    branch = branch_ref[...]
    grad_attended[...] = nt(branch, weight_ref[:, 4 * width :]).astype(BF16)

    def row(r, carry):
        rows = slice(r * length, (r + 1) * length)
        mem_rows = slice(r * mem_length, (r + 1) * mem_length)
        for p in range(PAIRS):
            lanes = slice(p * LANES, (p + 1) * LANES)
            upper = slice(width + p * LANES, width + (p + 1) * LANES)
            value = kv_ref[mem_rows, upper]
            grad_outs = head_masks(grad_attended[rows, lanes])
            grad_scores = []
            for h, grad_out in enumerate(grad_outs):
                prob = prob_ref[r, p, :, h * length : (h + 1) * length]
                grad_scores.append(score_grads(prob, nt(value, grad_out)).astype(BF16))
            grad_score = jnp.concatenate(grad_scores, axis=1)
            query = head_pair(query_ref[rows, lanes])
            grad_kv_ref[mem_rows, lanes] = nn(grad_score, query).astype(BF16)
            grad_kv_ref[mem_rows, upper] = nn(
                prob_ref[r, p], jnp.concatenate(grad_outs, axis=0)
            ).astype(BF16)
            key = kv_ref[mem_rows, lanes].T
            grad_query_ref[rows, lanes] = fold_pair(nn(key, grad_score), length)

    each_row(row, STEP_ROWS)
    grad_query = grad_query_ref[...]
    grad_normed = nt(grad_query, weight_ref[:, width : 2 * width])
    grad, terms = norm_back(middle_ref[...].astype(F32), gains_ref[1:2, :], grad_normed)
    branch_a = (branch.astype(F32) + grad).astype(BF16)
    branch_a_ref[...] = branch_a
    gain_sums(terms, step_rows(dec_ref, step, STEP_ROWS), total_ref, square_ref.at[0])
    grad_w[:, :width] += tn(attended_a_ref[...], branch_a)
    grad_w[:, width : 2 * width] += tn(input_ref[...], grad_query)
    grad_w[:, 2 * width : 4 * width] += tn(memory_ref[...], grad_kv_ref[...])
    grad_w[:, 4 * width :] += tn(attended_ref[...], branch)

    @pl.when(step == pl.num_programs(0) - 1)
    def _():
        store_slots(me_ref, low_ref, high_ref, partial(read_rows, grad_w))


def self_scores_kernel(branch_ref, qkv_ref, prob_ref, dec_ref, buckets_ref, weight_ref,
                       grad_qkv_ref, table_ref, table_square_ref, grad_attended, bands):
    step = pl.program_id(0)
    length = prob_ref.shape[2]
    width = branch_ref.shape[1]
    grad_attended[...] = nt(branch_ref[...], weight_ref[:, :width]).astype(BF16)

    @pl.when(step == 0)
    def _():
        table_ref[...] = jnp.zeros_like(table_ref)
        bands[...] = jnp.zeros_like(bands)

    row_i = lax.broadcasted_iota(jnp.int32, (length, length), 0)
    col_i = lax.broadcasted_iota(jnp.int32, (length, length), 1)
    flip = (row_i + col_i == length - 1).astype(F32).astype(BF16)
    columns = token_columns(step_rows(dec_ref, step, STEP_ROWS)).astype(BF16)
    turned = nn(flip, columns)

    def row(r, carry):
        rows = slice(r * length, (r + 1) * length)
        member = [
            jnp.broadcast_to((turned[:, r : r + 1] == float(e)).astype(F32), (length, length))
            for e in range(NSEG)
        ]
        for p in range(PAIRS):
            lanes = slice(p * LANES, (p + 1) * LANES)
            middle = slice(width + p * LANES, width + (p + 1) * LANES)
            upper = slice(2 * width + p * LANES, 2 * width + (p + 1) * LANES)
            value = qkv_ref[rows, upper]
            query = head_pair(qkv_ref[rows, lanes])
            grad_out = head_pair(grad_attended[rows, lanes])
            prob = prob_ref[r, p]
            grad_score = score_grads(prob, nt(value, grad_out)).astype(BF16)
            grad_qkv_ref[rows, middle] = nn(grad_score, query).astype(BF16)
            grad_qkv_ref[rows, upper] = nn(prob, grad_out).astype(BF16)
            key = jnp.concatenate([qkv_ref[rows, middle].T, flip], axis=0)
            both = nn(key, grad_score)
            grad_qkv_ref[rows, lanes] = fold_pair(both[:length], length)
            for h in range(2):
                own = both[length:, h * length : (h + 1) * length]
                own = pltpu.roll(own, 1, 1, stride=1, stride_axis=0)
                for e in range(NSEG):
                    bands[r, 2 * p + h, e : e + 1, :] = jnp.sum(
                        own * member[e], axis=0, keepdims=True
                    )

    each_row(row, STEP_ROWS)
    bucket = lax.broadcasted_iota(jnp.int32, (LANES, length), 0)
    near = (bucket == buckets_ref[...]).astype(F32)
    flat = bands[...].reshape(STEP_ROWS * H * 8, length)
    per_bucket = lax.dot_general(
        flat, near, (((1,), (1,)), ((), ())), preferred_element_type=F32,
        precision=lax.Precision.HIGHEST,
    ).reshape(STEP_ROWS, H, 8, LANES)
    table_ref[...] += jnp.sum(jnp.sum(per_bucket, axis=0), axis=1)
    squares = jnp.sum(jnp.sum(per_bucket * per_bucket, axis=1), axis=-1, keepdims=True)
    table_square_ref[0] = jnp.broadcast_to(squares, (STEP_ROWS, 8, LANES))


def self_weights_kernel(me_ref, branch_ref, tokens_ref, input_ref, grad_qkv_ref, dec_ref,
                        gains_ref, weight_ref, table_ref, total_b_ref, total_c_ref,
                        grad_tokens_ref, low_ref, high_ref, square_ref, grad_w, total_ref,
                        small_ref):
    step = pl.program_id(0)
    width = tokens_ref.shape[1]
    grad_qkv = grad_qkv_ref[...]
    grad_normed = nt(grad_qkv, weight_ref[...])
    grad, terms = norm_back(tokens_ref[...].astype(F32), gains_ref[0:1, :], grad_normed)
    grad_tokens_ref[...] = (branch_ref[...].astype(F32) + grad).astype(BF16)

    @pl.when(step == 0)
    def _():
        grad_w[...] = jnp.zeros_like(grad_w)
        total_ref[...] = jnp.zeros_like(total_ref)

    gain_sums(terms, step_rows(dec_ref, step, STEP_ROWS), total_ref, square_ref.at[0])
    grad_w[...] += tn(input_ref[...], grad_qkv)

    @pl.when(step == pl.num_programs(0) - 1)
    def _():
        bucket = lax.broadcasted_iota(jnp.int32, (LANES, width), 0)
        place = lax.broadcasted_iota(jnp.int32, (LANES, width), 1)
        spread = nn(table_ref[...].astype(BF16), (place // 16 == bucket).astype(F32).astype(BF16))
        head = lax.broadcasted_iota(jnp.int32, (H, width), 0)
        lane = lax.broadcasted_iota(jnp.int32, (H, width), 1)
        table = jnp.sum(jnp.where(lane % 16 == head, spread, 0.0), axis=0, keepdims=True)
        small = jnp.zeros((LANES, width), F32)
        row_i = lax.broadcasted_iota(jnp.int32, (LANES, width), 0)
        for k, line in enumerate((total_ref[...], total_b_ref[...], total_c_ref[...], table)):
            small = jnp.where(row_i == k, line, small)
        small_ref[...] = small.T

        def read(block):
            return jnp.concatenate(
                [read_rows(grad_w, block), read_rows(small_ref, block)], axis=1
            )

        store_slots(me_ref, low_ref, high_ref, read)


def pair_sum_kernel(low_ref, sent_ref, *refs):
    outs, (low, sent, total, load_sems, store_sems) = refs[:4], refs[4:]
    places = [pl.ds(4 * t, 4) for t in range(4)]
    lows = start_copies([(low_ref.at[p], low.at[p]) for p in places], load_sems.at[0])
    sents = start_copies([(sent_ref.at[p], sent.at[p]) for p in places], load_sems.at[1])
    stores = []
    for t, p in enumerate(places):
        lows[t].wait()
        sents[t].wait()
        total[p] = (low[p].astype(F32) + sent[p].astype(F32)).astype(BF16)
        stores.append(pltpu.make_async_copy(total.at[p], outs[t], store_sems.at[t]))
        stores[t].start()
    for store in stores:
        store.wait()


def pair_sum(low, sent, after):
    piece = shape_of((4,) + low.shape[1:], BF16)
    return pl.pallas_call(
        ignoring(pair_sum_kernel, 2, len(after)),
        out_shape=(piece,) * 4,
        in_specs=[pl.BlockSpec(memory_space=pl.ANY)] * (2 + len(after)),
        out_specs=[pl.BlockSpec(memory_space=pl.ANY)] * 4,
        scratch_shapes=[pltpu.VMEM(low.shape, BF16)] * 3
        + [pltpu.SemaphoreType.DMA((2, 4)), pltpu.SemaphoreType.DMA((4,))],
        compiler_params=pltpu.CompilerParams(vmem_limit_bytes=SHARED_LIMIT),
    )(in_hbm(low), sent, *after)


def plane_sum_kernel(*refs):
    own_ref, outs = refs[8], refs[9:]
    start = 0
    for group in (refs[:4], refs[4:8]):
        cols = slice(start, start + group[0].shape[2])
        start = cols.stop
        for s in range(4):
            total = sum(ref[s].astype(F32) for ref in group)
            if s == 0:
                own_ref[:, cols] = total
            else:
                outs[s - 1][:, cols] = total.astype(BF16)


def plane_sum(groups, after):
    line = (16, sum(group[0].shape[2] for group in groups))
    return small_call(
        plane_sum_kernel, [*groups[0], *groups[1]], after,
        (shape_of(line, F32),) + (shape_of(line, BF16),) * 3,
    )


def square_sum(values):
    return jnp.sum(jnp.sum(values * values, axis=0, keepdims=True), axis=1, keepdims=True)


def feed_end_kernel(sum_ref, hidden_ref, back_ref, square_ref):
    total = sum_ref[...].astype(F32)
    width = total.shape[1]
    for j in range(4):
        hidden_ref[:, j * width : (j + 1) * width] = total[16 * j : 16 * (j + 1)]
    back_ref[...] = total[64:]
    square_ref[...] = jnp.broadcast_to(square_sum(total), square_ref.shape)


def column_end_kernel(own_ref, b_ref, c_ref, d_ref, *refs):
    squares, outs, square_ref = refs[:1], refs[1:-1], refs[-1]
    total = own_ref[...] + b_ref[...].astype(F32)
    total = total + c_ref[...].astype(F32) + d_ref[...].astype(F32)
    start = 0
    for out in outs:
        out[...] = total[:, start : start + out.shape[1]]
        start += out.shape[1]
    square = square_sum(total)
    for given in squares:
        square = square + given[0:1, 0:1]
    square_ref[...] = jnp.broadcast_to(square, square_ref.shape)


def staged(kernel, ins, outs):
    def run(*refs):
        count = ins + outs
        given, inner, sems = refs[:count], refs[count : 2 * count], refs[2 * count]
        for copy in start_copies(list(zip(given[:ins], inner[:ins])), sems):
            copy.wait()
        kernel(*inner)
        for copy in start_copies(list(zip(inner[ins:], given[ins:])), sems):
            copy.wait()

    return run


def small_call(kernel, ins, after, outs):
    arrays = [*ins, *outs]
    return pl.pallas_call(
        ignoring(staged(kernel, len(ins), len(outs)), len(ins), len(after)),
        out_shape=outs,
        in_specs=[pl.BlockSpec(memory_space=pl.ANY)] * (len(ins) + len(after)),
        out_specs=[pl.BlockSpec(memory_space=pl.ANY)] * len(outs),
        scratch_shapes=[pltpu.VMEM(array.shape, array.dtype) for array in arrays]
        + [pltpu.SemaphoreType.DMA((len(arrays),))],
        compiler_params=pltpu.CompilerParams(vmem_limit_bytes=SHARED_LIMIT),
    )(*ins, *after)


def pack_kernel(*refs):
    ins, (self_ref, cross_ref, feed_ref) = refs[:11], refs[11:]
    width = ins[0].shape[1]
    for k in range(3):
        self_ref[:, k * width : (k + 1) * width] = ins[k][...]
    self_ref[:, 3 * width :] = ins[10][...]
    for k in range(5):
        cross_ref[:, k * width : (k + 1) * width] = ins[3 + k][...]
    for j in range(ins[8].shape[1] // width):
        feed_ref[16 * j : 16 * (j + 1), :] = ins[8][:, j * width : (j + 1) * width]
    feed_ref[64:, :] = ins[9][...]


def pack(weights, small):
    width = weights[0].shape[1]
    outs = [shape_of((16, cols), BF16) for cols in (3 * width + LANES, 5 * width)]
    outs.append(shape_of((128, width), BF16))
    return small_call(pack_kernel, (*map(in_hbm, weights), small), (), outs)


def memory_backward_kernel(memory_ref, grad_kv_ref, mem_ref, weight_ref, grad_memory_ref,
                           token_ref):
    mem_length = mem_ref.shape[1]
    width = memory_ref.shape[1]
    weight = weight_ref[:, 2 * width : 4 * width]
    grad_memory_ref[...] = nt(grad_kv_ref[...], weight).astype(BF16)
    count = memory_ref.shape[0] // mem_length
    segments = step_rows(mem_ref, pl.program_id(0), count)
    columns = token_columns(segments)
    for r in range(count):
        rows = slice(r * mem_length, (r + 1) * mem_length)
        products = gram(memory_ref[rows, :]) * gram(grad_kv_ref[rows, :])
        token_ref[0, r : r + 1, :] = same_sum(products, segments, columns, r)


def gram_kernel(*refs):
    pairs, dec_ref, token_ref = refs[:-2], refs[-2], refs[-1]
    length = dec_ref.shape[1]
    count = pairs[0].shape[0] // length
    segments = step_rows(dec_ref, pl.program_id(0), count)
    columns = token_columns(segments)
    for r in range(count):
        rows = slice(r * length, (r + 1) * length)
        products = sum(
            gram(left[rows, :]) * gram(right[rows, :])
            for left, right in zip(pairs[::2], pairs[1::2])
        )
        token_ref[0, r : r + 1, :] = same_sum(products, segments, columns, r)


def rows_spec(array, steps):
    shape = (array.shape[0] // steps,) + array.shape[1:]
    return pl.BlockSpec(shape, lambda i, *_: (i,) + (0,) * (len(shape) - 1))


class Cut:
    def __init__(self, array, shape, index):
        self.array, self.spec = array, pl.BlockSpec(shape, index)


def whole_spec(array):
    return pl.BlockSpec(array.shape, lambda i, *_: (0,) * len(array.shape))


def in_hbm(array):
    return pltpu.with_memory_space_constraint(array, pltpu.HBM)


def ignoring(kernel, first, count):
    return lambda *refs: kernel(*refs[:first], *refs[first + count :])


def call(kernel, steps, me, blocked, whole, pieces, outs_blocked, outs_whole, scratch, flops,
         order, after=(), limit=VMEM_LIMIT):
    ins, in_specs = [], []
    blocked, whole = list(blocked), list(whole)
    for kind in order[0]:
        array = (blocked if kind == "i" else whole).pop(0)
        if isinstance(array, Cut):
            ins.append(array.array)
            in_specs.append(array.spec)
            continue
        ins.append(array)
        in_specs.append(rows_spec(array, steps) if kind == "i" else whole_spec(array))
    ins = [in_hbm(array) for array in ins]
    kernel = ignoring(kernel, len(ins) + len(pieces) + (me is not None), len(after))
    ins += [*pieces, *after]
    in_specs += [pl.BlockSpec(memory_space=pl.ANY)] * (len(pieces) + len(after))
    outs, out_specs = [], []
    outs_blocked, outs_whole = list(outs_blocked), list(outs_whole)
    for kind in order[1]:
        out = (outs_blocked if kind == "i" else outs_whole).pop(0)
        outs.append(out)
        if kind == "a":
            out_specs.append(pl.BlockSpec(memory_space=pl.ANY))
        else:
            out_specs.append(rows_spec(out, steps) if kind == "i" else whole_spec(out))
    moved = sum(math.prod(a.shape) * a.dtype.itemsize for a in ins + outs)
    prefetch = 0 if me is None else 1
    return pl.pallas_call(
        kernel,
        out_shape=outs,
        grid_spec=pltpu.PrefetchScalarGridSpec(
            num_scalar_prefetch=prefetch,
            grid=(steps,),
            in_specs=in_specs,
            out_specs=out_specs,
            scratch_shapes=scratch,
        ),
        compiler_params=pltpu.CompilerParams(
            dimension_semantics=("arbitrary",), vmem_limit_bytes=limit
        ),
        cost_estimate=pl.CostEstimate(flops=flops, bytes_accessed=moved, transcendentals=0),
    )(*(() if me is None else (me,)), *ins)


FINE = ("z", "y", "core", "x")


def shape_of(shape, dtype):
    return jax.ShapeDtypeStruct(shape, dtype)


def kept(shape, dtype):
    return pltpu.HBM(shape, dtype)


def shift(array, mask):
    return lax.ppermute(array, FINE, [(i, i ^ mask) for i in range(32)])


def hold(array, after):
    return lax.optimization_barrier((array, after))[0]


def pack_feed(hidden, back):
    width = back.shape[1]
    hidden = hidden.reshape(-1, 16, 4, width).transpose(0, 2, 1, 3).reshape(-1, 64, width)
    return jnp.concatenate([hidden, back.reshape(-1, 64, width)], axis=1)


def unpack_feed(blocks):
    width = blocks.shape[2]
    hidden = blocks[:, :64].reshape(-1, 4, 16, width).transpose(0, 2, 1, 3)
    return hidden.reshape(-1, 4 * width), blocks[:, 64:].reshape(-1, width)


def small_row(gains, table):
    table = jnp.pad(table.reshape(-1, H), ((0, 0), (0, 16 - H)))
    row = jnp.concatenate([gain.reshape(-1, 16) for gain in gains] + [table], axis=1)
    row = jnp.pad(row, ((0, 0), (0, LANES - row.shape[1])))
    return jnp.pad(row[:, None], ((0, 0), (0, 15), (0, 0))).reshape(-1, LANES)


def in_order(slots):
    return slots[jnp.array([CODES.index(block) for block in range(32)])]


def as_rows(slots):
    return in_order(slots).reshape(-1, slots.shape[2]).astype(F32)


def shift_plane(pieces):
    return [shift(piece, mask) for piece, mask in zip(pieces, PLANE[1:])]


def shift_column(pieces):
    return [shift(piece, code) for piece, code in zip(pieces, COLUMN[1:])]


class Near:
    axes = FINE

    def __init__(self, weights):
        self.me = lax.axis_index(FINE)
        small = small_row(weights[10:13], weights[13])
        own, self.cross_shard, feed = pack(weights[:10], small)
        self.feed = lax.all_gather(feed, FINE, axis=0)
        column = jnp.stack([own, *shift_column([own] * 3)])
        line = hold(self.cross_shard, column)
        line = jnp.stack([line, *shift_column([line] * 3)])
        plane = [column, *shift_plane([column] * 3)]
        line = hold(line, plane[3])
        self.plane = [line, *shift_plane([line] * 3)]
        self.own = plane + [shift(piece, 2) for piece in plane]

    def cross(self, after):
        plane = [hold(piece, after) for piece in self.plane]
        return plane + [shift(piece, 2) for piece in plane]

    def feed_core(self, slots):
        return lax.psum_scatter(slots.reshape((2, 4, 4) + slots.shape[1:]), "core")

    def feed_plane(self, slots):
        return lax.psum_scatter(slots, ("y", "x"))

    def feed_column(self, slots):
        return lax.psum_scatter(slots, "z")


class Far:
    axes = ("wide", "narrow")
    me = 0

    def __init__(self, weights):
        weights = [lax.all_gather(w, self.axes, axis=0, tiled=True) for w in weights]
        self.take(weights)

    def take(self, weights):
        self.own = self.pieces(*weights[:3], small_row(weights[10:13], weights[13]))
        self.rest = self.pieces(*weights[3:8])
        self.feed = pack_feed(weights[8], weights[9])

    def pieces(self, *parts):
        blocks = jnp.concatenate(parts, axis=1).reshape(32, 16, -1)[jnp.array(CODES)]
        return [blocks[4 * t : 4 * t + 4] for t in range(8)]

    def cross(self, after):
        return self.rest

    def feed_core(self, slots):
        return slots

    feed_plane = feed_column = feed_core


def on_device(near, tokens, memory, cotangent, dec_segments, mem_segments, padding, buckets,
              *weights):
    way = (Near if near else Far)(weights)
    result, grad_tokens, grad_memory, grads, examples, square = local_part(
        way, tokens, memory, cotangent, dec_segments, mem_segments, padding, buckets
    )
    if near:
        sent = lax.all_to_all(square, FINE, 0, 0, tiled=True)
        global_norm = jnp.sum(sent[:, 0])
    else:
        grads = [lax.psum_scatter(g, way.axes, scatter_dimension=0, tiled=True) for g in grads]
        global_norm = lax.psum(sum(jnp.sum(g * g) for g in grads), way.axes)
    return (result, grad_tokens, grad_memory, *grads, examples, global_norm / COUNT)


def local_part(way, tokens, memory, cotangent, dec_segments, mem_segments, padding, buckets):
    seqs, length, width = tokens.shape
    mem_length = memory.shape[1]
    steps = seqs // STEP_ROWS
    small_steps = seqs // SMALL_ROWS
    dec, mem = seqs * length, seqs * mem_length
    step_dec = STEP_ROWS * length
    ff = 4 * width

    buckets = buckets[None]
    tokens2, memory2, cotangent2 = (
        array.reshape(-1, width) for array in (tokens, memory, cotangent)
    )
    dma = pltpu.SemaphoreType.DMA

    me = jnp.full((1,), way.me, jnp.int32)
    flops = 2 * dec * width * width

    input_a, qkv_a, prob_a, attended_a, self_w, gains = call(
        self_forward_kernel, small_steps, me, (tokens2,), (dec_segments, padding, buckets), way.own,
        (
            kept((dec, width), BF16),
            kept((dec, 3 * width), BF16),
            kept((seqs, PAIRS, length, 2 * length), BF16),
            kept((dec, width), BF16),
        ),
        (kept((width, 3 * width), BF16), kept((8, width), F32)),
        [pltpu.VMEM((PAIRS, length, 2 * length), F32), pltpu.VMEM((width, LANES), BF16), dma((64,))],
        6 * flops, ("iwww", "iiiiww"), (), SHARED_LIMIT,
    )
    kv_b, cross_w = call(
        memory_forward_kernel, small_steps, me, (memory2,), (), way.cross(attended_a),
        (kept((mem, 2 * width), BF16),), (kept((width, 5 * width), BF16),), [dma((32,))],
        4 * flops, ("i", "iw"), (), SHARED_LIMIT,
    )
    middle, input_b, query_b, prob_b, attended_b, after_cross = call(
        cross_forward_kernel, small_steps, None, (tokens2, attended_a, kv_b),
        (dec_segments, mem_segments, gains, cross_w), (),
        (
            kept((dec, width), BF16),
            kept((dec, width), BF16),
            kept((dec, width), BF16),
            kept((seqs, PAIRS, mem_length, 2 * length), BF16),
            kept((dec, width), BF16),
            kept((dec, width), BF16),
        ),
        (), [], 6 * flops, ("iiiwwww", "iiiiii"),
    )
    total, square = kept((1, width), F32), shape_of((steps, 4 * STEP_ROWS, LANES), F32)
    token_shape = shape_of((steps, 8, length), F32)
    small_token = shape_of((small_steps, 8, length), F32)
    in_part = Cut(way.feed, (32, 16, width), lambda i, *_: (0, i, 0))
    out_part = Cut(way.feed, (8, 64, width), lambda i, *_: (i, 1, 0))
    result, branch_b, feed_slots, gain_c, square_c, token_c = call(
        feed_kernel, ff // width, None, (),
        (after_cross, cotangent2, dec_segments, padding, gains, in_part,
         out_part),
        (), (),
        (
            shape_of((dec, width), BF16),
            kept((dec, width), BF16),
            shape_of((32, 128, width), BF16),
            total,
            square,
            token_shape,
        ),
        [
            *[pltpu.VMEM((dec, width), BF16)] * 4,
            *[pltpu.VMEM((dec, width), F32)] * 2,
            pltpu.VMEM((2, seqs, length, length), F32),
            pltpu.VMEM((32, 16, width), BF16),
            pltpu.VMEM((8, 64, width), BF16),
            dma((9,)),
        ],
        26 * flops, ("wwwwwww", "wwawww"),
    )
    feed_sum = way.feed_core(feed_slots)
    slot = shape_of((16, 16, 5 * width), BF16)
    grad_query_b, grad_kv_b, branch_a, cross_low, cross_high, gain_b, square_b = call(
        cross_backward_kernel, steps, me,
        (branch_b, middle, memory2, attended_a, input_b, query_b, kv_b, prob_b, attended_b),
        (dec_segments, gains, cross_w), (),
        (
            kept((dec, width), BF16),
            kept((mem, 2 * width), BF16),
            kept((dec, width), BF16),
            square,
        ),
        (kept(slot.shape, BF16), slot, total),
        [pltpu.VMEM((width, 5 * width), F32), pltpu.VMEM((step_dec, width), BF16)],
        20 * flops, ("iiiiiiiiiwww", "iiiwwwi"),
    )
    feed_sum = way.feed_plane(hold(feed_sum, grad_query_b))
    near = isinstance(way, Near)
    if near:
        sent = shift(cross_high, 2)
    grad_qkv_a, table, table_square = call(
        self_scores_kernel, steps, None, (branch_a, qkv_a, prob_a),
        (dec_segments, buckets, cross_w), (),
        (kept((dec, 3 * width), BF16), shape_of((steps, STEP_ROWS, 8, LANES), F32)),
        (kept((H, LANES), F32),),
        [pltpu.VMEM((step_dec, width), BF16), pltpu.VMEM((STEP_ROWS, H, 8, length), F32)],
        10 * flops, ("iiiwww", "iwi"),
    )
    waits = ()
    if near:
        cross_parts = pair_sum(cross_low, sent, (grad_qkv_a,))
        crossed = shift_plane(cross_parts[1:])
        waits = (cross_parts[0],)
    slot = shape_of((16, 16, 3 * width + LANES), BF16)
    grad_tokens, self_low, self_high, square_a = call(
        self_weights_kernel, steps, me, (branch_a, tokens2, input_a, grad_qkv_a),
        (dec_segments, gains, self_w, table, gain_b, gain_c), (),
        (shape_of((dec, width), BF16), square),
        (kept(slot.shape, BF16), slot),
        [
            pltpu.VMEM((width, 3 * width), F32),
            pltpu.VMEM((1, width), F32),
            pltpu.VMEM((width, LANES), F32),
        ],
        7 * flops, ("iiiiwwwwww", "iwwi"), waits,
    )

    def grams(pairs, *after):
        (tokens_part,) = call(
            gram_kernel, small_steps, None, pairs, (dec_segments,), (), (small_token,), (), [],
            2 * flops, ("i" * len(pairs) + "w", "i"), after, SHARED_LIMIT,
        )
        return tokens_part

    def fill_cross(*after):
        return grams((input_b, grad_query_b, attended_b, branch_b), *after)

    def fill_self(*after):
        return grams((input_a, grad_qkv_a, attended_a, branch_a), *after)

    def fill_memory(*after):
        return call(
            memory_backward_kernel, small_steps, None, (memory2, grad_kv_b),
            (mem_segments, cross_w), (),
            (shape_of((mem, width), BF16), shape_of((small_steps, 8, mem_length), F32)), (), [],
            10 * flops, ("iiww", "ii"), after, SHARED_LIMIT,
        )

    if near:
        sent = shift(hold(self_high, crossed[0]), 2)
        token_b = fill_cross(self_low)
        self_parts = pair_sum(self_low, sent, (token_b,))
        self_sent = shift_plane(self_parts[1:])
        feed_sum = hold(feed_sum, token_b)
        token_a = fill_self(self_parts[0], feed_sum)
        feed_sum = way.feed_column(feed_sum)
        groups = [[self_parts[0], *self_sent], [cross_parts[0], *crossed]]
        own, *rest = plane_sum(groups, (token_a,))
        line_sent = shift_column(rest)
        grad_memory, token_m = fill_memory(own)
        feed_sum = hold(feed_sum, token_m).reshape(128, width)
        grad_hidden, grad_back, square = small_call(
            feed_end_kernel, (feed_sum,), (token_m,),
            [shape_of((16, ff), F32), shape_of((64, width), F32), shape_of((8, LANES), F32)],
        )
        line = shape_of((slot.shape[1], width), F32)
        *parts, square = small_call(
            column_end_kernel, (own, *line_sent, square), (token_m,),
            [line] * 3 + [shape_of((16, LANES), F32)] + [line] * 5 + [shape_of((32, LANES), F32)],
        )
        self_grads, small, cross_grads = parts[:3], parts[3], parts[4:]
        token_m = hold(token_m, square)
    else:
        token_b, token_a = fill_cross(), fill_self()
        grad_memory, token_m = fill_memory()
        cross_sum = as_rows(jnp.concatenate([cross_low, cross_high]))
        self_sum = as_rows(jnp.concatenate([self_low, self_high]))
        cross_grads = [cross_sum[:, k * width : (k + 1) * width] for k in range(5)]
        self_grads = [self_sum[:, k * width : (k + 1) * width] for k in range(3)]
        small = self_sum[:, 3 * width :]
        grad_hidden, grad_back = unpack_feed(in_order(feed_sum).astype(F32))
        square = None
    grads = self_grads + cross_grads + [grad_hidden, grad_back]
    grads += [small[:, k] for k in range(3)]
    grads.append(small[:, 3].reshape(-1, 16)[:, :H].reshape(-1))

    def row_parts(parts, count):
        return parts[:, :count].reshape(seqs, -1)

    def by_example(part, segments):
        hits = segments[:, None, :] == lax.broadcasted_iota(jnp.int32, (1, NSEG, 1), 1)
        return jnp.sum(jnp.where(hits, part[:, None, :], 0.0), axis=-1)

    token_d = row_parts(token_a + token_b, SMALL_ROWS) + row_parts(token_c, STEP_ROWS)
    examples = by_example(token_d, dec_segments)
    examples = examples + by_example(row_parts(token_m, SMALL_ROWS), mem_segments)
    squares = (square_a + square_b + square_c)[:, :, 0].reshape(seqs, NSEG)
    examples = examples + squares + table_square[..., :NSEG, 0].reshape(seqs, NSEG)
    return (
        result.reshape(tokens.shape),
        grad_tokens.reshape(tokens.shape),
        grad_memory.reshape(memory.shape),
        grads,
        examples / COUNT,
        square,
    )


def solution(mesh):
    near = tuple(mesh.shape.values()) == (16, 2)
    if near:
        mesh = jax.sharding.Mesh(mesh.devices.reshape(4, 2, 2, 2), FINE)
    axes = tuple(mesh.axis_names)
    rows = P(axes)
    arrays, weights, vectors = (P(axes, None, None),) * 3, (P(axes, None),) * 10, (rows,) * 4
    placed = arrays + (P(axes, None),) * 3 + (P(),) + weights + vectors
    return jax.shard_map(
        partial(on_device, near),
        mesh=mesh,
        in_specs=placed,
        out_specs=arrays + weights + vectors + (P(axes, None), P()),
        check_vma=False,
    )
```

```python
import math
from functools import partial

import jax
import jax.numpy as jnp
from jax import lax
from jax.experimental import pallas as pl
from jax.experimental.pallas import tpu as pltpu
from jax.sharding import PartitionSpec as P

H = 8
DH = 64
NB = 32
NSEG = 4
COUNT = 4196096
EPSILON = 1e-06
FLOOR = -1e30
F32 = jnp.float32
BF16 = jnp.bfloat16
PAIRS = H // 2
LANES = 128
STEP_ROWS = 4
SMALL_ROWS = 4
VMEM_LIMIT = 60 * 2**20
SHARED_LIMIT = 48 * 2**20

COLUMN = (0, 8, 16, 24)
PLANE = (0, 1, 4, 5)
CODES = tuple(2 * c + mask + z for c in (0, 1) for mask in PLANE for z in COLUMN)


def nn(left, right):
    return lax.dot_general(left, right, (((1,), (0,)), ((), ())), preferred_element_type=F32)


def nt(left, right):
    return lax.dot_general(left, right, (((1,), (1,)), ((), ())), preferred_element_type=F32)


def tn(left, right):
    return lax.dot_general(left, right, (((0,), (0,)), ((), ())), preferred_element_type=F32)


def inverse_root(values):
    return lax.rsqrt(jnp.mean(values * values, axis=-1, keepdims=True) + EPSILON)


def head_masks(values):
    low = (lax.broadcasted_iota(jnp.int32, (1, LANES), 1) < DH).astype(BF16)
    return values * low, values * (1 - low)


def head_pair(values):
    return jnp.concatenate(head_masks(values), axis=0)


def fold_pair(both, queries):
    own = jnp.concatenate([both[:DH, :queries], both[DH:, queries:]], axis=0)
    return own.astype(BF16).T


def block_rows(block):
    return pl.ds(pl.multiple_of(block * 16, 16), 16)


def start_copies(pairs, sems):
    copies = [pltpu.make_async_copy(*pair, sems.at[i]) for i, pair in enumerate(pairs)]
    for copy in copies:
        copy.start()
    return copies


def read_rows(grad_w, block):
    return grad_w[block_rows(block), :].astype(BF16)


def store_slots(me_ref, low_ref, high_ref, read):
    for k, code in enumerate(CODES):
        target = low_ref if k < 16 else high_ref
        target[k % 16] = read(me_ref[0] ^ code)


def softmax_columns(scores):
    shifted = jnp.exp(scores - jnp.max(scores, axis=0, keepdims=True))
    return (shifted * (1.0 / jnp.sum(shifted, axis=0, keepdims=True))).astype(BF16)


def step_rows(ref, step, count):
    whole = ref[...].astype(F32)
    rows = whole[:count]
    for s in range(1, whole.shape[0] // count):
        rows = jnp.where(step == s, whole[s * count : (s + 1) * count], rows)
    return rows


def token_columns(lines):
    pad = 8 - lines.shape[0] % 8
    return jnp.concatenate([lines] + [lines[:1]] * (pad % 8), axis=0).T


def member_lines(lines):
    count, length = lines.shape
    codes = jnp.concatenate([lines[r : r + 1] + float(NSEG * r) for r in range(count)], axis=1)
    places = lax.broadcasted_iota(jnp.int32, (NSEG * count, count * length), 0).astype(F32)
    return (codes == places).astype(F32).astype(BF16)


def same_sum(products, lines, columns, r):
    same = columns[:, r : r + 1] == lines[r : r + 1]
    return jnp.sum(jnp.where(same, products, 0.0), axis=0, keepdims=True)


def pipelined(items, *stages):
    state = {}
    for tick in range(len(items) + len(stages) - 1):
        for depth, stage in enumerate(stages):
            n = tick - depth
            if 0 <= n < len(items):
                state[n] = stage(items[n], state.get(n))


def row_pairs(count):
    return [(r, p) for r in range(count) for p in range(PAIRS)]


def gram(left):
    return nt(left, left)


def self_forward_kernel(me_ref, tokens_ref, dec_ref, padding_ref, buckets_ref, *refs):
    pieces, refs = refs[:8], refs[8:]
    input_ref, qkv_ref, prob_ref, attended_ref, weight_ref, gains_ref = refs[:6]
    bias_ref, small_ref, sems = refs[6:]
    length = dec_ref.shape[1]
    width = tokens_ref.shape[1]

    @pl.when(pl.program_id(0) == 0)
    def _():
        pairs = []
        for k, code in enumerate(CODES):
            rows = block_rows(me_ref[0] ^ code)
            source = pieces[k // 4].at[k % 4]
            pairs.append((source.at[:, : 3 * width], weight_ref.at[rows, :]))
            pairs.append((source.at[:, 3 * width :], small_ref.at[rows, :]))
        for copy in start_copies(pairs, sems):
            copy.wait()
        first = lax.broadcasted_iota(jnp.int32, (32, width), 1)
        pick = first == 16 * lax.broadcasted_iota(jnp.int32, (32, width), 0)
        small = nn(pick.astype(F32).astype(BF16), small_ref[...]).astype(BF16)
        lane = lax.broadcasted_iota(jnp.int32, (LANES, width), 0)
        feature = lax.broadcasted_iota(jnp.int32, (LANES, width), 1)
        block = lax.broadcasted_iota(jnp.int32, (32, width), 0)
        lines = []
        for k in range(4):
            spread = nn(small, (lane == 16 * k + feature % 16).astype(F32).astype(BF16))
            lines.append(
                jnp.sum(jnp.where(block == first // 16, spread, 0.0), axis=0, keepdims=True)
            )
        gains_ref[...] = jnp.concatenate(lines + lines, axis=0)
        place = lax.broadcasted_iota(jnp.int32, (H, width), 1) % 16
        head = lax.broadcasted_iota(jnp.int32, (H, width), 0)
        table = jnp.where(place == head, lines[3], 0.0).astype(BF16)
        bucket = lax.broadcasted_iota(jnp.int32, (width, length), 0) // 16
        curves = nn(table, (bucket == buckets_ref[...]).astype(F32).astype(BF16))
        for h in range(H):
            curve = jnp.broadcast_to(curves[h : h + 1, :], (length, length))
            lanes = slice((h % 2) * length, (h % 2 + 1) * length)
            bias_ref[h // 2, :, lanes] = pltpu.roll(curve, 0, 1, stride=1, stride_axis=0)

    values = tokens_ref[...].astype(F32)
    normed = (values * inverse_root(values) * gains_ref[0:1, :]).astype(BF16)
    input_ref[...] = normed
    for k in range(3):
        cols = slice(k * width, (k + 1) * width)
        qkv_ref[:, cols] = nn(normed, weight_ref[:, cols]).astype(BF16)

    step = pl.program_id(0)
    count = tokens_ref.shape[0] // length
    segments, real = step_rows(dec_ref, step, count), step_rows(padding_ref, step, count)
    segment_columns, real_columns = token_columns(segments), token_columns(real)
    key_i = lax.broadcasted_iota(jnp.int32, (length, length), 0)
    query_i = lax.broadcasted_iota(jnp.int32, (length, length), 1)

    masks = []
    for r in range(count):
        allowed = (segment_columns[:, r : r + 1] == segments[r : r + 1]) & (key_i <= query_i)
        allowed = allowed & ((real_columns[:, r : r + 1] > 0.0) | (key_i == query_i))
        mask = jnp.where(allowed, 0.0, FLOOR)
        masks.append(jnp.concatenate([mask, mask], axis=1))

    def part(item, k):
        r, p = item
        return qkv_ref[r * length : (r + 1) * length, k * width + p * LANES : k * width + (p + 1) * LANES]

    def scores(item, _):
        return nt(part(item, 1), head_pair(part(item, 0)))

    def weigh(item, score):
        r, p = item
        prob = softmax_columns(score + bias_ref[p] + masks[r])
        prob_ref[r, p] = prob
        return prob, part(item, 2).T

    def mix(item, given):
        r, p = item
        prob, value = given
        rows, lanes = slice(r * length, (r + 1) * length), slice(p * LANES, (p + 1) * LANES)
        attended_ref[rows, lanes] = fold_pair(nn(value, prob), length)

    pipelined(row_pairs(count), scores, weigh, mix)


def memory_forward_kernel(me_ref, memory_ref, *refs):
    pieces, (kv_ref, weight_ref, sems) = refs[:-3], refs[-3:]
    width = memory_ref.shape[1]

    @pl.when(pl.program_id(0) == 0)
    def _():
        pairs = []
        for k, code in enumerate(CODES):
            source = pieces[k // 4].at[k % 4]
            pairs.append((source, weight_ref.at[block_rows(me_ref[0] ^ code), :]))
        for copy in start_copies(pairs, sems):
            copy.wait()

    for k in range(2):
        kv_ref[:, k * width : (k + 1) * width] = nn(
            memory_ref[...], weight_ref[:, (k + 2) * width : (k + 3) * width]
        ).astype(BF16)


def cross_forward_kernel(tokens_ref, attended_a_ref, kv_ref, dec_ref, mem_ref, gains_ref,
                         weight_ref, middle_ref, input_ref, query_ref, prob_ref, attended_ref, after_ref):
    mem_length, length = mem_ref.shape[1], dec_ref.shape[1]
    width = tokens_ref.shape[1]
    values = tokens_ref[...].astype(F32) + nn(attended_a_ref[...], weight_ref[:, :width])
    middle_ref[...] = values.astype(BF16)
    normed = (values * inverse_root(values) * gains_ref[1:2, :]).astype(BF16)
    input_ref[...] = normed
    query_ref[...] = nn(normed, weight_ref[:, width : 2 * width]).astype(BF16)

    step = pl.program_id(0)
    count = tokens_ref.shape[0] // length
    segments = step_rows(dec_ref, step, count)
    mem_columns = token_columns(step_rows(mem_ref, step, count))

    masks = []
    for r in range(count):
        mask = jnp.where(mem_columns[:, r : r + 1] == segments[r : r + 1], 0.0, FLOOR)
        masks.append(jnp.concatenate([mask, mask], axis=1))

    def places(item):
        r, p = item
        rows, lanes = slice(r * length, (r + 1) * length), slice(p * LANES, (p + 1) * LANES)
        upper = slice(width + p * LANES, width + (p + 1) * LANES)
        return rows, slice(r * mem_length, (r + 1) * mem_length), lanes, upper

    def scores(item, _):
        rows, mem_rows, lanes, _ = places(item)
        return nt(kv_ref[mem_rows, lanes], head_pair(query_ref[rows, lanes]))

    def weigh(item, score):
        r, p = item
        _, mem_rows, _, upper = places(item)
        prob = softmax_columns(score + masks[r])
        prob_ref[r, p] = prob
        return prob, kv_ref[mem_rows, upper].T

    def mix(item, given):
        rows, _, lanes, _ = places(item)
        prob, value = given
        attended_ref[rows, lanes] = fold_pair(nn(value, prob), length)

    pipelined(row_pairs(count), scores, weigh, mix)
    after = values + nn(attended_ref[...], weight_ref[:, 4 * width :])
    after_ref[...] = after.astype(BF16)


def norm_back(values, gain, grad_normed):
    inverse = inverse_root(values)
    scaled = values * inverse
    upper = grad_normed * gain
    grad = inverse * (upper - scaled * jnp.mean(upper * scaled, axis=-1, keepdims=True))
    return grad, grad_normed * scaled


def gain_sums(terms, segments, total_ref, square_ref):
    sums = nn(member_lines(segments), terms.astype(BF16))
    total_ref[...] += jnp.sum(sums, axis=0, keepdims=True)
    square = jnp.sum(sums * sums, axis=1, keepdims=True)
    square_ref[...] = jnp.broadcast_to(square, square_ref.shape)


def feed_kernel(after_ref, cotangent_ref, dec_ref, padding_ref, gains_ref, in_ref, out_ref,
                result_ref, branch_b_ref, slots_ref, total_ref, square_ref, token_ref, normed_ref,
                branch_ref, normed_flip, branch_flip, active_ref, grad_ref, sum_ref, back_ref, gram_ref, in_slots,
                out_slots, sems):
    part = pl.program_id(0)
    count, length = dec_ref.shape
    dec, width = after_ref.shape
    tile = STEP_ROWS * length
    tiles = [slice(t * tile, (t + 1) * tile) for t in range(dec // tile)]

    @pl.when(part == 0)
    def _():
        real = token_columns(padding_ref[...].astype(F32))
        for r in range(count):
            rows = slice(r * length, (r + 1) * length)
            branch_ref[rows, :] = (
                cotangent_ref[rows, :].astype(F32) * real[:, r : r + 1]
            ).astype(BF16)
        for rows in tiles:
            values = after_ref[rows, :].astype(F32)
            normed = (values * inverse_root(values) * gains_ref[2:3, :]).astype(BF16)
            normed_ref[rows, :] = normed
            normed_flip[:, rows] = normed.T
            branch_flip[:, rows] = branch_ref[rows, :].T
        sum_ref[...] = jnp.zeros_like(sum_ref)
        back_ref[...] = jnp.zeros_like(back_ref)
        gram_ref[...] = jnp.zeros_like(gram_ref)

    w_in = in_ref[...].reshape(width, width)
    w_out = out_ref[...].reshape(width, width)
    root = 0.7978845608028654

    def enter(rows, _):
        return nn(normed_ref[rows, :], w_in), nt(branch_ref[rows, :], w_out)

    def bend(rows, given):
        hidden, grad_active = given
        square = hidden * hidden
        bent = jnp.tanh(hidden * (root + (root * 0.044715) * square))
        half = 0.5 + 0.5 * bent
        slope = hidden * (2.0 * root + (6.0 * root * 0.044715) * square)
        slope = half + half * (slope * (1.0 - half))
        active_ref[rows, :] = (hidden * half).astype(BF16)
        grad_ref[rows, :] = (grad_active * slope).astype(BF16)

    def leave(rows, _):
        sum_ref[rows, :] += nn(active_ref[rows, :], w_out)
        back_ref[rows, :] += nt(grad_ref[rows, :], w_in)
        for r in range(rows.start // length, rows.stop // length):
            own = slice(r * length, (r + 1) * length)
            gram_ref[0, r] += gram(active_ref[own, :])
            gram_ref[1, r] += gram(grad_ref[own, :])

    pipelined(tiles, enter, bend, leave)
    grad_in = nn(normed_flip[...], grad_ref[...]).astype(BF16)
    grad_out = nn(branch_flip[...], active_ref[...]).astype(BF16).T

    def sends(which):
        pairs = [(in_slots, slots_ref.at[:, pl.ds(pl.multiple_of(which * 16, 16), 16), :])]
        for i, k in enumerate(range(0, 32, 4)):
            pairs.append((out_slots.at[i], slots_ref.at[k + which, 64:, :]))
        return [pltpu.make_async_copy(*pair, sems.at[i]) for i, pair in enumerate(pairs)]

    @pl.when(part > 0)
    def _():
        for copy in sends(part - 1):
            copy.wait()

    for k, block in enumerate(CODES):
        in_slots[k] = grad_in[16 * block : 16 * block + 16]
    for i, k in enumerate(range(0, 32, 4)):
        block = CODES[k]
        out_slots[i] = grad_out[64 * block : 64 * block + 64]
    for copy in sends(part):
        copy.start()

    @pl.when(part == pl.num_programs(0) - 1)
    def _():
        segments = dec_ref[...].astype(F32)
        columns = token_columns(segments)
        total_ref[...] = jnp.zeros_like(total_ref)
        for t, rows in enumerate(tiles):
            values = after_ref[rows, :].astype(F32)
            result_ref[rows, :] = (values + sum_ref[rows, :]).astype(BF16)
            grad, terms = norm_back(values, gains_ref[2:3, :], back_ref[rows, :])
            branch_b_ref[rows, :] = (branch_ref[rows, :].astype(F32) + grad).astype(BF16)
            own = segments[t * STEP_ROWS : (t + 1) * STEP_ROWS]
            gain_sums(terms, own, total_ref, square_ref.at[t])
        for r in range(count):
            own = slice(r * length, (r + 1) * length)
            products = gram_ref[0, r] * gram(branch_ref[own, :])
            products = products + gram_ref[1, r] * gram(normed_ref[own, :])
            token_ref[r // STEP_ROWS, r % STEP_ROWS : r % STEP_ROWS + 1, :] = same_sum(
                products, segments, columns, r
            )
        for copy in sends(part):
            copy.wait()


def score_grads(prob, grad_prob):
    prob = prob.astype(F32)
    dots = jnp.sum(prob * grad_prob, axis=0, keepdims=True)
    return prob * (grad_prob - dots)


def cross_backward_kernel(me_ref, branch_ref, middle_ref, memory_ref, attended_a_ref, input_ref,
                          query_ref, kv_ref, prob_ref, attended_ref, dec_ref, gains_ref,
                          weight_ref, grad_query_ref, grad_kv_ref, branch_a_ref, low_ref, high_ref,
                          total_ref, square_ref, grad_w, grad_attended):
    step = pl.program_id(0)
    mem_length = prob_ref.shape[2]
    length = prob_ref.shape[3] // 2
    width = branch_ref.shape[1]

    @pl.when(step == 0)
    def _():
        grad_w[...] = jnp.zeros_like(grad_w)
        total_ref[...] = jnp.zeros_like(total_ref)

    branch = branch_ref[...]
    grad_attended[...] = nt(branch, weight_ref[:, 4 * width :]).astype(BF16)

    def places(item):
        r, p = item
        rows, lanes = slice(r * length, (r + 1) * length), slice(p * LANES, (p + 1) * LANES)
        upper = slice(width + p * LANES, width + (p + 1) * LANES)
        return rows, slice(r * mem_length, (r + 1) * mem_length), lanes, upper

    def enter(item, _):
        rows, mem_rows, lanes, upper = places(item)
        grad_out = head_pair(grad_attended[rows, lanes])
        return grad_out, nt(kv_ref[mem_rows, upper], grad_out)

    def bend(item, given):
        r, p = item
        grad_out, grad_prob = given
        _, mem_rows, lanes, _ = places(item)
        grad_score = score_grads(prob_ref[r, p], grad_prob).astype(BF16)
        return grad_out, grad_score, kv_ref[mem_rows, lanes].T

    def leave(item, given):
        r, p = item
        grad_out, grad_score, key = given
        rows, mem_rows, lanes, upper = places(item)
        query = head_pair(query_ref[rows, lanes])
        grad_kv_ref[mem_rows, lanes] = nn(grad_score, query).astype(BF16)
        grad_kv_ref[mem_rows, upper] = nn(prob_ref[r, p], grad_out).astype(BF16)
        grad_query_ref[rows, lanes] = fold_pair(nn(key, grad_score), length)

    pipelined(row_pairs(STEP_ROWS), enter, bend, leave)
    grad_query = grad_query_ref[...]
    grad_normed = nt(grad_query, weight_ref[:, width : 2 * width])
    grad, terms = norm_back(middle_ref[...].astype(F32), gains_ref[1:2, :], grad_normed)
    branch_a = (branch.astype(F32) + grad).astype(BF16)
    branch_a_ref[...] = branch_a
    gain_sums(terms, step_rows(dec_ref, step, STEP_ROWS), total_ref, square_ref.at[0])
    grad_w[:, :width] += tn(attended_a_ref[...], branch_a)
    grad_w[:, width : 2 * width] += tn(input_ref[...], grad_query)
    grad_w[:, 2 * width : 4 * width] += tn(memory_ref[...], grad_kv_ref[...])
    grad_w[:, 4 * width :] += tn(attended_ref[...], branch)

    @pl.when(step == pl.num_programs(0) - 1)
    def _():
        store_slots(me_ref, low_ref, high_ref, partial(read_rows, grad_w))


def self_scores_kernel(branch_ref, qkv_ref, prob_ref, dec_ref, buckets_ref, weight_ref,
                       grad_qkv_ref, table_ref, table_square_ref, grad_attended, bands):
    step = pl.program_id(0)
    length = prob_ref.shape[2]
    width = branch_ref.shape[1]
    grad_attended[...] = nt(branch_ref[...], weight_ref[:, :width]).astype(BF16)

    @pl.when(step == 0)
    def _():
        table_ref[...] = jnp.zeros_like(table_ref)
        bands[...] = jnp.zeros_like(bands)

    row_i = lax.broadcasted_iota(jnp.int32, (length, length), 0)
    col_i = lax.broadcasted_iota(jnp.int32, (length, length), 1)
    flip = (row_i + col_i == length - 1).astype(F32).astype(BF16)
    columns = token_columns(step_rows(dec_ref, step, STEP_ROWS)).astype(BF16)
    turned = nn(flip, columns)

    members = [
        [
            jnp.broadcast_to((turned[:, r : r + 1] == float(e)).astype(F32), (length, length))
            for e in range(NSEG)
        ]
        for r in range(STEP_ROWS)
    ]

    def part(item, k):
        r, p = item
        lanes = slice(k * width + p * LANES, k * width + (p + 1) * LANES)
        return slice(r * length, (r + 1) * length), lanes

    def enter(item, _):
        grad_out = head_pair(grad_attended[part(item, 0)])
        return grad_out, nt(qkv_ref[part(item, 2)], grad_out)

    def bend(item, given):
        r, p = item
        grad_out, grad_prob = given
        grad_score = score_grads(prob_ref[r, p], grad_prob).astype(BF16)
        return grad_out, grad_score, jnp.concatenate([qkv_ref[part(item, 1)].T, flip], axis=0)

    def leave(item, given):
        r, p = item
        grad_out, grad_score, key = given
        query = head_pair(qkv_ref[part(item, 0)])
        grad_qkv_ref[part(item, 1)] = nn(grad_score, query).astype(BF16)
        grad_qkv_ref[part(item, 2)] = nn(prob_ref[r, p], grad_out).astype(BF16)
        both = nn(key, grad_score)
        grad_qkv_ref[part(item, 0)] = fold_pair(both[:length], length)
        return both[length:]

    def count_buckets(item, turned_score):
        r, p = item
        for h in range(2):
            own = turned_score[:, h * length : (h + 1) * length]
            own = pltpu.roll(own, 1, 1, stride=1, stride_axis=0)
            for e in range(NSEG):
                bands[r, 2 * p + h, e : e + 1, :] = jnp.sum(
                    own * members[r][e], axis=0, keepdims=True
                )

    pipelined(row_pairs(STEP_ROWS), enter, bend, leave, count_buckets)
    bucket = lax.broadcasted_iota(jnp.int32, (LANES, length), 0)
    near = (bucket == buckets_ref[...]).astype(F32)
    flat = bands[...].reshape(STEP_ROWS * H * 8, length)
    per_bucket = lax.dot_general(
        flat, near, (((1,), (1,)), ((), ())), preferred_element_type=F32,
        precision=lax.Precision.HIGHEST,
    ).reshape(STEP_ROWS, H, 8, LANES)
    table_ref[...] += jnp.sum(jnp.sum(per_bucket, axis=0), axis=1)
    squares = jnp.sum(jnp.sum(per_bucket * per_bucket, axis=1), axis=-1, keepdims=True)
    table_square_ref[0] = jnp.broadcast_to(squares, (STEP_ROWS, 8, LANES))


def self_weights_kernel(me_ref, branch_ref, tokens_ref, input_ref, grad_qkv_ref, dec_ref,
                        gains_ref, weight_ref, table_ref, total_b_ref, total_c_ref,
                        grad_tokens_ref, low_ref, high_ref, square_ref, grad_w, total_ref,
                        small_ref):
    step = pl.program_id(0)
    width = tokens_ref.shape[1]
    grad_qkv = grad_qkv_ref[...]
    grad_normed = nt(grad_qkv, weight_ref[...])
    grad, terms = norm_back(tokens_ref[...].astype(F32), gains_ref[0:1, :], grad_normed)
    grad_tokens_ref[...] = (branch_ref[...].astype(F32) + grad).astype(BF16)

    @pl.when(step == 0)
    def _():
        grad_w[...] = jnp.zeros_like(grad_w)
        total_ref[...] = jnp.zeros_like(total_ref)

    gain_sums(terms, step_rows(dec_ref, step, STEP_ROWS), total_ref, square_ref.at[0])
    grad_w[...] += tn(input_ref[...], grad_qkv)

    @pl.when(step == pl.num_programs(0) - 1)
    def _():
        bucket = lax.broadcasted_iota(jnp.int32, (LANES, width), 0)
        place = lax.broadcasted_iota(jnp.int32, (LANES, width), 1)
        spread = nn(table_ref[...].astype(BF16), (place // 16 == bucket).astype(F32).astype(BF16))
        head = lax.broadcasted_iota(jnp.int32, (H, width), 0)
        lane = lax.broadcasted_iota(jnp.int32, (H, width), 1)
        table = jnp.sum(jnp.where(lane % 16 == head, spread, 0.0), axis=0, keepdims=True)
        small = jnp.zeros((LANES, width), F32)
        row_i = lax.broadcasted_iota(jnp.int32, (LANES, width), 0)
        for k, line in enumerate((total_ref[...], total_b_ref[...], total_c_ref[...], table)):
            small = jnp.where(row_i == k, line, small)
        small_ref[...] = small.T

        def read(block):
            return jnp.concatenate(
                [read_rows(grad_w, block), read_rows(small_ref, block)], axis=1
            )

        store_slots(me_ref, low_ref, high_ref, read)


def pair_sum_kernel(low_ref, sent_ref, *refs):
    outs, (low, sent, total, load_sems, store_sems) = refs[:4], refs[4:]
    places = [pl.ds(4 * t, 4) for t in range(4)]
    lows = start_copies([(low_ref.at[p], low.at[p]) for p in places], load_sems.at[0])
    sents = start_copies([(sent_ref.at[p], sent.at[p]) for p in places], load_sems.at[1])
    stores = []
    for t, p in enumerate(places):
        lows[t].wait()
        sents[t].wait()
        total[p] = (low[p].astype(F32) + sent[p].astype(F32)).astype(BF16)
        stores.append(pltpu.make_async_copy(total.at[p], outs[t], store_sems.at[t]))
        stores[t].start()
    for store in stores:
        store.wait()


def pair_sum(low, sent, after):
    piece = shape_of((4,) + low.shape[1:], BF16)
    return pl.pallas_call(
        ignoring(pair_sum_kernel, 2, len(after)),
        out_shape=(piece,) * 4,
        in_specs=[pl.BlockSpec(memory_space=pl.ANY)] * (2 + len(after)),
        out_specs=[pl.BlockSpec(memory_space=pl.ANY)] * 4,
        scratch_shapes=[pltpu.VMEM(low.shape, BF16)] * 3
        + [pltpu.SemaphoreType.DMA((2, 4)), pltpu.SemaphoreType.DMA((4,))],
        compiler_params=pltpu.CompilerParams(vmem_limit_bytes=SHARED_LIMIT),
    )(in_hbm(low), sent, *after)


def plane_sum_kernel(*refs):
    own_ref, outs = refs[8], refs[9:]
    start = 0
    for group in (refs[:4], refs[4:8]):
        cols = slice(start, start + group[0].shape[2])
        start = cols.stop
        for s in range(4):
            total = sum(ref[s].astype(F32) for ref in group)
            if s == 0:
                own_ref[:, cols] = total
            else:
                outs[s - 1][:, cols] = total.astype(BF16)


def plane_sum(groups, after):
    line = (16, sum(group[0].shape[2] for group in groups))
    return small_call(
        plane_sum_kernel, [*groups[0], *groups[1]], after,
        (shape_of(line, F32),) + (shape_of(line, BF16),) * 3,
    )


def square_sum(values):
    return jnp.sum(jnp.sum(values * values, axis=0, keepdims=True), axis=1, keepdims=True)


def feed_end_kernel(sum_ref, hidden_ref, back_ref, square_ref):
    total = sum_ref[...].astype(F32)
    width = total.shape[1]
    for j in range(4):
        hidden_ref[:, j * width : (j + 1) * width] = total[16 * j : 16 * (j + 1)]
    back_ref[...] = total[64:]
    square_ref[...] = jnp.broadcast_to(square_sum(total), square_ref.shape)


def column_end_kernel(own_ref, b_ref, c_ref, d_ref, *refs):
    squares, outs, square_ref = refs[:1], refs[1:-1], refs[-1]
    total = own_ref[...] + b_ref[...].astype(F32)
    total = total + c_ref[...].astype(F32) + d_ref[...].astype(F32)
    start = 0
    for out in outs:
        out[...] = total[:, start : start + out.shape[1]]
        start += out.shape[1]
    square = square_sum(total)
    for given in squares:
        square = square + given[0:1, 0:1]
    square_ref[...] = jnp.broadcast_to(square, square_ref.shape)


def staged(kernel, ins, outs):
    def run(*refs):
        count = ins + outs
        given, inner, sems = refs[:count], refs[count : 2 * count], refs[2 * count]
        for copy in start_copies(list(zip(given[:ins], inner[:ins])), sems):
            copy.wait()
        kernel(*inner)
        for copy in start_copies(list(zip(inner[ins:], given[ins:])), sems):
            copy.wait()

    return run


def small_call(kernel, ins, after, outs):
    arrays = [*ins, *outs]
    return pl.pallas_call(
        ignoring(staged(kernel, len(ins), len(outs)), len(ins), len(after)),
        out_shape=outs,
        in_specs=[pl.BlockSpec(memory_space=pl.ANY)] * (len(ins) + len(after)),
        out_specs=[pl.BlockSpec(memory_space=pl.ANY)] * len(outs),
        scratch_shapes=[pltpu.VMEM(array.shape, array.dtype) for array in arrays]
        + [pltpu.SemaphoreType.DMA((len(arrays),))],
        compiler_params=pltpu.CompilerParams(vmem_limit_bytes=SHARED_LIMIT),
    )(*ins, *after)


def split_kernel(*refs):
    lines, (own_ref, rest_ref) = refs[:4], refs[4:]
    split = own_ref.shape[2]
    for s, line in enumerate(lines):
        own_ref[s] = line[:, :split]
        rest_ref[s] = line[:, split:]


def split_column(lines, split):
    rows, cols = lines[0].shape
    outs = [shape_of((4, rows, part), BF16) for part in (split, cols - split)]
    return small_call(split_kernel, lines, (), outs)


def pack_kernel(*refs):
    ins, (shard_ref, feed_ref) = refs[:11], refs[11:]
    width = ins[0].shape[1]
    start = 0
    for line in (*ins[:3], ins[10], *ins[3:8]):
        shard_ref[:, start : start + line.shape[1]] = line[...]
        start += line.shape[1]
    for j in range(ins[8].shape[1] // width):
        feed_ref[16 * j : 16 * (j + 1), :] = ins[8][:, j * width : (j + 1) * width]
    feed_ref[64:, :] = ins[9][...]


def pack(weights, small):
    width = weights[0].shape[1]
    outs = [shape_of((16, 8 * width + LANES), BF16), shape_of((128, width), BF16)]
    return small_call(pack_kernel, (*map(in_hbm, weights), small), (), outs)


def memory_backward_kernel(memory_ref, grad_kv_ref, mem_ref, weight_ref, grad_memory_ref,
                           token_ref):
    mem_length = mem_ref.shape[1]
    width = memory_ref.shape[1]
    weight = weight_ref[:, 2 * width : 4 * width]
    grad_memory_ref[...] = nt(grad_kv_ref[...], weight).astype(BF16)
    count = memory_ref.shape[0] // mem_length
    segments = step_rows(mem_ref, pl.program_id(0), count)
    columns = token_columns(segments)
    for r in range(count):
        rows = slice(r * mem_length, (r + 1) * mem_length)
        products = gram(memory_ref[rows, :]) * gram(grad_kv_ref[rows, :])
        token_ref[0, r : r + 1, :] = same_sum(products, segments, columns, r)


def gram_kernel(*refs):
    pairs, dec_ref, token_ref = refs[:-2], refs[-2], refs[-1]
    length = dec_ref.shape[1]
    count = pairs[0].shape[0] // length
    segments = step_rows(dec_ref, pl.program_id(0), count)
    columns = token_columns(segments)
    for r in range(count):
        rows = slice(r * length, (r + 1) * length)
        products = sum(
            gram(left[rows, :]) * gram(right[rows, :])
            for left, right in zip(pairs[::2], pairs[1::2])
        )
        token_ref[0, r : r + 1, :] = same_sum(products, segments, columns, r)


def rows_spec(array, steps):
    shape = (array.shape[0] // steps,) + array.shape[1:]
    return pl.BlockSpec(shape, lambda i, *_: (i,) + (0,) * (len(shape) - 1))


class Cut:
    def __init__(self, array, shape, index):
        self.array, self.spec = array, pl.BlockSpec(shape, index)


def whole_spec(array):
    return pl.BlockSpec(array.shape, lambda i, *_: (0,) * len(array.shape))


def in_hbm(array):
    return pltpu.with_memory_space_constraint(array, pltpu.HBM)


def ignoring(kernel, first, count):
    return lambda *refs: kernel(*refs[:first], *refs[first + count :])


def call(kernel, steps, me, blocked, whole, pieces, outs_blocked, outs_whole, scratch, flops,
         order, after=(), limit=VMEM_LIMIT):
    ins, in_specs = [], []
    blocked, whole = list(blocked), list(whole)
    for kind in order[0]:
        array = (blocked if kind == "i" else whole).pop(0)
        if isinstance(array, Cut):
            ins.append(array.array)
            in_specs.append(array.spec)
            continue
        ins.append(array)
        in_specs.append(rows_spec(array, steps) if kind == "i" else whole_spec(array))
    ins = [in_hbm(array) for array in ins]
    kernel = ignoring(kernel, len(ins) + len(pieces) + (me is not None), len(after))
    ins += [*pieces, *after]
    in_specs += [pl.BlockSpec(memory_space=pl.ANY)] * (len(pieces) + len(after))
    outs, out_specs = [], []
    outs_blocked, outs_whole = list(outs_blocked), list(outs_whole)
    for kind in order[1]:
        out = (outs_blocked if kind == "i" else outs_whole).pop(0)
        outs.append(out)
        if kind == "a":
            out_specs.append(pl.BlockSpec(memory_space=pl.ANY))
        else:
            out_specs.append(rows_spec(out, steps) if kind == "i" else whole_spec(out))
    moved = sum(math.prod(a.shape) * a.dtype.itemsize for a in ins + outs)
    prefetch = 0 if me is None else 1
    return pl.pallas_call(
        kernel,
        out_shape=outs,
        grid_spec=pltpu.PrefetchScalarGridSpec(
            num_scalar_prefetch=prefetch,
            grid=(steps,),
            in_specs=in_specs,
            out_specs=out_specs,
            scratch_shapes=scratch,
        ),
        compiler_params=pltpu.CompilerParams(
            dimension_semantics=("arbitrary",), vmem_limit_bytes=limit
        ),
        cost_estimate=pl.CostEstimate(flops=flops, bytes_accessed=moved, transcendentals=0),
    )(*(() if me is None else (me,)), *ins)


FINE = ("z", "y", "core", "x")


def shape_of(shape, dtype):
    return jax.ShapeDtypeStruct(shape, dtype)


def kept(shape, dtype):
    return pltpu.HBM(shape, dtype)


def shift(array, mask):
    return lax.ppermute(array, FINE, [(i, i ^ mask) for i in range(32)])


def hold(array, after):
    return lax.optimization_barrier((array, after))[0]


def pack_feed(hidden, back):
    width = back.shape[1]
    hidden = hidden.reshape(-1, 16, 4, width).transpose(0, 2, 1, 3).reshape(-1, 64, width)
    return jnp.concatenate([hidden, back.reshape(-1, 64, width)], axis=1)


def unpack_feed(blocks):
    width = blocks.shape[2]
    hidden = blocks[:, :64].reshape(-1, 4, 16, width).transpose(0, 2, 1, 3)
    return hidden.reshape(-1, 4 * width), blocks[:, 64:].reshape(-1, width)


def small_row(gains, table):
    table = jnp.pad(table.reshape(-1, H), ((0, 0), (0, 16 - H)))
    row = jnp.concatenate([gain.reshape(-1, 16) for gain in gains] + [table], axis=1)
    row = jnp.pad(row, ((0, 0), (0, LANES - row.shape[1])))
    return jnp.pad(row[:, None], ((0, 0), (0, 15), (0, 0))).reshape(-1, LANES)


def in_order(slots):
    return slots[jnp.array([CODES.index(block) for block in range(32)])]


def as_rows(slots):
    return in_order(slots).reshape(-1, slots.shape[2]).astype(F32)


def shift_plane(pieces):
    return [shift(piece, mask) for piece, mask in zip(pieces, PLANE[1:])]


def shift_column(pieces):
    return [shift(piece, code) for piece, code in zip(pieces, COLUMN[1:])]


class Near:
    axes = FINE

    def __init__(self, weights):
        self.me = lax.axis_index(FINE)
        small = small_row(weights[10:13], weights[13])
        shard, feed = pack(weights[:10], small)
        self.feed = lax.all_gather(feed, FINE, axis=0)
        column = [shard, *shift_column([shard] * 3)]
        own, rest = split_column(column, 3 * weights[0].shape[1] + LANES)
        plane = [own, *shift_plane([own] * 3)]
        rest = hold(rest, plane[1])
        self.plane = [rest, *shift_plane([rest] * 3)]
        self.own = plane + [shift(piece, 2) for piece in plane]

    def cross(self, after):
        plane = [hold(piece, after) for piece in self.plane]
        return plane + [shift(piece, 2) for piece in plane]

    def feed_core(self, slots):
        return lax.psum_scatter(slots.reshape((2, 4, 4) + slots.shape[1:]), "core")

    def feed_plane(self, slots):
        return lax.psum_scatter(slots, ("y", "x"))

    def feed_column(self, slots):
        return lax.psum_scatter(slots, "z")


class Far:
    axes = ("wide", "narrow")
    me = 0

    def __init__(self, weights):
        weights = [lax.all_gather(w, self.axes, axis=0, tiled=True) for w in weights]
        self.take(weights)

    def take(self, weights):
        self.own = self.pieces(*weights[:3], small_row(weights[10:13], weights[13]))
        self.rest = self.pieces(*weights[3:8])
        self.feed = pack_feed(weights[8], weights[9])

    def pieces(self, *parts):
        blocks = jnp.concatenate(parts, axis=1).reshape(32, 16, -1)[jnp.array(CODES)]
        return [blocks[4 * t : 4 * t + 4] for t in range(8)]

    def cross(self, after):
        return self.rest

    def feed_core(self, slots):
        return slots

    feed_plane = feed_column = feed_core


def on_device(near, tokens, memory, cotangent, dec_segments, mem_segments, padding, buckets,
              *weights):
    way = (Near if near else Far)(weights)
    result, grad_tokens, grad_memory, grads, examples, square = local_part(
        way, tokens, memory, cotangent, dec_segments, mem_segments, padding, buckets
    )
    if near:
        sent = lax.all_to_all(square, FINE, 0, 0, tiled=True)
        global_norm = jnp.sum(sent[:, 0])
    else:
        grads = [lax.psum_scatter(g, way.axes, scatter_dimension=0, tiled=True) for g in grads]
        global_norm = lax.psum(sum(jnp.sum(g * g) for g in grads), way.axes)
    return (result, grad_tokens, grad_memory, *grads, examples, global_norm / COUNT)


def local_part(way, tokens, memory, cotangent, dec_segments, mem_segments, padding, buckets):
    seqs, length, width = tokens.shape
    mem_length = memory.shape[1]
    steps = seqs // STEP_ROWS
    small_steps = seqs // SMALL_ROWS
    dec, mem = seqs * length, seqs * mem_length
    step_dec = STEP_ROWS * length
    ff = 4 * width

    buckets = buckets[None]
    tokens2, memory2, cotangent2 = (
        array.reshape(-1, width) for array in (tokens, memory, cotangent)
    )
    dma = pltpu.SemaphoreType.DMA

    me = jnp.full((1,), way.me, jnp.int32)
    flops = 2 * dec * width * width

    input_a, qkv_a, prob_a, attended_a, self_w, gains = call(
        self_forward_kernel, small_steps, me, (tokens2,), (dec_segments, padding, buckets), way.own,
        (
            kept((dec, width), BF16),
            kept((dec, 3 * width), BF16),
            kept((seqs, PAIRS, length, 2 * length), BF16),
            kept((dec, width), BF16),
        ),
        (kept((width, 3 * width), BF16), kept((8, width), F32)),
        [pltpu.VMEM((PAIRS, length, 2 * length), F32), pltpu.VMEM((width, LANES), BF16), dma((64,))],
        6 * flops, ("iwww", "iiiiww"), (), SHARED_LIMIT,
    )
    kv_b, cross_w = call(
        memory_forward_kernel, small_steps, me, (memory2,), (), way.cross(attended_a),
        (kept((mem, 2 * width), BF16),), (kept((width, 5 * width), BF16),), [dma((32,))],
        4 * flops, ("i", "iw"), (), SHARED_LIMIT,
    )
    middle, input_b, query_b, prob_b, attended_b, after_cross = call(
        cross_forward_kernel, small_steps, None, (tokens2, attended_a, kv_b),
        (dec_segments, mem_segments, gains, cross_w), (),
        (
            kept((dec, width), BF16),
            kept((dec, width), BF16),
            kept((dec, width), BF16),
            kept((seqs, PAIRS, mem_length, 2 * length), BF16),
            kept((dec, width), BF16),
            kept((dec, width), BF16),
        ),
        (), [], 6 * flops, ("iiiwwww", "iiiiii"),
    )
    total, square = kept((1, width), F32), shape_of((steps, 4 * STEP_ROWS, LANES), F32)
    token_shape = shape_of((steps, 8, length), F32)
    small_token = shape_of((small_steps, 8, length), F32)
    in_part = Cut(way.feed, (32, 16, width), lambda i, *_: (0, i, 0))
    out_part = Cut(way.feed, (8, 64, width), lambda i, *_: (i, 1, 0))
    result, branch_b, feed_slots, gain_c, square_c, token_c = call(
        feed_kernel, ff // width, None, (),
        (after_cross, cotangent2, dec_segments, padding, gains, in_part,
         out_part),
        (), (),
        (
            shape_of((dec, width), BF16),
            kept((dec, width), BF16),
            shape_of((32, 128, width), BF16),
            total,
            square,
            token_shape,
        ),
        [
            *[pltpu.VMEM((dec, width), BF16)] * 2,
            *[pltpu.VMEM((width, dec), BF16)] * 2,
            *[pltpu.VMEM((dec, width), BF16)] * 2,
            *[pltpu.VMEM((dec, width), F32)] * 2,
            pltpu.VMEM((2, seqs, length, length), F32),
            pltpu.VMEM((32, 16, width), BF16),
            pltpu.VMEM((8, 64, width), BF16),
            dma((9,)),
        ],
        26 * flops, ("wwwwwww", "wwawww"),
    )
    feed_sum = way.feed_core(feed_slots)
    slot = shape_of((16, 16, 5 * width), BF16)
    grad_query_b, grad_kv_b, branch_a, cross_low, cross_high, gain_b, square_b = call(
        cross_backward_kernel, steps, me,
        (branch_b, middle, memory2, attended_a, input_b, query_b, kv_b, prob_b, attended_b),
        (dec_segments, gains, cross_w), (),
        (
            kept((dec, width), BF16),
            kept((mem, 2 * width), BF16),
            kept((dec, width), BF16),
            square,
        ),
        (kept(slot.shape, BF16), slot, total),
        [pltpu.VMEM((width, 5 * width), F32), pltpu.VMEM((step_dec, width), BF16)],
        20 * flops, ("iiiiiiiiiwww", "iiiwwwi"),
    )
    feed_sum = way.feed_plane(hold(feed_sum, grad_query_b))
    near = isinstance(way, Near)
    if near:
        sent = shift(cross_high, 2)
    grad_qkv_a, table, table_square = call(
        self_scores_kernel, steps, None, (branch_a, qkv_a, prob_a),
        (dec_segments, buckets, cross_w), (),
        (kept((dec, 3 * width), BF16), shape_of((steps, STEP_ROWS, 8, LANES), F32)),
        (kept((H, LANES), F32),),
        [pltpu.VMEM((step_dec, width), BF16), pltpu.VMEM((STEP_ROWS, H, 8, length), F32)],
        10 * flops, ("iiiwww", "iwi"),
    )
    waits = ()
    if near:
        cross_parts = pair_sum(cross_low, sent, (grad_qkv_a,))
        crossed = shift_plane(cross_parts[1:])
        waits = (cross_parts[0],)
    slot = shape_of((16, 16, 3 * width + LANES), BF16)
    grad_tokens, self_low, self_high, square_a = call(
        self_weights_kernel, steps, me, (branch_a, tokens2, input_a, grad_qkv_a),
        (dec_segments, gains, self_w, table, gain_b, gain_c), (),
        (shape_of((dec, width), BF16), square),
        (kept(slot.shape, BF16), slot),
        [
            pltpu.VMEM((width, 3 * width), F32),
            pltpu.VMEM((1, width), F32),
            pltpu.VMEM((width, LANES), F32),
        ],
        7 * flops, ("iiiiwwwwww", "iwwi"), waits,
    )

    def grams(pairs, *after):
        (tokens_part,) = call(
            gram_kernel, small_steps, None, pairs, (dec_segments,), (), (small_token,), (), [],
            2 * flops, ("i" * len(pairs) + "w", "i"), after, SHARED_LIMIT,
        )
        return tokens_part

    def fill_cross(*after):
        return grams((input_b, grad_query_b, attended_b, branch_b), *after)

    def fill_self(*after):
        return grams((input_a, grad_qkv_a, attended_a, branch_a), *after)

    def fill_memory(*after):
        return call(
            memory_backward_kernel, small_steps, None, (memory2, grad_kv_b),
            (mem_segments, cross_w), (),
            (shape_of((mem, width), BF16), shape_of((small_steps, 8, mem_length), F32)), (), [],
            10 * flops, ("iiww", "ii"), after, SHARED_LIMIT,
        )

    if near:
        sent = shift(hold(self_high, crossed[0]), 2)
        token_b = fill_cross(self_low)
        self_parts = pair_sum(self_low, sent, (token_b,))
        self_sent = shift_plane(self_parts[1:])
        feed_sum = hold(feed_sum, token_b)
        token_a = fill_self(self_parts[0], feed_sum)
        feed_sum = way.feed_column(feed_sum)
        groups = [[self_parts[0], *self_sent], [cross_parts[0], *crossed]]
        own, *rest = plane_sum(groups, (token_a,))
        line_sent = shift_column(rest)
        grad_memory, token_m = fill_memory(own)
        feed_sum = hold(feed_sum, token_m).reshape(128, width)
        grad_hidden, grad_back, square = small_call(
            feed_end_kernel, (feed_sum,), (token_m,),
            [shape_of((16, ff), F32), shape_of((64, width), F32), shape_of((8, LANES), F32)],
        )
        line = shape_of((slot.shape[1], width), F32)
        *parts, square = small_call(
            column_end_kernel, (own, *line_sent, square), (token_m,),
            [line] * 3 + [shape_of((16, LANES), F32)] + [line] * 5 + [shape_of((32, LANES), F32)],
        )
        self_grads, small, cross_grads = parts[:3], parts[3], parts[4:]
        token_m = hold(token_m, square)
    else:
        token_b, token_a = fill_cross(), fill_self()
        grad_memory, token_m = fill_memory()
        cross_sum = as_rows(jnp.concatenate([cross_low, cross_high]))
        self_sum = as_rows(jnp.concatenate([self_low, self_high]))
        cross_grads = [cross_sum[:, k * width : (k + 1) * width] for k in range(5)]
        self_grads = [self_sum[:, k * width : (k + 1) * width] for k in range(3)]
        small = self_sum[:, 3 * width :]
        grad_hidden, grad_back = unpack_feed(in_order(feed_sum).astype(F32))
        square = None
    grads = self_grads + cross_grads + [grad_hidden, grad_back]
    grads += [small[:, k] for k in range(3)]
    grads.append(small[:, 3].reshape(-1, 16)[:, :H].reshape(-1))

    def row_parts(parts, count):
        return parts[:, :count].reshape(seqs, -1)

    def by_example(part, segments):
        hits = segments[:, None, :] == lax.broadcasted_iota(jnp.int32, (1, NSEG, 1), 1)
        return jnp.sum(jnp.where(hits, part[:, None, :], 0.0), axis=-1)

    token_d = row_parts(token_a + token_b, SMALL_ROWS) + row_parts(token_c, STEP_ROWS)
    examples = by_example(token_d, dec_segments)
    examples = examples + by_example(row_parts(token_m, SMALL_ROWS), mem_segments)
    squares = (square_a + square_b + square_c)[:, :, 0].reshape(seqs, NSEG)
    examples = examples + squares + table_square[..., :NSEG, 0].reshape(seqs, NSEG)
    return (
        result.reshape(tokens.shape),
        grad_tokens.reshape(tokens.shape),
        grad_memory.reshape(memory.shape),
        grads,
        examples / COUNT,
        square,
    )


def solution(mesh):
    near = tuple(mesh.shape.values()) == (16, 2)
    if near:
        mesh = jax.sharding.Mesh(mesh.devices.reshape(4, 2, 2, 2), FINE)
    axes = tuple(mesh.axis_names)
    rows = P(axes)
    arrays, weights, vectors = (P(axes, None, None),) * 3, (P(axes, None),) * 10, (rows,) * 4
    placed = arrays + (P(axes, None),) * 3 + (P(),) + weights + vectors
    return jax.shard_map(
        partial(on_device, near),
        mesh=mesh,
        in_specs=placed,
        out_specs=arrays + weights + vectors + (P(axes, None), P()),
        check_vma=False,
    )
```

```python
import math
from functools import partial

import jax
import jax.numpy as jnp
from jax import lax
from jax.experimental import pallas as pl
from jax.experimental.pallas import tpu as pltpu
from jax.sharding import PartitionSpec as P

H = 8
DH = 64
NB = 32
NSEG = 4
COUNT = 4196096
EPSILON = 1e-06
FLOOR = -1e30
F32 = jnp.float32
BF16 = jnp.bfloat16
PAIRS = H // 2
LANES = 128
STEP_ROWS = 4
SMALL_ROWS = 4
VMEM_LIMIT = 60 * 2**20
SHARED_LIMIT = 48 * 2**20

COLUMN = (0, 8, 16, 24)
PLANE = (0, 1, 4, 5)
CODES = tuple(2 * c + mask + z for c in (0, 1) for mask in PLANE for z in COLUMN)


def nn(left, right):
    return lax.dot_general(left, right, (((1,), (0,)), ((), ())), preferred_element_type=F32)


def nt(left, right):
    return lax.dot_general(left, right, (((1,), (1,)), ((), ())), preferred_element_type=F32)


def tn(left, right):
    return lax.dot_general(left, right, (((0,), (0,)), ((), ())), preferred_element_type=F32)


def inverse_root(values):
    return lax.rsqrt(jnp.mean(values * values, axis=-1, keepdims=True) + EPSILON)


def head_masks(values):
    low = (lax.broadcasted_iota(jnp.int32, (1, LANES), 1) < DH).astype(BF16)
    return values * low, values * (1 - low)


def head_pair(values):
    return jnp.concatenate(head_masks(values), axis=0)


def fold_pair(both, queries):
    own = jnp.concatenate([both[:DH, :queries], both[DH:, queries:]], axis=0)
    return own.astype(BF16).T


def block_rows(block):
    return pl.ds(pl.multiple_of(block * 16, 16), 16)


def start_copies(pairs, sems):
    copies = [pltpu.make_async_copy(*pair, sems.at[i]) for i, pair in enumerate(pairs)]
    for copy in copies:
        copy.start()
    return copies


def read_rows(grad_w, block):
    return grad_w[block_rows(block), :].astype(BF16)


def store_slots(me_ref, low_ref, high_ref, read):
    for k, code in enumerate(CODES):
        target = low_ref if k < 16 else high_ref
        target[k % 16] = read(me_ref[0] ^ code)


def softmax_columns(scores):
    shifted = jnp.exp(scores - jnp.max(scores, axis=0, keepdims=True))
    return (shifted * (1.0 / jnp.sum(shifted, axis=0, keepdims=True))).astype(BF16)


def step_rows(ref, step, count):
    whole = ref[...].astype(F32)
    rows = whole[:count]
    for s in range(1, whole.shape[0] // count):
        rows = jnp.where(step == s, whole[s * count : (s + 1) * count], rows)
    return rows


def token_columns(lines):
    pad = 8 - lines.shape[0] % 8
    return jnp.concatenate([lines] + [lines[:1]] * (pad % 8), axis=0).T


def member_lines(lines):
    count, length = lines.shape
    codes = jnp.concatenate([lines[r : r + 1] + float(NSEG * r) for r in range(count)], axis=1)
    places = lax.broadcasted_iota(jnp.int32, (NSEG * count, count * length), 0).astype(F32)
    return (codes == places).astype(F32).astype(BF16)


def same_sum(products, lines, columns, r):
    same = columns[:, r : r + 1] == lines[r : r + 1]
    return jnp.sum(jnp.where(same, products, 0.0), axis=0, keepdims=True)


def pipelined(items, *stages):
    state = {}
    for tick in range(len(items) + len(stages) - 1):
        for depth, stage in enumerate(stages):
            n = tick - depth
            if 0 <= n < len(items):
                state[n] = stage(items[n], state.get(n))


def row_pairs(count):
    return [(r, p) for r in range(count) for p in range(PAIRS)]


def gram(left):
    return nt(left, left)


def self_forward_kernel(me_ref, tokens_ref, dec_ref, padding_ref, buckets_ref, *refs):
    pieces, refs = refs[:8], refs[8:]
    input_ref, qkv_ref, prob_ref, attended_ref, weight_ref, gains_ref = refs[:6]
    bias_ref, small_ref, sems = refs[6:]
    length = dec_ref.shape[1]
    width = tokens_ref.shape[1]

    @pl.when(pl.program_id(0) == 0)
    def _():
        pairs = []
        for k, code in enumerate(CODES):
            rows = block_rows(me_ref[0] ^ code)
            source = pieces[k // 4].at[k % 4]
            pairs.append((source.at[:, : 3 * width], weight_ref.at[rows, :]))
            pairs.append((source.at[:, 3 * width :], small_ref.at[rows, :]))
        for copy in start_copies(pairs, sems):
            copy.wait()
        first = lax.broadcasted_iota(jnp.int32, (32, width), 1)
        pick = first == 16 * lax.broadcasted_iota(jnp.int32, (32, width), 0)
        small = nn(pick.astype(F32).astype(BF16), small_ref[...]).astype(BF16)
        lane = lax.broadcasted_iota(jnp.int32, (LANES, width), 0)
        feature = lax.broadcasted_iota(jnp.int32, (LANES, width), 1)
        block = lax.broadcasted_iota(jnp.int32, (32, width), 0)
        lines = []
        for k in range(4):
            spread = nn(small, (lane == 16 * k + feature % 16).astype(F32).astype(BF16))
            lines.append(
                jnp.sum(jnp.where(block == first // 16, spread, 0.0), axis=0, keepdims=True)
            )
        gains_ref[...] = jnp.concatenate(lines + lines, axis=0)
        place = lax.broadcasted_iota(jnp.int32, (H, width), 1) % 16
        head = lax.broadcasted_iota(jnp.int32, (H, width), 0)
        table = jnp.where(place == head, lines[3], 0.0).astype(BF16)
        bucket = lax.broadcasted_iota(jnp.int32, (width, length), 0) // 16
        curves = nn(table, (bucket == buckets_ref[...]).astype(F32).astype(BF16))
        for h in range(H):
            curve = jnp.broadcast_to(curves[h : h + 1, :], (length, length))
            lanes = slice((h % 2) * length, (h % 2 + 1) * length)
            bias_ref[h // 2, :, lanes] = pltpu.roll(curve, 0, 1, stride=1, stride_axis=0)

    values = tokens_ref[...].astype(F32)
    normed = (values * inverse_root(values) * gains_ref[0:1, :]).astype(BF16)
    input_ref[...] = normed
    for first in range(0, 3 * width, 256):
        cols = slice(first, first + 256)
        qkv_ref[:, cols] = nn(normed, weight_ref[:, cols]).astype(BF16)

    step = pl.program_id(0)
    count = tokens_ref.shape[0] // length
    segments, real = step_rows(dec_ref, step, count), step_rows(padding_ref, step, count)
    segment_columns, real_columns = token_columns(segments), token_columns(real)
    key_i = lax.broadcasted_iota(jnp.int32, (length, length), 0)
    query_i = lax.broadcasted_iota(jnp.int32, (length, length), 1)

    masks = []
    for r in range(count):
        allowed = (segment_columns[:, r : r + 1] == segments[r : r + 1]) & (key_i <= query_i)
        allowed = allowed & ((real_columns[:, r : r + 1] > 0.0) | (key_i == query_i))
        mask = jnp.where(allowed, 0.0, FLOOR)
        masks.append(jnp.concatenate([mask, mask], axis=1))

    def part(item, k):
        r, p = item
        return qkv_ref[r * length : (r + 1) * length, k * width + p * LANES : k * width + (p + 1) * LANES]

    def scores(item, _):
        return nt(part(item, 1), head_pair(part(item, 0)))

    def weigh(item, score):
        r, p = item
        prob = softmax_columns(score + bias_ref[p] + masks[r])
        prob_ref[r, p] = prob
        return prob, part(item, 2).T

    def mix(item, given):
        r, p = item
        prob, value = given
        rows, lanes = slice(r * length, (r + 1) * length), slice(p * LANES, (p + 1) * LANES)
        attended_ref[rows, lanes] = fold_pair(nn(value, prob), length)

    pipelined(row_pairs(count), scores, weigh, mix)


def memory_forward_kernel(me_ref, memory_ref, *refs):
    pieces, (kv_ref, weight_ref, sems) = refs[:-3], refs[-3:]
    width = memory_ref.shape[1]

    @pl.when(pl.program_id(0) == 0)
    def _():
        pairs = []
        for k, code in enumerate(CODES):
            source = pieces[k // 4].at[k % 4]
            pairs.append((source, weight_ref.at[block_rows(me_ref[0] ^ code), :]))
        for copy in start_copies(pairs, sems):
            copy.wait()

    for first in range(0, 2 * width, 256):
        kv_ref[:, first : first + 256] = nn(
            memory_ref[...], weight_ref[:, 2 * width + first : 2 * width + first + 256]
        ).astype(BF16)


def cross_forward_kernel(tokens_ref, attended_a_ref, kv_ref, dec_ref, mem_ref, gains_ref,
                         weight_ref, middle_ref, input_ref, query_ref, prob_ref, attended_ref, after_ref):
    mem_length, length = mem_ref.shape[1], dec_ref.shape[1]
    width = tokens_ref.shape[1]
    values = tokens_ref[...].astype(F32) + nn(attended_a_ref[...], weight_ref[:, :width])
    middle_ref[...] = values.astype(BF16)
    normed = (values * inverse_root(values) * gains_ref[1:2, :]).astype(BF16)
    input_ref[...] = normed
    query_ref[...] = nn(normed, weight_ref[:, width : 2 * width]).astype(BF16)

    step = pl.program_id(0)
    count = tokens_ref.shape[0] // length
    segments = step_rows(dec_ref, step, count)
    mem_columns = token_columns(step_rows(mem_ref, step, count))

    masks = []
    for r in range(count):
        mask = jnp.where(mem_columns[:, r : r + 1] == segments[r : r + 1], 0.0, FLOOR)
        masks.append(jnp.concatenate([mask, mask], axis=1))

    def places(item):
        r, p = item
        rows, lanes = slice(r * length, (r + 1) * length), slice(p * LANES, (p + 1) * LANES)
        upper = slice(width + p * LANES, width + (p + 1) * LANES)
        return rows, slice(r * mem_length, (r + 1) * mem_length), lanes, upper

    def scores(item, _):
        rows, mem_rows, lanes, _ = places(item)
        return nt(kv_ref[mem_rows, lanes], head_pair(query_ref[rows, lanes]))

    def weigh(item, score):
        r, p = item
        _, mem_rows, _, upper = places(item)
        prob = softmax_columns(score + masks[r])
        prob_ref[r, p] = prob
        return prob, kv_ref[mem_rows, upper].T

    def mix(item, given):
        rows, _, lanes, _ = places(item)
        prob, value = given
        attended_ref[rows, lanes] = fold_pair(nn(value, prob), length)

    pipelined(row_pairs(count), scores, weigh, mix)
    after = values + nn(attended_ref[...], weight_ref[:, 4 * width :])
    after_ref[...] = after.astype(BF16)


def norm_back(values, gain, grad_normed):
    inverse = inverse_root(values)
    scaled = values * inverse
    upper = grad_normed * gain
    grad = inverse * (upper - scaled * jnp.mean(upper * scaled, axis=-1, keepdims=True))
    return grad, grad_normed * scaled


def gain_sums(terms, segments, total_ref, square_ref):
    sums = nn(member_lines(segments), terms.astype(BF16))
    total_ref[...] += jnp.sum(sums, axis=0, keepdims=True)
    square = jnp.sum(sums * sums, axis=1, keepdims=True)
    square_ref[...] = jnp.broadcast_to(square, square_ref.shape)


def feed_kernel(after_ref, cotangent_ref, dec_ref, padding_ref, gains_ref, gathered_ref,
                result_ref, branch_b_ref, slots_ref, total_ref, square_ref, token_ref, w_in_ref,
                w_out_ref, normed_ref, branch_ref, normed_flip, branch_flip, active_ref, grad_ref,
                in_slots, out_slots, load_sems, sems):
    part = pl.program_id(0)
    parts = pl.num_programs(0)
    count, length = dec_ref.shape
    dec, width = after_ref.shape
    ff = w_in_ref.shape[2]
    tile = STEP_ROWS * length
    tiles = [slice(t * tile, (t + 1) * tile) for t in range(dec // tile)]

    def loads(which):
        rows = pl.ds(pl.multiple_of(which * 16, 16), 16)
        cols = pl.ds(pl.multiple_of(which * width, width), width)
        blocks = pl.ds(which * 8, 8)
        pairs = (
            (gathered_ref.at[:, rows, :], w_in_ref.at[:, :, cols]),
            (gathered_ref.at[blocks, 64:, :], w_out_ref.at[blocks]),
        )
        return [
            pltpu.make_async_copy(*pair, load_sems.at[which, i]) for i, pair in enumerate(pairs)
        ]

    @pl.when(part == 0)
    def _():
        for which in range(ff // width):
            for copy in loads(which):
                copy.start()
        real = token_columns(padding_ref[...].astype(F32))
        for r in range(count):
            rows = slice(r * length, (r + 1) * length)
            branch_ref[rows, :] = (
                cotangent_ref[rows, :].astype(F32) * real[:, r : r + 1]
            ).astype(BF16)
        for rows in tiles:
            values = after_ref[rows, :].astype(F32)
            normed = (values * inverse_root(values) * gains_ref[2:3, :]).astype(BF16)
            normed_ref[rows, :] = normed
            normed_flip[:, rows] = normed.T
            branch_flip[:, rows] = branch_ref[rows, :].T

    for copy in loads(part):
        copy.wait()
    root = 0.7978845608028654
    half_width = width // 2
    for sub in range(2):
        first = pl.multiple_of(part * width + sub * half_width, half_width)
        cols = pl.ds(first, half_width)
        hidden = nn(normed_ref[...], w_in_ref[:, :, cols].reshape(width, half_width))
        square = hidden * hidden
        bent = jnp.tanh(hidden * (root + (root * 0.044715) * square))
        half = 0.5 + 0.5 * bent
        slope = hidden * (2.0 * root + (6.0 * root * 0.044715) * square)
        slope = half + half * (slope * (1.0 - half))
        active_ref[:, cols] = (hidden * half).astype(BF16)
        w_out = w_out_ref[pl.ds(part * 8 + sub * 4, 4)].reshape(half_width, width)
        grad_ref[:, cols] = (nt(branch_ref[...], w_out) * slope).astype(BF16)
    cols = pl.ds(pl.multiple_of(part * width, width), width)
    grad_in = nn(normed_flip[...], grad_ref[:, cols]).astype(BF16)
    grad_out = nn(branch_flip[...], active_ref[:, cols]).astype(BF16).T

    def sends(which):
        pairs = [(in_slots, slots_ref.at[:, pl.ds(pl.multiple_of(which * 16, 16), 16), :])]
        for i, k in enumerate(range(0, 32, 4)):
            pairs.append((out_slots.at[i], slots_ref.at[k + which, 64:, :]))
        return [pltpu.make_async_copy(*pair, sems.at[i]) for i, pair in enumerate(pairs)]

    @pl.when(part > 0)
    def _():
        for copy in sends(part - 1):
            copy.wait()

    for k, block in enumerate(CODES):
        in_slots[k] = grad_in[16 * block : 16 * block + 16]
    for i, k in enumerate(range(0, 32, 4)):
        block = CODES[k]
        out_slots[i] = grad_out[64 * block : 64 * block + 64]
    for copy in sends(part):
        copy.start()

    @pl.when(part == parts - 1)
    def _():
        segments = dec_ref[...].astype(F32)
        columns = token_columns(segments)
        total_ref[...] = jnp.zeros_like(total_ref)
        w_in, w_out = w_in_ref[...].reshape(width, ff), w_out_ref[...].reshape(ff, width)
        for t, rows in enumerate(tiles):
            values = after_ref[rows, :].astype(F32)
            result_ref[rows, :] = (values + nn(active_ref[rows, :], w_out)).astype(BF16)
            grad, terms = norm_back(values, gains_ref[2:3, :], nt(grad_ref[rows, :], w_in))
            branch_b_ref[rows, :] = (branch_ref[rows, :].astype(F32) + grad).astype(BF16)
            own = segments[t * STEP_ROWS : (t + 1) * STEP_ROWS]
            gain_sums(terms, own, total_ref, square_ref.at[t])
        for r in range(count):
            own = slice(r * length, (r + 1) * length)
            products = gram(active_ref[own, :]) * gram(branch_ref[own, :])
            products = products + gram(grad_ref[own, :]) * gram(normed_ref[own, :])
            token_ref[r // STEP_ROWS, r % STEP_ROWS : r % STEP_ROWS + 1, :] = same_sum(
                products, segments, columns, r
            )
        for copy in sends(part):
            copy.wait()


def score_grads(prob, grad_prob):
    prob = prob.astype(F32)
    dots = jnp.sum(prob * grad_prob, axis=0, keepdims=True)
    return prob * (grad_prob - dots)


def cross_backward_kernel(me_ref, branch_ref, middle_ref, memory_ref, attended_a_ref, input_ref,
                          query_ref, kv_ref, prob_ref, attended_ref, dec_ref, gains_ref,
                          weight_ref, grad_query_ref, grad_kv_ref, branch_a_ref, low_ref, high_ref,
                          total_ref, square_ref, grad_w, grad_attended):
    step = pl.program_id(0)
    mem_length = prob_ref.shape[2]
    length = prob_ref.shape[3] // 2
    width = branch_ref.shape[1]

    @pl.when(step == 0)
    def _():
        grad_w[...] = jnp.zeros_like(grad_w)
        total_ref[...] = jnp.zeros_like(total_ref)

    branch = branch_ref[...]
    grad_attended[...] = nt(branch, weight_ref[:, 4 * width :]).astype(BF16)

    def places(item):
        r, p = item
        rows, lanes = slice(r * length, (r + 1) * length), slice(p * LANES, (p + 1) * LANES)
        upper = slice(width + p * LANES, width + (p + 1) * LANES)
        return rows, slice(r * mem_length, (r + 1) * mem_length), lanes, upper

    def enter(item, _):
        rows, mem_rows, lanes, upper = places(item)
        grad_out = head_pair(grad_attended[rows, lanes])
        return grad_out, nt(kv_ref[mem_rows, upper], grad_out)

    def bend(item, given):
        r, p = item
        grad_out, grad_prob = given
        _, mem_rows, lanes, _ = places(item)
        grad_score = score_grads(prob_ref[r, p], grad_prob).astype(BF16)
        return grad_out, grad_score, kv_ref[mem_rows, lanes].T

    def leave(item, given):
        r, p = item
        grad_out, grad_score, key = given
        rows, mem_rows, lanes, upper = places(item)
        query = head_pair(query_ref[rows, lanes])
        grad_kv_ref[mem_rows, lanes] = nn(grad_score, query).astype(BF16)
        grad_kv_ref[mem_rows, upper] = nn(prob_ref[r, p], grad_out).astype(BF16)
        grad_query_ref[rows, lanes] = fold_pair(nn(key, grad_score), length)

    pipelined(row_pairs(STEP_ROWS), enter, bend, leave)
    grad_query = grad_query_ref[...]
    grad_normed = nt(grad_query, weight_ref[:, width : 2 * width])
    grad, terms = norm_back(middle_ref[...].astype(F32), gains_ref[1:2, :], grad_normed)
    branch_a = (branch.astype(F32) + grad).astype(BF16)
    branch_a_ref[...] = branch_a
    gain_sums(terms, step_rows(dec_ref, step, STEP_ROWS), total_ref, square_ref.at[0])
    grad_w[:, :width] += tn(attended_a_ref[...], branch_a)
    grad_w[:, width : 2 * width] += tn(input_ref[...], grad_query)
    grad_w[:, 2 * width : 4 * width] += tn(memory_ref[...], grad_kv_ref[...])
    grad_w[:, 4 * width :] += tn(attended_ref[...], branch)

    @pl.when(step == pl.num_programs(0) - 1)
    def _():
        store_slots(me_ref, low_ref, high_ref, partial(read_rows, grad_w))


def self_scores_kernel(branch_ref, qkv_ref, prob_ref, dec_ref, buckets_ref, weight_ref,
                       grad_qkv_ref, table_ref, table_square_ref, grad_attended, bands):
    step = pl.program_id(0)
    length = prob_ref.shape[2]
    width = branch_ref.shape[1]
    grad_attended[...] = nt(branch_ref[...], weight_ref[:, :width]).astype(BF16)

    @pl.when(step == 0)
    def _():
        table_ref[...] = jnp.zeros_like(table_ref)
        bands[...] = jnp.zeros_like(bands)

    row_i = lax.broadcasted_iota(jnp.int32, (length, length), 0)
    col_i = lax.broadcasted_iota(jnp.int32, (length, length), 1)
    flip = (row_i + col_i == length - 1).astype(F32).astype(BF16)
    columns = token_columns(step_rows(dec_ref, step, STEP_ROWS)).astype(BF16)
    turned = nn(flip, columns)

    members = [
        [
            jnp.broadcast_to((turned[:, r : r + 1] == float(e)).astype(F32), (length, length))
            for e in range(NSEG)
        ]
        for r in range(STEP_ROWS)
    ]

    def part(item, k):
        r, p = item
        lanes = slice(k * width + p * LANES, k * width + (p + 1) * LANES)
        return slice(r * length, (r + 1) * length), lanes

    def enter(item, _):
        grad_out = head_pair(grad_attended[part(item, 0)])
        return grad_out, nt(qkv_ref[part(item, 2)], grad_out)

    def bend(item, given):
        r, p = item
        grad_out, grad_prob = given
        grad_score = score_grads(prob_ref[r, p], grad_prob).astype(BF16)
        return grad_out, grad_score, jnp.concatenate([qkv_ref[part(item, 1)].T, flip], axis=0)

    def leave(item, given):
        r, p = item
        grad_out, grad_score, key = given
        query = head_pair(qkv_ref[part(item, 0)])
        grad_qkv_ref[part(item, 1)] = nn(grad_score, query).astype(BF16)
        grad_qkv_ref[part(item, 2)] = nn(prob_ref[r, p], grad_out).astype(BF16)
        both = nn(key, grad_score)
        grad_qkv_ref[part(item, 0)] = fold_pair(both[:length], length)
        return both[length:]

    def count_buckets(item, turned_score):
        r, p = item
        for h in range(2):
            own = turned_score[:, h * length : (h + 1) * length]
            own = pltpu.roll(own, 1, 1, stride=1, stride_axis=0)
            for e in range(NSEG):
                bands[r, 2 * p + h, e : e + 1, :] = jnp.sum(
                    own * members[r][e], axis=0, keepdims=True
                )

    pipelined(row_pairs(STEP_ROWS), enter, bend, leave, count_buckets)
    bucket = lax.broadcasted_iota(jnp.int32, (LANES, length), 0)
    near = (bucket == buckets_ref[...]).astype(F32)
    flat = bands[...].reshape(STEP_ROWS * H * 8, length)
    per_bucket = lax.dot_general(
        flat, near, (((1,), (1,)), ((), ())), preferred_element_type=F32,
        precision=lax.Precision.HIGHEST,
    ).reshape(STEP_ROWS, H, 8, LANES)
    table_ref[...] += jnp.sum(jnp.sum(per_bucket, axis=0), axis=1)
    squares = jnp.sum(jnp.sum(per_bucket * per_bucket, axis=1), axis=-1, keepdims=True)
    table_square_ref[0] = jnp.broadcast_to(squares, (STEP_ROWS, 8, LANES))


def self_weights_kernel(me_ref, branch_ref, tokens_ref, input_ref, grad_qkv_ref, dec_ref,
                        gains_ref, weight_ref, table_ref, total_b_ref, total_c_ref,
                        grad_tokens_ref, low_ref, high_ref, square_ref, grad_w, total_ref,
                        small_ref):
    step = pl.program_id(0)
    width = tokens_ref.shape[1]
    grad_qkv = grad_qkv_ref[...]
    grad_normed = nt(grad_qkv, weight_ref[...])
    grad, terms = norm_back(tokens_ref[...].astype(F32), gains_ref[0:1, :], grad_normed)
    grad_tokens_ref[...] = (branch_ref[...].astype(F32) + grad).astype(BF16)

    @pl.when(step == 0)
    def _():
        grad_w[...] = jnp.zeros_like(grad_w)
        total_ref[...] = jnp.zeros_like(total_ref)

    gain_sums(terms, step_rows(dec_ref, step, STEP_ROWS), total_ref, square_ref.at[0])
    flipped = input_ref[...].T
    for first in range(0, 3 * width, 256):
        grad_w[:, first : first + 256] += nn(flipped, grad_qkv_ref[:, first : first + 256])

    @pl.when(step == pl.num_programs(0) - 1)
    def _():
        bucket = lax.broadcasted_iota(jnp.int32, (LANES, width), 0)
        place = lax.broadcasted_iota(jnp.int32, (LANES, width), 1)
        spread = nn(table_ref[...].astype(BF16), (place // 16 == bucket).astype(F32).astype(BF16))
        head = lax.broadcasted_iota(jnp.int32, (H, width), 0)
        lane = lax.broadcasted_iota(jnp.int32, (H, width), 1)
        table = jnp.sum(jnp.where(lane % 16 == head, spread, 0.0), axis=0, keepdims=True)
        small = jnp.zeros((LANES, width), F32)
        row_i = lax.broadcasted_iota(jnp.int32, (LANES, width), 0)
        for k, line in enumerate((total_ref[...], total_b_ref[...], total_c_ref[...], table)):
            small = jnp.where(row_i == k, line, small)
        small_ref[...] = small.T

        def read(block):
            return jnp.concatenate(
                [read_rows(grad_w, block), read_rows(small_ref, block)], axis=1
            )

        store_slots(me_ref, low_ref, high_ref, read)


def pair_sum_kernel(low_ref, sent_ref, *refs):
    outs, (low, sent, total, load_sems, store_sems) = refs[:4], refs[4:]
    places = [pl.ds(4 * t, 4) for t in range(4)]
    lows = start_copies([(low_ref.at[p], low.at[p]) for p in places], load_sems.at[0])
    sents = start_copies([(sent_ref.at[p], sent.at[p]) for p in places], load_sems.at[1])
    stores = []
    for t, p in enumerate(places):
        lows[t].wait()
        sents[t].wait()
        total[p] = (low[p].astype(F32) + sent[p].astype(F32)).astype(BF16)
        stores.append(pltpu.make_async_copy(total.at[p], outs[t], store_sems.at[t]))
        stores[t].start()
    for store in stores:
        store.wait()


def pair_sum(low, sent, after):
    piece = shape_of((4,) + low.shape[1:], BF16)
    return pl.pallas_call(
        ignoring(pair_sum_kernel, 2, len(after)),
        out_shape=(piece,) * 4,
        in_specs=[pl.BlockSpec(memory_space=pl.ANY)] * (2 + len(after)),
        out_specs=[pl.BlockSpec(memory_space=pl.ANY)] * 4,
        scratch_shapes=[pltpu.VMEM(low.shape, BF16)] * 3
        + [pltpu.SemaphoreType.DMA((2, 4)), pltpu.SemaphoreType.DMA((4,))],
        compiler_params=pltpu.CompilerParams(vmem_limit_bytes=SHARED_LIMIT),
    )(in_hbm(low), sent, *after)


def plane_sum_kernel(*refs):
    own_ref, outs = refs[8], refs[9:]
    start = 0
    for group in (refs[:4], refs[4:8]):
        cols = slice(start, start + group[0].shape[2])
        start = cols.stop
        for s in range(4):
            total = sum(ref[s].astype(F32) for ref in group)
            if s == 0:
                own_ref[:, cols] = total
            else:
                outs[s - 1][:, cols] = total.astype(BF16)


def plane_sum(groups, after):
    line = (16, sum(group[0].shape[2] for group in groups))
    return small_call(
        plane_sum_kernel, [*groups[0], *groups[1]], after,
        (shape_of(line, F32),) + (shape_of(line, BF16),) * 3,
    )


def square_sum(values):
    return jnp.sum(jnp.sum(values * values, axis=0, keepdims=True), axis=1, keepdims=True)


def feed_end_kernel(sum_ref, hidden_ref, back_ref, square_ref):
    total = sum_ref[...].astype(F32)
    width = total.shape[1]
    for j in range(4):
        hidden_ref[:, j * width : (j + 1) * width] = total[16 * j : 16 * (j + 1)]
    back_ref[...] = total[64:]
    square_ref[...] = jnp.broadcast_to(square_sum(total), square_ref.shape)


def column_end_kernel(own_ref, b_ref, c_ref, d_ref, *refs):
    squares, outs, square_ref = refs[:1], refs[1:-1], refs[-1]
    total = own_ref[...] + b_ref[...].astype(F32)
    total = total + c_ref[...].astype(F32) + d_ref[...].astype(F32)
    start = 0
    for out in outs:
        out[...] = total[:, start : start + out.shape[1]]
        start += out.shape[1]
    square = square_sum(total)
    for given in squares:
        square = square + given[0:1, 0:1]
    square_ref[...] = jnp.broadcast_to(square, square_ref.shape)


def staged(kernel, ins, outs):
    def run(*refs):
        count = ins + outs
        given, inner, sems = refs[:count], refs[count : 2 * count], refs[2 * count]
        for copy in start_copies(list(zip(given[:ins], inner[:ins])), sems):
            copy.wait()
        kernel(*inner)
        for copy in start_copies(list(zip(inner[ins:], given[ins:])), sems):
            copy.wait()

    return run


def small_call(kernel, ins, after, outs):
    arrays = [*ins, *outs]
    return pl.pallas_call(
        ignoring(staged(kernel, len(ins), len(outs)), len(ins), len(after)),
        out_shape=outs,
        in_specs=[pl.BlockSpec(memory_space=pl.ANY)] * (len(ins) + len(after)),
        out_specs=[pl.BlockSpec(memory_space=pl.ANY)] * len(outs),
        scratch_shapes=[pltpu.VMEM(array.shape, array.dtype) for array in arrays]
        + [pltpu.SemaphoreType.DMA((len(arrays),))],
        compiler_params=pltpu.CompilerParams(vmem_limit_bytes=SHARED_LIMIT),
    )(*ins, *after)


def split_kernel(*refs):
    lines, (own_ref, rest_ref) = refs[:4], refs[4:]
    split = own_ref.shape[2]
    for s, line in enumerate(lines):
        own_ref[s] = line[:, :split]
        rest_ref[s] = line[:, split:]


def split_column(lines, split):
    rows, cols = lines[0].shape
    outs = [shape_of((4, rows, part), BF16) for part in (split, cols - split)]
    return small_call(split_kernel, lines, (), outs)


def pack_kernel(*refs):
    ins, (shard_ref, feed_ref) = refs[:11], refs[11:]
    width = ins[0].shape[1]
    start = 0
    for line in (*ins[:3], ins[10], *ins[3:8]):
        shard_ref[:, start : start + line.shape[1]] = line[...]
        start += line.shape[1]
    for j in range(ins[8].shape[1] // width):
        feed_ref[16 * j : 16 * (j + 1), :] = ins[8][:, j * width : (j + 1) * width]
    feed_ref[64:, :] = ins[9][...]


def pack(weights, small):
    width = weights[0].shape[1]
    outs = [shape_of((16, 8 * width + LANES), BF16), shape_of((128, width), BF16)]
    return small_call(pack_kernel, (*map(in_hbm, weights), small), (), outs)


def memory_backward_kernel(memory_ref, grad_kv_ref, mem_ref, weight_ref, grad_memory_ref,
                           token_ref):
    mem_length = mem_ref.shape[1]
    width = memory_ref.shape[1]
    for first in range(0, width, 256):
        rows = slice(first, first + 256)
        grad_memory_ref[:, rows] = nt(
            grad_kv_ref[...], weight_ref[rows, 2 * width : 4 * width]
        ).astype(BF16)
    count = memory_ref.shape[0] // mem_length
    segments = step_rows(mem_ref, pl.program_id(0), count)
    columns = token_columns(segments)
    for r in range(count):
        rows = slice(r * mem_length, (r + 1) * mem_length)
        products = gram(memory_ref[rows, :]) * gram(grad_kv_ref[rows, :])
        token_ref[0, r : r + 1, :] = same_sum(products, segments, columns, r)


def gram_kernel(*refs):
    pairs, dec_ref, token_ref = refs[:-2], refs[-2], refs[-1]
    length = dec_ref.shape[1]
    count = pairs[0].shape[0] // length
    segments = step_rows(dec_ref, pl.program_id(0), count)
    columns = token_columns(segments)
    for r in range(count):
        rows = slice(r * length, (r + 1) * length)
        products = sum(
            gram(left[rows, :]) * gram(right[rows, :])
            for left, right in zip(pairs[::2], pairs[1::2])
        )
        token_ref[0, r : r + 1, :] = same_sum(products, segments, columns, r)


def rows_spec(array, steps):
    shape = (array.shape[0] // steps,) + array.shape[1:]
    return pl.BlockSpec(shape, lambda i, *_: (i,) + (0,) * (len(shape) - 1))


def whole_spec(array):
    return pl.BlockSpec(array.shape, lambda i, *_: (0,) * len(array.shape))


def in_hbm(array):
    return pltpu.with_memory_space_constraint(array, pltpu.HBM)


def ignoring(kernel, first, count):
    return lambda *refs: kernel(*refs[:first], *refs[first + count :])


def call(kernel, steps, me, blocked, whole, pieces, outs_blocked, outs_whole, scratch, flops,
         order, after=(), limit=VMEM_LIMIT):
    ins, in_specs = [], []
    blocked, whole = list(blocked), list(whole)
    for kind in order[0]:
        array = (blocked if kind == "i" else whole).pop(0)
        ins.append(array)
        in_specs.append(rows_spec(array, steps) if kind == "i" else whole_spec(array))
    ins = [in_hbm(array) for array in ins]
    kernel = ignoring(kernel, len(ins) + len(pieces) + (me is not None), len(after))
    ins += [*pieces, *after]
    in_specs += [pl.BlockSpec(memory_space=pl.ANY)] * (len(pieces) + len(after))
    outs, out_specs = [], []
    outs_blocked, outs_whole = list(outs_blocked), list(outs_whole)
    for kind in order[1]:
        out = (outs_blocked if kind == "i" else outs_whole).pop(0)
        outs.append(out)
        if kind == "a":
            out_specs.append(pl.BlockSpec(memory_space=pl.ANY))
        else:
            out_specs.append(rows_spec(out, steps) if kind == "i" else whole_spec(out))
    moved = sum(math.prod(a.shape) * a.dtype.itemsize for a in ins + outs)
    prefetch = 0 if me is None else 1
    return pl.pallas_call(
        kernel,
        out_shape=outs,
        grid_spec=pltpu.PrefetchScalarGridSpec(
            num_scalar_prefetch=prefetch,
            grid=(steps,),
            in_specs=in_specs,
            out_specs=out_specs,
            scratch_shapes=scratch,
        ),
        compiler_params=pltpu.CompilerParams(
            dimension_semantics=("arbitrary",), vmem_limit_bytes=limit
        ),
        cost_estimate=pl.CostEstimate(flops=flops, bytes_accessed=moved, transcendentals=0),
    )(*(() if me is None else (me,)), *ins)


FINE = ("z", "y", "core", "x")


def shape_of(shape, dtype):
    return jax.ShapeDtypeStruct(shape, dtype)


def kept(shape, dtype):
    return pltpu.HBM(shape, dtype)


def shift(array, mask):
    return lax.ppermute(array, FINE, [(i, i ^ mask) for i in range(32)])


def hold(array, after):
    return lax.optimization_barrier((array, after))[0]


def pack_feed(hidden, back):
    width = back.shape[1]
    hidden = hidden.reshape(-1, 16, 4, width).transpose(0, 2, 1, 3).reshape(-1, 64, width)
    return jnp.concatenate([hidden, back.reshape(-1, 64, width)], axis=1)


def unpack_feed(blocks):
    width = blocks.shape[2]
    hidden = blocks[:, :64].reshape(-1, 4, 16, width).transpose(0, 2, 1, 3)
    return hidden.reshape(-1, 4 * width), blocks[:, 64:].reshape(-1, width)


def small_row(gains, table):
    table = jnp.pad(table.reshape(-1, H), ((0, 0), (0, 16 - H)))
    row = jnp.concatenate([gain.reshape(-1, 16) for gain in gains] + [table], axis=1)
    row = jnp.pad(row, ((0, 0), (0, LANES - row.shape[1])))
    return jnp.pad(row[:, None], ((0, 0), (0, 15), (0, 0))).reshape(-1, LANES)


def in_order(slots):
    return slots[jnp.array([CODES.index(block) for block in range(32)])]


def as_rows(slots):
    return in_order(slots).reshape(-1, slots.shape[2]).astype(F32)


def shift_plane(pieces):
    return [shift(piece, mask) for piece, mask in zip(pieces, PLANE[1:])]


def shift_column(pieces):
    return [shift(piece, code) for piece, code in zip(pieces, COLUMN[1:])]


class Near:
    axes = FINE

    def __init__(self, weights):
        self.me = lax.axis_index(FINE)
        small = small_row(weights[10:13], weights[13])
        shard, feed = pack(weights[:10], small)
        self.feed = lax.all_gather(feed, FINE, axis=0)
        column = [shard, *shift_column([shard] * 3)]
        own, rest = split_column(column, 3 * weights[0].shape[1] + LANES)
        plane = [own, *shift_plane([own] * 3)]
        self.plane = [rest, *shift_plane([rest] * 3)]
        self.own = plane + [shift(piece, 2) for piece in plane]

    def cross(self, after):
        plane = [hold(piece, after) for piece in self.plane]
        return plane + [shift(piece, 2) for piece in plane]

    def feed_core(self, slots):
        return lax.psum_scatter(slots.reshape((2, 4, 4) + slots.shape[1:]), "core")

    def feed_plane(self, slots):
        return lax.psum_scatter(slots, ("y", "x"))

    def feed_column(self, slots):
        return lax.psum_scatter(slots, "z")


class Far:
    axes = ("wide", "narrow")
    me = 0

    def __init__(self, weights):
        weights = [lax.all_gather(w, self.axes, axis=0, tiled=True) for w in weights]
        self.take(weights)

    def take(self, weights):
        self.own = self.pieces(*weights[:3], small_row(weights[10:13], weights[13]))
        self.rest = self.pieces(*weights[3:8])
        self.feed = pack_feed(weights[8], weights[9])

    def pieces(self, *parts):
        blocks = jnp.concatenate(parts, axis=1).reshape(32, 16, -1)[jnp.array(CODES)]
        return [blocks[4 * t : 4 * t + 4] for t in range(8)]

    def cross(self, after):
        return self.rest

    def feed_core(self, slots):
        return slots

    feed_plane = feed_column = feed_core


def on_device(near, tokens, memory, cotangent, dec_segments, mem_segments, padding, buckets,
              *weights):
    way = (Near if near else Far)(weights)
    result, grad_tokens, grad_memory, grads, examples, square = local_part(
        way, tokens, memory, cotangent, dec_segments, mem_segments, padding, buckets
    )
    if near:
        sent = lax.all_to_all(square, FINE, 0, 0, tiled=True)
        global_norm = jnp.sum(sent[:, 0])
    else:
        grads = [lax.psum_scatter(g, way.axes, scatter_dimension=0, tiled=True) for g in grads]
        global_norm = lax.psum(sum(jnp.sum(g * g) for g in grads), way.axes)
    return (result, grad_tokens, grad_memory, *grads, examples, global_norm / COUNT)


def local_part(way, tokens, memory, cotangent, dec_segments, mem_segments, padding, buckets):
    seqs, length, width = tokens.shape
    mem_length = memory.shape[1]
    steps = seqs // STEP_ROWS
    small_steps = seqs // SMALL_ROWS
    dec, mem = seqs * length, seqs * mem_length
    step_dec = STEP_ROWS * length
    ff = 4 * width

    buckets = buckets[None]
    tokens2, memory2, cotangent2 = (
        array.reshape(-1, width) for array in (tokens, memory, cotangent)
    )
    dma = pltpu.SemaphoreType.DMA

    me = jnp.full((1,), way.me, jnp.int32)
    flops = 2 * dec * width * width

    input_a, qkv_a, prob_a, attended_a, self_w, gains = call(
        self_forward_kernel, small_steps, me, (tokens2,), (dec_segments, padding, buckets), way.own,
        (
            kept((dec, width), BF16),
            kept((dec, 3 * width), BF16),
            kept((seqs, PAIRS, length, 2 * length), BF16),
            kept((dec, width), BF16),
        ),
        (kept((width, 3 * width), BF16), kept((8, width), F32)),
        [pltpu.VMEM((PAIRS, length, 2 * length), F32), pltpu.VMEM((width, LANES), BF16), dma((64,))],
        6 * flops, ("iwww", "iiiiww"), (), SHARED_LIMIT,
    )
    kv_b, cross_w = call(
        memory_forward_kernel, small_steps, me, (memory2,), (), way.cross(attended_a),
        (kept((mem, 2 * width), BF16),), (kept((width, 5 * width), BF16),), [dma((32,))],
        4 * flops, ("i", "iw"), (), SHARED_LIMIT,
    )
    middle, input_b, query_b, prob_b, attended_b, after_cross = call(
        cross_forward_kernel, small_steps, None, (tokens2, attended_a, kv_b),
        (dec_segments, mem_segments, gains, cross_w), (),
        (
            kept((dec, width), BF16),
            kept((dec, width), BF16),
            kept((dec, width), BF16),
            kept((seqs, PAIRS, mem_length, 2 * length), BF16),
            kept((dec, width), BF16),
            kept((dec, width), BF16),
        ),
        (), [], 6 * flops, ("iiiwwww", "iiiiii"),
    )
    total, square = kept((1, width), F32), shape_of((steps, 4 * STEP_ROWS, LANES), F32)
    token_shape = shape_of((steps, 8, length), F32)
    small_token = shape_of((small_steps, 8, length), F32)
    result, branch_b, feed_slots, gain_c, square_c, token_c = call(
        feed_kernel, ff // width, None, (),
        (after_cross, cotangent2, dec_segments, padding, gains), (way.feed,), (),
        (
            shape_of((dec, width), BF16),
            kept((dec, width), BF16),
            shape_of((32, 128, width), BF16),
            total,
            square,
            token_shape,
        ),
        [
            pltpu.VMEM((32, 16, ff), BF16),
            pltpu.VMEM((32, 64, width), BF16),
            *[pltpu.VMEM((dec, width), BF16)] * 2,
            *[pltpu.VMEM((width, dec), BF16)] * 2,
            *[pltpu.VMEM((dec, ff), BF16)] * 2,
            pltpu.VMEM((32, 16, width), BF16),
            pltpu.VMEM((8, 64, width), BF16),
            dma((4, 2)),
            dma((9,)),
        ],
        26 * flops, ("wwwww", "wwawww"),
    )
    feed_sum = way.feed_core(feed_slots)
    slot = shape_of((16, 16, 5 * width), BF16)
    grad_query_b, grad_kv_b, branch_a, cross_low, cross_high, gain_b, square_b = call(
        cross_backward_kernel, steps, me,
        (branch_b, middle, memory2, attended_a, input_b, query_b, kv_b, prob_b, attended_b),
        (dec_segments, gains, cross_w), (),
        (
            kept((dec, width), BF16),
            kept((mem, 2 * width), BF16),
            kept((dec, width), BF16),
            square,
        ),
        (kept(slot.shape, BF16), slot, total),
        [pltpu.VMEM((width, 5 * width), F32), pltpu.VMEM((step_dec, width), BF16)],
        20 * flops, ("iiiiiiiiiwww", "iiiwwwi"),
    )
    feed_sum = way.feed_plane(hold(feed_sum, grad_query_b))
    near = isinstance(way, Near)
    if near:
        sent = shift(cross_high, 2)
    grad_qkv_a, table, table_square = call(
        self_scores_kernel, steps, None, (branch_a, qkv_a, prob_a),
        (dec_segments, buckets, cross_w), (),
        (kept((dec, 3 * width), BF16), shape_of((steps, STEP_ROWS, 8, LANES), F32)),
        (kept((H, LANES), F32),),
        [pltpu.VMEM((step_dec, width), BF16), pltpu.VMEM((STEP_ROWS, H, 8, length), F32)],
        10 * flops, ("iiiwww", "iwi"),
    )
    waits = ()
    if near:
        cross_parts = pair_sum(cross_low, sent, (grad_qkv_a,))
        crossed = shift_plane(cross_parts[1:])
        waits = (cross_parts[0],)
    slot = shape_of((16, 16, 3 * width + LANES), BF16)
    grad_tokens, self_low, self_high, square_a = call(
        self_weights_kernel, steps, me, (branch_a, tokens2, input_a, grad_qkv_a),
        (dec_segments, gains, self_w, table, gain_b, gain_c), (),
        (shape_of((dec, width), BF16), square),
        (kept(slot.shape, BF16), slot),
        [
            pltpu.VMEM((width, 3 * width), F32),
            pltpu.VMEM((1, width), F32),
            pltpu.VMEM((width, LANES), F32),
        ],
        7 * flops, ("iiiiwwwwww", "iwwi"), waits,
    )

    def grams(pairs, *after):
        (tokens_part,) = call(
            gram_kernel, small_steps, None, pairs, (dec_segments,), (), (small_token,), (), [],
            2 * flops, ("i" * len(pairs) + "w", "i"), after, SHARED_LIMIT,
        )
        return tokens_part

    def fill_cross(*after):
        return grams((input_b, grad_query_b, attended_b, branch_b), *after)

    def fill_self(*after):
        return grams((input_a, grad_qkv_a, attended_a, branch_a), *after)

    def fill_memory(*after):
        return call(
            memory_backward_kernel, small_steps, None, (memory2, grad_kv_b),
            (mem_segments, cross_w), (),
            (shape_of((mem, width), BF16), shape_of((small_steps, 8, mem_length), F32)), (), [],
            10 * flops, ("iiww", "ii"), after, SHARED_LIMIT,
        )

    if near:
        sent = shift(hold(self_high, crossed[0]), 2)
        token_b = fill_cross(self_low)
        self_parts = pair_sum(self_low, sent, (token_b,))
        self_sent = shift_plane(self_parts[1:])
        feed_sum = hold(feed_sum, token_b)
        token_a = fill_self(self_parts[0], feed_sum)
        feed_sum = way.feed_column(feed_sum)
        groups = [[self_parts[0], *self_sent], [cross_parts[0], *crossed]]
        own, *rest = plane_sum(groups, (token_a,))
        line_sent = shift_column(rest)
        grad_memory, token_m = fill_memory(own)
        feed_sum = hold(feed_sum, token_m).reshape(128, width)
        grad_hidden, grad_back, square = small_call(
            feed_end_kernel, (feed_sum,), (token_m,),
            [shape_of((16, ff), F32), shape_of((64, width), F32), shape_of((8, LANES), F32)],
        )
        line = shape_of((slot.shape[1], width), F32)
        *parts, square = small_call(
            column_end_kernel, (own, *line_sent, square), (token_m,),
            [line] * 3 + [shape_of((16, LANES), F32)] + [line] * 5 + [shape_of((32, LANES), F32)],
        )
        self_grads, small, cross_grads = parts[:3], parts[3], parts[4:]
        token_m = hold(token_m, square)
    else:
        token_b, token_a = fill_cross(), fill_self()
        grad_memory, token_m = fill_memory()
        cross_sum = as_rows(jnp.concatenate([cross_low, cross_high]))
        self_sum = as_rows(jnp.concatenate([self_low, self_high]))
        cross_grads = [cross_sum[:, k * width : (k + 1) * width] for k in range(5)]
        self_grads = [self_sum[:, k * width : (k + 1) * width] for k in range(3)]
        small = self_sum[:, 3 * width :]
        grad_hidden, grad_back = unpack_feed(in_order(feed_sum).astype(F32))
        square = None
    grads = self_grads + cross_grads + [grad_hidden, grad_back]
    grads += [small[:, k] for k in range(3)]
    grads.append(small[:, 3].reshape(-1, 16)[:, :H].reshape(-1))

    def row_parts(parts, count):
        return parts[:, :count].reshape(seqs, -1)

    def by_example(part, segments):
        hits = segments[:, None, :] == lax.broadcasted_iota(jnp.int32, (1, NSEG, 1), 1)
        return jnp.sum(jnp.where(hits, part[:, None, :], 0.0), axis=-1)

    token_d = row_parts(token_a + token_b, SMALL_ROWS) + row_parts(token_c, STEP_ROWS)
    examples = by_example(token_d, dec_segments)
    examples = examples + by_example(row_parts(token_m, SMALL_ROWS), mem_segments)
    squares = (square_a + square_b + square_c)[:, :, 0].reshape(seqs, NSEG)
    examples = examples + squares + table_square[..., :NSEG, 0].reshape(seqs, NSEG)
    return (
        result.reshape(tokens.shape),
        grad_tokens.reshape(tokens.shape),
        grad_memory.reshape(memory.shape),
        grads,
        examples / COUNT,
        square,
    )


def solution(mesh):
    near = tuple(mesh.shape.values()) == (16, 2)
    if near:
        mesh = jax.sharding.Mesh(mesh.devices.reshape(4, 2, 2, 2), FINE)
    axes = tuple(mesh.axis_names)
    rows = P(axes)
    arrays, weights, vectors = (P(axes, None, None),) * 3, (P(axes, None),) * 10, (rows,) * 4
    placed = arrays + (P(axes, None),) * 3 + (P(),) + weights + vectors
    return jax.shard_map(
        partial(on_device, near),
        mesh=mesh,
        in_specs=placed,
        out_specs=arrays + weights + vectors + (P(axes, None), P()),
        check_vma=False,
    )
```

```python
import math
from functools import partial

import jax
import jax.numpy as jnp
from jax import lax
from jax.experimental import pallas as pl
from jax.experimental.pallas import tpu as pltpu
from jax.sharding import PartitionSpec as P

H = 8
DH = 64
NB = 32
NSEG = 4
COUNT = 4196096
EPSILON = 1e-06
FLOOR = -1e30
F32 = jnp.float32
BF16 = jnp.bfloat16
PAIRS = H // 2
LANES = 128
STEP_ROWS = 4
SMALL_ROWS = 4
VMEM_LIMIT = 60 * 2**20
SHARED_LIMIT = 48 * 2**20

COLUMN = (0, 8, 16, 24)
PLANE = (0, 1, 4, 5)
CODES = tuple(2 * c + mask + z for c in (0, 1) for mask in PLANE for z in COLUMN)


def nn(left, right):
    return lax.dot_general(left, right, (((1,), (0,)), ((), ())), preferred_element_type=F32)


def nt(left, right):
    return lax.dot_general(left, right, (((1,), (1,)), ((), ())), preferred_element_type=F32)


def tn(left, right):
    return lax.dot_general(left, right, (((0,), (0,)), ((), ())), preferred_element_type=F32)


def inverse_root(values):
    return lax.rsqrt(jnp.mean(values * values, axis=-1, keepdims=True) + EPSILON)


def head_masks(values):
    low = (lax.broadcasted_iota(jnp.int32, (1, LANES), 1) < DH).astype(BF16)
    return values * low, values * (1 - low)


def head_pair(values):
    return jnp.concatenate(head_masks(values), axis=0)


def fold_pair(both, queries):
    own = jnp.concatenate([both[:DH, :queries], both[DH:, queries:]], axis=0)
    return own.astype(BF16).T


def block_rows(block):
    return pl.ds(pl.multiple_of(block * 16, 16), 16)


def start_copies(pairs, sems):
    copies = [pltpu.make_async_copy(*pair, sems.at[i]) for i, pair in enumerate(pairs)]
    for copy in copies:
        copy.start()
    return copies


def column_pairs(me_ref, pieces, weight_ref):
    return [
        (piece, weight_ref.at[:, (me_ref[0] ^ CODES[4 * t]) & 7]) for t, piece in enumerate(pieces)
    ]


def read_rows(grad_w, block):
    return grad_w[block_rows(block), :].astype(BF16)


def store_slots(me_ref, low_ref, high_ref, read):
    for k, code in enumerate(CODES):
        target = low_ref if k < 16 else high_ref
        target[k % 16] = read(me_ref[0] ^ code)


def softmax_columns(scores):
    shifted = jnp.exp(scores - jnp.max(scores, axis=0, keepdims=True))
    return (shifted * (1.0 / jnp.sum(shifted, axis=0, keepdims=True))).astype(BF16)


def step_rows(ref, step, count):
    whole = ref[...].astype(F32)
    rows = whole[:count]
    for s in range(1, whole.shape[0] // count):
        rows = jnp.where(step == s, whole[s * count : (s + 1) * count], rows)
    return rows


def token_columns(lines):
    pad = 8 - lines.shape[0] % 8
    return jnp.concatenate([lines] + [lines[:1]] * (pad % 8), axis=0).T


def member_lines(lines):
    count, length = lines.shape
    codes = jnp.concatenate([lines[r : r + 1] + float(NSEG * r) for r in range(count)], axis=1)
    places = lax.broadcasted_iota(jnp.int32, (NSEG * count, count * length), 0).astype(F32)
    return (codes == places).astype(F32).astype(BF16)


def same_sum(products, lines, columns, r):
    same = columns[:, r : r + 1] == lines[r : r + 1]
    return jnp.sum(jnp.where(same, products, 0.0), axis=0, keepdims=True)


def pipelined(items, *stages):
    state = {}
    for tick in range(len(items) + len(stages) - 1):
        for depth, stage in enumerate(stages):
            n = tick - depth
            if 0 <= n < len(items):
                state[n] = stage(items[n], state.get(n))


def row_pairs(count):
    return [(r, p) for r in range(count) for p in range(PAIRS)]


def gram(left):
    return nt(left, left)


def self_forward_kernel(me_ref, tokens_ref, dec_ref, padding_ref, buckets_ref, *refs):
    pieces, refs = refs[:8], refs[8:]
    input_ref, qkv_ref, prob_ref, attended_ref, weight_ref, gains_ref = refs[:6]
    bias_ref, sems = refs[6:]
    length = dec_ref.shape[1]
    width = tokens_ref.shape[1]

    @pl.when(pl.program_id(0) == 0)
    def _():
        for copy in start_copies(column_pairs(me_ref, pieces, weight_ref), sems):
            copy.wait()
        small_lines = weight_ref[:, :, :, 3 * width :].reshape(width, LANES)
        first = lax.broadcasted_iota(jnp.int32, (32, width), 1)
        pick = first == 16 * lax.broadcasted_iota(jnp.int32, (32, width), 0)
        small = nn(pick.astype(F32).astype(BF16), small_lines).astype(BF16)
        lane = lax.broadcasted_iota(jnp.int32, (LANES, width), 0)
        feature = lax.broadcasted_iota(jnp.int32, (LANES, width), 1)
        block = lax.broadcasted_iota(jnp.int32, (32, width), 0)
        lines = []
        for k in range(4):
            spread = nn(small, (lane == 16 * k + feature % 16).astype(F32).astype(BF16))
            lines.append(
                jnp.sum(jnp.where(block == first // 16, spread, 0.0), axis=0, keepdims=True)
            )
        gains_ref[...] = jnp.concatenate(lines + lines, axis=0)
        place = lax.broadcasted_iota(jnp.int32, (H, width), 1) % 16
        head = lax.broadcasted_iota(jnp.int32, (H, width), 0)
        table = jnp.where(place == head, lines[3], 0.0).astype(BF16)
        bucket = lax.broadcasted_iota(jnp.int32, (width, length), 0) // 16
        curves = nn(table, (bucket == buckets_ref[...]).astype(F32).astype(BF16))
        for h in range(H):
            curve = jnp.broadcast_to(curves[h : h + 1, :], (length, length))
            lanes = slice((h % 2) * length, (h % 2 + 1) * length)
            bias_ref[h // 2, :, lanes] = pltpu.roll(curve, 0, 1, stride=1, stride_axis=0)

    values = tokens_ref[...].astype(F32)
    normed = (values * inverse_root(values) * gains_ref[0:1, :]).astype(BF16)
    input_ref[...] = normed
    for first in range(0, 3 * width, 256):
        cols = slice(first, first + 256)
        qkv_ref[:, cols] = nn(
            normed, weight_ref[:, :, :, cols].reshape(width, 256)
        ).astype(BF16)

    step = pl.program_id(0)
    count = tokens_ref.shape[0] // length
    segments, real = step_rows(dec_ref, step, count), step_rows(padding_ref, step, count)
    segment_columns, real_columns = token_columns(segments), token_columns(real)
    key_i = lax.broadcasted_iota(jnp.int32, (length, length), 0)
    query_i = lax.broadcasted_iota(jnp.int32, (length, length), 1)

    masks = []
    for r in range(count):
        allowed = (segment_columns[:, r : r + 1] == segments[r : r + 1]) & (key_i <= query_i)
        allowed = allowed & ((real_columns[:, r : r + 1] > 0.0) | (key_i == query_i))
        mask = jnp.where(allowed, 0.0, FLOOR)
        masks.append(jnp.concatenate([mask, mask], axis=1))

    def part(item, k):
        r, p = item
        return qkv_ref[r * length : (r + 1) * length, k * width + p * LANES : k * width + (p + 1) * LANES]

    def scores(item, _):
        return nt(part(item, 1), head_pair(part(item, 0)))

    def weigh(item, score):
        r, p = item
        prob = softmax_columns(score + bias_ref[p] + masks[r])
        prob_ref[r, p] = prob
        return prob, part(item, 2).T

    def mix(item, given):
        r, p = item
        prob, value = given
        rows, lanes = slice(r * length, (r + 1) * length), slice(p * LANES, (p + 1) * LANES)
        attended_ref[rows, lanes] = fold_pair(nn(value, prob), length)

    pipelined(row_pairs(count), scores, weigh, mix)


def cross_forward_kernel(me_ref, tokens_ref, attended_a_ref, memory_ref, dec_ref, mem_ref,
                         gains_ref, *refs):
    pieces, refs = refs[:8], refs[8:]
    (middle_ref, input_ref, query_ref, kv_ref, prob_ref, attended_ref, after_ref, weight_ref,
     sems) = refs
    mem_length, length = mem_ref.shape[1], dec_ref.shape[1]
    width = tokens_ref.shape[1]

    @pl.when(pl.program_id(0) == 0)
    def _():
        for copy in start_copies(column_pairs(me_ref, pieces, weight_ref), sems):
            copy.wait()

    def weight(k):
        return weight_ref[:, :, :, k * width : (k + 1) * width].reshape(width, width)

    for k in range(2):
        kv_ref[:, k * width : (k + 1) * width] = nn(memory_ref[...], weight(k + 2)).astype(BF16)
    values = tokens_ref[...].astype(F32) + nn(attended_a_ref[...], weight(0))
    middle_ref[...] = values.astype(BF16)
    normed = (values * inverse_root(values) * gains_ref[1:2, :]).astype(BF16)
    input_ref[...] = normed
    query_ref[...] = nn(normed, weight(1)).astype(BF16)

    step = pl.program_id(0)
    count = tokens_ref.shape[0] // length
    segments = step_rows(dec_ref, step, count)
    mem_columns = token_columns(step_rows(mem_ref, step, count))

    masks = []
    for r in range(count):
        mask = jnp.where(mem_columns[:, r : r + 1] == segments[r : r + 1], 0.0, FLOOR)
        masks.append(jnp.concatenate([mask, mask], axis=1))

    def places(item):
        r, p = item
        rows, lanes = slice(r * length, (r + 1) * length), slice(p * LANES, (p + 1) * LANES)
        upper = slice(width + p * LANES, width + (p + 1) * LANES)
        return rows, slice(r * mem_length, (r + 1) * mem_length), lanes, upper

    def scores(item, _):
        rows, mem_rows, lanes, _ = places(item)
        return nt(kv_ref[mem_rows, lanes], head_pair(query_ref[rows, lanes]))

    def weigh(item, score):
        r, p = item
        _, mem_rows, _, upper = places(item)
        prob = softmax_columns(score + masks[r])
        prob_ref[r, p] = prob
        return prob, kv_ref[mem_rows, upper].T

    def mix(item, given):
        rows, _, lanes, _ = places(item)
        prob, value = given
        attended_ref[rows, lanes] = fold_pair(nn(value, prob), length)

    pipelined(row_pairs(count), scores, weigh, mix)
    after = values + nn(attended_ref[...], weight(4))
    after_ref[...] = after.astype(BF16)


def norm_back(values, gain, grad_normed):
    inverse = inverse_root(values)
    scaled = values * inverse
    upper = grad_normed * gain
    grad = inverse * (upper - scaled * jnp.mean(upper * scaled, axis=-1, keepdims=True))
    return grad, grad_normed * scaled


def gain_sums(terms, segments, total_ref, square_ref):
    sums = nn(member_lines(segments), terms.astype(BF16))
    total_ref[...] += jnp.sum(sums, axis=0, keepdims=True)
    square = jnp.sum(sums * sums, axis=1, keepdims=True)
    square_ref[...] = jnp.broadcast_to(square, square_ref.shape)


def feed_kernel(after_ref, cotangent_ref, dec_ref, padding_ref, gains_ref, gathered_ref,
                result_ref, branch_b_ref, slots_ref, total_ref, square_ref, token_ref, w_in_ref,
                w_out_ref, normed_ref, branch_ref, normed_flip, branch_flip, active_ref, grad_ref,
                in_slots, out_slots, load_sems, sems):
    part = pl.program_id(0)
    parts = pl.num_programs(0)
    count, length = dec_ref.shape
    dec, width = after_ref.shape
    ff = w_in_ref.shape[2]
    tile = STEP_ROWS * length
    tiles = [slice(t * tile, (t + 1) * tile) for t in range(dec // tile)]

    def loads(which):
        rows = pl.ds(pl.multiple_of(which * 16, 16), 16)
        cols = pl.ds(pl.multiple_of(which * width, width), width)
        blocks = pl.ds(which * 8, 8)
        pairs = (
            (gathered_ref.at[:, rows, :], w_in_ref.at[:, :, cols]),
            (gathered_ref.at[blocks, 64:, :], w_out_ref.at[blocks]),
        )
        return [
            pltpu.make_async_copy(*pair, load_sems.at[which, i]) for i, pair in enumerate(pairs)
        ]

    @pl.when(part == 0)
    def _():
        for which in range(ff // width):
            for copy in loads(which):
                copy.start()
        real = token_columns(padding_ref[...].astype(F32))
        for r in range(count):
            rows = slice(r * length, (r + 1) * length)
            branch_ref[rows, :] = (
                cotangent_ref[rows, :].astype(F32) * real[:, r : r + 1]
            ).astype(BF16)
        for rows in tiles:
            values = after_ref[rows, :].astype(F32)
            normed = (values * inverse_root(values) * gains_ref[2:3, :]).astype(BF16)
            normed_ref[rows, :] = normed
            normed_flip[:, rows] = normed.T
            branch_flip[:, rows] = branch_ref[rows, :].T

    for copy in loads(part):
        copy.wait()
    root = 0.7978845608028654
    half_width = width // 2
    for sub in range(2):
        first = pl.multiple_of(part * width + sub * half_width, half_width)
        cols = pl.ds(first, half_width)
        hidden = nn(normed_ref[...], w_in_ref[:, :, cols].reshape(width, half_width))
        square = hidden * hidden
        bent = jnp.tanh(hidden * (root + (root * 0.044715) * square))
        half = 0.5 + 0.5 * bent
        slope = hidden * (2.0 * root + (6.0 * root * 0.044715) * square)
        slope = half + half * (slope * (1.0 - half))
        active_ref[:, cols] = (hidden * half).astype(BF16)
        w_out = w_out_ref[pl.ds(part * 8 + sub * 4, 4)].reshape(half_width, width)
        grad_ref[:, cols] = (nt(branch_ref[...], w_out) * slope).astype(BF16)
    cols = pl.ds(pl.multiple_of(part * width, width), width)
    grad_in = nn(normed_flip[...], grad_ref[:, cols]).astype(BF16)
    grad_out = nn(branch_flip[...], active_ref[:, cols]).astype(BF16).T

    def sends(which):
        pairs = [(in_slots, slots_ref.at[:, pl.ds(pl.multiple_of(which * 16, 16), 16), :])]
        for i, k in enumerate(range(0, 32, 4)):
            pairs.append((out_slots.at[i], slots_ref.at[k + which, 64:, :]))
        return [pltpu.make_async_copy(*pair, sems.at[i]) for i, pair in enumerate(pairs)]

    @pl.when(part > 0)
    def _():
        for copy in sends(part - 1):
            copy.wait()

    for k, block in enumerate(CODES):
        in_slots[k] = grad_in[16 * block : 16 * block + 16]
    for i, k in enumerate(range(0, 32, 4)):
        block = CODES[k]
        out_slots[i] = grad_out[64 * block : 64 * block + 64]
    for copy in sends(part):
        copy.start()

    @pl.when(part == parts - 1)
    def _():
        segments = dec_ref[...].astype(F32)
        columns = token_columns(segments)
        total_ref[...] = jnp.zeros_like(total_ref)
        w_in, w_out = w_in_ref[...].reshape(width, ff), w_out_ref[...].reshape(ff, width)
        for t, rows in enumerate(tiles):
            values = after_ref[rows, :].astype(F32)
            result_ref[rows, :] = (values + nn(active_ref[rows, :], w_out)).astype(BF16)
            grad, terms = norm_back(values, gains_ref[2:3, :], nt(grad_ref[rows, :], w_in))
            branch_b_ref[rows, :] = (branch_ref[rows, :].astype(F32) + grad).astype(BF16)
            own = segments[t * STEP_ROWS : (t + 1) * STEP_ROWS]
            gain_sums(terms, own, total_ref, square_ref.at[t])
        for r in range(count):
            own = slice(r * length, (r + 1) * length)
            products = gram(active_ref[own, :]) * gram(branch_ref[own, :])
            products = products + gram(grad_ref[own, :]) * gram(normed_ref[own, :])
            token_ref[r // STEP_ROWS, r % STEP_ROWS : r % STEP_ROWS + 1, :] = same_sum(
                products, segments, columns, r
            )
        for copy in sends(part):
            copy.wait()


def score_grads(prob, grad_prob):
    prob = prob.astype(F32)
    dots = jnp.sum(prob * grad_prob, axis=0, keepdims=True)
    return prob * (grad_prob - dots)


def cross_backward_kernel(me_ref, branch_ref, middle_ref, memory_ref, attended_a_ref, input_ref,
                          query_ref, kv_ref, prob_ref, attended_ref, dec_ref, gains_ref,
                          weight_ref, grad_query_ref, grad_kv_ref, branch_a_ref, low_ref, high_ref,
                          total_ref, square_ref, grad_w, grad_attended):
    step = pl.program_id(0)
    mem_length = prob_ref.shape[2]
    length = prob_ref.shape[3] // 2
    width = branch_ref.shape[1]

    @pl.when(step == 0)
    def _():
        grad_w[...] = jnp.zeros_like(grad_w)
        total_ref[...] = jnp.zeros_like(total_ref)

    branch = branch_ref[...]
    grad_attended[...] = nt(branch, weight_ref[:, 4 * width :]).astype(BF16)

    def places(item):
        r, p = item
        rows, lanes = slice(r * length, (r + 1) * length), slice(p * LANES, (p + 1) * LANES)
        upper = slice(width + p * LANES, width + (p + 1) * LANES)
        return rows, slice(r * mem_length, (r + 1) * mem_length), lanes, upper

    def enter(item, _):
        rows, mem_rows, lanes, upper = places(item)
        grad_out = head_pair(grad_attended[rows, lanes])
        return grad_out, nt(kv_ref[mem_rows, upper], grad_out)

    def bend(item, given):
        r, p = item
        grad_out, grad_prob = given
        _, mem_rows, lanes, _ = places(item)
        grad_score = score_grads(prob_ref[r, p], grad_prob).astype(BF16)
        return grad_out, grad_score, kv_ref[mem_rows, lanes].T

    def leave(item, given):
        r, p = item
        grad_out, grad_score, key = given
        rows, mem_rows, lanes, upper = places(item)
        query = head_pair(query_ref[rows, lanes])
        grad_kv_ref[mem_rows, lanes] = nn(grad_score, query).astype(BF16)
        grad_kv_ref[mem_rows, upper] = nn(prob_ref[r, p], grad_out).astype(BF16)
        grad_query_ref[rows, lanes] = fold_pair(nn(key, grad_score), length)

    pipelined(row_pairs(STEP_ROWS), enter, bend, leave)
    grad_query = grad_query_ref[...]
    grad_normed = nt(grad_query, weight_ref[:, width : 2 * width])
    grad, terms = norm_back(middle_ref[...].astype(F32), gains_ref[1:2, :], grad_normed)
    branch_a = (branch.astype(F32) + grad).astype(BF16)
    branch_a_ref[...] = branch_a
    gain_sums(terms, step_rows(dec_ref, step, STEP_ROWS), total_ref, square_ref.at[0])
    grad_w[:, :width] += tn(attended_a_ref[...], branch_a)
    grad_w[:, width : 2 * width] += tn(input_ref[...], grad_query)
    grad_w[:, 2 * width : 4 * width] += tn(memory_ref[...], grad_kv_ref[...])
    grad_w[:, 4 * width :] += tn(attended_ref[...], branch)

    @pl.when(step == pl.num_programs(0) - 1)
    def _():
        store_slots(me_ref, low_ref, high_ref, partial(read_rows, grad_w))


def self_scores_kernel(branch_ref, qkv_ref, prob_ref, dec_ref, buckets_ref, weight_ref,
                       grad_qkv_ref, table_ref, table_square_ref, grad_attended, bands):
    step = pl.program_id(0)
    length = prob_ref.shape[2]
    width = branch_ref.shape[1]
    grad_attended[...] = nt(branch_ref[...], weight_ref[:, :width]).astype(BF16)

    @pl.when(step == 0)
    def _():
        table_ref[...] = jnp.zeros_like(table_ref)
        bands[...] = jnp.zeros_like(bands)

    row_i = lax.broadcasted_iota(jnp.int32, (length, length), 0)
    col_i = lax.broadcasted_iota(jnp.int32, (length, length), 1)
    flip = (row_i + col_i == length - 1).astype(F32).astype(BF16)
    columns = token_columns(step_rows(dec_ref, step, STEP_ROWS)).astype(BF16)
    turned = nn(flip, columns)

    members = [
        [
            jnp.broadcast_to((turned[:, r : r + 1] == float(e)).astype(F32), (length, length))
            for e in range(NSEG)
        ]
        for r in range(STEP_ROWS)
    ]

    def part(item, k):
        r, p = item
        lanes = slice(k * width + p * LANES, k * width + (p + 1) * LANES)
        return slice(r * length, (r + 1) * length), lanes

    def enter(item, _):
        grad_out = head_pair(grad_attended[part(item, 0)])
        return grad_out, nt(qkv_ref[part(item, 2)], grad_out)

    def bend(item, given):
        r, p = item
        grad_out, grad_prob = given
        grad_score = score_grads(prob_ref[r, p], grad_prob).astype(BF16)
        return grad_out, grad_score, jnp.concatenate([qkv_ref[part(item, 1)].T, flip], axis=0)

    def leave(item, given):
        r, p = item
        grad_out, grad_score, key = given
        query = head_pair(qkv_ref[part(item, 0)])
        grad_qkv_ref[part(item, 1)] = nn(grad_score, query).astype(BF16)
        grad_qkv_ref[part(item, 2)] = nn(prob_ref[r, p], grad_out).astype(BF16)
        both = nn(key, grad_score)
        grad_qkv_ref[part(item, 0)] = fold_pair(both[:length], length)
        return both[length:]

    def count_buckets(item, turned_score):
        r, p = item
        for h in range(2):
            own = turned_score[:, h * length : (h + 1) * length]
            own = pltpu.roll(own, 1, 1, stride=1, stride_axis=0)
            for e in range(NSEG):
                bands[r, 2 * p + h, e : e + 1, :] = jnp.sum(
                    own * members[r][e], axis=0, keepdims=True
                )

    pipelined(row_pairs(STEP_ROWS), enter, bend, leave, count_buckets)
    bucket = lax.broadcasted_iota(jnp.int32, (LANES, length), 0)
    near = (bucket == buckets_ref[...]).astype(F32)
    flat = bands[...].reshape(STEP_ROWS * H * 8, length)
    per_bucket = lax.dot_general(
        flat, near, (((1,), (1,)), ((), ())), preferred_element_type=F32,
        precision=lax.Precision.HIGHEST,
    ).reshape(STEP_ROWS, H, 8, LANES)
    table_ref[...] += jnp.sum(jnp.sum(per_bucket, axis=0), axis=1)
    squares = jnp.sum(jnp.sum(per_bucket * per_bucket, axis=1), axis=-1, keepdims=True)
    table_square_ref[0] = jnp.broadcast_to(squares, (STEP_ROWS, 8, LANES))


def self_weights_kernel(me_ref, branch_ref, tokens_ref, input_ref, grad_qkv_ref, dec_ref,
                        gains_ref, weight_ref, table_ref, total_b_ref, total_c_ref,
                        grad_tokens_ref, low_ref, high_ref, square_ref, grad_w, total_ref,
                        small_ref):
    step = pl.program_id(0)
    width = tokens_ref.shape[1]
    grad_qkv = grad_qkv_ref[...]
    grad_normed = nt(grad_qkv, weight_ref[:, : 3 * width])
    grad, terms = norm_back(tokens_ref[...].astype(F32), gains_ref[0:1, :], grad_normed)
    grad_tokens_ref[...] = (branch_ref[...].astype(F32) + grad).astype(BF16)

    @pl.when(step == 0)
    def _():
        grad_w[...] = jnp.zeros_like(grad_w)
        total_ref[...] = jnp.zeros_like(total_ref)

    gain_sums(terms, step_rows(dec_ref, step, STEP_ROWS), total_ref, square_ref.at[0])
    flipped = input_ref[...].T
    for first in range(0, 3 * width, 256):
        grad_w[:, first : first + 256] += nn(flipped, grad_qkv_ref[:, first : first + 256])

    @pl.when(step == pl.num_programs(0) - 1)
    def _():
        bucket = lax.broadcasted_iota(jnp.int32, (LANES, width), 0)
        place = lax.broadcasted_iota(jnp.int32, (LANES, width), 1)
        spread = nn(table_ref[...].astype(BF16), (place // 16 == bucket).astype(F32).astype(BF16))
        head = lax.broadcasted_iota(jnp.int32, (H, width), 0)
        lane = lax.broadcasted_iota(jnp.int32, (H, width), 1)
        table = jnp.sum(jnp.where(lane % 16 == head, spread, 0.0), axis=0, keepdims=True)
        small = jnp.zeros((LANES, width), F32)
        row_i = lax.broadcasted_iota(jnp.int32, (LANES, width), 0)
        for k, line in enumerate((total_ref[...], total_b_ref[...], total_c_ref[...], table)):
            small = jnp.where(row_i == k, line, small)
        small_ref[...] = small.T

        def read(block):
            return jnp.concatenate(
                [read_rows(grad_w, block), read_rows(small_ref, block)], axis=1
            )

        store_slots(me_ref, low_ref, high_ref, read)


def pair_sum_kernel(low_ref, sent_ref, *refs):
    outs, (low, sent, total, load_sems, store_sems) = refs[:4], refs[4:]
    places = [pl.ds(4 * t, 4) for t in range(4)]
    lows = start_copies([(low_ref.at[p], low.at[p]) for p in places], load_sems.at[0])
    sents = start_copies([(sent_ref.at[p], sent.at[p]) for p in places], load_sems.at[1])
    stores = []
    for t, p in enumerate(places):
        lows[t].wait()
        sents[t].wait()
        total[p] = (low[p].astype(F32) + sent[p].astype(F32)).astype(BF16)
        stores.append(pltpu.make_async_copy(total.at[p], outs[t], store_sems.at[t]))
        stores[t].start()
    for store in stores:
        store.wait()


def pair_sum(low, sent, after):
    piece = shape_of((4,) + low.shape[1:], BF16)
    return pl.pallas_call(
        ignoring(pair_sum_kernel, 2, len(after)),
        out_shape=(piece,) * 4,
        in_specs=[pl.BlockSpec(memory_space=pl.ANY)] * (2 + len(after)),
        out_specs=[pl.BlockSpec(memory_space=pl.ANY)] * 4,
        scratch_shapes=[pltpu.VMEM(low.shape, BF16)] * 3
        + [pltpu.SemaphoreType.DMA((2, 4)), pltpu.SemaphoreType.DMA((4,))],
        compiler_params=pltpu.CompilerParams(vmem_limit_bytes=SHARED_LIMIT),
    )(in_hbm(low), sent, *after)


def plane_sum_kernel(*refs):
    own_ref, outs = refs[8], refs[9:]
    start = 0
    for group in (refs[:4], refs[4:8]):
        cols = slice(start, start + group[0].shape[2])
        start = cols.stop
        for s in range(4):
            total = sum(ref[s].astype(F32) for ref in group)
            if s == 0:
                own_ref[:, cols] = total
            else:
                outs[s - 1][:, cols] = total.astype(BF16)


def plane_sum(groups, after):
    line = (16, sum(group[0].shape[2] for group in groups))
    return small_call(
        plane_sum_kernel, [*groups[0], *groups[1]], after,
        (shape_of(line, F32),) + (shape_of(line, BF16),) * 3,
    )


def square_sum(values):
    return jnp.sum(jnp.sum(values * values, axis=0, keepdims=True), axis=1, keepdims=True)


def feed_end_kernel(sum_ref, hidden_ref, back_ref, square_ref):
    total = sum_ref[...].astype(F32)
    width = total.shape[1]
    for j in range(4):
        hidden_ref[:, j * width : (j + 1) * width] = total[16 * j : 16 * (j + 1)]
    back_ref[...] = total[64:]
    square_ref[...] = jnp.broadcast_to(square_sum(total), square_ref.shape)


def column_end_kernel(own_ref, b_ref, c_ref, d_ref, *refs):
    squares, outs, square_ref = refs[:1], refs[1:-1], refs[-1]
    total = own_ref[...] + b_ref[...].astype(F32)
    total = total + c_ref[...].astype(F32) + d_ref[...].astype(F32)
    start = 0
    for out in outs:
        out[...] = total[:, start : start + out.shape[1]]
        start += out.shape[1]
    square = square_sum(total)
    for given in squares:
        square = square + given[0:1, 0:1]
    square_ref[...] = jnp.broadcast_to(square, square_ref.shape)


def staged(kernel, ins, outs):
    def run(*refs):
        count = ins + outs
        given, inner, sems = refs[:count], refs[count : 2 * count], refs[2 * count]
        for copy in start_copies(list(zip(given[:ins], inner[:ins])), sems):
            copy.wait()
        kernel(*inner)
        for copy in start_copies(list(zip(inner[ins:], given[ins:])), sems):
            copy.wait()

    return run


def small_call(kernel, ins, after, outs):
    arrays = [*ins, *outs]
    return pl.pallas_call(
        ignoring(staged(kernel, len(ins), len(outs)), len(ins), len(after)),
        out_shape=outs,
        in_specs=[pl.BlockSpec(memory_space=pl.ANY)] * (len(ins) + len(after)),
        out_specs=[pl.BlockSpec(memory_space=pl.ANY)] * len(outs),
        scratch_shapes=[pltpu.VMEM(array.shape, array.dtype) for array in arrays]
        + [pltpu.SemaphoreType.DMA((len(arrays),))],
        compiler_params=pltpu.CompilerParams(vmem_limit_bytes=SHARED_LIMIT),
    )(*ins, *after)


def stack_kernel(me_ref, *refs):
    lines, out_ref, sems = refs[:-2], refs[-2], refs[-1]
    pairs = [(line, out_ref.at[me_ref[0] ^ s]) for s, line in enumerate(lines)]
    for copy in start_copies(pairs, sems):
        copy.wait()


def stack_lines(place, lines):
    return pl.pallas_call(
        stack_kernel,
        out_shape=shape_of((len(lines),) + lines[0].shape, BF16),
        in_specs=[pl.BlockSpec(memory_space=pltpu.SMEM)]
        + [pl.BlockSpec(memory_space=pl.ANY)] * len(lines),
        out_specs=pl.BlockSpec(memory_space=pl.ANY),
        scratch_shapes=[pltpu.SemaphoreType.DMA((len(lines),))],
        compiler_params=pltpu.CompilerParams(vmem_limit_bytes=SHARED_LIMIT),
    )(jnp.full((1,), place, jnp.int32), *lines)


def pack_kernel(*refs):
    ins, (own_ref, cross_ref, feed_ref) = refs[:11], refs[11:]
    width = ins[0].shape[1]
    for k, line in enumerate((*ins[:3], ins[10])):
        own_ref[:, k * width : k * width + line.shape[1]] = line[...]
    for k in range(5):
        cross_ref[:, k * width : (k + 1) * width] = ins[3 + k][...]
    for j in range(ins[8].shape[1] // width):
        feed_ref[16 * j : 16 * (j + 1), :] = ins[8][:, j * width : (j + 1) * width]
    feed_ref[64:, :] = ins[9][...]


def pack(weights, small):
    width = weights[0].shape[1]
    outs = [shape_of((16, cols), BF16) for cols in (3 * width + LANES, 5 * width)]
    outs.append(shape_of((128, width), BF16))
    return small_call(pack_kernel, (*map(in_hbm, weights), small), (), outs)


def memory_backward_kernel(memory_ref, grad_kv_ref, mem_ref, weight_ref, grad_memory_ref,
                           token_ref):
    mem_length = mem_ref.shape[1]
    width = memory_ref.shape[1]
    for first in range(0, width, 256):
        rows = slice(first, first + 256)
        grad_memory_ref[:, rows] = nt(
            grad_kv_ref[...], weight_ref[rows, 2 * width : 4 * width]
        ).astype(BF16)
    count = memory_ref.shape[0] // mem_length
    segments = step_rows(mem_ref, pl.program_id(0), count)
    columns = token_columns(segments)
    for r in range(count):
        rows = slice(r * mem_length, (r + 1) * mem_length)
        products = gram(memory_ref[rows, :]) * gram(grad_kv_ref[rows, :])
        token_ref[0, r : r + 1, :] = same_sum(products, segments, columns, r)


def gram_kernel(*refs):
    pairs, dec_ref, token_ref = refs[:-2], refs[-2], refs[-1]
    length = dec_ref.shape[1]
    count = pairs[0].shape[0] // length
    segments = step_rows(dec_ref, pl.program_id(0), count)
    columns = token_columns(segments)
    for r in range(count):
        rows = slice(r * length, (r + 1) * length)
        products = sum(
            gram(left[rows, :]) * gram(right[rows, :])
            for left, right in zip(pairs[::2], pairs[1::2])
        )
        token_ref[0, r : r + 1, :] = same_sum(products, segments, columns, r)


def rows_spec(array, steps):
    shape = (array.shape[0] // steps,) + array.shape[1:]
    return pl.BlockSpec(shape, lambda i, *_: (i,) + (0,) * (len(shape) - 1))


def whole_spec(array):
    return pl.BlockSpec(array.shape, lambda i, *_: (0,) * len(array.shape))


def in_hbm(array):
    return pltpu.with_memory_space_constraint(array, pltpu.HBM)


def ignoring(kernel, first, count):
    return lambda *refs: kernel(*refs[:first], *refs[first + count :])


def call(kernel, steps, me, blocked, whole, pieces, outs_blocked, outs_whole, scratch, flops,
         order, after=(), limit=VMEM_LIMIT):
    ins, in_specs = [], []
    blocked, whole = list(blocked), list(whole)
    for kind in order[0]:
        array = (blocked if kind == "i" else whole).pop(0)
        ins.append(array)
        in_specs.append(rows_spec(array, steps) if kind == "i" else whole_spec(array))
    ins = [in_hbm(array) for array in ins]
    kernel = ignoring(kernel, len(ins) + len(pieces) + (me is not None), len(after))
    ins += [*pieces, *after]
    in_specs += [pl.BlockSpec(memory_space=pl.ANY)] * (len(pieces) + len(after))
    outs, out_specs = [], []
    outs_blocked, outs_whole = list(outs_blocked), list(outs_whole)
    for kind in order[1]:
        out = (outs_blocked if kind == "i" else outs_whole).pop(0)
        outs.append(out)
        if kind == "a":
            out_specs.append(pl.BlockSpec(memory_space=pl.ANY))
        else:
            out_specs.append(rows_spec(out, steps) if kind == "i" else whole_spec(out))
    moved = sum(math.prod(a.shape) * a.dtype.itemsize for a in ins + outs)
    prefetch = 0 if me is None else 1
    return pl.pallas_call(
        kernel,
        out_shape=outs,
        grid_spec=pltpu.PrefetchScalarGridSpec(
            num_scalar_prefetch=prefetch,
            grid=(steps,),
            in_specs=in_specs,
            out_specs=out_specs,
            scratch_shapes=scratch,
        ),
        compiler_params=pltpu.CompilerParams(
            dimension_semantics=("arbitrary",), vmem_limit_bytes=limit
        ),
        cost_estimate=pl.CostEstimate(flops=flops, bytes_accessed=moved, transcendentals=0),
    )(*(() if me is None else (me,)), *ins)


FINE = ("z", "y", "core", "x")


def shape_of(shape, dtype):
    return jax.ShapeDtypeStruct(shape, dtype)


def kept(shape, dtype):
    return pltpu.HBM(shape, dtype)


def shift(array, mask):
    return lax.ppermute(array, FINE, [(i, i ^ mask) for i in range(32)])


def hold(array, after):
    return lax.optimization_barrier((array, after))[0]


def pack_feed(hidden, back):
    width = back.shape[1]
    hidden = hidden.reshape(-1, 16, 4, width).transpose(0, 2, 1, 3).reshape(-1, 64, width)
    return jnp.concatenate([hidden, back.reshape(-1, 64, width)], axis=1)


def unpack_feed(blocks):
    width = blocks.shape[2]
    hidden = blocks[:, :64].reshape(-1, 4, 16, width).transpose(0, 2, 1, 3)
    return hidden.reshape(-1, 4 * width), blocks[:, 64:].reshape(-1, width)


def small_row(gains, table):
    table = jnp.pad(table.reshape(-1, H), ((0, 0), (0, 16 - H)))
    row = jnp.concatenate([gain.reshape(-1, 16) for gain in gains] + [table], axis=1)
    row = jnp.pad(row, ((0, 0), (0, LANES - row.shape[1])))
    return jnp.pad(row[:, None], ((0, 0), (0, 15), (0, 0))).reshape(-1, LANES)


def in_order(slots):
    return slots[jnp.array([CODES.index(block) for block in range(32)])]


def as_rows(slots):
    return in_order(slots).reshape(-1, slots.shape[2]).astype(F32)


def shift_plane(pieces):
    return [shift(piece, mask) for piece, mask in zip(pieces, PLANE[1:])]


def shift_column(pieces):
    return [shift(piece, code) for piece, code in zip(pieces, COLUMN[1:])]


class Near:
    axes = FINE

    def __init__(self, weights):
        self.me = lax.axis_index(FINE)
        small = small_row(weights[10:13], weights[13])
        own, rest, feed = pack(weights[:10], small)
        self.feed = lax.all_gather(feed, FINE, axis=0)
        z = self.me >> 3
        own = stack_lines(z, [own, *shift_column([own] * 3)])
        rest = hold(rest, own)
        pair = stack_lines(z & 1, [rest, shift(rest, COLUMN[1])])
        other = shift(pair, COLUMN[2])
        rest = stack_lines(z >> 1, [pair, other]).reshape((4,) + rest.shape)
        plane = [own, *shift_plane([own] * 3)]
        self.own = plane + [shift(hold(piece, other), 2) for piece in plane]
        rest = hold(rest, plane[1])
        self.plane = [rest, *shift_plane([rest] * 3)]

    def cross(self, after):
        plane = [hold(piece, after) for piece in self.plane]
        return plane + [shift(piece, 2) for piece in plane]

    def feed_core(self, slots):
        return lax.psum_scatter(slots.reshape((2, 4, 4) + slots.shape[1:]), "core")

    def feed_plane(self, slots):
        return lax.psum_scatter(slots, ("y", "x"))

    def feed_column(self, slots):
        return lax.psum_scatter(slots, "z")


class Far:
    axes = ("wide", "narrow")
    me = 0

    def __init__(self, weights):
        weights = [lax.all_gather(w, self.axes, axis=0, tiled=True) for w in weights]
        self.take(weights)

    def take(self, weights):
        self.own = self.pieces(*weights[:3], small_row(weights[10:13], weights[13]))
        self.rest = self.pieces(*weights[3:8])
        self.feed = pack_feed(weights[8], weights[9])

    def pieces(self, *parts):
        blocks = jnp.concatenate(parts, axis=1).reshape(32, 16, -1)[jnp.array(CODES)]
        return [blocks[4 * t : 4 * t + 4] for t in range(8)]

    def cross(self, after):
        return self.rest

    def feed_core(self, slots):
        return slots

    feed_plane = feed_column = feed_core


def on_device(near, tokens, memory, cotangent, dec_segments, mem_segments, padding, buckets,
              *weights):
    way = (Near if near else Far)(weights)
    result, grad_tokens, grad_memory, grads, examples, square = local_part(
        way, tokens, memory, cotangent, dec_segments, mem_segments, padding, buckets
    )
    if near:
        sent = lax.all_to_all(square, FINE, 0, 0, tiled=True)
        global_norm = jnp.sum(sent[:, 0])
    else:
        grads = [lax.psum_scatter(g, way.axes, scatter_dimension=0, tiled=True) for g in grads]
        global_norm = lax.psum(sum(jnp.sum(g * g) for g in grads), way.axes)
    return (result, grad_tokens, grad_memory, *grads, examples, global_norm / COUNT)


def local_part(way, tokens, memory, cotangent, dec_segments, mem_segments, padding, buckets):
    seqs, length, width = tokens.shape
    mem_length = memory.shape[1]
    steps = seqs // STEP_ROWS
    small_steps = seqs // SMALL_ROWS
    dec, mem = seqs * length, seqs * mem_length
    step_dec = STEP_ROWS * length
    ff = 4 * width

    buckets = buckets[None]
    tokens2, memory2, cotangent2 = (
        array.reshape(-1, width) for array in (tokens, memory, cotangent)
    )
    dma = pltpu.SemaphoreType.DMA

    me = jnp.full((1,), way.me, jnp.int32)
    flops = 2 * dec * width * width

    input_a, qkv_a, prob_a, attended_a, self_w, gains = call(
        self_forward_kernel, small_steps, me, (tokens2,), (dec_segments, padding, buckets), way.own,
        (
            kept((dec, width), BF16),
            kept((dec, 3 * width), BF16),
            kept((seqs, PAIRS, length, 2 * length), BF16),
            kept((dec, width), BF16),
        ),
        (kept((4, 8, 16, 3 * width + LANES), BF16), kept((8, width), F32)),
        [pltpu.VMEM((PAIRS, length, 2 * length), F32), dma((8,))],
        6 * flops, ("iwww", "iiiiww"), (), SHARED_LIMIT,
    )
    middle, input_b, query_b, kv_b, prob_b, attended_b, after_cross, cross_w = call(
        cross_forward_kernel, steps, me, (tokens2, attended_a, memory2),
        (dec_segments, mem_segments, gains), way.cross(attended_a),
        (
            kept((dec, width), BF16),
            kept((dec, width), BF16),
            kept((dec, width), BF16),
            kept((mem, 2 * width), BF16),
            kept((seqs, PAIRS, mem_length, 2 * length), BF16),
            kept((dec, width), BF16),
            kept((dec, width), BF16),
        ),
        (kept((4, 8, 16, 5 * width), BF16),),
        [dma((8,))],
        10 * flops, ("iiiwww", "iiiiiiiw"), (), SHARED_LIMIT,
    )
    self_w, cross_w = self_w.reshape(width, -1), cross_w.reshape(width, -1)
    total, square = kept((1, width), F32), shape_of((steps, 4 * STEP_ROWS, LANES), F32)
    token_shape = shape_of((steps, 8, length), F32)
    small_token = shape_of((small_steps, 8, length), F32)
    result, branch_b, feed_slots, gain_c, square_c, token_c = call(
        feed_kernel, ff // width, None, (),
        (after_cross, cotangent2, dec_segments, padding, gains), (way.feed,), (),
        (
            shape_of((dec, width), BF16),
            kept((dec, width), BF16),
            shape_of((32, 128, width), BF16),
            total,
            square,
            token_shape,
        ),
        [
            pltpu.VMEM((32, 16, ff), BF16),
            pltpu.VMEM((32, 64, width), BF16),
            *[pltpu.VMEM((dec, width), BF16)] * 2,
            *[pltpu.VMEM((width, dec), BF16)] * 2,
            *[pltpu.VMEM((dec, ff), BF16)] * 2,
            pltpu.VMEM((32, 16, width), BF16),
            pltpu.VMEM((8, 64, width), BF16),
            dma((4, 2)),
            dma((9,)),
        ],
        26 * flops, ("wwwww", "wwawww"),
    )
    feed_sum = way.feed_core(feed_slots)
    slot = shape_of((16, 16, 5 * width), BF16)
    grad_query_b, grad_kv_b, branch_a, cross_low, cross_high, gain_b, square_b = call(
        cross_backward_kernel, steps, me,
        (branch_b, middle, memory2, attended_a, input_b, query_b, kv_b, prob_b, attended_b),
        (dec_segments, gains, cross_w), (),
        (
            kept((dec, width), BF16),
            kept((mem, 2 * width), BF16),
            kept((dec, width), BF16),
            square,
        ),
        (kept(slot.shape, BF16), slot, total),
        [pltpu.VMEM((width, 5 * width), F32), pltpu.VMEM((step_dec, width), BF16)],
        20 * flops, ("iiiiiiiiiwww", "iiiwwwi"),
    )
    feed_sum = way.feed_plane(hold(feed_sum, grad_query_b))
    near = isinstance(way, Near)
    if near:
        sent = shift(cross_high, 2)
    grad_qkv_a, table, table_square = call(
        self_scores_kernel, steps, None, (branch_a, qkv_a, prob_a),
        (dec_segments, buckets, cross_w), (),
        (kept((dec, 3 * width), BF16), shape_of((steps, STEP_ROWS, 8, LANES), F32)),
        (kept((H, LANES), F32),),
        [pltpu.VMEM((step_dec, width), BF16), pltpu.VMEM((STEP_ROWS, H, 8, length), F32)],
        10 * flops, ("iiiwww", "iwi"),
    )
    waits = ()
    if near:
        cross_parts = pair_sum(cross_low, sent, (grad_qkv_a,))
        crossed = shift_plane(cross_parts[1:])
        waits = (cross_parts[0],)
    slot = shape_of((16, 16, 3 * width + LANES), BF16)
    grad_tokens, self_low, self_high, square_a = call(
        self_weights_kernel, steps, me, (branch_a, tokens2, input_a, grad_qkv_a),
        (dec_segments, gains, self_w, table, gain_b, gain_c), (),
        (shape_of((dec, width), BF16), square),
        (kept(slot.shape, BF16), slot),
        [
            pltpu.VMEM((width, 3 * width), F32),
            pltpu.VMEM((1, width), F32),
            pltpu.VMEM((width, LANES), F32),
        ],
        7 * flops, ("iiiiwwwwww", "iwwi"), waits,
    )

    def grams(pairs, *after):
        (tokens_part,) = call(
            gram_kernel, small_steps, None, pairs, (dec_segments,), (), (small_token,), (), [],
            2 * flops, ("i" * len(pairs) + "w", "i"), after, SHARED_LIMIT,
        )
        return tokens_part

    def fill_cross(*after):
        return grams((input_b, grad_query_b, attended_b, branch_b), *after)

    def fill_self(*after):
        return grams((input_a, grad_qkv_a, attended_a, branch_a), *after)

    def fill_memory(*after):
        return call(
            memory_backward_kernel, small_steps, None, (memory2, grad_kv_b),
            (mem_segments, cross_w), (),
            (shape_of((mem, width), BF16), shape_of((small_steps, 8, mem_length), F32)), (), [],
            10 * flops, ("iiww", "ii"), after, SHARED_LIMIT,
        )

    if near:
        sent = shift(hold(self_high, crossed[0]), 2)
        token_b = fill_cross(self_low)
        self_parts = pair_sum(self_low, sent, (token_b,))
        self_sent = shift_plane(self_parts[1:])
        feed_sum = hold(feed_sum, token_b)
        token_a = fill_self(self_parts[0], feed_sum)
        feed_sum = way.feed_column(feed_sum)
        groups = [[self_parts[0], *self_sent], [cross_parts[0], *crossed]]
        own, *rest = plane_sum(groups, (token_a,))
        line_sent = shift_column(rest)
        grad_memory, token_m = fill_memory(own)
        feed_sum = hold(feed_sum, token_m).reshape(128, width)
        grad_hidden, grad_back, square = small_call(
            feed_end_kernel, (feed_sum,), (token_m,),
            [shape_of((16, ff), F32), shape_of((64, width), F32), shape_of((8, LANES), F32)],
        )
        line = shape_of((slot.shape[1], width), F32)
        *parts, square = small_call(
            column_end_kernel, (own, *line_sent, square), (token_m,),
            [line] * 3 + [shape_of((16, LANES), F32)] + [line] * 5 + [shape_of((32, LANES), F32)],
        )
        self_grads, small, cross_grads = parts[:3], parts[3], parts[4:]
        token_m = hold(token_m, square)
    else:
        token_b, token_a = fill_cross(), fill_self()
        grad_memory, token_m = fill_memory()
        cross_sum = as_rows(jnp.concatenate([cross_low, cross_high]))
        self_sum = as_rows(jnp.concatenate([self_low, self_high]))
        cross_grads = [cross_sum[:, k * width : (k + 1) * width] for k in range(5)]
        self_grads = [self_sum[:, k * width : (k + 1) * width] for k in range(3)]
        small = self_sum[:, 3 * width :]
        grad_hidden, grad_back = unpack_feed(in_order(feed_sum).astype(F32))
        square = None
    grads = self_grads + cross_grads + [grad_hidden, grad_back]
    grads += [small[:, k] for k in range(3)]
    grads.append(small[:, 3].reshape(-1, 16)[:, :H].reshape(-1))

    def row_parts(parts, count):
        return parts[:, :count].reshape(seqs, -1)

    def by_example(part, segments):
        hits = segments[:, None, :] == lax.broadcasted_iota(jnp.int32, (1, NSEG, 1), 1)
        return jnp.sum(jnp.where(hits, part[:, None, :], 0.0), axis=-1)

    token_d = row_parts(token_a + token_b, SMALL_ROWS) + row_parts(token_c, STEP_ROWS)
    examples = by_example(token_d, dec_segments)
    examples = examples + by_example(row_parts(token_m, SMALL_ROWS), mem_segments)
    squares = (square_a + square_b + square_c)[:, :, 0].reshape(seqs, NSEG)
    examples = examples + squares + table_square[..., :NSEG, 0].reshape(seqs, NSEG)
    return (
        result.reshape(tokens.shape),
        grad_tokens.reshape(tokens.shape),
        grad_memory.reshape(memory.shape),
        grads,
        examples / COUNT,
        square,
    )


def solution(mesh):
    near = tuple(mesh.shape.values()) == (16, 2)
    if near:
        mesh = jax.sharding.Mesh(mesh.devices.reshape(4, 2, 2, 2), FINE)
    axes = tuple(mesh.axis_names)
    rows = P(axes)
    arrays, weights, vectors = (P(axes, None, None),) * 3, (P(axes, None),) * 10, (rows,) * 4
    placed = arrays + (P(axes, None),) * 3 + (P(),) + weights + vectors
    return jax.shard_map(
        partial(on_device, near),
        mesh=mesh,
        in_specs=placed,
        out_specs=arrays + weights + vectors + (P(axes, None), P()),
        check_vma=False,
    )
```

```python
import math
from functools import partial

import jax
import jax.numpy as jnp
from jax import lax
from jax.experimental import pallas as pl
from jax.experimental.pallas import tpu as pltpu
from jax.sharding import PartitionSpec as P

H = 8
DH = 64
NB = 32
NSEG = 4
COUNT = 4196096
EPSILON = 1e-06
FLOOR = -1e30
F32 = jnp.float32
BF16 = jnp.bfloat16
PAIRS = H // 2
LANES = 128
STEP_ROWS = 4
SMALL_ROWS = 4
VMEM_LIMIT = 62 * 2**20
SHARED_LIMIT = 48 * 2**20

COLUMN = (0, 8, 16, 24)
PLANE = (0, 1, 4, 5)
CODES = tuple(2 * c + mask + z for c in (0, 1) for mask in PLANE for z in COLUMN)


def nn(left, right):
    return lax.dot_general(left, right, (((1,), (0,)), ((), ())), preferred_element_type=F32)


def nt(left, right):
    return lax.dot_general(left, right, (((1,), (1,)), ((), ())), preferred_element_type=F32)


def tn(left, right):
    return lax.dot_general(left, right, (((0,), (0,)), ((), ())), preferred_element_type=F32)


def inverse_root(values):
    return lax.rsqrt(jnp.mean(values * values, axis=-1, keepdims=True) + EPSILON)


def head_masks(values):
    low = (lax.broadcasted_iota(jnp.int32, (1, LANES), 1) < DH).astype(BF16)
    return values * low, values * (1 - low)


def head_pair(values):
    return jnp.concatenate(head_masks(values), axis=0)


def fold_pair(both, queries):
    own = jnp.concatenate([both[:DH, :queries], both[DH:, queries:]], axis=0)
    return own.astype(BF16).T


def block_rows(block):
    return pl.ds(pl.multiple_of(block * 16, 16), 16)


def start_copies(pairs, sems):
    copies = [pltpu.make_async_copy(*pair, sems.at[i]) for i, pair in enumerate(pairs)]
    for copy in copies:
        copy.start()
    return copies


def column_pairs(me_ref, pieces, weight_ref):
    return [
        (piece, weight_ref.at[:, (me_ref[0] ^ CODES[4 * t]) & 7]) for t, piece in enumerate(pieces)
    ]


def read_rows(grad_w, block):
    return grad_w[block_rows(block), :].astype(BF16)


def store_slots(me_ref, low_ref, high_ref, read):
    for k, code in enumerate(CODES):
        target = low_ref if k < 16 else high_ref
        target[k % 16] = read(me_ref[0] ^ code)


def softmax_columns(scores):
    shifted = jnp.exp(scores - jnp.max(scores, axis=0, keepdims=True))
    return (shifted * (1.0 / jnp.sum(shifted, axis=0, keepdims=True))).astype(BF16)


def step_rows(ref, step, count):
    whole = ref[...].astype(F32)
    rows = whole[:count]
    for s in range(1, whole.shape[0] // count):
        rows = jnp.where(step == s, whole[s * count : (s + 1) * count], rows)
    return rows


def token_columns(lines):
    pad = 8 - lines.shape[0] % 8
    return jnp.concatenate([lines] + [lines[:1]] * (pad % 8), axis=0).T


def member_lines(lines):
    count, length = lines.shape
    codes = jnp.concatenate([lines[r : r + 1] + float(NSEG * r) for r in range(count)], axis=1)
    places = lax.broadcasted_iota(jnp.int32, (NSEG * count, count * length), 0).astype(F32)
    return (codes == places).astype(F32).astype(BF16)


def same_sum(products, lines, columns, r):
    same = columns[:, r : r + 1] == lines[r : r + 1]
    return jnp.sum(jnp.where(same, products, 0.0), axis=0, keepdims=True)


def pipelined(items, *stages):
    state = {}
    for tick in range(len(items) + len(stages) - 1):
        for depth, stage in enumerate(stages):
            n = tick - depth
            if 0 <= n < len(items):
                state[n] = stage(items[n], state.get(n))


def row_pairs(count):
    return [(r, p) for r in range(count) for p in range(PAIRS)]


def gram(left):
    return nt(left, left)


def self_forward_kernel(me_ref, tokens_ref, dec_ref, padding_ref, buckets_ref, *refs):
    pieces, refs = refs[:8], refs[8:]
    input_ref, qkv_ref, prob_ref, attended_ref, weight_ref, gains_ref = refs[:6]
    bias_ref, sems = refs[6:]
    length = dec_ref.shape[1]
    width = tokens_ref.shape[1]

    @pl.when(pl.program_id(0) == 0)
    def _():
        for copy in start_copies(column_pairs(me_ref, pieces, weight_ref), sems):
            copy.wait()
        small_lines = weight_ref[:, :, :, 3 * width :].reshape(width, LANES)
        first = lax.broadcasted_iota(jnp.int32, (32, width), 1)
        pick = first == 16 * lax.broadcasted_iota(jnp.int32, (32, width), 0)
        small = nn(pick.astype(F32).astype(BF16), small_lines).astype(BF16)
        lane = lax.broadcasted_iota(jnp.int32, (LANES, width), 0)
        feature = lax.broadcasted_iota(jnp.int32, (LANES, width), 1)
        block = lax.broadcasted_iota(jnp.int32, (32, width), 0)
        lines = []
        for k in range(4):
            spread = nn(small, (lane == 16 * k + feature % 16).astype(F32).astype(BF16))
            lines.append(
                jnp.sum(jnp.where(block == first // 16, spread, 0.0), axis=0, keepdims=True)
            )
        gains_ref[...] = jnp.concatenate(lines + lines, axis=0)
        place = lax.broadcasted_iota(jnp.int32, (H, width), 1) % 16
        head = lax.broadcasted_iota(jnp.int32, (H, width), 0)
        table = jnp.where(place == head, lines[3], 0.0).astype(BF16)
        bucket = lax.broadcasted_iota(jnp.int32, (width, length), 0) // 16
        curves = nn(table, (bucket == buckets_ref[...]).astype(F32).astype(BF16))
        for h in range(H):
            curve = jnp.broadcast_to(curves[h : h + 1, :], (length, length))
            lanes = slice((h % 2) * length, (h % 2 + 1) * length)
            bias_ref[h // 2, :, lanes] = pltpu.roll(curve, 0, 1, stride=1, stride_axis=0)

    values = tokens_ref[...].astype(F32)
    normed = (values * inverse_root(values) * gains_ref[0:1, :]).astype(BF16)
    input_ref[...] = normed
    for first in range(0, 3 * width, 256):
        cols = slice(first, first + 256)
        qkv_ref[:, cols] = nn(
            normed, weight_ref[:, :, :, cols].reshape(width, 256)
        ).astype(BF16)

    step = pl.program_id(0)
    count = tokens_ref.shape[0] // length
    segments, real = step_rows(dec_ref, step, count), step_rows(padding_ref, step, count)
    segment_columns, real_columns = token_columns(segments), token_columns(real)
    key_i = lax.broadcasted_iota(jnp.int32, (length, length), 0)
    query_i = lax.broadcasted_iota(jnp.int32, (length, length), 1)

    masks = []
    for r in range(count):
        allowed = (segment_columns[:, r : r + 1] == segments[r : r + 1]) & (key_i <= query_i)
        allowed = allowed & ((real_columns[:, r : r + 1] > 0.0) | (key_i == query_i))
        mask = jnp.where(allowed, 0.0, FLOOR)
        masks.append(jnp.concatenate([mask, mask], axis=1))

    def part(item, k):
        r, p = item
        return qkv_ref[r * length : (r + 1) * length, k * width + p * LANES : k * width + (p + 1) * LANES]

    def scores(item, _):
        return nt(part(item, 1), head_pair(part(item, 0)))

    def weigh(item, score):
        r, p = item
        prob = softmax_columns(score + bias_ref[p] + masks[r])
        prob_ref[r, p] = prob
        return prob, part(item, 2).T

    def mix(item, given):
        r, p = item
        prob, value = given
        rows, lanes = slice(r * length, (r + 1) * length), slice(p * LANES, (p + 1) * LANES)
        attended_ref[rows, lanes] = fold_pair(nn(value, prob), length)

    pipelined(row_pairs(count), scores, weigh, mix)


def cross_forward_kernel(me_ref, tokens_ref, attended_a_ref, memory_ref, dec_ref, mem_ref,
                         gains_ref, *refs):
    pieces, refs = refs[:8], refs[8:]
    (middle_ref, input_ref, query_ref, kv_ref, prob_ref, attended_ref, after_ref, weight_ref,
     sems) = refs
    mem_length, length = mem_ref.shape[1], dec_ref.shape[1]
    width = tokens_ref.shape[1]

    @pl.when(pl.program_id(0) == 0)
    def _():
        for copy in start_copies(column_pairs(me_ref, pieces, weight_ref), sems):
            copy.wait()

    def weight(k):
        return weight_ref[:, :, :, k * width : (k + 1) * width].reshape(width, width)

    for k in range(2):
        kv_ref[:, k * width : (k + 1) * width] = nn(memory_ref[...], weight(k + 2)).astype(BF16)
    values = tokens_ref[...].astype(F32) + nn(attended_a_ref[...], weight(0))
    middle_ref[...] = values.astype(BF16)
    normed = (values * inverse_root(values) * gains_ref[1:2, :]).astype(BF16)
    input_ref[...] = normed
    query_ref[...] = nn(normed, weight(1)).astype(BF16)

    step = pl.program_id(0)
    count = tokens_ref.shape[0] // length
    segments = step_rows(dec_ref, step, count)
    mem_columns = token_columns(step_rows(mem_ref, step, count))

    masks = []
    for r in range(count):
        mask = jnp.where(mem_columns[:, r : r + 1] == segments[r : r + 1], 0.0, FLOOR)
        masks.append(jnp.concatenate([mask, mask], axis=1))

    def places(item):
        r, p = item
        rows, lanes = slice(r * length, (r + 1) * length), slice(p * LANES, (p + 1) * LANES)
        upper = slice(width + p * LANES, width + (p + 1) * LANES)
        return rows, slice(r * mem_length, (r + 1) * mem_length), lanes, upper

    def scores(item, _):
        rows, mem_rows, lanes, _ = places(item)
        return nt(kv_ref[mem_rows, lanes], head_pair(query_ref[rows, lanes]))

    def weigh(item, score):
        r, p = item
        _, mem_rows, _, upper = places(item)
        prob = softmax_columns(score + masks[r])
        prob_ref[r, p] = prob
        return prob, kv_ref[mem_rows, upper].T

    def mix(item, given):
        rows, _, lanes, _ = places(item)
        prob, value = given
        attended_ref[rows, lanes] = fold_pair(nn(value, prob), length)

    pipelined(row_pairs(count), scores, weigh, mix)
    after = values + nn(attended_ref[...], weight(4))
    after_ref[...] = after.astype(BF16)


def norm_back(values, gain, grad_normed):
    inverse = inverse_root(values)
    scaled = values * inverse
    upper = grad_normed * gain
    grad = inverse * (upper - scaled * jnp.mean(upper * scaled, axis=-1, keepdims=True))
    return grad, grad_normed * scaled


def gain_sums(terms, segments, total_ref, square_ref):
    sums = nn(member_lines(segments), terms.astype(BF16))
    total_ref[...] += jnp.sum(sums, axis=0, keepdims=True)
    square = jnp.sum(sums * sums, axis=1, keepdims=True)
    square_ref[...] = jnp.broadcast_to(square, square_ref.shape)


def feed_kernel(after_ref, cotangent_ref, dec_ref, padding_ref, gains_ref, gathered_ref,
                result_ref, branch_b_ref, slots_ref, total_ref, square_ref, token_ref, w_in_ref,
                w_out_ref, normed_ref, branch_ref, normed_flip, branch_flip, active_ref, grad_ref,
                in_slots, out_slots, result_tile, branch_tile, load_sems, sems, end_sems):
    part = pl.program_id(0)
    parts = pl.num_programs(0)
    count, length = dec_ref.shape
    dec, width = after_ref.shape
    ff = w_in_ref.shape[2]
    tile = STEP_ROWS * length
    tiles = [slice(t * tile, (t + 1) * tile) for t in range(dec // tile)]

    def loads(which):
        rows = pl.ds(pl.multiple_of(which * 16, 16), 16)
        cols = pl.ds(pl.multiple_of(which * width, width), width)
        blocks = pl.ds(which * 8, 8)
        pairs = (
            (gathered_ref.at[:, rows, :], w_in_ref.at[:, :, cols]),
            (gathered_ref.at[blocks, 64:, :], w_out_ref.at[blocks]),
        )
        return [
            pltpu.make_async_copy(*pair, load_sems.at[which, i]) for i, pair in enumerate(pairs)
        ]

    @pl.when(part == 0)
    def _():
        for which in range(ff // width):
            for copy in loads(which):
                copy.start()
        real = token_columns(padding_ref[...].astype(F32))
        for r in range(count):
            rows = slice(r * length, (r + 1) * length)
            branch_ref[rows, :] = (
                cotangent_ref[rows, :].astype(F32) * real[:, r : r + 1]
            ).astype(BF16)
        for rows in tiles:
            values = after_ref[rows, :].astype(F32)
            normed = (values * inverse_root(values) * gains_ref[2:3, :]).astype(BF16)
            normed_ref[rows, :] = normed
            normed_flip[:, rows] = normed.T
            branch_flip[:, rows] = branch_ref[rows, :].T

    for copy in loads(part):
        copy.wait()
    root = 0.7978845608028654
    half_width = width // 2
    for sub in range(2):
        first = pl.multiple_of(part * width + sub * half_width, half_width)
        cols = pl.ds(first, half_width)
        hidden = nn(normed_ref[...], w_in_ref[:, :, cols].reshape(width, half_width))
        square = hidden * hidden
        bent = jnp.tanh(hidden * (root + (root * 0.044715) * square))
        half = 0.5 + 0.5 * bent
        slope = hidden * (2.0 * root + (6.0 * root * 0.044715) * square)
        slope = half + half * (slope * (1.0 - half))
        active_ref[:, cols] = (hidden * half).astype(BF16)
        w_out = w_out_ref[pl.ds(part * 8 + sub * 4, 4)].reshape(half_width, width)
        grad_ref[:, cols] = (nt(branch_ref[...], w_out) * slope).astype(BF16)
    cols = pl.ds(pl.multiple_of(part * width, width), width)
    grad_in = nn(normed_flip[...], grad_ref[:, cols]).astype(BF16)
    grad_out = nn(branch_flip[...], active_ref[:, cols]).astype(BF16).T

    def sends(which):
        pairs = [(in_slots, slots_ref.at[:, pl.ds(pl.multiple_of(which * 16, 16), 16), :])]
        for i, k in enumerate(range(0, 32, 4)):
            pairs.append((out_slots.at[i], slots_ref.at[k + which, 64:, :]))
        return [pltpu.make_async_copy(*pair, sems.at[i]) for i, pair in enumerate(pairs)]

    @pl.when(part > 0)
    def _():
        for copy in sends(part - 1):
            copy.wait()

    for k, block in enumerate(CODES):
        in_slots[k] = grad_in[16 * block : 16 * block + 16]
    for i, k in enumerate(range(0, 32, 4)):
        block = CODES[k]
        out_slots[i] = grad_out[64 * block : 64 * block + 64]
    for copy in sends(part):
        copy.start()

    @pl.when(part == parts - 1)
    def _():
        segments = dec_ref[...].astype(F32)
        columns = token_columns(segments)
        total_ref[...] = jnp.zeros_like(total_ref)
        ends = []
        w_in, w_out = w_in_ref[...].reshape(width, ff), w_out_ref[...].reshape(ff, width)
        for t, rows in enumerate(tiles):
            values = after_ref[rows, :].astype(F32)
            result_tile[rows, :] = (values + nn(active_ref[rows, :], w_out)).astype(BF16)
            grad, terms = norm_back(values, gains_ref[2:3, :], nt(grad_ref[rows, :], w_in))
            branch_tile[rows, :] = (branch_ref[rows, :].astype(F32) + grad).astype(BF16)
            pairs = [(result_tile.at[rows], result_ref.at[rows])]
            pairs.append((branch_tile.at[rows], branch_b_ref.at[rows]))
            ends.extend(start_copies(pairs, end_sems.at[t]))
            own = segments[t * STEP_ROWS : (t + 1) * STEP_ROWS]
            gain_sums(terms, own, total_ref, square_ref.at[t])
        for r in range(count):
            own = slice(r * length, (r + 1) * length)
            products = gram(active_ref[own, :]) * gram(branch_ref[own, :])
            products = products + gram(grad_ref[own, :]) * gram(normed_ref[own, :])
            token_ref[r // STEP_ROWS, r % STEP_ROWS : r % STEP_ROWS + 1, :] = same_sum(
                products, segments, columns, r
            )
        for copy in sends(part) + ends:
            copy.wait()


def score_grads(prob, grad_prob):
    prob = prob.astype(F32)
    dots = jnp.sum(prob * grad_prob, axis=0, keepdims=True)
    return prob * (grad_prob - dots)


def cross_backward_kernel(me_ref, branch_ref, middle_ref, memory_ref, attended_a_ref, input_ref,
                          query_ref, kv_ref, prob_ref, attended_ref, dec_ref, gains_ref,
                          query_w_ref, out_w_ref, grad_query_ref, grad_kv_ref, branch_a_ref, low_ref, high_ref,
                          total_ref, square_ref, grad_w, grad_attended):
    step = pl.program_id(0)
    mem_length = prob_ref.shape[2]
    length = prob_ref.shape[3] // 2
    width = branch_ref.shape[1]

    @pl.when(step == 0)
    def _():
        grad_w[...] = jnp.zeros_like(grad_w)
        total_ref[...] = jnp.zeros_like(total_ref)

    branch = branch_ref[...]
    grad_attended[...] = nt(branch, out_w_ref[...]).astype(BF16)

    def places(item):
        r, p = item
        rows, lanes = slice(r * length, (r + 1) * length), slice(p * LANES, (p + 1) * LANES)
        upper = slice(width + p * LANES, width + (p + 1) * LANES)
        return rows, slice(r * mem_length, (r + 1) * mem_length), lanes, upper

    def enter(item, _):
        rows, mem_rows, lanes, upper = places(item)
        grad_out = head_pair(grad_attended[rows, lanes])
        return grad_out, nt(kv_ref[mem_rows, upper], grad_out)

    def bend(item, given):
        r, p = item
        grad_out, grad_prob = given
        _, mem_rows, lanes, _ = places(item)
        grad_score = score_grads(prob_ref[r, p], grad_prob).astype(BF16)
        return grad_out, grad_score, kv_ref[mem_rows, lanes].T

    def leave(item, given):
        r, p = item
        grad_out, grad_score, key = given
        rows, mem_rows, lanes, upper = places(item)
        query = head_pair(query_ref[rows, lanes])
        grad_kv_ref[mem_rows, lanes] = nn(grad_score, query).astype(BF16)
        grad_kv_ref[mem_rows, upper] = nn(prob_ref[r, p], grad_out).astype(BF16)
        grad_query_ref[rows, lanes] = fold_pair(nn(key, grad_score), length)

    pipelined(row_pairs(STEP_ROWS), enter, bend, leave)
    grad_query = grad_query_ref[...]
    grad_normed = nt(grad_query, query_w_ref[...])
    grad, terms = norm_back(middle_ref[...].astype(F32), gains_ref[1:2, :], grad_normed)
    branch_a = (branch.astype(F32) + grad).astype(BF16)
    branch_a_ref[...] = branch_a
    gain_sums(terms, step_rows(dec_ref, step, STEP_ROWS), total_ref, square_ref.at[0])
    grad_w[:, :width] += tn(attended_a_ref[...], branch_a)
    grad_w[:, width : 2 * width] += tn(input_ref[...], grad_query)
    grad_w[:, 2 * width : 4 * width] += tn(memory_ref[...], grad_kv_ref[...])
    grad_w[:, 4 * width :] += tn(attended_ref[...], branch)

    @pl.when(step == pl.num_programs(0) - 1)
    def _():
        store_slots(me_ref, low_ref, high_ref, partial(read_rows, grad_w))


def self_backward_kernel(me_ref, branch_ref, tokens_ref, input_ref, qkv_ref, prob_ref, dec_ref,
                         buckets_ref, gains_ref, out_w_ref, weight_ref, total_b_ref, total_c_ref,
                         grad_qkv_ref, grad_tokens_ref, low_ref, high_ref, square_ref,
                         table_square_ref, grad_w, total_ref, small_ref, table_ref, grad_attended,
                         bands):
    step = pl.program_id(0)
    length = prob_ref.shape[2]
    width = branch_ref.shape[1]
    grad_attended[...] = nt(branch_ref[...], out_w_ref[...]).astype(BF16)

    @pl.when(step == 0)
    def _():
        table_ref[...] = jnp.zeros_like(table_ref)
        bands[...] = jnp.zeros_like(bands)
        grad_w[...] = jnp.zeros_like(grad_w)
        total_ref[...] = jnp.zeros_like(total_ref)

    row_i = lax.broadcasted_iota(jnp.int32, (length, length), 0)
    col_i = lax.broadcasted_iota(jnp.int32, (length, length), 1)
    flip = (row_i + col_i == length - 1).astype(F32).astype(BF16)
    columns = token_columns(step_rows(dec_ref, step, STEP_ROWS)).astype(BF16)
    turned = nn(flip, columns)

    members = [
        [
            jnp.broadcast_to((turned[:, r : r + 1] == float(e)).astype(F32), (length, length))
            for e in range(NSEG)
        ]
        for r in range(STEP_ROWS)
    ]

    def part(item, k):
        r, p = item
        lanes = slice(k * width + p * LANES, k * width + (p + 1) * LANES)
        return slice(r * length, (r + 1) * length), lanes

    def enter(item, _):
        grad_out = head_pair(grad_attended[part(item, 0)])
        return grad_out, nt(qkv_ref[part(item, 2)], grad_out)

    def bend(item, given):
        r, p = item
        grad_out, grad_prob = given
        grad_score = score_grads(prob_ref[r, p], grad_prob).astype(BF16)
        return grad_out, grad_score, jnp.concatenate([qkv_ref[part(item, 1)].T, flip], axis=0)

    def leave(item, given):
        r, p = item
        grad_out, grad_score, key = given
        query = head_pair(qkv_ref[part(item, 0)])
        grad_qkv_ref[part(item, 1)] = nn(grad_score, query).astype(BF16)
        grad_qkv_ref[part(item, 2)] = nn(prob_ref[r, p], grad_out).astype(BF16)
        both = nn(key, grad_score)
        grad_qkv_ref[part(item, 0)] = fold_pair(both[:length], length)
        return both[length:]

    def count_buckets(item, turned_score):
        r, p = item
        for h in range(2):
            own = turned_score[:, h * length : (h + 1) * length]
            own = pltpu.roll(own, 1, 1, stride=1, stride_axis=0)
            for e in range(NSEG):
                bands[r, 2 * p + h, e : e + 1, :] = jnp.sum(
                    own * members[r][e], axis=0, keepdims=True
                )

    pipelined(row_pairs(STEP_ROWS), enter, bend, leave, count_buckets)
    bucket = lax.broadcasted_iota(jnp.int32, (LANES, length), 0)
    near = (bucket == buckets_ref[...]).astype(F32)
    flat = bands[...].reshape(STEP_ROWS * H * 8, length)
    per_bucket = lax.dot_general(
        flat, near, (((1,), (1,)), ((), ())), preferred_element_type=F32,
        precision=lax.Precision.HIGHEST,
    ).reshape(STEP_ROWS, H, 8, LANES)
    table_ref[...] += jnp.sum(jnp.sum(per_bucket, axis=0), axis=1)
    squares = jnp.sum(jnp.sum(per_bucket * per_bucket, axis=1), axis=-1, keepdims=True)
    table_square_ref[0] = jnp.broadcast_to(squares, (STEP_ROWS, 8, LANES))

    grad_qkv = grad_qkv_ref[...]
    grad_normed = nt(grad_qkv, weight_ref[...])
    grad, terms = norm_back(tokens_ref[...].astype(F32), gains_ref[0:1, :], grad_normed)
    grad_tokens_ref[...] = (branch_ref[...].astype(F32) + grad).astype(BF16)

    gain_sums(terms, step_rows(dec_ref, step, STEP_ROWS), total_ref, square_ref.at[0])
    flipped = input_ref[...].T
    for first in range(0, 3 * width, 256):
        grad_w[:, first : first + 256] += nn(flipped, grad_qkv_ref[:, first : first + 256])

    @pl.when(step == pl.num_programs(0) - 1)
    def _():
        bucket = lax.broadcasted_iota(jnp.int32, (LANES, width), 0)
        place = lax.broadcasted_iota(jnp.int32, (LANES, width), 1)
        spread = nn(table_ref[...].astype(BF16), (place // 16 == bucket).astype(F32).astype(BF16))
        head = lax.broadcasted_iota(jnp.int32, (H, width), 0)
        lane = lax.broadcasted_iota(jnp.int32, (H, width), 1)
        table = jnp.sum(jnp.where(lane % 16 == head, spread, 0.0), axis=0, keepdims=True)
        small = jnp.zeros((LANES, width), F32)
        row_i = lax.broadcasted_iota(jnp.int32, (LANES, width), 0)
        for k, line in enumerate((total_ref[...], total_b_ref[...], total_c_ref[...], table)):
            small = jnp.where(row_i == k, line, small)
        small_ref[...] = small.T

        def read(block):
            return jnp.concatenate(
                [read_rows(grad_w, block), read_rows(small_ref, block)], axis=1
            )

        store_slots(me_ref, low_ref, high_ref, read)


def pair_sum_kernel(*refs):
    groups, outs, buffers, total = (refs[:2], refs[2:4]), refs[4:8], refs[8:12], refs[12]
    load_sems, store_sems = refs[13:]
    places = [pl.ds(4 * t, 4) for t in range(4)]
    loads = []
    for i, ref in enumerate((*groups[0], *groups[1])):
        pairs = [(ref.at[p], buffers[i].at[p]) for p in places]
        loads.append(start_copies(pairs, load_sems.at[i]))
    stores = []
    for t, p in enumerate(places):
        start = 0
        for low, sent in ((0, 1), (2, 3)):
            loads[low][t].wait()
            loads[sent][t].wait()
            own = buffers[low][p].astype(F32) + buffers[sent][p].astype(F32)
            total[p, :, start : start + own.shape[2]] = own.astype(BF16)
            start += own.shape[2]
        stores.append(pltpu.make_async_copy(total.at[p], outs[t], store_sems.at[t]))
        stores[t].start()
    for store in stores:
        store.wait()


def pair_sum(groups):
    arrays = [array for group in groups for array in group]
    lanes = sum(low.shape[2] for low, _ in groups)
    shape = arrays[0].shape[:2] + (lanes,)
    return pl.pallas_call(
        pair_sum_kernel,
        out_shape=(shape_of((4,) + shape[1:], BF16),) * 4,
        in_specs=[pl.BlockSpec(memory_space=pl.ANY)] * 4,
        out_specs=[pl.BlockSpec(memory_space=pl.ANY)] * 4,
        scratch_shapes=[pltpu.VMEM(array.shape, BF16) for array in arrays]
        + [pltpu.VMEM(shape, BF16)]
        + [pltpu.SemaphoreType.DMA((4, 4)), pltpu.SemaphoreType.DMA((4,))],
        compiler_params=pltpu.CompilerParams(vmem_limit_bytes=SHARED_LIMIT),
    )(*[in_hbm(a) if i % 2 == 0 else a for i, a in enumerate(arrays)])


def plane_sum_kernel(a_ref, b_ref, c_ref, d_ref, own_ref, *outs):
    for s in range(4):
        total = a_ref[s].astype(F32) + b_ref[s].astype(F32)
        total = total + c_ref[s].astype(F32) + d_ref[s].astype(F32)
        if s == 0:
            own_ref[...] = total
        else:
            outs[s - 1][...] = total.astype(BF16)


def plane_sum(pieces, after):
    line = pieces[0].shape[1:]
    return small_call(
        plane_sum_kernel, pieces, after, (shape_of(line, F32),) + (shape_of(line, BF16),) * 3
    )


def square_sum(values):
    return jnp.sum(jnp.sum(values * values, axis=0, keepdims=True), axis=1, keepdims=True)


def feed_end_kernel(sum_ref, hidden_ref, back_ref, square_ref):
    total = sum_ref[...].astype(F32)
    width = total.shape[1]
    for j in range(4):
        hidden_ref[:, j * width : (j + 1) * width] = total[16 * j : 16 * (j + 1)]
    back_ref[...] = total[64:]
    square_ref[...] = jnp.broadcast_to(square_sum(total), square_ref.shape)


def column_end_kernel(own_ref, b_ref, c_ref, d_ref, *refs):
    squares, outs, square_ref = refs[:1], refs[1:-1], refs[-1]
    total = own_ref[...] + b_ref[...].astype(F32)
    total = total + c_ref[...].astype(F32) + d_ref[...].astype(F32)
    start = 0
    for out in outs:
        out[...] = total[:, start : start + out.shape[1]]
        start += out.shape[1]
    square = square_sum(total)
    for given in squares:
        square = square + given[0:1, 0:1]
    square_ref[...] = jnp.broadcast_to(square, square_ref.shape)


def staged(kernel, ins, outs):
    def run(*refs):
        count = ins + outs
        given, inner, sems = refs[:count], refs[count : 2 * count], refs[2 * count]
        for copy in start_copies(list(zip(given[:ins], inner[:ins])), sems):
            copy.wait()
        kernel(*inner)
        for copy in start_copies(list(zip(inner[ins:], given[ins:])), sems):
            copy.wait()

    return run


def small_call(kernel, ins, after, outs):
    arrays = [*ins, *outs]
    return pl.pallas_call(
        ignoring(staged(kernel, len(ins), len(outs)), len(ins), len(after)),
        out_shape=outs,
        in_specs=[pl.BlockSpec(memory_space=pl.ANY)] * (len(ins) + len(after)),
        out_specs=[pl.BlockSpec(memory_space=pl.ANY)] * len(outs),
        scratch_shapes=[pltpu.VMEM(array.shape, array.dtype) for array in arrays]
        + [pltpu.SemaphoreType.DMA((len(arrays),))],
        compiler_params=pltpu.CompilerParams(vmem_limit_bytes=SHARED_LIMIT),
    )(*ins, *after)


def stack_kernel(me_ref, *refs):
    lines, out_ref, sems = refs[:-2], refs[-2], refs[-1]
    pairs = [(line, out_ref.at[me_ref[0] ^ s]) for s, line in enumerate(lines)]
    for copy in start_copies(pairs, sems):
        copy.wait()


def stack_lines(place, lines):
    return pl.pallas_call(
        stack_kernel,
        out_shape=shape_of((len(lines),) + lines[0].shape, BF16),
        in_specs=[pl.BlockSpec(memory_space=pltpu.SMEM)]
        + [pl.BlockSpec(memory_space=pl.ANY)] * len(lines),
        out_specs=pl.BlockSpec(memory_space=pl.ANY),
        scratch_shapes=[pltpu.SemaphoreType.DMA((len(lines),))],
        compiler_params=pltpu.CompilerParams(vmem_limit_bytes=SHARED_LIMIT),
    )(jnp.full((1,), place, jnp.int32), *lines)


def pack_kernel(*refs):
    ins, (own_ref, cross_ref, feed_ref) = refs[:11], refs[11:]
    width = ins[0].shape[1]
    for k, line in enumerate((*ins[:3], ins[10])):
        own_ref[:, k * width : k * width + line.shape[1]] = line[...]
    for k in range(5):
        cross_ref[:, k * width : (k + 1) * width] = ins[3 + k][...]
    for j in range(ins[8].shape[1] // width):
        feed_ref[16 * j : 16 * (j + 1), :] = ins[8][:, j * width : (j + 1) * width]
    feed_ref[64:, :] = ins[9][...]


def pack(weights, small):
    width = weights[0].shape[1]
    outs = [shape_of((16, cols), BF16) for cols in (3 * width + LANES, 5 * width)]
    outs.append(shape_of((128, width), BF16))
    return small_call(pack_kernel, (*map(in_hbm, weights), small), (), outs)


def memory_backward_kernel(memory_ref, grad_kv_ref, mem_ref, weight_ref, grad_memory_ref,
                           token_ref):
    mem_length = mem_ref.shape[1]
    width = memory_ref.shape[1]
    for first in range(0, width, 256):
        rows = slice(first, first + 256)
        grad_memory_ref[:, rows] = nt(
            grad_kv_ref[...], weight_ref[rows, :]
        ).astype(BF16)
    count = memory_ref.shape[0] // mem_length
    segments = step_rows(mem_ref, pl.program_id(0), count)
    columns = token_columns(segments)
    for r in range(count):
        rows = slice(r * mem_length, (r + 1) * mem_length)
        products = gram(memory_ref[rows, :]) * gram(grad_kv_ref[rows, :])
        token_ref[0, r : r + 1, :] = same_sum(products, segments, columns, r)


def gram_kernel(*refs):
    pairs, dec_ref, token_ref = refs[:-2], refs[-2], refs[-1]
    length = dec_ref.shape[1]
    count = pairs[0].shape[0] // length
    segments = step_rows(dec_ref, pl.program_id(0), count)
    columns = token_columns(segments)
    for r in range(count):
        rows = slice(r * length, (r + 1) * length)
        products = sum(
            gram(left[rows, :]) * gram(right[rows, :])
            for left, right in zip(pairs[::2], pairs[1::2])
        )
        token_ref[0, r : r + 1, :] = same_sum(products, segments, columns, r)


def rows_spec(array, steps):
    shape = (array.shape[0] // steps,) + array.shape[1:]
    return pl.BlockSpec(shape, lambda i, *_: (i,) + (0,) * (len(shape) - 1))


class Cut:
    def __init__(self, array, shape, *index):
        self.array, self.spec = array, pl.BlockSpec(shape, lambda i, *_: index)


def whole_spec(array):
    return pl.BlockSpec(array.shape, lambda i, *_: (0,) * len(array.shape))


def in_hbm(array):
    return pltpu.with_memory_space_constraint(array, pltpu.HBM)


def ignoring(kernel, first, count):
    return lambda *refs: kernel(*refs[:first], *refs[first + count :])


def call(kernel, steps, me, blocked, whole, pieces, outs_blocked, outs_whole, scratch, flops,
         order, after=(), limit=VMEM_LIMIT):
    ins, in_specs = [], []
    blocked, whole = list(blocked), list(whole)
    for kind in order[0]:
        array = (blocked if kind == "i" else whole).pop(0)
        if isinstance(array, Cut):
            ins.append(array.array)
            in_specs.append(array.spec)
            continue
        ins.append(array)
        in_specs.append(rows_spec(array, steps) if kind == "i" else whole_spec(array))
    ins = [in_hbm(array) for array in ins]
    kernel = ignoring(kernel, len(ins) + len(pieces) + (me is not None), len(after))
    ins += [*pieces, *after]
    in_specs += [pl.BlockSpec(memory_space=pl.ANY)] * (len(pieces) + len(after))
    outs, out_specs = [], []
    outs_blocked, outs_whole = list(outs_blocked), list(outs_whole)
    for kind in order[1]:
        out = (outs_blocked if kind == "i" else outs_whole).pop(0)
        outs.append(out)
        if kind == "a":
            out_specs.append(pl.BlockSpec(memory_space=pl.ANY))
        else:
            out_specs.append(rows_spec(out, steps) if kind == "i" else whole_spec(out))
    moved = sum(math.prod(a.shape) * a.dtype.itemsize for a in ins + outs)
    prefetch = 0 if me is None else 1
    return pl.pallas_call(
        kernel,
        out_shape=outs,
        grid_spec=pltpu.PrefetchScalarGridSpec(
            num_scalar_prefetch=prefetch,
            grid=(steps,),
            in_specs=in_specs,
            out_specs=out_specs,
            scratch_shapes=scratch,
        ),
        compiler_params=pltpu.CompilerParams(
            dimension_semantics=("arbitrary",), vmem_limit_bytes=limit
        ),
        cost_estimate=pl.CostEstimate(flops=flops, bytes_accessed=moved, transcendentals=0),
    )(*(() if me is None else (me,)), *ins)


FINE = ("z", "y", "core", "x")


def shape_of(shape, dtype):
    return jax.ShapeDtypeStruct(shape, dtype)


def kept(shape, dtype):
    return pltpu.HBM(shape, dtype)


def shift(array, mask):
    return lax.ppermute(array, FINE, [(i, i ^ mask) for i in range(32)])


def hold(array, after):
    return lax.optimization_barrier((array, after))[0]


def pack_feed(hidden, back):
    width = back.shape[1]
    hidden = hidden.reshape(-1, 16, 4, width).transpose(0, 2, 1, 3).reshape(-1, 64, width)
    return jnp.concatenate([hidden, back.reshape(-1, 64, width)], axis=1)


def unpack_feed(blocks):
    width = blocks.shape[2]
    hidden = blocks[:, :64].reshape(-1, 4, 16, width).transpose(0, 2, 1, 3)
    return hidden.reshape(-1, 4 * width), blocks[:, 64:].reshape(-1, width)


def small_row(gains, table):
    table = jnp.pad(table.reshape(-1, H), ((0, 0), (0, 16 - H)))
    row = jnp.concatenate([gain.reshape(-1, 16) for gain in gains] + [table], axis=1)
    row = jnp.pad(row, ((0, 0), (0, LANES - row.shape[1])))
    return jnp.pad(row[:, None], ((0, 0), (0, 15), (0, 0))).reshape(-1, LANES)


def in_order(slots):
    return slots[jnp.array([CODES.index(block) for block in range(32)])]


def as_rows(slots):
    return in_order(slots).reshape(-1, slots.shape[2]).astype(F32)


def shift_plane(pieces):
    return [shift(piece, mask) for piece, mask in zip(pieces, PLANE[1:])]


def shift_column(pieces):
    return [shift(piece, code) for piece, code in zip(pieces, COLUMN[1:])]


class Near:
    axes = FINE

    def __init__(self, weights):
        self.me = lax.axis_index(FINE)
        small = small_row(weights[10:13], weights[13])
        own, rest, feed = pack(weights[:10], small)
        self.feed = lax.all_gather(feed, FINE, axis=0)
        z = self.me >> 3
        own = stack_lines(z, [own, *shift_column([own] * 3)])
        rest = hold(rest, own)
        pair = stack_lines(z & 1, [rest, shift(rest, COLUMN[1])])
        other = shift(pair, COLUMN[2])
        rest = stack_lines(z >> 1, [pair, other]).reshape((4,) + rest.shape)
        plane = [own, *shift_plane([own] * 3)]
        self.own = plane + [shift(hold(piece, other), 2) for piece in plane]
        rest = hold(rest, plane[1])
        self.plane = [rest, *shift_plane([rest] * 3)]

    def cross(self, after):
        plane = [hold(piece, after) for piece in self.plane]
        return plane + [shift(piece, 2) for piece in plane]

    def feed_core(self, slots):
        return lax.psum_scatter(slots.reshape((2, 4, 4) + slots.shape[1:]), "core")

    def feed_plane(self, slots):
        return lax.psum_scatter(slots, ("y", "x"))

    def feed_column(self, slots):
        return lax.psum_scatter(slots, "z")


class Far:
    axes = ("wide", "narrow")
    me = 0

    def __init__(self, weights):
        weights = [lax.all_gather(w, self.axes, axis=0, tiled=True) for w in weights]
        self.take(weights)

    def take(self, weights):
        self.own = self.pieces(*weights[:3], small_row(weights[10:13], weights[13]))
        self.rest = self.pieces(*weights[3:8])
        self.feed = pack_feed(weights[8], weights[9])

    def pieces(self, *parts):
        blocks = jnp.concatenate(parts, axis=1).reshape(32, 16, -1)[jnp.array(CODES)]
        return [blocks[4 * t : 4 * t + 4] for t in range(8)]

    def cross(self, after):
        return self.rest

    def feed_core(self, slots):
        return slots

    feed_plane = feed_column = feed_core


def on_device(near, tokens, memory, cotangent, dec_segments, mem_segments, padding, buckets,
              *weights):
    way = (Near if near else Far)(weights)
    result, grad_tokens, grad_memory, grads, examples, square = local_part(
        way, tokens, memory, cotangent, dec_segments, mem_segments, padding, buckets
    )
    if near:
        sent = lax.all_to_all(square, FINE, 0, 0, tiled=True)
        global_norm = jnp.sum(sent[:, 0])
    else:
        grads = [lax.psum_scatter(g, way.axes, scatter_dimension=0, tiled=True) for g in grads]
        global_norm = lax.psum(sum(jnp.sum(g * g) for g in grads), way.axes)
    return (result, grad_tokens, grad_memory, *grads, examples, global_norm / COUNT)


def local_part(way, tokens, memory, cotangent, dec_segments, mem_segments, padding, buckets):
    seqs, length, width = tokens.shape
    mem_length = memory.shape[1]
    steps = seqs // STEP_ROWS
    small_steps = seqs // SMALL_ROWS
    dec, mem = seqs * length, seqs * mem_length
    step_dec = STEP_ROWS * length
    ff = 4 * width

    buckets = buckets[None]
    tokens2, memory2, cotangent2 = (
        array.reshape(-1, width) for array in (tokens, memory, cotangent)
    )
    dma = pltpu.SemaphoreType.DMA

    me = jnp.full((1,), way.me, jnp.int32)
    flops = 2 * dec * width * width

    input_a, qkv_a, prob_a, attended_a, self_w, gains = call(
        self_forward_kernel, small_steps, me, (tokens2,), (dec_segments, padding, buckets), way.own,
        (
            kept((dec, width), BF16),
            kept((dec, 3 * width), BF16),
            kept((seqs, PAIRS, length, 2 * length), BF16),
            kept((dec, width), BF16),
        ),
        (kept((4, 8, 16, 3 * width + LANES), BF16), kept((8, width), F32)),
        [pltpu.VMEM((PAIRS, length, 2 * length), F32), dma((8,))],
        6 * flops, ("iwww", "iiiiww"), (), SHARED_LIMIT,
    )
    middle, input_b, query_b, kv_b, prob_b, attended_b, after_cross, cross_w = call(
        cross_forward_kernel, steps, me, (tokens2, attended_a, memory2),
        (dec_segments, mem_segments, gains), way.cross(attended_a),
        (
            kept((dec, width), BF16),
            kept((dec, width), BF16),
            kept((dec, width), BF16),
            kept((mem, 2 * width), BF16),
            kept((seqs, PAIRS, mem_length, 2 * length), BF16),
            kept((dec, width), BF16),
            kept((dec, width), BF16),
        ),
        (kept((4, 8, 16, 5 * width), BF16),),
        [dma((8,))],
        10 * flops, ("iiiwww", "iiiiiiiw"), (), SHARED_LIMIT,
    )
    self_w, cross_w = self_w.reshape(width, -1), cross_w.reshape(width, -1)
    total, square = kept((1, width), F32), shape_of((steps, 4 * STEP_ROWS, LANES), F32)
    token_shape = shape_of((steps, 8, length), F32)
    small_token = shape_of((small_steps, 8, length), F32)
    result, branch_b, feed_slots, gain_c, square_c, token_c = call(
        feed_kernel, ff // width, None, (),
        (after_cross, cotangent2, dec_segments, padding, gains), (way.feed,), (),
        (
            shape_of((dec, width), BF16),
            kept((dec, width), BF16),
            shape_of((32, 128, width), BF16),
            total,
            square,
            token_shape,
        ),
        [
            pltpu.VMEM((32, 16, ff), BF16),
            pltpu.VMEM((32, 64, width), BF16),
            *[pltpu.VMEM((dec, width), BF16)] * 2,
            *[pltpu.VMEM((width, dec), BF16)] * 2,
            *[pltpu.VMEM((dec, ff), BF16)] * 2,
            pltpu.VMEM((32, 16, width), BF16),
            pltpu.VMEM((8, 64, width), BF16),
            *[pltpu.VMEM((dec, width), BF16)] * 2,
            dma((4, 2)),
            dma((9,)),
            dma((steps, 2)),
        ],
        26 * flops, ("wwwww", "aaawww"),
    )
    feed_sum = way.feed_core(feed_slots)
    slot = shape_of((16, 16, 5 * width), BF16)
    grad_query_b, grad_kv_b, branch_a, cross_low, cross_high, gain_b, square_b = call(
        cross_backward_kernel, steps, me,
        (branch_b, middle, memory2, attended_a, input_b, query_b, kv_b, prob_b, attended_b),
        (dec_segments, gains, Cut(cross_w, (width, width), 0, 1),
         Cut(cross_w, (width, width), 0, 4)), (),
        (
            kept((dec, width), BF16),
            kept((mem, 2 * width), BF16),
            kept((dec, width), BF16),
            square,
        ),
        (kept(slot.shape, BF16), slot, total),
        [pltpu.VMEM((width, 5 * width), F32), pltpu.VMEM((step_dec, width), BF16)],
        20 * flops, ("iiiiiiiiiwwww", "iiiwwwi"),
    )
    feed_sum = way.feed_plane(hold(feed_sum, grad_query_b))
    near = isinstance(way, Near)
    if near:
        sent = shift(cross_high, 2)
    slot = shape_of((16, 16, 3 * width + LANES), BF16)
    grad_qkv_a, grad_tokens, self_low, self_high, square_a, table_square = call(
        self_backward_kernel, steps, me, (branch_a, tokens2, input_a, qkv_a, prob_a),
        (dec_segments, buckets, gains, Cut(cross_w, (width, width), 0, 0),
         Cut(self_w, (width, 3 * width), 0, 0), gain_b, gain_c),
        (),
        (
            kept((dec, 3 * width), BF16),
            shape_of((dec, width), BF16),
            square,
            shape_of((steps, STEP_ROWS, 8, LANES), F32),
        ),
        (kept(slot.shape, BF16), slot),
        [
            pltpu.VMEM((width, 3 * width), F32),
            pltpu.VMEM((1, width), F32),
            pltpu.VMEM((width, LANES), F32),
            pltpu.VMEM((H, LANES), F32),
            pltpu.VMEM((step_dec, width), BF16),
            pltpu.VMEM((STEP_ROWS, H, 8, length), F32),
        ],
        17 * flops, ("iiiiiwwwwwww", "iiwwii"),
    )

    def grams(pairs, *after):
        (tokens_part,) = call(
            gram_kernel, small_steps, None, pairs, (dec_segments,), (), (small_token,), (), [],
            2 * flops, ("i" * len(pairs) + "w", "i"), after, SHARED_LIMIT,
        )
        return tokens_part

    def fill_cross(*after):
        return grams((input_b, grad_query_b, attended_b, branch_b), *after)

    def fill_self(*after):
        return grams((input_a, grad_qkv_a, attended_a, branch_a), *after)

    def fill_memory(*after):
        return call(
            memory_backward_kernel, small_steps, None, (memory2, grad_kv_b),
            (mem_segments, Cut(cross_w, (width, 2 * width), 0, 1)), (),
            (shape_of((mem, width), BF16), shape_of((small_steps, 8, mem_length), F32)), (), [],
            10 * flops, ("iiww", "ii"), after, SHARED_LIMIT,
        )

    if near:
        self_sent = shift(self_high, 2)
        parts = pair_sum(((self_low, self_sent), (cross_low, sent)))
        crossed = shift_plane(parts[1:])
        token_b = fill_cross(parts[0])
        feed_sum = hold(feed_sum, token_b)
        grad_memory, token_m = fill_memory(feed_sum)
        feed_sum = way.feed_column(feed_sum)
        own, *rest = plane_sum([parts[0], *crossed], (token_m,))
        line_sent = shift_column(rest)
        token_a = fill_self(own)
        feed_sum = hold(feed_sum, token_a).reshape(128, width)
        grad_hidden, grad_back, square = small_call(
            feed_end_kernel, (feed_sum,), (token_a,),
            [shape_of((16, ff), F32), shape_of((64, width), F32), shape_of((8, LANES), F32)],
        )
        line = shape_of((slot.shape[1], width), F32)
        *parts, square = small_call(
            column_end_kernel, (own, *line_sent, square), (token_a,),
            [line] * 3 + [shape_of((16, LANES), F32)] + [line] * 5 + [shape_of((32, LANES), F32)],
        )
        self_grads, small, cross_grads = parts[:3], parts[3], parts[4:]
        token_a = hold(token_a, square)
    else:
        token_b, token_a = fill_cross(), fill_self()
        grad_memory, token_m = fill_memory()
        cross_sum = as_rows(jnp.concatenate([cross_low, cross_high]))
        self_sum = as_rows(jnp.concatenate([self_low, self_high]))
        cross_grads = [cross_sum[:, k * width : (k + 1) * width] for k in range(5)]
        self_grads = [self_sum[:, k * width : (k + 1) * width] for k in range(3)]
        small = self_sum[:, 3 * width :]
        grad_hidden, grad_back = unpack_feed(in_order(feed_sum).astype(F32))
        square = None
    grads = self_grads + cross_grads + [grad_hidden, grad_back]
    grads += [small[:, k] for k in range(3)]
    grads.append(small[:, 3].reshape(-1, 16)[:, :H].reshape(-1))

    def row_parts(parts, count):
        return parts[:, :count].reshape(seqs, -1)

    def by_example(part, segments):
        hits = segments[:, None, :] == lax.broadcasted_iota(jnp.int32, (1, NSEG, 1), 1)
        return jnp.sum(jnp.where(hits, part[:, None, :], 0.0), axis=-1)

    token_d = row_parts(token_a + token_b, SMALL_ROWS) + row_parts(token_c, STEP_ROWS)
    examples = by_example(token_d, dec_segments)
    examples = examples + by_example(row_parts(token_m, SMALL_ROWS), mem_segments)
    squares = (square_a + square_b + square_c)[:, :, 0].reshape(seqs, NSEG)
    examples = examples + squares + table_square[..., :NSEG, 0].reshape(seqs, NSEG)
    return (
        result.reshape(tokens.shape),
        grad_tokens.reshape(tokens.shape),
        grad_memory.reshape(memory.shape),
        grads,
        examples / COUNT,
        square,
    )


def solution(mesh):
    near = tuple(mesh.shape.values()) == (16, 2)
    if near:
        mesh = jax.sharding.Mesh(mesh.devices.reshape(4, 2, 2, 2), FINE)
    axes = tuple(mesh.axis_names)
    rows = P(axes)
    arrays, weights, vectors = (P(axes, None, None),) * 3, (P(axes, None),) * 10, (rows,) * 4
    placed = arrays + (P(axes, None),) * 3 + (P(),) + weights + vectors
    return jax.shard_map(
        partial(on_device, near),
        mesh=mesh,
        in_specs=placed,
        out_specs=arrays + weights + vectors + (P(axes, None), P()),
        check_vma=False,
    )
```

```python
import math
from functools import partial

import jax
import jax.numpy as jnp
from jax import lax
from jax.experimental import pallas as pl
from jax.experimental.pallas import tpu as pltpu
from jax.sharding import PartitionSpec as P

H = 8
DH = 64
NB = 32
NSEG = 4
COUNT = 4196096
EPSILON = 1e-06
FLOOR = -1e30
F32 = jnp.float32
BF16 = jnp.bfloat16
PAIRS = H // 2
LANES = 128
STEP_ROWS = 4
SMALL_ROWS = 4
VMEM_LIMIT = 62 * 2**20
SHARED_LIMIT = 48 * 2**20

COLUMN = (0, 8, 16, 24)
PLANE = (0, 1, 4, 5)
CODES = tuple(2 * c + mask + z for c in (0, 1) for mask in PLANE for z in COLUMN)


def nn(left, right):
    return lax.dot_general(left, right, (((1,), (0,)), ((), ())), preferred_element_type=F32)


def nt(left, right):
    return lax.dot_general(left, right, (((1,), (1,)), ((), ())), preferred_element_type=F32)


def tn(left, right):
    return lax.dot_general(left, right, (((0,), (0,)), ((), ())), preferred_element_type=F32)


def inverse_root(values):
    return lax.rsqrt(jnp.mean(values * values, axis=-1, keepdims=True) + EPSILON)


def head_masks(values):
    low = (lax.broadcasted_iota(jnp.int32, (1, LANES), 1) < DH).astype(BF16)
    return values * low, values * (1 - low)


def head_pair(values):
    return jnp.concatenate(head_masks(values), axis=0)


def fold_pair(both, queries):
    own = jnp.concatenate([both[:DH, :queries], both[DH:, queries:]], axis=0)
    return own.astype(BF16).T


def block_rows(block):
    return pl.ds(pl.multiple_of(block * 16, 16), 16)


def start_copies(pairs, sems):
    copies = [pltpu.make_async_copy(*pair, sems.at[i]) for i, pair in enumerate(pairs)]
    for copy in copies:
        copy.start()
    return copies


def column_pairs(me_ref, pieces, weight_ref):
    return [
        (piece, weight_ref.at[:, (me_ref[0] ^ CODES[4 * t]) & 7]) for t, piece in enumerate(pieces)
    ]


def read_rows(grad_w, block):
    return grad_w[block_rows(block), :].astype(BF16)


def store_slots(me_ref, low_ref, high_ref, read):
    for k, code in enumerate(CODES):
        target = low_ref if k < 16 else high_ref
        target[k % 16] = read(me_ref[0] ^ code)


def softmax_columns(scores):
    shifted = jnp.exp(scores - jnp.max(scores, axis=0, keepdims=True))
    return (shifted * (1.0 / jnp.sum(shifted, axis=0, keepdims=True))).astype(BF16)


def step_rows(ref, step, count):
    whole = ref[...].astype(F32)
    rows = whole[:count]
    for s in range(1, whole.shape[0] // count):
        rows = jnp.where(step == s, whole[s * count : (s + 1) * count], rows)
    return rows


def token_columns(lines):
    pad = 8 - lines.shape[0] % 8
    return jnp.concatenate([lines] + [lines[:1]] * (pad % 8), axis=0).T


def member_lines(lines):
    count, length = lines.shape
    codes = jnp.concatenate([lines[r : r + 1] + float(NSEG * r) for r in range(count)], axis=1)
    places = lax.broadcasted_iota(jnp.int32, (NSEG * count, count * length), 0).astype(F32)
    return (codes == places).astype(F32).astype(BF16)


def same_sum(products, lines, columns, r):
    same = columns[:, r : r + 1] == lines[r : r + 1]
    return jnp.sum(jnp.where(same, products, 0.0), axis=0, keepdims=True)


def pipelined(items, *stages):
    state = {}
    for tick in range(len(items) + len(stages) - 1):
        for depth, stage in enumerate(stages):
            n = tick - depth
            if 0 <= n < len(items):
                state[n] = stage(items[n], state.get(n))


def row_pairs(count):
    return [(r, p) for r in range(count) for p in range(PAIRS)]


def gram(left):
    return nt(left, left)


def self_forward_kernel(me_ref, tokens_ref, dec_ref, padding_ref, buckets_ref, *refs):
    pieces, refs = refs[:8], refs[8:]
    input_ref, qkv_ref, prob_ref, attended_ref, weight_ref, gains_ref = refs[:6]
    bias_ref, sems = refs[6:]
    length = dec_ref.shape[1]
    width = tokens_ref.shape[1]

    @pl.when(pl.program_id(0) == 0)
    def _():
        for copy in start_copies(column_pairs(me_ref, pieces, weight_ref), sems):
            copy.wait()
        small_lines = weight_ref[:, :, :, 3 * width :].reshape(width, LANES)
        first = lax.broadcasted_iota(jnp.int32, (32, width), 1)
        pick = first == 16 * lax.broadcasted_iota(jnp.int32, (32, width), 0)
        small = nn(pick.astype(F32).astype(BF16), small_lines).astype(BF16)
        lane = lax.broadcasted_iota(jnp.int32, (LANES, width), 0)
        feature = lax.broadcasted_iota(jnp.int32, (LANES, width), 1)
        block = lax.broadcasted_iota(jnp.int32, (32, width), 0)
        lines = []
        for k in range(4):
            spread = nn(small, (lane == 16 * k + feature % 16).astype(F32).astype(BF16))
            lines.append(
                jnp.sum(jnp.where(block == first // 16, spread, 0.0), axis=0, keepdims=True)
            )
        gains_ref[...] = jnp.concatenate(lines + lines, axis=0)
        place = lax.broadcasted_iota(jnp.int32, (H, width), 1) % 16
        head = lax.broadcasted_iota(jnp.int32, (H, width), 0)
        table = jnp.where(place == head, lines[3], 0.0).astype(BF16)
        bucket = lax.broadcasted_iota(jnp.int32, (width, length), 0) // 16
        curves = nn(table, (bucket == buckets_ref[...]).astype(F32).astype(BF16))
        for h in range(H):
            curve = jnp.broadcast_to(curves[h : h + 1, :], (length, length))
            lanes = slice((h % 2) * length, (h % 2 + 1) * length)
            bias_ref[h // 2, :, lanes] = pltpu.roll(curve, 0, 1, stride=1, stride_axis=0)

    values = tokens_ref[...].astype(F32)
    normed = (values * inverse_root(values) * gains_ref[0:1, :]).astype(BF16)
    input_ref[...] = normed
    for first in range(0, 3 * width, 256):
        cols = slice(first, first + 256)
        qkv_ref[:, cols] = nn(
            normed, weight_ref[:, :, :, cols].reshape(width, 256)
        ).astype(BF16)

    step = pl.program_id(0)
    count = tokens_ref.shape[0] // length
    segments, real = step_rows(dec_ref, step, count), step_rows(padding_ref, step, count)
    segment_columns, real_columns = token_columns(segments), token_columns(real)
    key_i = lax.broadcasted_iota(jnp.int32, (length, length), 0)
    query_i = lax.broadcasted_iota(jnp.int32, (length, length), 1)

    masks = []
    for r in range(count):
        allowed = (segment_columns[:, r : r + 1] == segments[r : r + 1]) & (key_i <= query_i)
        allowed = allowed & ((real_columns[:, r : r + 1] > 0.0) | (key_i == query_i))
        mask = jnp.where(allowed, 0.0, FLOOR)
        masks.append(jnp.concatenate([mask, mask], axis=1))

    def part(item, k):
        r, p = item
        return qkv_ref[r * length : (r + 1) * length, k * width + p * LANES : k * width + (p + 1) * LANES]

    def scores(item, _):
        return nt(part(item, 1), head_pair(part(item, 0)))

    def weigh(item, score):
        r, p = item
        prob = softmax_columns(score + bias_ref[p] + masks[r])
        prob_ref[r, p] = prob
        return prob, part(item, 2).T

    def mix(item, given):
        r, p = item
        prob, value = given
        rows, lanes = slice(r * length, (r + 1) * length), slice(p * LANES, (p + 1) * LANES)
        attended_ref[rows, lanes] = fold_pair(nn(value, prob), length)

    pipelined(row_pairs(count), scores, weigh, mix)


def cross_forward_kernel(me_ref, tokens_ref, attended_a_ref, memory_ref, dec_ref, mem_ref,
                         gains_ref, *refs):
    pieces, refs = refs[:8], refs[8:]
    (middle_ref, input_ref, query_ref, kv_ref, prob_ref, attended_ref, after_ref, weight_ref,
     sems) = refs
    mem_length, length = mem_ref.shape[1], dec_ref.shape[1]
    width = tokens_ref.shape[1]

    @pl.when(pl.program_id(0) == 0)
    def _():
        for copy in start_copies(column_pairs(me_ref, pieces, weight_ref), sems):
            copy.wait()

    def weight(k):
        return weight_ref[:, :, :, k * width : (k + 1) * width].reshape(width, width)

    for k in range(2):
        kv_ref[:, k * width : (k + 1) * width] = nn(memory_ref[...], weight(k + 2)).astype(BF16)
    values = tokens_ref[...].astype(F32) + nn(attended_a_ref[...], weight(0))
    middle_ref[...] = values.astype(BF16)
    normed = (values * inverse_root(values) * gains_ref[1:2, :]).astype(BF16)
    input_ref[...] = normed
    query_ref[...] = nn(normed, weight(1)).astype(BF16)

    step = pl.program_id(0)
    count = tokens_ref.shape[0] // length
    segments = step_rows(dec_ref, step, count)
    mem_columns = token_columns(step_rows(mem_ref, step, count))

    masks = []
    for r in range(count):
        mask = jnp.where(mem_columns[:, r : r + 1] == segments[r : r + 1], 0.0, FLOOR)
        masks.append(jnp.concatenate([mask, mask], axis=1))

    def places(item):
        r, p = item
        rows, lanes = slice(r * length, (r + 1) * length), slice(p * LANES, (p + 1) * LANES)
        upper = slice(width + p * LANES, width + (p + 1) * LANES)
        return rows, slice(r * mem_length, (r + 1) * mem_length), lanes, upper

    def scores(item, _):
        rows, mem_rows, lanes, _ = places(item)
        return nt(kv_ref[mem_rows, lanes], head_pair(query_ref[rows, lanes]))

    def weigh(item, score):
        r, p = item
        _, mem_rows, _, upper = places(item)
        prob = softmax_columns(score + masks[r])
        prob_ref[r, p] = prob
        return prob, kv_ref[mem_rows, upper].T

    def mix(item, given):
        rows, _, lanes, _ = places(item)
        prob, value = given
        attended_ref[rows, lanes] = fold_pair(nn(value, prob), length)

    pipelined(row_pairs(count), scores, weigh, mix)
    after = values + nn(attended_ref[...], weight(4))
    after_ref[...] = after.astype(BF16)


def norm_back(values, gain, grad_normed):
    inverse = inverse_root(values)
    scaled = values * inverse
    upper = grad_normed * gain
    grad = inverse * (upper - scaled * jnp.mean(upper * scaled, axis=-1, keepdims=True))
    return grad, grad_normed * scaled


def gain_sums(terms, segments, total_ref, square_ref):
    sums = nn(member_lines(segments), terms.astype(BF16))
    total_ref[...] += jnp.sum(sums, axis=0, keepdims=True)
    square = jnp.sum(sums * sums, axis=1, keepdims=True)
    square_ref[...] = jnp.broadcast_to(square, square_ref.shape)


def feed_kernel(after_ref, cotangent_ref, dec_ref, padding_ref, gains_ref, gathered_ref,
                result_ref, branch_b_ref, slots_ref, active_out, grad_out_ref, normed_out,
                branch_out, total_ref, square_ref, w_in_ref, w_out_ref, normed_ref, branch_ref,
                normed_flip, branch_flip, active_ref, grad_ref, in_slots, out_slots, result_tile,
                branch_tile, load_sems, sems, end_sems, keep_sems, line_sems):
    part = pl.program_id(0)
    parts = pl.num_programs(0)
    count, length = dec_ref.shape
    dec, width = after_ref.shape
    ff = w_in_ref.shape[2]
    tile = STEP_ROWS * length
    tiles = [slice(t * tile, (t + 1) * tile) for t in range(dec // tile)]

    def loads(which):
        rows = pl.ds(pl.multiple_of(which * 16, 16), 16)
        cols = pl.ds(pl.multiple_of(which * width, width), width)
        blocks = pl.ds(which * 8, 8)
        pairs = (
            (gathered_ref.at[:, rows, :], w_in_ref.at[:, :, cols]),
            (gathered_ref.at[blocks, 64:, :], w_out_ref.at[blocks]),
        )
        return [
            pltpu.make_async_copy(*pair, load_sems.at[which, i]) for i, pair in enumerate(pairs)
        ]

    def keeps(which):
        cols = pl.ds(pl.multiple_of(which * width, width), width)
        pairs = ((active_ref, active_out), (grad_ref, grad_out_ref))
        return [
            pltpu.make_async_copy(source.at[:, cols], target.at[:, cols], keep_sems.at[which, i])
            for i, (source, target) in enumerate(pairs)
        ]

    lines = [
        pltpu.make_async_copy(normed_ref, normed_out, line_sems.at[0]),
        pltpu.make_async_copy(branch_ref, branch_out, line_sems.at[1]),
    ]

    @pl.when(part == 0)
    def _():
        for which in range(ff // width):
            for copy in loads(which):
                copy.start()
        real = token_columns(padding_ref[...].astype(F32))
        for r in range(count):
            rows = slice(r * length, (r + 1) * length)
            branch_ref[rows, :] = (
                cotangent_ref[rows, :].astype(F32) * real[:, r : r + 1]
            ).astype(BF16)
        for rows in tiles:
            values = after_ref[rows, :].astype(F32)
            normed = (values * inverse_root(values) * gains_ref[2:3, :]).astype(BF16)
            normed_ref[rows, :] = normed
            normed_flip[:, rows] = normed.T
            branch_flip[:, rows] = branch_ref[rows, :].T

        for copy in lines:
            copy.start()

    for copy in loads(part):
        copy.wait()
    root = 0.7978845608028654
    half_width = width // 2
    for sub in range(2):
        first = pl.multiple_of(part * width + sub * half_width, half_width)
        cols = pl.ds(first, half_width)
        hidden = nn(normed_ref[...], w_in_ref[:, :, cols].reshape(width, half_width))
        square = hidden * hidden
        bent = jnp.tanh(hidden * (root + (root * 0.044715) * square))
        half = 0.5 + 0.5 * bent
        slope = hidden * (2.0 * root + (6.0 * root * 0.044715) * square)
        slope = half + half * (slope * (1.0 - half))
        active_ref[:, cols] = (hidden * half).astype(BF16)
        w_out = w_out_ref[pl.ds(part * 8 + sub * 4, 4)].reshape(half_width, width)
        grad_ref[:, cols] = (nt(branch_ref[...], w_out) * slope).astype(BF16)
    for copy in keeps(part):
        copy.start()
    cols = pl.ds(pl.multiple_of(part * width, width), width)
    grad_in = nn(normed_flip[...], grad_ref[:, cols]).astype(BF16)
    grad_out = nn(branch_flip[...], active_ref[:, cols]).astype(BF16).T

    def sends(which):
        pairs = [(in_slots, slots_ref.at[:, pl.ds(pl.multiple_of(which * 16, 16), 16), :])]
        for i, k in enumerate(range(0, 32, 4)):
            pairs.append((out_slots.at[i], slots_ref.at[k + which, 64:, :]))
        return [pltpu.make_async_copy(*pair, sems.at[i]) for i, pair in enumerate(pairs)]

    @pl.when(part > 0)
    def _():
        for copy in sends(part - 1):
            copy.wait()

    for k, block in enumerate(CODES):
        in_slots[k] = grad_in[16 * block : 16 * block + 16]
    for i, k in enumerate(range(0, 32, 4)):
        block = CODES[k]
        out_slots[i] = grad_out[64 * block : 64 * block + 64]
    for copy in sends(part):
        copy.start()

    @pl.when(part == parts - 1)
    def _():
        segments = dec_ref[...].astype(F32)
        total_ref[...] = jnp.zeros_like(total_ref)
        ends = []
        w_in, w_out = w_in_ref[...].reshape(width, ff), w_out_ref[...].reshape(ff, width)
        for t, rows in enumerate(tiles):
            values = after_ref[rows, :].astype(F32)
            result_tile[rows, :] = (values + nn(active_ref[rows, :], w_out)).astype(BF16)
            grad, terms = norm_back(values, gains_ref[2:3, :], nt(grad_ref[rows, :], w_in))
            branch_tile[rows, :] = (branch_ref[rows, :].astype(F32) + grad).astype(BF16)
            pairs = [(result_tile.at[rows], result_ref.at[rows])]
            pairs.append((branch_tile.at[rows], branch_b_ref.at[rows]))
            ends.extend(start_copies(pairs, end_sems.at[t]))
            own = segments[t * STEP_ROWS : (t + 1) * STEP_ROWS]
            gain_sums(terms, own, total_ref, square_ref.at[t])
        for which in range(ff // width):
            for copy in keeps(which):
                copy.wait()
        for copy in sends(part) + ends + lines:
            copy.wait()


def score_grads(prob, grad_prob):
    prob = prob.astype(F32)
    dots = jnp.sum(prob * grad_prob, axis=0, keepdims=True)
    return prob * (grad_prob - dots)


def cross_backward_kernel(me_ref, branch_ref, middle_ref, memory_ref, attended_a_ref, input_ref,
                          query_ref, kv_ref, prob_ref, attended_ref, dec_ref, gains_ref,
                          query_w_ref, out_w_ref, grad_query_ref, grad_kv_ref, branch_a_ref, low_ref, high_ref,
                          total_ref, square_ref, grad_w, grad_attended):
    step = pl.program_id(0)
    mem_length = prob_ref.shape[2]
    length = prob_ref.shape[3] // 2
    width = branch_ref.shape[1]

    @pl.when(step == 0)
    def _():
        grad_w[...] = jnp.zeros_like(grad_w)
        total_ref[...] = jnp.zeros_like(total_ref)

    branch = branch_ref[...]
    grad_attended[...] = nt(branch, out_w_ref[...]).astype(BF16)

    def places(item):
        r, p = item
        rows, lanes = slice(r * length, (r + 1) * length), slice(p * LANES, (p + 1) * LANES)
        upper = slice(width + p * LANES, width + (p + 1) * LANES)
        return rows, slice(r * mem_length, (r + 1) * mem_length), lanes, upper

    def enter(item, _):
        rows, mem_rows, lanes, upper = places(item)
        grad_out = head_pair(grad_attended[rows, lanes])
        return grad_out, nt(kv_ref[mem_rows, upper], grad_out)

    def bend(item, given):
        r, p = item
        grad_out, grad_prob = given
        _, mem_rows, lanes, _ = places(item)
        grad_score = score_grads(prob_ref[r, p], grad_prob).astype(BF16)
        return grad_out, grad_score, kv_ref[mem_rows, lanes].T

    def leave(item, given):
        r, p = item
        grad_out, grad_score, key = given
        rows, mem_rows, lanes, upper = places(item)
        query = head_pair(query_ref[rows, lanes])
        grad_kv_ref[mem_rows, lanes] = nn(grad_score, query).astype(BF16)
        grad_kv_ref[mem_rows, upper] = nn(prob_ref[r, p], grad_out).astype(BF16)
        grad_query_ref[rows, lanes] = fold_pair(nn(key, grad_score), length)

    pipelined(row_pairs(STEP_ROWS), enter, bend, leave)
    grad_query = grad_query_ref[...]
    grad_normed = nt(grad_query, query_w_ref[...])
    grad, terms = norm_back(middle_ref[...].astype(F32), gains_ref[1:2, :], grad_normed)
    branch_a = (branch.astype(F32) + grad).astype(BF16)
    branch_a_ref[...] = branch_a
    gain_sums(terms, step_rows(dec_ref, step, STEP_ROWS), total_ref, square_ref.at[0])
    grad_w[:, :width] += tn(attended_a_ref[...], branch_a)
    grad_w[:, width : 2 * width] += tn(input_ref[...], grad_query)
    grad_w[:, 2 * width : 4 * width] += tn(memory_ref[...], grad_kv_ref[...])
    grad_w[:, 4 * width :] += tn(attended_ref[...], branch)

    @pl.when(step == pl.num_programs(0) - 1)
    def _():
        store_slots(me_ref, low_ref, high_ref, partial(read_rows, grad_w))


def self_backward_kernel(me_ref, branch_ref, tokens_ref, input_ref, qkv_ref, prob_ref, dec_ref,
                         buckets_ref, gains_ref, out_w_ref, weight_ref, total_b_ref, total_c_ref,
                         grad_qkv_ref, grad_tokens_ref, low_ref, high_ref, square_ref,
                         table_square_ref, grad_w, total_ref, small_ref, table_ref, grad_attended,
                         bands):
    step = pl.program_id(0)
    length = prob_ref.shape[2]
    width = branch_ref.shape[1]
    grad_attended[...] = nt(branch_ref[...], out_w_ref[...]).astype(BF16)

    @pl.when(step == 0)
    def _():
        table_ref[...] = jnp.zeros_like(table_ref)
        bands[...] = jnp.zeros_like(bands)
        grad_w[...] = jnp.zeros_like(grad_w)
        total_ref[...] = jnp.zeros_like(total_ref)

    row_i = lax.broadcasted_iota(jnp.int32, (length, length), 0)
    col_i = lax.broadcasted_iota(jnp.int32, (length, length), 1)
    flip = (row_i + col_i == length - 1).astype(F32).astype(BF16)
    columns = token_columns(step_rows(dec_ref, step, STEP_ROWS)).astype(BF16)
    turned = nn(flip, columns)

    members = [
        [
            jnp.broadcast_to((turned[:, r : r + 1] == float(e)).astype(F32), (length, length))
            for e in range(NSEG)
        ]
        for r in range(STEP_ROWS)
    ]

    def part(item, k):
        r, p = item
        lanes = slice(k * width + p * LANES, k * width + (p + 1) * LANES)
        return slice(r * length, (r + 1) * length), lanes

    def enter(item, _):
        grad_out = head_pair(grad_attended[part(item, 0)])
        return grad_out, nt(qkv_ref[part(item, 2)], grad_out)

    def bend(item, given):
        r, p = item
        grad_out, grad_prob = given
        grad_score = score_grads(prob_ref[r, p], grad_prob).astype(BF16)
        return grad_out, grad_score, jnp.concatenate([qkv_ref[part(item, 1)].T, flip], axis=0)

    def leave(item, given):
        r, p = item
        grad_out, grad_score, key = given
        query = head_pair(qkv_ref[part(item, 0)])
        grad_qkv_ref[part(item, 1)] = nn(grad_score, query).astype(BF16)
        grad_qkv_ref[part(item, 2)] = nn(prob_ref[r, p], grad_out).astype(BF16)
        both = nn(key, grad_score)
        grad_qkv_ref[part(item, 0)] = fold_pair(both[:length], length)
        return both[length:]

    def count_buckets(item, turned_score):
        r, p = item
        for h in range(2):
            own = turned_score[:, h * length : (h + 1) * length]
            own = pltpu.roll(own, 1, 1, stride=1, stride_axis=0)
            for e in range(NSEG):
                bands[r, 2 * p + h, e : e + 1, :] = jnp.sum(
                    own * members[r][e], axis=0, keepdims=True
                )

    pipelined(row_pairs(STEP_ROWS), enter, bend, leave, count_buckets)
    bucket = lax.broadcasted_iota(jnp.int32, (LANES, length), 0)
    near = (bucket == buckets_ref[...]).astype(F32)
    flat = bands[...].reshape(STEP_ROWS * H * 8, length)
    per_bucket = lax.dot_general(
        flat, near, (((1,), (1,)), ((), ())), preferred_element_type=F32,
        precision=lax.Precision.HIGHEST,
    ).reshape(STEP_ROWS, H, 8, LANES)
    table_ref[...] += jnp.sum(jnp.sum(per_bucket, axis=0), axis=1)
    squares = jnp.sum(jnp.sum(per_bucket * per_bucket, axis=1), axis=-1, keepdims=True)
    table_square_ref[0] = jnp.broadcast_to(squares, (STEP_ROWS, 8, LANES))

    grad_qkv = grad_qkv_ref[...]
    grad_normed = nt(grad_qkv, weight_ref[...])
    grad, terms = norm_back(tokens_ref[...].astype(F32), gains_ref[0:1, :], grad_normed)
    grad_tokens_ref[...] = (branch_ref[...].astype(F32) + grad).astype(BF16)

    gain_sums(terms, step_rows(dec_ref, step, STEP_ROWS), total_ref, square_ref.at[0])
    flipped = input_ref[...].T
    for first in range(0, 3 * width, 256):
        grad_w[:, first : first + 256] += nn(flipped, grad_qkv_ref[:, first : first + 256])

    @pl.when(step == pl.num_programs(0) - 1)
    def _():
        bucket = lax.broadcasted_iota(jnp.int32, (LANES, width), 0)
        place = lax.broadcasted_iota(jnp.int32, (LANES, width), 1)
        spread = nn(table_ref[...].astype(BF16), (place // 16 == bucket).astype(F32).astype(BF16))
        head = lax.broadcasted_iota(jnp.int32, (H, width), 0)
        lane = lax.broadcasted_iota(jnp.int32, (H, width), 1)
        table = jnp.sum(jnp.where(lane % 16 == head, spread, 0.0), axis=0, keepdims=True)
        small = jnp.zeros((LANES, width), F32)
        row_i = lax.broadcasted_iota(jnp.int32, (LANES, width), 0)
        for k, line in enumerate((total_ref[...], total_b_ref[...], total_c_ref[...], table)):
            small = jnp.where(row_i == k, line, small)
        small_ref[...] = small.T

        def read(block):
            return jnp.concatenate(
                [read_rows(grad_w, block), read_rows(small_ref, block)], axis=1
            )

        store_slots(me_ref, low_ref, high_ref, read)


def pair_sum_kernel(*refs):
    groups, outs, buffers, total = (refs[:2], refs[2:4]), refs[4:8], refs[8:12], refs[12]
    load_sems, store_sems = refs[13:]
    places = [pl.ds(4 * t, 4) for t in range(4)]
    loads = []
    for i, ref in enumerate((*groups[0], *groups[1])):
        pairs = [(ref.at[p], buffers[i].at[p]) for p in places]
        loads.append(start_copies(pairs, load_sems.at[i]))
    stores = []
    for t, p in enumerate(places):
        start = 0
        for low, sent in ((0, 1), (2, 3)):
            loads[low][t].wait()
            loads[sent][t].wait()
            own = buffers[low][p].astype(F32) + buffers[sent][p].astype(F32)
            total[p, :, start : start + own.shape[2]] = own.astype(BF16)
            start += own.shape[2]
        stores.append(pltpu.make_async_copy(total.at[p], outs[t], store_sems.at[t]))
        stores[t].start()
    for store in stores:
        store.wait()


def pair_sum(groups):
    arrays = [array for group in groups for array in group]
    lanes = sum(low.shape[2] for low, _ in groups)
    shape = arrays[0].shape[:2] + (lanes,)
    return pl.pallas_call(
        pair_sum_kernel,
        out_shape=(shape_of((4,) + shape[1:], BF16),) * 4,
        in_specs=[pl.BlockSpec(memory_space=pl.ANY)] * 4,
        out_specs=[pl.BlockSpec(memory_space=pl.ANY)] * 4,
        scratch_shapes=[pltpu.VMEM(array.shape, BF16) for array in arrays]
        + [pltpu.VMEM(shape, BF16)]
        + [pltpu.SemaphoreType.DMA((4, 4)), pltpu.SemaphoreType.DMA((4,))],
        compiler_params=pltpu.CompilerParams(vmem_limit_bytes=SHARED_LIMIT),
    )(*[in_hbm(a) if i % 2 == 0 else a for i, a in enumerate(arrays)])


def plane_sum_kernel(a_ref, b_ref, c_ref, d_ref, own_ref, *outs):
    for s in range(4):
        total = a_ref[s].astype(F32) + b_ref[s].astype(F32)
        total = total + c_ref[s].astype(F32) + d_ref[s].astype(F32)
        if s == 0:
            own_ref[...] = total
        else:
            outs[s - 1][...] = total.astype(BF16)


def plane_sum(pieces, after):
    line = pieces[0].shape[1:]
    return small_call(
        plane_sum_kernel, pieces, after, (shape_of(line, F32),) + (shape_of(line, BF16),) * 3
    )


def square_sum(values):
    return jnp.sum(jnp.sum(values * values, axis=0, keepdims=True), axis=1, keepdims=True)


def feed_end_kernel(sum_ref, hidden_ref, back_ref, square_ref):
    total = sum_ref[...].astype(F32)
    width = total.shape[1]
    for j in range(4):
        hidden_ref[:, j * width : (j + 1) * width] = total[16 * j : 16 * (j + 1)]
    back_ref[...] = total[64:]
    square_ref[...] = jnp.broadcast_to(square_sum(total), square_ref.shape)


def column_end_kernel(own_ref, b_ref, c_ref, d_ref, *refs):
    squares, outs, square_ref = refs[:1], refs[1:-1], refs[-1]
    total = own_ref[...] + b_ref[...].astype(F32)
    total = total + c_ref[...].astype(F32) + d_ref[...].astype(F32)
    start = 0
    for out in outs:
        out[...] = total[:, start : start + out.shape[1]]
        start += out.shape[1]
    square = square_sum(total)
    for given in squares:
        square = square + given[0:1, 0:1]
    square_ref[...] = jnp.broadcast_to(square, square_ref.shape)


def staged(kernel, ins, outs):
    def run(*refs):
        count = ins + outs
        given, inner, sems = refs[:count], refs[count : 2 * count], refs[2 * count]
        for copy in start_copies(list(zip(given[:ins], inner[:ins])), sems):
            copy.wait()
        kernel(*inner)
        for copy in start_copies(list(zip(inner[ins:], given[ins:])), sems):
            copy.wait()

    return run


def small_call(kernel, ins, after, outs):
    arrays = [*ins, *outs]
    return pl.pallas_call(
        ignoring(staged(kernel, len(ins), len(outs)), len(ins), len(after)),
        out_shape=outs,
        in_specs=[pl.BlockSpec(memory_space=pl.ANY)] * (len(ins) + len(after)),
        out_specs=[pl.BlockSpec(memory_space=pl.ANY)] * len(outs),
        scratch_shapes=[pltpu.VMEM(array.shape, array.dtype) for array in arrays]
        + [pltpu.SemaphoreType.DMA((len(arrays),))],
        compiler_params=pltpu.CompilerParams(vmem_limit_bytes=SHARED_LIMIT),
    )(*ins, *after)


def stack_kernel(me_ref, *refs):
    lines, out_ref, sems = refs[:-2], refs[-2], refs[-1]
    pairs = [(line, out_ref.at[me_ref[0] ^ s]) for s, line in enumerate(lines)]
    for copy in start_copies(pairs, sems):
        copy.wait()


def stack_lines(place, lines):
    return pl.pallas_call(
        stack_kernel,
        out_shape=shape_of((len(lines),) + lines[0].shape, BF16),
        in_specs=[pl.BlockSpec(memory_space=pltpu.SMEM)]
        + [pl.BlockSpec(memory_space=pl.ANY)] * len(lines),
        out_specs=pl.BlockSpec(memory_space=pl.ANY),
        scratch_shapes=[pltpu.SemaphoreType.DMA((len(lines),))],
        compiler_params=pltpu.CompilerParams(vmem_limit_bytes=SHARED_LIMIT),
    )(jnp.full((1,), place, jnp.int32), *lines)


def pack_kernel(*refs):
    ins, (own_ref, cross_ref, feed_ref) = refs[:11], refs[11:]
    width = ins[0].shape[1]
    for k, line in enumerate((*ins[:3], ins[10])):
        own_ref[:, k * width : k * width + line.shape[1]] = line[...]
    for k in range(5):
        cross_ref[:, k * width : (k + 1) * width] = ins[3 + k][...]
    for j in range(ins[8].shape[1] // width):
        feed_ref[16 * j : 16 * (j + 1), :] = ins[8][:, j * width : (j + 1) * width]
    feed_ref[64:, :] = ins[9][...]


def pack(weights, small):
    width = weights[0].shape[1]
    outs = [shape_of((16, cols), BF16) for cols in (3 * width + LANES, 5 * width)]
    outs.append(shape_of((128, width), BF16))
    return small_call(pack_kernel, (*map(in_hbm, weights), small), (), outs)


def fill_kernel(memory_ref, grad_kv_ref, *refs):
    pairs, (mem_ref, dec_ref, weight_ref, grad_memory_ref, token_m_ref, token_ref) = (
        refs[:4], refs[4:]
    )
    mem_length, length = mem_ref.shape[1], dec_ref.shape[1]
    width = memory_ref.shape[1]
    for first in range(0, width, 256):
        rows = slice(first, first + 256)
        grad_memory_ref[:, rows] = nt(grad_kv_ref[...], weight_ref[rows, :]).astype(BF16)
    count = memory_ref.shape[0] // mem_length
    segments = step_rows(mem_ref, pl.program_id(0), count)
    columns = token_columns(segments)
    for r in range(count):
        rows = slice(r * mem_length, (r + 1) * mem_length)
        products = gram(memory_ref[rows, :]) * gram(grad_kv_ref[rows, :])
        token_m_ref[0, r : r + 1, :] = same_sum(products, segments, columns, r)
    gram_kernel(*pairs, dec_ref, token_ref)


def gram_kernel(*refs):
    pairs, dec_ref, token_ref = refs[:-2], refs[-2], refs[-1]
    length = dec_ref.shape[1]
    count = pairs[0].shape[0] // length
    segments = step_rows(dec_ref, pl.program_id(0), count)
    columns = token_columns(segments)
    for r in range(count):
        rows = slice(r * length, (r + 1) * length)
        products = sum(
            gram(left[rows, :]) * gram(right[rows, :])
            for left, right in zip(pairs[::2], pairs[1::2])
        )
        token_ref[0, r : r + 1, :] = same_sum(products, segments, columns, r)


def rows_spec(array, steps):
    shape = (array.shape[0] // steps,) + array.shape[1:]
    return pl.BlockSpec(shape, lambda i, *_: (i,) + (0,) * (len(shape) - 1))


class Cut:
    def __init__(self, array, shape, *index):
        self.array, self.spec = array, pl.BlockSpec(shape, lambda i, *_: index)


def whole_spec(array):
    return pl.BlockSpec(array.shape, lambda i, *_: (0,) * len(array.shape))


def in_hbm(array):
    return pltpu.with_memory_space_constraint(array, pltpu.HBM)


def ignoring(kernel, first, count):
    return lambda *refs: kernel(*refs[:first], *refs[first + count :])


def call(kernel, steps, me, blocked, whole, pieces, outs_blocked, outs_whole, scratch, flops,
         order, after=(), limit=VMEM_LIMIT):
    ins, in_specs = [], []
    blocked, whole = list(blocked), list(whole)
    for kind in order[0]:
        array = (blocked if kind == "i" else whole).pop(0)
        if isinstance(array, Cut):
            ins.append(array.array)
            in_specs.append(array.spec)
            continue
        ins.append(array)
        in_specs.append(rows_spec(array, steps) if kind == "i" else whole_spec(array))
    ins = [in_hbm(array) for array in ins]
    kernel = ignoring(kernel, len(ins) + len(pieces) + (me is not None), len(after))
    ins += [*pieces, *after]
    in_specs += [pl.BlockSpec(memory_space=pl.ANY)] * (len(pieces) + len(after))
    outs, out_specs = [], []
    outs_blocked, outs_whole = list(outs_blocked), list(outs_whole)
    for kind in order[1]:
        out = (outs_blocked if kind == "i" else outs_whole).pop(0)
        outs.append(out)
        if kind == "a":
            out_specs.append(pl.BlockSpec(memory_space=pl.ANY))
        else:
            out_specs.append(rows_spec(out, steps) if kind == "i" else whole_spec(out))
    moved = sum(math.prod(a.shape) * a.dtype.itemsize for a in ins + outs) if flops else 0
    prefetch = 0 if me is None else 1
    return pl.pallas_call(
        kernel,
        out_shape=outs,
        grid_spec=pltpu.PrefetchScalarGridSpec(
            num_scalar_prefetch=prefetch,
            grid=(steps,),
            in_specs=in_specs,
            out_specs=out_specs,
            scratch_shapes=scratch,
        ),
        compiler_params=pltpu.CompilerParams(
            dimension_semantics=("arbitrary",), vmem_limit_bytes=limit
        ),
        cost_estimate=pl.CostEstimate(flops=flops, bytes_accessed=moved, transcendentals=0),
    )(*(() if me is None else (me,)), *ins)


FINE = ("z", "y", "core", "x")


def shape_of(shape, dtype):
    return jax.ShapeDtypeStruct(shape, dtype)


def kept(shape, dtype):
    return pltpu.HBM(shape, dtype)


def shift(array, mask):
    return lax.ppermute(array, FINE, [(i, i ^ mask) for i in range(32)])


def hold(array, after):
    return lax.optimization_barrier((array, after))[0]


def pack_feed(hidden, back):
    width = back.shape[1]
    hidden = hidden.reshape(-1, 16, 4, width).transpose(0, 2, 1, 3).reshape(-1, 64, width)
    return jnp.concatenate([hidden, back.reshape(-1, 64, width)], axis=1)


def unpack_feed(blocks):
    width = blocks.shape[2]
    hidden = blocks[:, :64].reshape(-1, 4, 16, width).transpose(0, 2, 1, 3)
    return hidden.reshape(-1, 4 * width), blocks[:, 64:].reshape(-1, width)


def small_row(gains, table):
    table = jnp.pad(table.reshape(-1, H), ((0, 0), (0, 16 - H)))
    row = jnp.concatenate([gain.reshape(-1, 16) for gain in gains] + [table], axis=1)
    row = jnp.pad(row, ((0, 0), (0, LANES - row.shape[1])))
    return jnp.pad(row[:, None], ((0, 0), (0, 15), (0, 0))).reshape(-1, LANES)


def in_order(slots):
    return slots[jnp.array([CODES.index(block) for block in range(32)])]


def as_rows(slots):
    return in_order(slots).reshape(-1, slots.shape[2]).astype(F32)


def shift_plane(pieces):
    return [shift(piece, mask) for piece, mask in zip(pieces, PLANE[1:])]


def shift_column(pieces):
    return [shift(piece, code) for piece, code in zip(pieces, COLUMN[1:])]


class Near:
    axes = FINE

    def __init__(self, weights):
        self.me = lax.axis_index(FINE)
        small = small_row(weights[10:13], weights[13])
        own, rest, feed = pack(weights[:10], small)
        self.feed = lax.all_gather(feed, FINE, axis=0)
        z = self.me >> 3
        own = stack_lines(z, [own, *shift_column([own] * 3)])
        rest = hold(rest, own)
        pair = stack_lines(z & 1, [rest, shift(rest, COLUMN[1])])
        other = shift(pair, COLUMN[2])
        rest = stack_lines(z >> 1, [pair, other]).reshape((4,) + rest.shape)
        plane = [own, *shift_plane([own] * 3)]
        self.own = plane + [shift(hold(piece, other), 2) for piece in plane]
        rest = hold(rest, plane[1])
        self.plane = [rest, *shift_plane([rest] * 3)]

    def cross(self, after):
        plane = [hold(piece, after) for piece in self.plane]
        return plane + [shift(piece, 2) for piece in plane]

    def feed_core(self, slots):
        return lax.psum_scatter(slots.reshape((2, 4, 4) + slots.shape[1:]), "core")

    def feed_plane(self, slots):
        return lax.psum_scatter(slots, ("y", "x"))

    def feed_column(self, slots):
        return lax.psum_scatter(slots, "z")


class Far:
    axes = ("wide", "narrow")
    me = 0

    def __init__(self, weights):
        weights = [lax.all_gather(w, self.axes, axis=0, tiled=True) for w in weights]
        self.take(weights)

    def take(self, weights):
        self.own = self.pieces(*weights[:3], small_row(weights[10:13], weights[13]))
        self.rest = self.pieces(*weights[3:8])
        self.feed = pack_feed(weights[8], weights[9])

    def pieces(self, *parts):
        blocks = jnp.concatenate(parts, axis=1).reshape(32, 16, -1)[jnp.array(CODES)]
        return [blocks[4 * t : 4 * t + 4] for t in range(8)]

    def cross(self, after):
        return self.rest

    def feed_core(self, slots):
        return slots

    feed_plane = feed_column = feed_core


def on_device(near, tokens, memory, cotangent, dec_segments, mem_segments, padding, buckets,
              *weights):
    way = (Near if near else Far)(weights)
    result, grad_tokens, grad_memory, grads, examples, square = local_part(
        way, tokens, memory, cotangent, dec_segments, mem_segments, padding, buckets
    )
    if near:
        sent = lax.all_to_all(square, FINE, 0, 0, tiled=True)
        global_norm = jnp.sum(sent[:, 0])
    else:
        grads = [lax.psum_scatter(g, way.axes, scatter_dimension=0, tiled=True) for g in grads]
        global_norm = lax.psum(sum(jnp.sum(g * g) for g in grads), way.axes)
    return (result, grad_tokens, grad_memory, *grads, examples, global_norm / COUNT)


def local_part(way, tokens, memory, cotangent, dec_segments, mem_segments, padding, buckets):
    seqs, length, width = tokens.shape
    mem_length = memory.shape[1]
    steps = seqs // STEP_ROWS
    small_steps = seqs // SMALL_ROWS
    dec, mem = seqs * length, seqs * mem_length
    step_dec = STEP_ROWS * length
    ff = 4 * width

    buckets = buckets[None]
    tokens2, memory2, cotangent2 = (
        array.reshape(-1, width) for array in (tokens, memory, cotangent)
    )
    dma = pltpu.SemaphoreType.DMA

    me = jnp.full((1,), way.me, jnp.int32)
    flops = 2 * dec * width * width

    input_a, qkv_a, prob_a, attended_a, self_w, gains = call(
        self_forward_kernel, small_steps, me, (tokens2,), (dec_segments, padding, buckets), way.own,
        (
            kept((dec, width), BF16),
            kept((dec, 3 * width), BF16),
            kept((seqs, PAIRS, length, 2 * length), BF16),
            kept((dec, width), BF16),
        ),
        (kept((4, 8, 16, 3 * width + LANES), BF16), kept((8, width), F32)),
        [pltpu.VMEM((PAIRS, length, 2 * length), F32), dma((8,))],
        6 * flops, ("iwww", "iiiiww"), (), SHARED_LIMIT,
    )
    middle, input_b, query_b, kv_b, prob_b, attended_b, after_cross, cross_w = call(
        cross_forward_kernel, steps, me, (tokens2, attended_a, memory2),
        (dec_segments, mem_segments, gains), way.cross(attended_a),
        (
            kept((dec, width), BF16),
            kept((dec, width), BF16),
            kept((dec, width), BF16),
            kept((mem, 2 * width), BF16),
            kept((seqs, PAIRS, mem_length, 2 * length), BF16),
            kept((dec, width), BF16),
            kept((dec, width), BF16),
        ),
        (kept((4, 8, 16, 5 * width), BF16),),
        [dma((8,))],
        10 * flops, ("iiiwww", "iiiiiiiw"), (), SHARED_LIMIT,
    )
    self_w, cross_w = self_w.reshape(width, -1), cross_w.reshape(width, -1)
    total, square = kept((1, width), F32), shape_of((steps, 4 * STEP_ROWS, LANES), F32)
    small_token = shape_of((small_steps, 8, length), F32)
    (result, branch_b, feed_slots, active, grad_hidden_c, input_c, branch_c, gain_c,
     square_c) = call(
        feed_kernel, ff // width, None, (),
        (after_cross, cotangent2, dec_segments, padding, gains), (way.feed,), (),
        (
            shape_of((dec, width), BF16),
            kept((dec, width), BF16),
            shape_of((32, 128, width), BF16),
            kept((dec, ff), BF16),
            kept((dec, ff), BF16),
            kept((dec, width), BF16),
            kept((dec, width), BF16),
            total,
            square,
        ),
        [
            pltpu.VMEM((32, 16, ff), BF16),
            pltpu.VMEM((32, 64, width), BF16),
            *[pltpu.VMEM((dec, width), BF16)] * 2,
            *[pltpu.VMEM((width, dec), BF16)] * 2,
            *[pltpu.VMEM((dec, ff), BF16)] * 2,
            pltpu.VMEM((32, 16, width), BF16),
            pltpu.VMEM((8, 64, width), BF16),
            *[pltpu.VMEM((dec, width), BF16)] * 2,
            dma((4, 2)),
            dma((9,)),
            dma((steps, 2)),
            dma((4, 2)),
            dma((2,)),
        ],
        24 * flops, ("wwwww", "aaaaaaaww"),
    )
    feed_sum = way.feed_core(feed_slots)
    slot = shape_of((16, 16, 5 * width), BF16)
    grad_query_b, grad_kv_b, branch_a, cross_low, cross_high, gain_b, square_b = call(
        cross_backward_kernel, steps, me,
        (branch_b, middle, memory2, attended_a, input_b, query_b, kv_b, prob_b, attended_b),
        (dec_segments, gains, Cut(cross_w, (width, width), 0, 1),
         Cut(cross_w, (width, width), 0, 4)), (),
        (
            kept((dec, width), BF16),
            kept((mem, 2 * width), BF16),
            kept((dec, width), BF16),
            square,
        ),
        (kept(slot.shape, BF16), slot, total),
        [pltpu.VMEM((width, 5 * width), F32), pltpu.VMEM((step_dec, width), BF16)],
        20 * flops, ("iiiiiiiiiwwww", "iiiwwwi"),
    )
    feed_sum = way.feed_plane(hold(feed_sum, grad_query_b))
    near = isinstance(way, Near)
    if near:
        sent = shift(cross_high, 2)
    slot = shape_of((16, 16, 3 * width + LANES), BF16)
    grad_qkv_a, grad_tokens, self_low, self_high, square_a, table_square = call(
        self_backward_kernel, steps, me, (branch_a, tokens2, input_a, qkv_a, prob_a),
        (dec_segments, buckets, gains, Cut(cross_w, (width, width), 0, 0),
         Cut(self_w, (width, 3 * width), 0, 0), gain_b, gain_c),
        (),
        (
            kept((dec, 3 * width), BF16),
            shape_of((dec, width), BF16),
            square,
            shape_of((steps, STEP_ROWS, 8, LANES), F32),
        ),
        (kept(slot.shape, BF16), slot),
        [
            pltpu.VMEM((width, 3 * width), F32),
            pltpu.VMEM((1, width), F32),
            pltpu.VMEM((width, LANES), F32),
            pltpu.VMEM((H, LANES), F32),
            pltpu.VMEM((step_dec, width), BF16),
            pltpu.VMEM((STEP_ROWS, H, 8, length), F32),
        ],
        17 * flops, ("iiiiiwwwwwww", "iiwwii"),
    )

    def grams(pairs, *after):
        (tokens_part,) = call(
            gram_kernel, small_steps, None, pairs, (dec_segments,), (), (small_token,), (), [],
            0, ("i" * len(pairs) + "w", "i"), after, SHARED_LIMIT,
        )
        return tokens_part

    def fill_self(*after):
        return grams((input_a, grad_qkv_a, attended_a, branch_a), *after)

    def fill_feed(*after):
        return grams((active, branch_c, grad_hidden_c, input_c), *after)

    def fill_rest(*after):
        return call(
            fill_kernel, small_steps, None,
            (memory2, grad_kv_b, input_b, grad_query_b, attended_b, branch_b),
            (mem_segments, dec_segments, Cut(cross_w, (width, 2 * width), 0, 1)), (),
            (
                shape_of((mem, width), BF16),
                shape_of((small_steps, 8, mem_length), F32),
                small_token,
            ),
            (), [], 0, ("i" * 6 + "www", "iii"), after, SHARED_LIMIT,
        )

    if near:
        self_sent = shift(self_high, 2)
        parts = pair_sum(((self_low, self_sent), (cross_low, sent)))
        crossed = shift_plane(parts[1:])
        grad_memory, token_m, token_b = fill_rest(parts[0])
        feed_sum = hold(feed_sum, token_b)
        token_c = fill_feed(token_b, feed_sum)
        feed_sum = way.feed_column(feed_sum)
        own, *rest = plane_sum([parts[0], *crossed], (token_c,))
        line_sent = shift_column(rest)
        token_a = fill_self(own)
        feed_sum = hold(feed_sum, token_a).reshape(128, width)
        grad_hidden, grad_back, square = small_call(
            feed_end_kernel, (feed_sum,), (token_a,),
            [shape_of((16, ff), F32), shape_of((64, width), F32), shape_of((8, LANES), F32)],
        )
        line = shape_of((slot.shape[1], width), F32)
        *parts, square = small_call(
            column_end_kernel, (own, *line_sent, square), (token_a,),
            [line] * 3 + [shape_of((16, LANES), F32)] + [line] * 5 + [shape_of((32, LANES), F32)],
        )
        self_grads, small, cross_grads = parts[:3], parts[3], parts[4:]
        token_a = hold(token_a, square)
    else:
        token_a, token_c = fill_self(), fill_feed()
        grad_memory, token_m, token_b = fill_rest()
        cross_sum = as_rows(jnp.concatenate([cross_low, cross_high]))
        self_sum = as_rows(jnp.concatenate([self_low, self_high]))
        cross_grads = [cross_sum[:, k * width : (k + 1) * width] for k in range(5)]
        self_grads = [self_sum[:, k * width : (k + 1) * width] for k in range(3)]
        small = self_sum[:, 3 * width :]
        grad_hidden, grad_back = unpack_feed(in_order(feed_sum).astype(F32))
        square = None
    grads = self_grads + cross_grads + [grad_hidden, grad_back]
    grads += [small[:, k] for k in range(3)]
    grads.append(small[:, 3].reshape(-1, 16)[:, :H].reshape(-1))

    def row_parts(parts, count):
        return parts[:, :count].reshape(seqs, -1)

    def by_example(part, segments):
        hits = segments[:, None, :] == lax.broadcasted_iota(jnp.int32, (1, NSEG, 1), 1)
        return jnp.sum(jnp.where(hits, part[:, None, :], 0.0), axis=-1)

    token_d = row_parts(token_a + token_b + token_c, SMALL_ROWS)
    examples = by_example(token_d, dec_segments)
    examples = examples + by_example(row_parts(token_m, SMALL_ROWS), mem_segments)
    squares = (square_a + square_b + square_c)[:, :, 0].reshape(seqs, NSEG)
    examples = examples + squares + table_square[..., :NSEG, 0].reshape(seqs, NSEG)
    return (
        result.reshape(tokens.shape),
        grad_tokens.reshape(tokens.shape),
        grad_memory.reshape(memory.shape),
        grads,
        examples / COUNT,
        square,
    )


def solution(mesh):
    near = tuple(mesh.shape.values()) == (16, 2)
    if near:
        mesh = jax.sharding.Mesh(mesh.devices.reshape(4, 2, 2, 2), FINE)
    axes = tuple(mesh.axis_names)
    rows = P(axes)
    arrays, weights, vectors = (P(axes, None, None),) * 3, (P(axes, None),) * 10, (rows,) * 4
    placed = arrays + (P(axes, None),) * 3 + (P(),) + weights + vectors
    return jax.shard_map(
        partial(on_device, near),
        mesh=mesh,
        in_specs=placed,
        out_specs=arrays + weights + vectors + (P(axes, None), P()),
        check_vma=False,
    )
```

```python
import math
from functools import partial

import jax
import jax.numpy as jnp
from jax import lax
from jax.experimental import pallas as pl
from jax.experimental.pallas import tpu as pltpu
from jax.sharding import PartitionSpec as P

H = 8
DH = 64
NB = 32
NSEG = 4
COUNT = 4196096
EPSILON = 1e-06
FLOOR = -1e30
F32 = jnp.float32
BF16 = jnp.bfloat16
PAIRS = H // 2
LANES = 128
STEP_ROWS = 4
SMALL_ROWS = 4
VMEM_LIMIT = 62 * 2**20
SHARED_LIMIT = 48 * 2**20

COLUMN = (0, 8, 16, 24)
PLANE = (0, 1, 4, 5)
CODES = tuple(2 * c + mask + z for c in (0, 1) for mask in PLANE for z in COLUMN)


def nn(left, right):
    return lax.dot_general(left, right, (((1,), (0,)), ((), ())), preferred_element_type=F32)


def nt(left, right):
    return lax.dot_general(left, right, (((1,), (1,)), ((), ())), preferred_element_type=F32)


def tn(left, right):
    return lax.dot_general(left, right, (((0,), (0,)), ((), ())), preferred_element_type=F32)


def inverse_root(values):
    return lax.rsqrt(jnp.mean(values * values, axis=-1, keepdims=True) + EPSILON)


def head_masks(values):
    low = (lax.broadcasted_iota(jnp.int32, (1, LANES), 1) < DH).astype(BF16)
    return values * low, values * (1 - low)


def head_pair(values):
    return jnp.concatenate(head_masks(values), axis=0)


def fold_pair(both, queries):
    own = jnp.concatenate([both[:DH, :queries], both[DH:, queries:]], axis=0)
    return own.astype(BF16).T


def block_rows(block):
    return pl.ds(pl.multiple_of(block * 16, 16), 16)


def start_copies(pairs, sems):
    copies = [pltpu.make_async_copy(*pair, sems.at[i]) for i, pair in enumerate(pairs)]
    for copy in copies:
        copy.start()
    return copies


def column_pairs(me_ref, pieces, weight_ref):
    return [
        (piece, weight_ref.at[:, (me_ref[0] ^ CODES[4 * t]) & 7]) for t, piece in enumerate(pieces)
    ]


def read_rows(grad_w, block):
    return grad_w[block_rows(block), :].astype(BF16)


def store_slots(me_ref, low_ref, high_ref, read):
    for k, code in enumerate(CODES):
        target = low_ref if k < 16 else high_ref
        target[k % 16] = read(me_ref[0] ^ code)


def softmax_columns(scores):
    shifted = jnp.exp(scores - jnp.max(scores, axis=0, keepdims=True))
    return (shifted * (1.0 / jnp.sum(shifted, axis=0, keepdims=True))).astype(BF16)


def step_rows(ref, step, count):
    whole = ref[...].astype(F32)
    rows = whole[:count]
    for s in range(1, whole.shape[0] // count):
        rows = jnp.where(step == s, whole[s * count : (s + 1) * count], rows)
    return rows


def token_columns(lines):
    pad = 8 - lines.shape[0] % 8
    return jnp.concatenate([lines] + [lines[:1]] * (pad % 8), axis=0).T


def member_lines(lines):
    count, length = lines.shape
    codes = jnp.concatenate([lines[r : r + 1] + float(NSEG * r) for r in range(count)], axis=1)
    places = lax.broadcasted_iota(jnp.int32, (NSEG * count, count * length), 0).astype(F32)
    return (codes == places).astype(F32).astype(BF16)


def same_sum(products, lines, columns, r):
    same = columns[:, r : r + 1] == lines[r : r + 1]
    return jnp.sum(jnp.where(same, products, 0.0), axis=0, keepdims=True)


def pipelined(items, *stages):
    state = {}
    for tick in range(len(items) + len(stages) - 1):
        for depth, stage in enumerate(stages):
            n = tick - depth
            if 0 <= n < len(items):
                state[n] = stage(items[n], state.get(n))


def row_pairs(count):
    return [(r, p) for r in range(count) for p in range(PAIRS)]


def gram(left):
    return nt(left, left)


def self_forward_kernel(me_ref, tokens_ref, dec_ref, padding_ref, buckets_ref, *refs):
    pieces, refs = refs[:8], refs[8:]
    input_ref, qkv_ref, prob_ref, attended_ref, weight_ref, gains_ref = refs[:6]
    bias_ref, sems = refs[6:]
    length = dec_ref.shape[1]
    width = tokens_ref.shape[1]

    @pl.when(pl.program_id(0) == 0)
    def _():
        for copy in start_copies(column_pairs(me_ref, pieces, weight_ref), sems):
            copy.wait()
        small_lines = weight_ref[:, :, :, 3 * width :].reshape(width, LANES)
        first = lax.broadcasted_iota(jnp.int32, (32, width), 1)
        pick = first == 16 * lax.broadcasted_iota(jnp.int32, (32, width), 0)
        small = nn(pick.astype(F32).astype(BF16), small_lines).astype(BF16)
        lane = lax.broadcasted_iota(jnp.int32, (LANES, width), 0)
        feature = lax.broadcasted_iota(jnp.int32, (LANES, width), 1)
        block = lax.broadcasted_iota(jnp.int32, (32, width), 0)
        lines = []
        for k in range(4):
            spread = nn(small, (lane == 16 * k + feature % 16).astype(F32).astype(BF16))
            lines.append(
                jnp.sum(jnp.where(block == first // 16, spread, 0.0), axis=0, keepdims=True)
            )
        gains_ref[...] = jnp.concatenate(lines + lines, axis=0)
        place = lax.broadcasted_iota(jnp.int32, (H, width), 1) % 16
        head = lax.broadcasted_iota(jnp.int32, (H, width), 0)
        table = jnp.where(place == head, lines[3], 0.0).astype(BF16)
        bucket = lax.broadcasted_iota(jnp.int32, (width, length), 0) // 16
        curves = nn(table, (bucket == buckets_ref[...]).astype(F32).astype(BF16))
        for h in range(H):
            curve = jnp.broadcast_to(curves[h : h + 1, :], (length, length))
            lanes = slice((h % 2) * length, (h % 2 + 1) * length)
            bias_ref[h // 2, :, lanes] = pltpu.roll(curve, 0, 1, stride=1, stride_axis=0)

    values = tokens_ref[...].astype(F32)
    normed = (values * inverse_root(values) * gains_ref[0:1, :]).astype(BF16)
    input_ref[...] = normed
    for first in range(0, 3 * width, 256):
        cols = slice(first, first + 256)
        qkv_ref[:, cols] = nn(
            normed, weight_ref[:, :, :, cols].reshape(width, 256)
        ).astype(BF16)

    step = pl.program_id(0)
    count = tokens_ref.shape[0] // length
    segments, real = step_rows(dec_ref, step, count), step_rows(padding_ref, step, count)
    segment_columns, real_columns = token_columns(segments), token_columns(real)
    key_i = lax.broadcasted_iota(jnp.int32, (length, length), 0)
    query_i = lax.broadcasted_iota(jnp.int32, (length, length), 1)

    masks = []
    for r in range(count):
        allowed = (segment_columns[:, r : r + 1] == segments[r : r + 1]) & (key_i <= query_i)
        allowed = allowed & ((real_columns[:, r : r + 1] > 0.0) | (key_i == query_i))
        mask = jnp.where(allowed, 0.0, FLOOR)
        masks.append(jnp.concatenate([mask, mask], axis=1))

    def part(item, k):
        r, p = item
        return qkv_ref[r * length : (r + 1) * length, k * width + p * LANES : k * width + (p + 1) * LANES]

    def scores(item, _):
        return nt(part(item, 1), head_pair(part(item, 0)))

    def weigh(item, score):
        r, p = item
        prob = softmax_columns(score + bias_ref[p] + masks[r])
        prob_ref[r, p] = prob
        return prob, part(item, 2).T

    def mix(item, given):
        r, p = item
        prob, value = given
        rows, lanes = slice(r * length, (r + 1) * length), slice(p * LANES, (p + 1) * LANES)
        attended_ref[rows, lanes] = fold_pair(nn(value, prob), length)

    pipelined(row_pairs(count), scores, weigh, mix)


def cross_forward_kernel(me_ref, tokens_ref, attended_a_ref, memory_ref, dec_ref, mem_ref,
                         gains_ref, *refs):
    pieces, refs = refs[:8], refs[8:]
    (middle_ref, input_ref, query_ref, kv_ref, prob_ref, attended_ref, after_ref, weight_ref,
     sems) = refs
    mem_length, length = mem_ref.shape[1], dec_ref.shape[1]
    width = tokens_ref.shape[1]

    @pl.when(pl.program_id(0) == 0)
    def _():
        for copy in start_copies(column_pairs(me_ref, pieces, weight_ref), sems):
            copy.wait()

    def weight(k):
        return weight_ref[:, :, :, k * width : (k + 1) * width].reshape(width, width)

    for k in range(2):
        kv_ref[:, k * width : (k + 1) * width] = nn(memory_ref[...], weight(k + 2)).astype(BF16)
    values = tokens_ref[...].astype(F32) + nn(attended_a_ref[...], weight(0))
    middle_ref[...] = values.astype(BF16)
    normed = (values * inverse_root(values) * gains_ref[1:2, :]).astype(BF16)
    input_ref[...] = normed
    query_ref[...] = nn(normed, weight(1)).astype(BF16)

    step = pl.program_id(0)
    count = tokens_ref.shape[0] // length
    segments = step_rows(dec_ref, step, count)
    mem_columns = token_columns(step_rows(mem_ref, step, count))

    masks = []
    for r in range(count):
        mask = jnp.where(mem_columns[:, r : r + 1] == segments[r : r + 1], 0.0, FLOOR)
        masks.append(jnp.concatenate([mask, mask], axis=1))

    def places(item):
        r, p = item
        rows, lanes = slice(r * length, (r + 1) * length), slice(p * LANES, (p + 1) * LANES)
        upper = slice(width + p * LANES, width + (p + 1) * LANES)
        return rows, slice(r * mem_length, (r + 1) * mem_length), lanes, upper

    def scores(item, _):
        rows, mem_rows, lanes, _ = places(item)
        return nt(kv_ref[mem_rows, lanes], head_pair(query_ref[rows, lanes]))

    def weigh(item, score):
        r, p = item
        _, mem_rows, _, upper = places(item)
        prob = softmax_columns(score + masks[r])
        prob_ref[r, p] = prob
        return prob, kv_ref[mem_rows, upper].T

    def mix(item, given):
        rows, _, lanes, _ = places(item)
        prob, value = given
        attended_ref[rows, lanes] = fold_pair(nn(value, prob), length)

    pipelined(row_pairs(count), scores, weigh, mix)
    after = values + nn(attended_ref[...], weight(4))
    after_ref[...] = after.astype(BF16)


def norm_back(values, gain, grad_normed):
    inverse = inverse_root(values)
    scaled = values * inverse
    upper = grad_normed * gain
    grad = inverse * (upper - scaled * jnp.mean(upper * scaled, axis=-1, keepdims=True))
    return grad, grad_normed * scaled


def gain_sums(terms, segments, total_ref, square_ref):
    sums = nn(member_lines(segments), terms.astype(BF16))
    total_ref[...] += jnp.sum(sums, axis=0, keepdims=True)
    square = jnp.sum(sums * sums, axis=1, keepdims=True)
    square_ref[...] = jnp.broadcast_to(square, square_ref.shape)


def feed_kernel(after_ref, cotangent_ref, dec_ref, padding_ref, gains_ref, gathered_ref,
                result_ref, branch_b_ref, slots_ref, total_ref, square_ref, token_ref, w_in_ref,
                w_out_ref, normed_ref, branch_ref, normed_flip, branch_flip, active_ref, grad_ref,
                in_slots, out_slots, result_tile, branch_tile, load_sems, sems, end_sems):
    part = pl.program_id(0)
    parts = pl.num_programs(0)
    count, length = dec_ref.shape
    dec, width = after_ref.shape
    ff = w_in_ref.shape[2]
    tile = STEP_ROWS * length
    tiles = [slice(t * tile, (t + 1) * tile) for t in range(dec // tile)]

    def loads(which):
        rows = pl.ds(pl.multiple_of(which * 16, 16), 16)
        cols = pl.ds(pl.multiple_of(which * width, width), width)
        blocks = pl.ds(which * 8, 8)
        pairs = (
            (gathered_ref.at[:, rows, :], w_in_ref.at[:, :, cols]),
            (gathered_ref.at[blocks, 64:, :], w_out_ref.at[blocks]),
        )
        return [
            pltpu.make_async_copy(*pair, load_sems.at[which, i]) for i, pair in enumerate(pairs)
        ]

    @pl.when(part == 0)
    def _():
        for which in range(ff // width):
            for copy in loads(which):
                copy.start()
        real = token_columns(padding_ref[...].astype(F32))
        for r in range(count):
            rows = slice(r * length, (r + 1) * length)
            branch_ref[rows, :] = (
                cotangent_ref[rows, :].astype(F32) * real[:, r : r + 1]
            ).astype(BF16)
        for rows in tiles:
            values = after_ref[rows, :].astype(F32)
            normed = (values * inverse_root(values) * gains_ref[2:3, :]).astype(BF16)
            normed_ref[rows, :] = normed
            normed_flip[:, rows] = normed.T
            branch_flip[:, rows] = branch_ref[rows, :].T

    for copy in loads(part):
        copy.wait()
    root = 0.7978845608028654
    half_width = width // 2
    for sub in range(2):
        first = pl.multiple_of(part * width + sub * half_width, half_width)
        cols = pl.ds(first, half_width)
        hidden = nn(normed_ref[...], w_in_ref[:, :, cols].reshape(width, half_width))
        square = hidden * hidden
        bent = jnp.tanh(hidden * (root + (root * 0.044715) * square))
        half = 0.5 + 0.5 * bent
        slope = hidden * (2.0 * root + (6.0 * root * 0.044715) * square)
        slope = half + half * (slope * (1.0 - half))
        active_ref[:, cols] = (hidden * half).astype(BF16)
        w_out = w_out_ref[pl.ds(part * 8 + sub * 4, 4)].reshape(half_width, width)
        grad_ref[:, cols] = (nt(branch_ref[...], w_out) * slope).astype(BF16)
    cols = pl.ds(pl.multiple_of(part * width, width), width)
    grad_in = nn(normed_flip[...], grad_ref[:, cols]).astype(BF16)
    grad_out = nn(branch_flip[...], active_ref[:, cols]).astype(BF16).T

    def sends(which):
        pairs = [(in_slots, slots_ref.at[:, pl.ds(pl.multiple_of(which * 16, 16), 16), :])]
        for i, k in enumerate(range(0, 32, 4)):
            pairs.append((out_slots.at[i], slots_ref.at[k + which, 64:, :]))
        return [pltpu.make_async_copy(*pair, sems.at[i]) for i, pair in enumerate(pairs)]

    @pl.when(part > 0)
    def _():
        for copy in sends(part - 1):
            copy.wait()

    for k, block in enumerate(CODES):
        in_slots[k] = grad_in[16 * block : 16 * block + 16]
    for i, k in enumerate(range(0, 32, 4)):
        block = CODES[k]
        out_slots[i] = grad_out[64 * block : 64 * block + 64]
    for copy in sends(part):
        copy.start()

    @pl.when(part == parts - 1)
    def _():
        segments = dec_ref[...].astype(F32)
        columns = token_columns(segments)
        total_ref[...] = jnp.zeros_like(total_ref)
        ends = []
        w_in, w_out = w_in_ref[...].reshape(width, ff), w_out_ref[...].reshape(ff, width)
        for t, rows in enumerate(tiles):
            values = after_ref[rows, :].astype(F32)
            result_tile[rows, :] = (values + nn(active_ref[rows, :], w_out)).astype(BF16)
            grad, terms = norm_back(values, gains_ref[2:3, :], nt(grad_ref[rows, :], w_in))
            branch_tile[rows, :] = (branch_ref[rows, :].astype(F32) + grad).astype(BF16)
            pairs = [(result_tile.at[rows], result_ref.at[rows])]
            pairs.append((branch_tile.at[rows], branch_b_ref.at[rows]))
            ends.extend(start_copies(pairs, end_sems.at[t]))
            own = segments[t * STEP_ROWS : (t + 1) * STEP_ROWS]
            gain_sums(terms, own, total_ref, square_ref.at[t])
        for r in range(count):
            own = slice(r * length, (r + 1) * length)
            products = gram(active_ref[own, :]) * gram(branch_ref[own, :])
            products = products + gram(grad_ref[own, :]) * gram(normed_ref[own, :])
            token_ref[r // STEP_ROWS, r % STEP_ROWS : r % STEP_ROWS + 1, :] = same_sum(
                products, segments, columns, r
            )
        for copy in sends(part) + ends:
            copy.wait()


def score_grads(prob, grad_prob):
    prob = prob.astype(F32)
    dots = jnp.sum(prob * grad_prob, axis=0, keepdims=True)
    return prob * (grad_prob - dots)


def cross_backward_kernel(me_ref, branch_ref, middle_ref, memory_ref, attended_a_ref, input_ref,
                          query_ref, kv_ref, prob_ref, attended_ref, dec_ref, gains_ref,
                          query_w_ref, out_w_ref, grad_query_ref, grad_kv_ref, branch_a_ref, low_ref, high_ref,
                          total_ref, square_ref, grad_w, grad_attended):
    step = pl.program_id(0)
    mem_length = prob_ref.shape[2]
    length = prob_ref.shape[3] // 2
    width = branch_ref.shape[1]

    @pl.when(step == 0)
    def _():
        grad_w[...] = jnp.zeros_like(grad_w)
        total_ref[...] = jnp.zeros_like(total_ref)

    branch = branch_ref[...]
    grad_attended[...] = nt(branch, out_w_ref[...]).astype(BF16)

    def places(item):
        r, p = item
        rows, lanes = slice(r * length, (r + 1) * length), slice(p * LANES, (p + 1) * LANES)
        upper = slice(width + p * LANES, width + (p + 1) * LANES)
        return rows, slice(r * mem_length, (r + 1) * mem_length), lanes, upper

    def enter(item, _):
        rows, mem_rows, lanes, upper = places(item)
        grad_out = head_pair(grad_attended[rows, lanes])
        return grad_out, nt(kv_ref[mem_rows, upper], grad_out)

    def bend(item, given):
        r, p = item
        grad_out, grad_prob = given
        _, mem_rows, lanes, _ = places(item)
        grad_score = score_grads(prob_ref[r, p], grad_prob).astype(BF16)
        return grad_out, grad_score, kv_ref[mem_rows, lanes].T

    def leave(item, given):
        r, p = item
        grad_out, grad_score, key = given
        rows, mem_rows, lanes, upper = places(item)
        query = head_pair(query_ref[rows, lanes])
        grad_kv_ref[mem_rows, lanes] = nn(grad_score, query).astype(BF16)
        grad_kv_ref[mem_rows, upper] = nn(prob_ref[r, p], grad_out).astype(BF16)
        grad_query_ref[rows, lanes] = fold_pair(nn(key, grad_score), length)

    pipelined(row_pairs(STEP_ROWS), enter, bend, leave)
    grad_query = grad_query_ref[...]
    grad_normed = nt(grad_query, query_w_ref[...])
    grad, terms = norm_back(middle_ref[...].astype(F32), gains_ref[1:2, :], grad_normed)
    branch_a = (branch.astype(F32) + grad).astype(BF16)
    branch_a_ref[...] = branch_a
    gain_sums(terms, step_rows(dec_ref, step, STEP_ROWS), total_ref, square_ref.at[0])
    grad_w[:, :width] += tn(attended_a_ref[...], branch_a)
    grad_w[:, width : 2 * width] += tn(input_ref[...], grad_query)
    grad_w[:, 2 * width : 4 * width] += tn(memory_ref[...], grad_kv_ref[...])
    grad_w[:, 4 * width :] += tn(attended_ref[...], branch)

    @pl.when(step == pl.num_programs(0) - 1)
    def _():
        store_slots(me_ref, low_ref, high_ref, partial(read_rows, grad_w))


def self_backward_kernel(me_ref, branch_ref, tokens_ref, input_ref, qkv_ref, prob_ref, dec_ref,
                         buckets_ref, gains_ref, out_w_ref, weight_ref, total_b_ref, total_c_ref,
                         grad_qkv_ref, grad_tokens_ref, low_ref, high_ref, square_ref,
                         table_square_ref, grad_w, total_ref, small_ref, table_ref, grad_attended,
                         bands):
    step = pl.program_id(0)
    length = prob_ref.shape[2]
    width = branch_ref.shape[1]
    grad_attended[...] = nt(branch_ref[...], out_w_ref[...]).astype(BF16)

    @pl.when(step == 0)
    def _():
        table_ref[...] = jnp.zeros_like(table_ref)
        bands[...] = jnp.zeros_like(bands)
        grad_w[...] = jnp.zeros_like(grad_w)
        total_ref[...] = jnp.zeros_like(total_ref)

    row_i = lax.broadcasted_iota(jnp.int32, (length, length), 0)
    col_i = lax.broadcasted_iota(jnp.int32, (length, length), 1)
    flip = (row_i + col_i == length - 1).astype(F32).astype(BF16)
    columns = token_columns(step_rows(dec_ref, step, STEP_ROWS)).astype(BF16)
    turned = nn(flip, columns)

    members = [
        [
            jnp.broadcast_to((turned[:, r : r + 1] == float(e)).astype(F32), (length, length))
            for e in range(NSEG)
        ]
        for r in range(STEP_ROWS)
    ]

    def part(item, k):
        r, p = item
        lanes = slice(k * width + p * LANES, k * width + (p + 1) * LANES)
        return slice(r * length, (r + 1) * length), lanes

    def enter(item, _):
        grad_out = head_pair(grad_attended[part(item, 0)])
        return grad_out, nt(qkv_ref[part(item, 2)], grad_out)

    def bend(item, given):
        r, p = item
        grad_out, grad_prob = given
        grad_score = score_grads(prob_ref[r, p], grad_prob).astype(BF16)
        return grad_out, grad_score, jnp.concatenate([qkv_ref[part(item, 1)].T, flip], axis=0)

    def leave(item, given):
        r, p = item
        grad_out, grad_score, key = given
        query = head_pair(qkv_ref[part(item, 0)])
        grad_qkv_ref[part(item, 1)] = nn(grad_score, query).astype(BF16)
        grad_qkv_ref[part(item, 2)] = nn(prob_ref[r, p], grad_out).astype(BF16)
        both = nn(key, grad_score)
        grad_qkv_ref[part(item, 0)] = fold_pair(both[:length], length)
        return both[length:]

    def count_buckets(item, turned_score):
        r, p = item
        for h in range(2):
            own = turned_score[:, h * length : (h + 1) * length]
            own = pltpu.roll(own, 1, 1, stride=1, stride_axis=0)
            for e in range(NSEG):
                bands[r, 2 * p + h, e : e + 1, :] = jnp.sum(
                    own * members[r][e], axis=0, keepdims=True
                )

    pipelined(row_pairs(STEP_ROWS), enter, bend, leave, count_buckets)
    bucket = lax.broadcasted_iota(jnp.int32, (LANES, length), 0)
    near = (bucket == buckets_ref[...]).astype(F32)
    flat = bands[...].reshape(STEP_ROWS * H * 8, length)
    per_bucket = lax.dot_general(
        flat, near, (((1,), (1,)), ((), ())), preferred_element_type=F32,
        precision=lax.Precision.HIGHEST,
    ).reshape(STEP_ROWS, H, 8, LANES)
    table_ref[...] += jnp.sum(jnp.sum(per_bucket, axis=0), axis=1)
    squares = jnp.sum(jnp.sum(per_bucket * per_bucket, axis=1), axis=-1, keepdims=True)
    table_square_ref[0] = jnp.broadcast_to(squares, (STEP_ROWS, 8, LANES))

    grad_qkv = grad_qkv_ref[...]
    grad_normed = nt(grad_qkv, weight_ref[...])
    grad, terms = norm_back(tokens_ref[...].astype(F32), gains_ref[0:1, :], grad_normed)
    grad_tokens_ref[...] = (branch_ref[...].astype(F32) + grad).astype(BF16)

    gain_sums(terms, step_rows(dec_ref, step, STEP_ROWS), total_ref, square_ref.at[0])
    flipped = input_ref[...].T
    for first in range(0, 3 * width, 256):
        grad_w[:, first : first + 256] += nn(flipped, grad_qkv_ref[:, first : first + 256])

    @pl.when(step == pl.num_programs(0) - 1)
    def _():
        bucket = lax.broadcasted_iota(jnp.int32, (LANES, width), 0)
        place = lax.broadcasted_iota(jnp.int32, (LANES, width), 1)
        spread = nn(table_ref[...].astype(BF16), (place // 16 == bucket).astype(F32).astype(BF16))
        head = lax.broadcasted_iota(jnp.int32, (H, width), 0)
        lane = lax.broadcasted_iota(jnp.int32, (H, width), 1)
        table = jnp.sum(jnp.where(lane % 16 == head, spread, 0.0), axis=0, keepdims=True)
        small = jnp.zeros((LANES, width), F32)
        row_i = lax.broadcasted_iota(jnp.int32, (LANES, width), 0)
        for k, line in enumerate((total_ref[...], total_b_ref[...], total_c_ref[...], table)):
            small = jnp.where(row_i == k, line, small)
        small_ref[...] = small.T

        def read(block):
            return jnp.concatenate(
                [read_rows(grad_w, block), read_rows(small_ref, block)], axis=1
            )

        store_slots(me_ref, low_ref, high_ref, read)


def pair_sum_kernel(*refs):
    groups, outs, buffers, total = (refs[:2], refs[2:4]), refs[4:8], refs[8:12], refs[12]
    load_sems, store_sems = refs[13:]
    places = [pl.ds(4 * t, 4) for t in range(4)]
    loads = []
    for i, ref in enumerate((*groups[0], *groups[1])):
        pairs = [(ref.at[p], buffers[i].at[p]) for p in places]
        loads.append(start_copies(pairs, load_sems.at[i]))
    stores = []
    for t, p in enumerate(places):
        start = 0
        for low, sent in ((0, 1), (2, 3)):
            loads[low][t].wait()
            loads[sent][t].wait()
            own = buffers[low][p].astype(F32) + buffers[sent][p].astype(F32)
            total[p, :, start : start + own.shape[2]] = own.astype(BF16)
            start += own.shape[2]
        stores.append(pltpu.make_async_copy(total.at[p], outs[t], store_sems.at[t]))
        stores[t].start()
    for store in stores:
        store.wait()


def pair_sum(groups):
    arrays = [array for group in groups for array in group]
    lanes = sum(low.shape[2] for low, _ in groups)
    shape = arrays[0].shape[:2] + (lanes,)
    return pl.pallas_call(
        pair_sum_kernel,
        out_shape=(shape_of((4,) + shape[1:], BF16),) * 4,
        in_specs=[pl.BlockSpec(memory_space=pl.ANY)] * 4,
        out_specs=[pl.BlockSpec(memory_space=pl.ANY)] * 4,
        scratch_shapes=[pltpu.VMEM(array.shape, BF16) for array in arrays]
        + [pltpu.VMEM(shape, BF16)]
        + [pltpu.SemaphoreType.DMA((4, 4)), pltpu.SemaphoreType.DMA((4,))],
        compiler_params=pltpu.CompilerParams(vmem_limit_bytes=SHARED_LIMIT),
    )(*[in_hbm(a) if i % 2 == 0 else a for i, a in enumerate(arrays)])


def plane_sum_kernel(a_ref, b_ref, c_ref, d_ref, own_ref, *outs):
    for s in range(4):
        total = a_ref[s].astype(F32) + b_ref[s].astype(F32)
        total = total + c_ref[s].astype(F32) + d_ref[s].astype(F32)
        if s == 0:
            own_ref[...] = total
        else:
            outs[s - 1][...] = total.astype(BF16)


def plane_sum(pieces, after):
    line = pieces[0].shape[1:]
    return small_call(
        plane_sum_kernel, pieces, after, (shape_of(line, F32),) + (shape_of(line, BF16),) * 3
    )


def square_sum(values):
    return jnp.sum(jnp.sum(values * values, axis=0, keepdims=True), axis=1, keepdims=True)


def feed_end_kernel(sum_ref, hidden_ref, back_ref, square_ref):
    total = sum_ref[...].astype(F32)
    width = total.shape[1]
    for j in range(4):
        hidden_ref[:, j * width : (j + 1) * width] = total[16 * j : 16 * (j + 1)]
    back_ref[...] = total[64:]
    square_ref[...] = jnp.broadcast_to(square_sum(total), square_ref.shape)


def column_end_kernel(own_ref, b_ref, c_ref, d_ref, *refs):
    squares, outs, square_ref = refs[:1], refs[1:-1], refs[-1]
    total = own_ref[...] + b_ref[...].astype(F32)
    total = total + c_ref[...].astype(F32) + d_ref[...].astype(F32)
    start = 0
    for out in outs:
        out[...] = total[:, start : start + out.shape[1]]
        start += out.shape[1]
    square = square_sum(total)
    for given in squares:
        square = square + given[0:1, 0:1]
    square_ref[...] = jnp.broadcast_to(square, square_ref.shape)


def staged(kernel, ins, outs):
    def run(*refs):
        count = ins + outs
        given, inner, sems = refs[:count], refs[count : 2 * count], refs[2 * count]
        for copy in start_copies(list(zip(given[:ins], inner[:ins])), sems):
            copy.wait()
        kernel(*inner)
        for copy in start_copies(list(zip(inner[ins:], given[ins:])), sems):
            copy.wait()

    return run


def small_call(kernel, ins, after, outs):
    arrays = [*ins, *outs]
    return pl.pallas_call(
        ignoring(staged(kernel, len(ins), len(outs)), len(ins), len(after)),
        out_shape=outs,
        in_specs=[pl.BlockSpec(memory_space=pl.ANY)] * (len(ins) + len(after)),
        out_specs=[pl.BlockSpec(memory_space=pl.ANY)] * len(outs),
        scratch_shapes=[pltpu.VMEM(array.shape, array.dtype) for array in arrays]
        + [pltpu.SemaphoreType.DMA((len(arrays),))],
        compiler_params=pltpu.CompilerParams(vmem_limit_bytes=SHARED_LIMIT),
    )(*ins, *after)


def stack_kernel(me_ref, *refs):
    lines, out_ref, sems = refs[:-2], refs[-2], refs[-1]
    pairs = [(line, out_ref.at[me_ref[0] ^ s]) for s, line in enumerate(lines)]
    for copy in start_copies(pairs, sems):
        copy.wait()


def stack_lines(place, lines):
    return pl.pallas_call(
        stack_kernel,
        out_shape=shape_of((len(lines),) + lines[0].shape, BF16),
        in_specs=[pl.BlockSpec(memory_space=pltpu.SMEM)]
        + [pl.BlockSpec(memory_space=pl.ANY)] * len(lines),
        out_specs=pl.BlockSpec(memory_space=pl.ANY),
        scratch_shapes=[pltpu.SemaphoreType.DMA((len(lines),))],
        compiler_params=pltpu.CompilerParams(vmem_limit_bytes=SHARED_LIMIT),
    )(jnp.full((1,), place, jnp.int32), *lines)


def pack_kernel(*refs):
    ins, (own_ref, cross_ref, feed_ref) = refs[:11], refs[11:]
    width = ins[0].shape[1]
    for k, line in enumerate((*ins[:3], ins[10])):
        own_ref[:, k * width : k * width + line.shape[1]] = line[...]
    for k in range(5):
        cross_ref[:, k * width : (k + 1) * width] = ins[3 + k][...]
    for j in range(ins[8].shape[1] // width):
        feed_ref[16 * j : 16 * (j + 1), :] = ins[8][:, j * width : (j + 1) * width]
    feed_ref[64:, :] = ins[9][...]


def pack(weights, small):
    width = weights[0].shape[1]
    outs = [shape_of((16, cols), BF16) for cols in (3 * width + LANES, 5 * width)]
    outs.append(shape_of((128, width), BF16))
    return small_call(pack_kernel, (*map(in_hbm, weights), small), (), outs)


def fill_kernel(memory_ref, grad_kv_ref, *refs):
    pairs, (mem_ref, dec_ref, weight_ref, grad_memory_ref, token_m_ref, token_ref) = (
        refs[:4], refs[4:]
    )
    mem_length, length = mem_ref.shape[1], dec_ref.shape[1]
    width = memory_ref.shape[1]
    for first in range(0, width, 256):
        rows = slice(first, first + 256)
        grad_memory_ref[:, rows] = nt(grad_kv_ref[...], weight_ref[rows, :]).astype(BF16)
    count = memory_ref.shape[0] // mem_length
    segments = step_rows(mem_ref, pl.program_id(0), count)
    columns = token_columns(segments)
    for r in range(count):
        rows = slice(r * mem_length, (r + 1) * mem_length)
        products = gram(memory_ref[rows, :]) * gram(grad_kv_ref[rows, :])
        token_m_ref[0, r : r + 1, :] = same_sum(products, segments, columns, r)
    gram_kernel(*pairs, dec_ref, token_ref)


def gram_kernel(*refs):
    pairs, dec_ref, token_ref = refs[:-2], refs[-2], refs[-1]
    length = dec_ref.shape[1]
    count = pairs[0].shape[0] // length
    segments = step_rows(dec_ref, pl.program_id(0), count)
    columns = token_columns(segments)
    for r in range(count):
        rows = slice(r * length, (r + 1) * length)
        products = sum(
            gram(left[rows, :]) * gram(right[rows, :])
            for left, right in zip(pairs[::2], pairs[1::2])
        )
        token_ref[0, r : r + 1, :] = same_sum(products, segments, columns, r)


def rows_spec(array, steps):
    shape = (array.shape[0] // steps,) + array.shape[1:]
    return pl.BlockSpec(shape, lambda i, *_: (i,) + (0,) * (len(shape) - 1))


class Cut:
    def __init__(self, array, shape, *index):
        self.array, self.spec = array, pl.BlockSpec(shape, lambda i, *_: index)


def whole_spec(array):
    return pl.BlockSpec(array.shape, lambda i, *_: (0,) * len(array.shape))


def in_hbm(array):
    return pltpu.with_memory_space_constraint(array, pltpu.HBM)


def ignoring(kernel, first, count):
    return lambda *refs: kernel(*refs[:first], *refs[first + count :])


def call(kernel, steps, me, blocked, whole, pieces, outs_blocked, outs_whole, scratch, flops,
         order, after=(), limit=VMEM_LIMIT):
    ins, in_specs = [], []
    blocked, whole = list(blocked), list(whole)
    for kind in order[0]:
        array = (blocked if kind == "i" else whole).pop(0)
        if isinstance(array, Cut):
            ins.append(array.array)
            in_specs.append(array.spec)
            continue
        ins.append(array)
        in_specs.append(rows_spec(array, steps) if kind == "i" else whole_spec(array))
    ins = [in_hbm(array) for array in ins]
    kernel = ignoring(kernel, len(ins) + len(pieces) + (me is not None), len(after))
    ins += [*pieces, *after]
    in_specs += [pl.BlockSpec(memory_space=pl.ANY)] * (len(pieces) + len(after))
    outs, out_specs = [], []
    outs_blocked, outs_whole = list(outs_blocked), list(outs_whole)
    for kind in order[1]:
        out = (outs_blocked if kind == "i" else outs_whole).pop(0)
        outs.append(out)
        if kind == "a":
            out_specs.append(pl.BlockSpec(memory_space=pl.ANY))
        else:
            out_specs.append(rows_spec(out, steps) if kind == "i" else whole_spec(out))
    moved = sum(math.prod(a.shape) * a.dtype.itemsize for a in ins + outs)
    prefetch = 0 if me is None else 1
    return pl.pallas_call(
        kernel,
        out_shape=outs,
        grid_spec=pltpu.PrefetchScalarGridSpec(
            num_scalar_prefetch=prefetch,
            grid=(steps,),
            in_specs=in_specs,
            out_specs=out_specs,
            scratch_shapes=scratch,
        ),
        compiler_params=pltpu.CompilerParams(
            dimension_semantics=("arbitrary",), vmem_limit_bytes=limit
        ),
        cost_estimate=pl.CostEstimate(flops=flops, bytes_accessed=moved, transcendentals=0),
    )(*(() if me is None else (me,)), *ins)


FINE = ("z", "y", "core", "x")


def shape_of(shape, dtype):
    return jax.ShapeDtypeStruct(shape, dtype)


def kept(shape, dtype):
    return pltpu.HBM(shape, dtype)


def shift(array, mask):
    return lax.ppermute(array, FINE, [(i, i ^ mask) for i in range(32)])


def hold(array, after):
    return lax.optimization_barrier((array, after))[0]


def pack_feed(hidden, back):
    width = back.shape[1]
    hidden = hidden.reshape(-1, 16, 4, width).transpose(0, 2, 1, 3).reshape(-1, 64, width)
    return jnp.concatenate([hidden, back.reshape(-1, 64, width)], axis=1)


def unpack_feed(blocks):
    width = blocks.shape[2]
    hidden = blocks[:, :64].reshape(-1, 4, 16, width).transpose(0, 2, 1, 3)
    return hidden.reshape(-1, 4 * width), blocks[:, 64:].reshape(-1, width)


def small_row(gains, table):
    table = jnp.pad(table.reshape(-1, H), ((0, 0), (0, 16 - H)))
    row = jnp.concatenate([gain.reshape(-1, 16) for gain in gains] + [table], axis=1)
    row = jnp.pad(row, ((0, 0), (0, LANES - row.shape[1])))
    return jnp.pad(row[:, None], ((0, 0), (0, 15), (0, 0))).reshape(-1, LANES)


def in_order(slots):
    return slots[jnp.array([CODES.index(block) for block in range(32)])]


def as_rows(slots):
    return in_order(slots).reshape(-1, slots.shape[2]).astype(F32)


def shift_plane(pieces):
    return [shift(piece, mask) for piece, mask in zip(pieces, PLANE[1:])]


def shift_column(pieces):
    return [shift(piece, code) for piece, code in zip(pieces, COLUMN[1:])]


class Near:
    axes = FINE

    def __init__(self, weights):
        self.me = lax.axis_index(FINE)
        small = small_row(weights[10:13], weights[13])
        own, rest, feed = pack(weights[:10], small)
        self.feed = lax.all_gather(feed, FINE, axis=0)
        z = self.me >> 3
        own = stack_lines(z, [own, *shift_column([own] * 3)])
        rest = hold(rest, own)
        pair = stack_lines(z & 1, [rest, shift(rest, COLUMN[1])])
        other = shift(pair, COLUMN[2])
        rest = stack_lines(z >> 1, [pair, other]).reshape((4,) + rest.shape)
        plane = [own, *shift_plane([own] * 3)]
        self.own = plane + [shift(hold(piece, other), 2) for piece in plane]
        rest = hold(rest, plane[1])
        self.plane = [rest, *shift_plane([rest] * 3)]

    def cross(self, after):
        plane = [hold(piece, after) for piece in self.plane]
        return plane + [shift(piece, 2) for piece in plane]

    def feed_core(self, slots):
        return lax.psum_scatter(slots.reshape((2, 4, 4) + slots.shape[1:]), "core")

    def feed_plane(self, slots):
        return lax.psum_scatter(slots, ("y", "x"))

    def feed_column(self, slots):
        return lax.psum_scatter(slots, "z")


class Far:
    axes = ("wide", "narrow")
    me = 0

    def __init__(self, weights):
        weights = [lax.all_gather(w, self.axes, axis=0, tiled=True) for w in weights]
        self.take(weights)

    def take(self, weights):
        self.own = self.pieces(*weights[:3], small_row(weights[10:13], weights[13]))
        self.rest = self.pieces(*weights[3:8])
        self.feed = pack_feed(weights[8], weights[9])

    def pieces(self, *parts):
        blocks = jnp.concatenate(parts, axis=1).reshape(32, 16, -1)[jnp.array(CODES)]
        return [blocks[4 * t : 4 * t + 4] for t in range(8)]

    def cross(self, after):
        return self.rest

    def feed_core(self, slots):
        return slots

    feed_plane = feed_column = feed_core


def on_device(near, tokens, memory, cotangent, dec_segments, mem_segments, padding, buckets,
              *weights):
    way = (Near if near else Far)(weights)
    result, grad_tokens, grad_memory, grads, examples, square = local_part(
        way, tokens, memory, cotangent, dec_segments, mem_segments, padding, buckets
    )
    if near:
        sent = lax.all_to_all(square, FINE, 0, 0, tiled=True)
        global_norm = jnp.sum(sent[:, 0])
    else:
        grads = [lax.psum_scatter(g, way.axes, scatter_dimension=0, tiled=True) for g in grads]
        global_norm = lax.psum(sum(jnp.sum(g * g) for g in grads), way.axes)
    return (result, grad_tokens, grad_memory, *grads, examples, global_norm / COUNT)


def local_part(way, tokens, memory, cotangent, dec_segments, mem_segments, padding, buckets):
    seqs, length, width = tokens.shape
    mem_length = memory.shape[1]
    steps = seqs // STEP_ROWS
    small_steps = seqs // SMALL_ROWS
    dec, mem = seqs * length, seqs * mem_length
    step_dec = STEP_ROWS * length
    ff = 4 * width

    buckets = buckets[None]
    tokens2, memory2, cotangent2 = (
        array.reshape(-1, width) for array in (tokens, memory, cotangent)
    )
    dma = pltpu.SemaphoreType.DMA

    me = jnp.full((1,), way.me, jnp.int32)
    flops = 2 * dec * width * width

    input_a, qkv_a, prob_a, attended_a, self_w, gains = call(
        self_forward_kernel, small_steps, me, (tokens2,), (dec_segments, padding, buckets), way.own,
        (
            kept((dec, width), BF16),
            kept((dec, 3 * width), BF16),
            kept((seqs, PAIRS, length, 2 * length), BF16),
            kept((dec, width), BF16),
        ),
        (kept((4, 8, 16, 3 * width + LANES), BF16), kept((8, width), F32)),
        [pltpu.VMEM((PAIRS, length, 2 * length), F32), dma((8,))],
        6 * flops, ("iwww", "iiiiww"), (), SHARED_LIMIT,
    )
    middle, input_b, query_b, kv_b, prob_b, attended_b, after_cross, cross_w = call(
        cross_forward_kernel, steps, me, (tokens2, attended_a, memory2),
        (dec_segments, mem_segments, gains), way.cross(attended_a),
        (
            kept((dec, width), BF16),
            kept((dec, width), BF16),
            kept((dec, width), BF16),
            kept((mem, 2 * width), BF16),
            kept((seqs, PAIRS, mem_length, 2 * length), BF16),
            kept((dec, width), BF16),
            kept((dec, width), BF16),
        ),
        (kept((4, 8, 16, 5 * width), BF16),),
        [dma((8,))],
        10 * flops, ("iiiwww", "iiiiiiiw"), (), SHARED_LIMIT,
    )
    self_w, cross_w = self_w.reshape(width, -1), cross_w.reshape(width, -1)
    total, square = kept((1, width), F32), shape_of((steps, 4 * STEP_ROWS, LANES), F32)
    token_shape = shape_of((steps, 8, length), F32)
    small_token = shape_of((small_steps, 8, length), F32)
    result, branch_b, feed_slots, gain_c, square_c, token_c = call(
        feed_kernel, ff // width, None, (),
        (after_cross, cotangent2, dec_segments, padding, gains), (way.feed,), (),
        (
            shape_of((dec, width), BF16),
            kept((dec, width), BF16),
            shape_of((32, 128, width), BF16),
            total,
            square,
            token_shape,
        ),
        [
            pltpu.VMEM((32, 16, ff), BF16),
            pltpu.VMEM((32, 64, width), BF16),
            *[pltpu.VMEM((dec, width), BF16)] * 2,
            *[pltpu.VMEM((width, dec), BF16)] * 2,
            *[pltpu.VMEM((dec, ff), BF16)] * 2,
            pltpu.VMEM((32, 16, width), BF16),
            pltpu.VMEM((8, 64, width), BF16),
            *[pltpu.VMEM((dec, width), BF16)] * 2,
            dma((4, 2)),
            dma((9,)),
            dma((steps, 2)),
        ],
        26 * flops, ("wwwww", "aaawww"),
    )
    feed_sum = way.feed_core(feed_slots)
    slot = shape_of((16, 16, 5 * width), BF16)
    grad_query_b, grad_kv_b, branch_a, cross_low, cross_high, gain_b, square_b = call(
        cross_backward_kernel, steps, me,
        (branch_b, middle, memory2, attended_a, input_b, query_b, kv_b, prob_b, attended_b),
        (dec_segments, gains, Cut(cross_w, (width, width), 0, 1),
         Cut(cross_w, (width, width), 0, 4)), (),
        (
            kept((dec, width), BF16),
            kept((mem, 2 * width), BF16),
            kept((dec, width), BF16),
            square,
        ),
        (kept(slot.shape, BF16), slot, total),
        [pltpu.VMEM((width, 5 * width), F32), pltpu.VMEM((step_dec, width), BF16)],
        20 * flops, ("iiiiiiiiiwwww", "iiiwwwi"),
    )
    feed_sum = way.feed_plane(hold(feed_sum, grad_query_b))
    near = isinstance(way, Near)
    if near:
        sent = shift(cross_high, 2)
    slot = shape_of((16, 16, 3 * width + LANES), BF16)
    grad_qkv_a, grad_tokens, self_low, self_high, square_a, table_square = call(
        self_backward_kernel, steps, me, (branch_a, tokens2, input_a, qkv_a, prob_a),
        (dec_segments, buckets, gains, Cut(cross_w, (width, width), 0, 0),
         Cut(self_w, (width, 3 * width), 0, 0), gain_b, gain_c),
        (),
        (
            kept((dec, 3 * width), BF16),
            shape_of((dec, width), BF16),
            square,
            shape_of((steps, STEP_ROWS, 8, LANES), F32),
        ),
        (kept(slot.shape, BF16), slot),
        [
            pltpu.VMEM((width, 3 * width), F32),
            pltpu.VMEM((1, width), F32),
            pltpu.VMEM((width, LANES), F32),
            pltpu.VMEM((H, LANES), F32),
            pltpu.VMEM((step_dec, width), BF16),
            pltpu.VMEM((STEP_ROWS, H, 8, length), F32),
        ],
        17 * flops, ("iiiiiwwwwwww", "iiwwii"),
    )

    def grams(pairs, *after):
        (tokens_part,) = call(
            gram_kernel, small_steps, None, pairs, (dec_segments,), (), (small_token,), (), [],
            2 * flops, ("i" * len(pairs) + "w", "i"), after, SHARED_LIMIT,
        )
        return tokens_part

    def fill_self(*after):
        return grams((input_a, grad_qkv_a, attended_a, branch_a), *after)

    def fill_rest(*after):
        return call(
            fill_kernel, small_steps, None,
            (memory2, grad_kv_b, input_b, grad_query_b, attended_b, branch_b),
            (mem_segments, dec_segments, Cut(cross_w, (width, 2 * width), 0, 1)), (),
            (
                shape_of((mem, width), BF16),
                shape_of((small_steps, 8, mem_length), F32),
                small_token,
            ),
            (), [], 12 * flops, ("i" * 6 + "www", "iii"), after, SHARED_LIMIT,
        )

    if near:
        self_sent = shift(self_high, 2)
        parts = pair_sum(((self_low, self_sent), (cross_low, sent)))
        crossed = shift_plane(parts[1:])
        grad_memory, token_m, token_b = fill_rest(parts[0])
        feed_sum = way.feed_column(hold(feed_sum, token_b))
        own, *rest = plane_sum([parts[0], *crossed], (token_m,))
        line_sent = shift_column(rest)
        token_a = fill_self(own)
        feed_sum = hold(feed_sum, token_a).reshape(128, width)
        grad_hidden, grad_back, square = small_call(
            feed_end_kernel, (feed_sum,), (token_a,),
            [shape_of((16, ff), F32), shape_of((64, width), F32), shape_of((8, LANES), F32)],
        )
        line = shape_of((slot.shape[1], width), F32)
        *parts, square = small_call(
            column_end_kernel, (own, *line_sent, square), (token_a,),
            [line] * 3 + [shape_of((16, LANES), F32)] + [line] * 5 + [shape_of((32, LANES), F32)],
        )
        self_grads, small, cross_grads = parts[:3], parts[3], parts[4:]
        token_a = hold(token_a, square)
    else:
        token_a = fill_self()
        grad_memory, token_m, token_b = fill_rest()
        cross_sum = as_rows(jnp.concatenate([cross_low, cross_high]))
        self_sum = as_rows(jnp.concatenate([self_low, self_high]))
        cross_grads = [cross_sum[:, k * width : (k + 1) * width] for k in range(5)]
        self_grads = [self_sum[:, k * width : (k + 1) * width] for k in range(3)]
        small = self_sum[:, 3 * width :]
        grad_hidden, grad_back = unpack_feed(in_order(feed_sum).astype(F32))
        square = None
    grads = self_grads + cross_grads + [grad_hidden, grad_back]
    grads += [small[:, k] for k in range(3)]
    grads.append(small[:, 3].reshape(-1, 16)[:, :H].reshape(-1))

    def row_parts(parts, count):
        return parts[:, :count].reshape(seqs, -1)

    def by_example(part, segments):
        hits = segments[:, None, :] == lax.broadcasted_iota(jnp.int32, (1, NSEG, 1), 1)
        return jnp.sum(jnp.where(hits, part[:, None, :], 0.0), axis=-1)

    token_d = row_parts(token_a + token_b, SMALL_ROWS) + row_parts(token_c, STEP_ROWS)
    examples = by_example(token_d, dec_segments)
    examples = examples + by_example(row_parts(token_m, SMALL_ROWS), mem_segments)
    squares = (square_a + square_b + square_c)[:, :, 0].reshape(seqs, NSEG)
    examples = examples + squares + table_square[..., :NSEG, 0].reshape(seqs, NSEG)
    return (
        result.reshape(tokens.shape),
        grad_tokens.reshape(tokens.shape),
        grad_memory.reshape(memory.shape),
        grads,
        examples / COUNT,
        square,
    )


def solution(mesh):
    near = tuple(mesh.shape.values()) == (16, 2)
    if near:
        mesh = jax.sharding.Mesh(mesh.devices.reshape(4, 2, 2, 2), FINE)
    axes = tuple(mesh.axis_names)
    rows = P(axes)
    arrays, weights, vectors = (P(axes, None, None),) * 3, (P(axes, None),) * 10, (rows,) * 4
    placed = arrays + (P(axes, None),) * 3 + (P(),) + weights + vectors
    return jax.shard_map(
        partial(on_device, near),
        mesh=mesh,
        in_specs=placed,
        out_specs=arrays + weights + vectors + (P(axes, None), P()),
        check_vma=False,
    )
```
